32 devices in a mesh: seg: 8 (over y, x, core), row: 4 (over z).
Axes of the slice: x: 2, y: 2, z: 4, core: 2. Of those that a mesh axis runs over, the one named last changes fastest.
Arguments:
- fill_blocks: int32 [16, 4], P('seg'), may hold values from 0 to 7, all different within a row
- fill_mask: int32 [16, 4], P('seg'), may hold values 0 or 1
- inv_diag: float32 [16, 512, 512], P('seg'), as said below
- factor_off: float32 [16, 256, 512], P('seg', 'row'), may hold values from -1.4375 to 1.4375
Outputs:
- cov_diag: float32 [16, 512, 512], P('seg', 'row')
- cov_off: float32 [16, 256, 512], P('seg', 'row')
The draws below stay inside these ranges and needn't reach their ends.
Inputs may be any that keep to these rules, and one draw needn't show every extreme that they name: The 4 entries of a row of fill_blocks are different. Each inv_diag[k] is lower triangular with a positive diagonal.
All inputs are finite; a program needn't handle non-finite values. No bound on the sum of `fill_mask` on one device may be relied on, other than what follows from the above.
Results may differ from the reference program's by a relative error of at most 0.0003.
Values sent between devices are 32-bit elements; how exact they have to be, the bound alone decides.
No kernel may reach another device: no remote copies, remote signals or barrier semaphores. Data moves between devices by JAX's collectives and lax.ppermute only.
A program may use at most 64 MiB of HBM per device.

```python
import jax
import jax.numpy as jnp
from jax import lax

BLOCK = 64
W = 512
FILL = 4
K = 16
FILL_ROWS = 256


def draw_inv_diag(key, part):
    key_scale, key_noise = jax.random.split(jax.random.fold_in(key, 17))
    rows_at = lax.broadcasted_iota(jnp.int32, (W, W), 0)
    cols_at = lax.broadcasted_iota(jnp.int32, (W, W), 1)
    spread = jnp.exp(jax.random.uniform(key_scale, (K, 1, W), jnp.float32, jnp.log(0.14), jnp.log(0.28)))
    noise = jax.random.normal(key_noise, (K, W, W), jnp.float32)
    lower_part = noise * spread * (0.3 / W ** 0.5)
    result = jnp.where(rows_at == cols_at, spread, jnp.where(rows_at > cols_at, lower_part, 0.0))
    return result.astype(jnp.float32)


def draw_factor_off(key, part):
    key_noise = jax.random.fold_in(key, 29)
    sigma = 5.04 / FILL_ROWS ** 0.5
    values = jnp.clip(jax.random.normal(key_noise, (K, FILL_ROWS, W), jnp.float32) * sigma, -4.5 * sigma, 4.5 * sigma)
    return values.astype(jnp.float32)


def place_ends(values, rng, least, high):
    shape = values.shape
    index_at = [jax.random.randint(jax.random.fold_in(rng, axis), (), 0, shape[axis]) for axis in range(len(shape))]
    values = values.at[tuple(index_at)].set(least)
    longest = shape.index(max(shape))
    index_at[longest] = (index_at[longest] + 1) % shape[longest]
    return values.at[tuple(index_at)].set(high)


def different_ones(stream_key, rows, number_of, top, lift):
    order = jax.random.permutation(jax.random.fold_in(stream_key, 1), number_of)
    pull = order
    for power in range(3):
        pull = pull * pull // number_of
    pull = pull * lift // number_of
    lots = jax.random.randint(jax.random.fold_in(stream_key, 2), (rows, number_of), 0, 4096) + pull
    sure = jax.random.permutation(jax.random.fold_in(stream_key, 3), rows)[jnp.arange(number_of) % rows]
    lots = jnp.where(jnp.arange(rows)[:, None] == sure[None, :], 1 << 14, lots)
    score = lots * number_of + jnp.arange(number_of)
    return lax.top_k(score.astype(jnp.int32), top)[1].astype(jnp.int32)


def setup_inputs(seed: int = 0) -> dict:
    seeds = jax.random.split(jax.random.key(seed), 5)
    fill_blocks = different_ones(seeds[0], K, W // BLOCK, FILL, 0)
    fill_mask = place_ends((jax.random.randint(seeds[1], (K, FILL), 0, 8) < 7).astype(jnp.int32), jax.random.fold_in(seeds[1], 1), 0, 1)
    inv_diag = draw_inv_diag(jax.random.fold_in(seeds[4], 71), 0)
    factor_off = draw_factor_off(jax.random.fold_in(seeds[4], 71), 0)
    return {"fill_blocks": fill_blocks, "fill_mask": fill_mask, "inv_diag": inv_diag, "factor_off": factor_off}


def product(left, right):
    return jnp.dot(left, right, precision=lax.Precision.HIGHEST, preferred_element_type=jnp.float32)


def select_blocks(matrix, chosen_blocks):
    row_blocks = matrix.shape[0] // BLOCK
    col_blocks = matrix.shape[1] // BLOCK
    tiles = matrix.reshape(row_blocks, BLOCK, col_blocks, BLOCK)
    tiles = jnp.take(tiles, chosen_blocks, axis=0)
    tiles = jnp.take(tiles, chosen_blocks, axis=2)
    count = chosen_blocks.shape[0] * BLOCK
    return tiles.reshape(count, count)


def reference(fill_blocks, fill_mask, inv_diag, factor_off):
    panels = inv_diag.shape[0]
    slot_live = fill_mask.astype(jnp.float32)
    not_last = (jnp.arange(panels) < panels - 1).astype(jnp.float32)
    row_keep = jnp.repeat(slot_live * not_last[:, None], BLOCK, axis=1)
    slot_keep = jnp.repeat(slot_live, BLOCK, axis=1)
    before_fill = jnp.concatenate([fill_blocks[:1], fill_blocks[:-1]], 0)

    def advance(carried, inputs):
        inverse, factor, keep_rows, keep_slots, earlier_fill = inputs
        factor_map = product(factor * keep_rows[:, None], inverse)
        weighted = product(carried, factor_map)
        prior_term = product(inverse.T, inverse)
        covariance = prior_term + product(factor_map.T, weighted)
        cross_cov = -weighted * keep_slots[:, None]
        following = select_blocks(covariance, earlier_fill)
        return following, (covariance, cross_cov)

    starting = jnp.zeros((FILL_ROWS, FILL_ROWS), jnp.float32)
    finished, outputs = lax.scan(advance, starting, (inv_diag, factor_off, row_keep, slot_keep, before_fill), reverse=True)
    return outputs[0], outputs[1]
```

```python
import functools

import jax
import jax.numpy as jnp
from jax import lax
from jax.experimental import pallas as pl
from jax.experimental.pallas import tpu as pltpu
from jax.sharding import PartitionSpec as P

BLOCK = 64
LANES = 128
F32 = jnp.float32
BF16 = jnp.bfloat16
NN = (((1,), (0,)), ((), ()))
NT = (((1,), (1,)), ((), ()))
TN = (((0,), (0,)), ((), ()))


def split(x):
    high = x.astype(BF16)
    return high, (x - high.astype(F32)).astype(BF16)


def mm(a, b, dims=NN):
    a = a if isinstance(a, tuple) else split(a)
    b = b if isinstance(b, tuple) else split(b)
    dot = functools.partial(lax.dot_general, dimension_numbers=dims, preferred_element_type=F32)
    return dot(a[0], b[0]) + (dot(a[0], b[1]) + dot(a[1], b[0]))


def carry(link_t, cov, base):
    link_t = link_t if isinstance(link_t, tuple) else split(link_t)
    return mm(mm(link_t, cov), link_t, NT) + base


def pack(cov):
    half = cov.shape[0] // 2
    return jnp.concatenate([cov[:half, :half], cov[:half, half:], cov[half:, half:]], 0)


def unpack(packed):
    half = packed.shape[0] // 3
    first, cross, second = packed[:half], packed[half : 2 * half], packed[2 * half :]
    top = jnp.concatenate([first, cross], 1)
    bottom = jnp.concatenate([cross.T, second], 1)
    return jnp.concatenate([top, bottom], 0)


def two_blocks(load, left, right):
    def placed(block, half):
        slab = load(lax.shift_right_logical(block, 1))
        return jnp.where((block & 1) == half, slab, pltpu.roll(slab, BLOCK, 1))

    a, b = placed(left, 0), placed(right, 1)
    lane = lax.broadcasted_iota(jnp.int32, a.shape, 1)
    return jnp.where(lane < BLOCK, a, b)


def tile_of(ref, *lead):
    def load(tile):
        return ref[(*lead, slice(None), pl.ds(pl.multiple_of(tile * LANES, LANES), LANES))]

    return load


def chosen_of(fill_ref, prior_ref, panel):
    slots = fill_ref.shape[1]
    if panel > 0:
        return [fill_ref[panel - 1, j] for j in range(slots)]
    first = lax.axis_index("seg") == 0
    return [jnp.where(first, fill_ref[0, j], prior_ref[0, j]) for j in range(slots)]


def order_of(chosen, blocks):
    slots = len(chosen)
    rest = [jnp.int32(0)] * (blocks - slots)
    place = []
    seen = jnp.int32(0)
    for b in range(blocks):
        hit = jnp.int32(0)
        where = jnp.int32(0)
        for j in range(slots):
            same = (chosen[j] == b).astype(jnp.int32)
            hit = hit + same
            where = where + same * j
        free = 1 - hit
        for q in range(blocks - slots):
            rest[q] = rest[q] + jnp.where(seen == q, free * b, 0)
        place.append(jnp.where(hit > 0, where, slots + seen))
        seen = seen + free
    return rest, place


def vmem(count):
    return [pl.BlockSpec(memory_space=pltpu.VMEM)] * count


def smem(count):
    return [pl.BlockSpec(memory_space=pltpu.SMEM)] * count


def call(kernel, outs, scalars, arrays, scratch=(), flops=0, mib=16, name=None):
    moved = sum(a.size * 4 for a in arrays) + sum(o.size * 4 for o in outs)
    return pl.pallas_call(
        kernel,
        out_shape=outs,
        in_specs=smem(len(scalars)) + vmem(len(arrays)),
        out_specs=vmem(len(outs)),
        scratch_shapes=list(scratch),
        cost_estimate=pl.CostEstimate(flops=flops, bytes_accessed=moved, transcendentals=0),
        compiler_params=pltpu.CompilerParams(vmem_limit_bytes=mib << 20),
        name=name,
    )(*scalars, *arrays)


def shape(*dims):
    return jax.ShapeDtypeStruct(dims, F32)


def local_map_kernel(mask_ref, factor_ref, inv_ref, map_ref):
    panels, rows, _ = factor_ref.shape
    seg_at, seg_count = lax.axis_index("seg"), lax.axis_size("seg")
    slots = rows // BLOCK
    row_at = lax.axis_index("row")
    for p in range(panels):
        alive = (seg_at * panels + p < seg_count * panels - 1).astype(F32)
        kept = []
        for s in range(slots):
            keep = mask_ref[p, row_at * slots + s].astype(F32) * alive
            kept.append(factor_ref[p, s * BLOCK : (s + 1) * BLOCK, :] * keep)
        kept = kept[0] if slots == 1 else jnp.concatenate(kept, 0)
        map_ref[p] = mm(kept, inv_ref[p])


def column_split_kernel(fill_ref, prior_ref, map_ref, link_ref, rest_ref):
    panels = map_ref.shape[0]
    blocks = map_ref.shape[2] // BLOCK
    for p in range(panels):
        chosen = chosen_of(fill_ref, prior_ref, p)
        rest, _ = order_of(chosen, blocks)
        for out_ref, wanted in ((link_ref, chosen), (rest_ref, rest)):
            for t in range(len(wanted) // 2):
                out_ref[p, :, t * LANES : (t + 1) * LANES] = two_blocks(
                    tile_of(map_ref, p), wanted[2 * t], wanted[2 * t + 1]
                )


def prior_kernel(fill_ref, prior_ref, inv_ref, base_ref, own_ref):
    panels = inv_ref.shape[0]
    own_cols = own_ref.shape[1]
    row_at = lax.axis_index("row")
    for p in range(panels):
        chosen = chosen_of(fill_ref, prior_ref, p)
        picked = split(
            jnp.concatenate(
                [
                    two_blocks(tile_of(inv_ref, p), chosen[2 * t], chosen[2 * t + 1])
                    for t in range(len(chosen) // 2)
                ],
                1,
            )
        )
        base_ref[p] = mm(picked, picked, TN)
        own = inv_ref[p, :, pl.ds(pl.multiple_of(row_at * own_cols, own_cols), own_cols)]
        own_ref[p] = mm(own, inv_ref[p], TN)


def segment_kernel(row_count, *refs):
    parts = refs[:row_count]
    base_ref, links_ref, links_t_ref, whole_ref = refs[row_count:]
    panels, rows, _ = parts[0].shape
    size = base_ref.shape[1]
    row_at = lax.axis_index("row")
    for d, part in enumerate(parts):
        at = lax.rem(row_at + (row_count - d), row_count) * rows
        links_ref[:, pl.ds(pl.multiple_of(at, rows), rows), :] = part[...]
    cov = base_ref[panels - 1]
    link_t = links_ref[panels - 1].T
    links_t_ref[panels - 1] = link_t
    for p in range(panels - 2, -1, -1):
        own_t = links_ref[p].T
        links_t_ref[p] = own_t
        own_t = split(own_t)
        cov = carry(own_t, cov, base_ref[p])
        link_t = mm(own_t, link_t)
    whole_ref[:size] = link_t
    whole_ref[size:] = cov


def chip_kernel(own_ref, other_ref, link_t_ref, cov_ref, packed_ref):
    size = cov_ref.shape[0]
    lower = (lax.axis_index("seg") & 1) == 0
    own, other = own_ref[...], other_ref[...]
    down = jnp.where(lower, own, other)
    up = jnp.where(lower, other, own)
    down_t = split(down[:size])
    cov = carry(down_t, up[size:], down[size:])
    link_t_ref[...] = mm(down_t, up[:size])
    cov_ref[...] = cov
    packed_ref[...] = pack(cov)


def extend_kernel(link_t_ref, cov_ref, after_ref, packed_ref):
    packed_ref[...] = pack(carry(link_t_ref[...], unpack(after_ref[...]), cov_ref[...]))


def extend_link_kernel(link_t_ref, after_t_ref, out_ref):
    out_ref[...] = mm(link_t_ref[...], after_t_ref[...])


def join_kernel(level, past_t_ref, past_ref, link_t_ref, cov_ref, out_t_ref, out_ref):
    chip = lax.axis_index("seg") // 2
    below = (lax.shift_right_logical(chip, level) & 1) == 0
    known = (chip & ((1 << level) - 1)) != (1 << level) - 1
    past_t, past = past_t_ref[...], past_ref[...]
    link_t, cov = link_t_ref[...], cov_ref[...]
    past_parts = split(past_t)
    joined = pack(carry(past_parts, unpack(cov), unpack(past)))
    joined_t = mm(past_parts, link_t)
    out_t_ref[...] = jnp.where(below, jnp.where(known, joined_t, link_t), past_t)
    out_ref[...] = jnp.where(below, jnp.where(known, joined, cov), past)


def prepare_kernel(
    has_past, fill_ref, prior_ref, links_ref, links_t_ref, rest_ref, base_ref, own_ref,
    other_ref, *refs
):
    if has_past:
        past_t_ref, past_ref = refs[:2]
        refs = refs[2:]
    left_ref, right_ref, const_ref, scratch = refs
    panels, size, _ = links_ref.shape
    own_cols = own_ref.shape[1]
    width = own_ref.shape[2]
    blocks = width // BLOCK
    row_count = lax.axis_size("row")
    row_at = lax.axis_index("row")
    rows = size // row_count
    seg_at = lax.axis_index("seg")
    chip_last = lax.axis_size("seg") // 2 - 1
    top = 1 << max(chip_last.bit_length() - 1, 0)
    at_row = lax.broadcasted_iota(jnp.int32, (size, size), 0)
    at_col = lax.broadcasted_iota(jnp.int32, (size, size), 1)
    eye = (at_row == at_col).astype(F32)
    if has_past:
        chip = seg_at // 2
        known = (chip & (top - 1)) != top - 1
        to_t = jnp.where(known, past_t_ref[...], eye)
        gain = unpack(past_ref[...])
    else:
        to_t = eye
        gain = jnp.zeros((size, size), F32)
    lower = (seg_at & 1) == 0
    other_t = split(other_ref[:size, :])
    to_t = jnp.where(lower, mm(other_t, to_t), to_t)
    gain = jnp.where(lower, carry(other_t, gain, other_ref[size:, :]), gain)
    for p in range(panels - 1, -1, -1):
        chosen = chosen_of(fill_ref, prior_ref, p)
        _, place = order_of(chosen, blocks)
        scratch[:, :size] = links_ref[p]
        scratch[:, size:] = rest_ref[p]
        whole = jnp.concatenate(
            [
                two_blocks(tile_of(scratch), place[2 * t], place[2 * t + 1])
                for t in range(blocks // 2)
            ],
            1,
        )
        scratch[...] = whole
        own_map = scratch[:, pl.ds(pl.multiple_of(row_at * own_cols, own_cols), own_cols)]
        own_t = split(own_map.T)
        whole = split(whole)
        scratch[:, :size] = to_t
        scratch[:, size:] = gain
        own_rows = pl.ds(pl.multiple_of(row_at * rows, rows), rows)
        to_parts = split(to_t)
        left_ref[p, :rows, :] = scratch[own_rows, :size]
        left_ref[p, rows:, :] = mm(own_t, to_parts)
        right_ref[p] = mm(to_parts, whole, TN)
        gains = jnp.concatenate([scratch[own_rows, size:], mm(own_t, gain)], 0)
        const = mm(gains, whole)
        const_ref[p, :rows, :] = const[:rows]
        const_ref[p, rows:, :] = const[rows:] + own_ref[p]
        if p > 0:
            link_t = split(links_t_ref[p])
            to_t = mm(link_t, to_t)
            gain = carry(link_t, gain, base_ref[p])


def finish_kernel(mask_ref, after_ref, left_ref, right_ref, const_ref, diag_ref, off_ref):
    panels, total, _ = left_ref.shape
    rows = off_ref.shape[1]
    slots = rows // BLOCK
    row_at = lax.axis_index("row")
    after = split(unpack(after_ref[...]))
    for p in range(panels):
        result = mm(mm(left_ref[p], after), right_ref[p]) + const_ref[p]
        diag_ref[p] = result[rows:]
        for s in range(slots):
            keep = mask_ref[p, row_at * slots + s].astype(F32)
            off_ref[p, s * BLOCK : (s + 1) * BLOCK, :] = -result[s * BLOCK : (s + 1) * BLOCK] * keep


def body(fill_blocks, fill_mask, inv_diag, factor_off):
    panels, width, _ = inv_diag.shape
    rows = factor_off.shape[1]
    seg_count = lax.axis_size("seg")
    row_count = lax.axis_size("row")
    size = rows * row_count
    own_cols = width // row_count
    slots = fill_blocks.shape[1]
    chosen_cols = slots * BLOCK
    rest_cols = width - chosen_cols
    chips = seg_count // 2

    prior_fill = lax.ppermute(
        fill_blocks[panels - 1 :], "seg", [(i, i + 1) for i in range(seg_count - 1)]
    )
    (local_map,) = call(
        local_map_kernel,
        [shape(panels, rows, width)],
        [fill_mask],
        [factor_off, inv_diag],
        flops=6 * panels * rows * width * width,
        name="local_map",
    )
    link_own, rest_own = call(
        column_split_kernel,
        [shape(panels, rows, chosen_cols), shape(panels, rows, rest_cols)],
        [fill_blocks, prior_fill],
        [local_map],
        name="column_split",
    )
    parts = [link_own] + [
        lax.ppermute(link_own, "row", [(i, (i + d) % row_count) for i in range(row_count)])
        for d in range(1, row_count)
    ]
    base, own_prior = call(
        prior_kernel,
        [shape(panels, chosen_cols, chosen_cols), shape(panels, own_cols, width)],
        [fill_blocks, prior_fill],
        [inv_diag],
        flops=6 * panels * width * (chosen_cols * chosen_cols + own_cols * width),
        mib=24,
        name="prior",
    )
    links, links_t, own_whole = call(
        functools.partial(segment_kernel, row_count),
        [shape(panels, size, size), shape(panels, size, size), shape(2 * size, size)],
        [],
        parts + [base],
        flops=18 * (panels - 1) * size**3,
        name="segment",
    )
    rest = lax.all_gather(rest_own, "row", axis=1, tiled=True)
    other_whole = lax.ppermute(own_whole, "seg", [(i, i ^ 1) for i in range(seg_count)])
    half = size // 2
    link_t, cov, packed = call(
        chip_kernel,
        [shape(size, size), shape(size, size), shape(3 * half, half)],
        [],
        [own_whole, other_whole],
        flops=18 * size**3,
        name="chip",
    )
    past = None
    send, send_t = packed, link_t
    after = jnp.zeros((3 * half, half), F32)
    levels = (chips - 1).bit_length()
    for level in range(levels):
        bit = 1 << level
        if level > 0:
            (send,) = call(
                extend_kernel, [shape(3 * half, half)], [], [link_t, cov, past[1]],
                flops=12 * size**3, name="extend",
            )
            if level < levels - 1:
                (send_t,) = call(
                    extend_link_kernel, [shape(size, size)], [], [link_t, past[0]],
                    flops=6 * size**3, name="extend_link",
                )
        got = got_t = None
        for step in range(bit):
            route = [
                (2 * (base_chip + bit) + core, 2 * (base_chip + step) + core)
                for base_chip in range(0, chips, 2 * bit)
                for core in range(2)
            ]
            piece = lax.ppermute(send, "seg", route)
            got = piece if got is None else got + piece
            if level < levels - 1:
                piece_t = lax.ppermute(send_t, "seg", route)
                got_t = piece_t if got_t is None else got_t + piece_t
        if level == levels - 1:
            after = got
        elif past is None:
            past = (got_t, got)
        else:
            past = call(
                functools.partial(join_kernel, level),
                [shape(size, size), shape(3 * half, half)],
                [],
                [past[0], past[1], got_t, got],
                flops=18 * size**3,
                name="join",
            )
    total = rows + own_cols
    left, right, const = call(
        functools.partial(prepare_kernel, past is not None),
        [shape(panels, total, size), shape(panels, size, width), shape(panels, total, width)],
        [fill_blocks, prior_fill],
        [links, links_t, rest, base, own_prior, other_whole, *(past or ())],
        scratch=[pltpu.VMEM((size, width), F32)],
        flops=6 * panels * size * (total * size + size * width + total * width + 3 * size * size),
        mib=24,
        name="prepare",
    )
    diag, off = call(
        finish_kernel,
        [shape(panels, own_cols, width), shape(panels, rows, width)],
        [fill_mask],
        [after, left, right, const],
        flops=6 * panels * total * size * (size + width),
        name="finish",
    )
    return diag, off


def solution(mesh):
    placed = (P("seg", None), P("seg", None), P("seg", None, None), P("seg", "row", None))
    return jax.shard_map(
        body,
        mesh=mesh,
        in_specs=placed,
        out_specs=(P("seg", "row", None), P("seg", "row", None)),
        check_vma=False,
    )
```

```python
import functools

import jax
import jax.numpy as jnp
from jax import lax
from jax.experimental import pallas as pl
from jax.experimental.pallas import tpu as pltpu
from jax.sharding import PartitionSpec as P

BLOCK = 64
LANES = 128
F32 = jnp.float32
BF16 = jnp.bfloat16
NN = (((1,), (0,)), ((), ()))
NT = (((1,), (1,)), ((), ()))
TN = (((0,), (0,)), ((), ()))


def split(x):
    high = x.astype(BF16)
    return high, (x - high.astype(F32)).astype(BF16)


def mm(a, b, dims=NN):
    a = a if isinstance(a, tuple) else split(a)
    b = b if isinstance(b, tuple) else split(b)
    dot = functools.partial(lax.dot_general, dimension_numbers=dims, preferred_element_type=F32)
    return dot(a[0], b[0]) + (dot(a[0], b[1]) + dot(a[1], b[0]))


def carry(link_t, cov, base):
    link_t = link_t if isinstance(link_t, tuple) else split(link_t)
    return mm(mm(link_t, cov), link_t, NT) + base


def pack(cov):
    half = cov.shape[0] // 2
    return jnp.concatenate([cov[:half, :half], cov[:half, half:], cov[half:, half:]], 0)


def unpack(packed):
    half = packed.shape[0] // 3
    first, cross, second = packed[:half], packed[half : 2 * half], packed[2 * half :]
    top = jnp.concatenate([first, cross], 1)
    bottom = jnp.concatenate([cross.T, second], 1)
    return jnp.concatenate([top, bottom], 0)


def is_lower():
    return (lax.axis_index("seg") & 1) == 0


def from_halves(own, other):
    lower = is_lower()
    return jnp.concatenate([jnp.where(lower, own, other), jnp.where(lower, other, own)], 0)


def joined_cores(own, other, halves):
    return from_halves(own, other) if halves else own + other


def own_half(whole):
    half = whole.shape[0] // 2
    return jnp.where(is_lower(), whole[:half], whole[half:])


def two_blocks(load, left, right):
    def placed(block, half):
        slab = load(lax.shift_right_logical(block, 1))
        return jnp.where((block & 1) == half, slab, pltpu.roll(slab, BLOCK, 1))

    a, b = placed(left, 0), placed(right, 1)
    lane = lax.broadcasted_iota(jnp.int32, a.shape, 1)
    return jnp.where(lane < BLOCK, a, b)


def tile_of(ref, *lead):
    def load(tile):
        return ref[(*lead, slice(None), pl.ds(pl.multiple_of(tile * LANES, LANES), LANES))]

    return load


def chosen_of(fill_ref, prior_ref, panel):
    slots = fill_ref.shape[1]
    if panel > 0:
        return [fill_ref[panel - 1, j] for j in range(slots)]
    first = lax.axis_index("seg") == 0
    return [jnp.where(first, fill_ref[0, j], prior_ref[prior_ref.shape[0] - 1, j]) for j in range(slots)]


def order_of(chosen, blocks):
    slots = len(chosen)
    rest = [jnp.int32(0)] * (blocks - slots)
    place = []
    seen = jnp.int32(0)
    for b in range(blocks):
        hit = jnp.int32(0)
        where = jnp.int32(0)
        for j in range(slots):
            same = (chosen[j] == b).astype(jnp.int32)
            hit = hit + same
            where = where + same * j
        free = 1 - hit
        for q in range(blocks - slots):
            rest[q] = rest[q] + jnp.where(seen == q, free * b, 0)
        place.append(jnp.where(hit > 0, where, slots + seen))
        seen = seen + free
    return rest, place


def vmem(count):
    return [pl.BlockSpec(memory_space=pltpu.VMEM)] * count


def smem(count):
    return [pl.BlockSpec(memory_space=pltpu.SMEM)] * count


def call(kernel, outs, scalars, arrays, far=(), through=(), scratch=(), flops=0, mib=16, name=None):
    moved = sum(a.size * 4 for a in (*arrays, *far)) + sum(o.size * 4 for o in outs)
    first = len(scalars) + len(arrays) + len(far)
    count = len(through)

    def inner(*refs):
        kernel(*refs[:first], *refs[first + count : first + count + len(outs)], *refs[first + 2 * count + len(outs) :])

    return pl.pallas_call(
        inner,
        out_shape=[*outs, *(jax.ShapeDtypeStruct(a.shape, a.dtype) for a in through)],
        in_specs=smem(len(scalars))
        + vmem(len(arrays))
        + [pl.BlockSpec(memory_space=pltpu.HBM)] * len(far)
        + [pl.BlockSpec(memory_space=pl.ANY)] * count,
        out_specs=vmem(len(outs)) + [pl.BlockSpec(memory_space=pl.ANY)] * count,
        scratch_shapes=list(scratch),
        input_output_aliases={first + i: len(outs) + i for i in range(count)},
        cost_estimate=pl.CostEstimate(flops=flops, bytes_accessed=moved, transcendentals=0),
        compiler_params=pltpu.CompilerParams(vmem_limit_bytes=mib << 20),
        name=name,
    )(*scalars, *arrays, *(pltpu.with_memory_space_constraint(a, pltpu.HBM) for a in far), *through)


def shape(*dims):
    return jax.ShapeDtypeStruct(dims, F32)


def local_map_kernel(mask_hbm, factor_hbm, inv_hbm, map_ref, mask_ref, factor_ref, inv_ref, sems):
    panels, rows, width = factor_ref.shape
    cut = width // 2
    first = pltpu.make_async_copy(mask_hbm, mask_ref, sems.at[0, 0])
    first.start()
    copies = []
    for p in range(panels):
        copies.append(
            [
                pltpu.make_async_copy(factor_hbm.at[p], factor_ref.at[p], sems.at[p + 1, 0]),
                pltpu.make_async_copy(
                    inv_hbm.at[p, cut:, :], inv_ref.at[p, cut:, :], sems.at[p + 1, 1]
                ),
                pltpu.make_async_copy(
                    inv_hbm.at[p, :cut, :cut], inv_ref.at[p, :cut, :cut], sems.at[p + 1, 2]
                ),
            ]
        )
    for group in reversed(copies):
        for copy in group:
            copy.start()
    first.wait()
    seg_at, seg_count = lax.axis_index("seg"), lax.axis_size("seg")
    slots = rows // BLOCK
    row_at = lax.axis_index("row")
    for p in range(panels - 1, -1, -1):
        for copy in copies[p]:
            copy.wait()
        alive = (seg_at * panels + p < seg_count * panels - 1).astype(F32)
        kept = []
        for s in range(slots):
            keep = mask_ref[p, row_at * slots + s].astype(F32) * alive
            kept.append(factor_ref[p, s * BLOCK : (s + 1) * BLOCK, :] * keep)
        kept = kept[0] if slots == 1 else jnp.concatenate(kept, 0)
        left, right = split(kept[:, :cut]), split(kept[:, cut:])
        lower = split(inv_ref[p, cut:, :])
        map_ref[p, :, cut:] = mm(right, (lower[0][:, cut:], lower[1][:, cut:]))
        map_ref[p, :, :cut] = mm(right, (lower[0][:, :cut], lower[1][:, :cut])) + mm(
            left, inv_ref[p, :cut, :cut]
        )


def column_split_kernel(fill_ref, prior_ref, map_ref, link_ref, rest_ref):
    panels = map_ref.shape[0]
    blocks = map_ref.shape[2] // BLOCK
    for p in range(panels):
        chosen = chosen_of(fill_ref, prior_ref, p)
        rest, _ = order_of(chosen, blocks)
        for out_ref, wanted in ((link_ref, chosen), (rest_ref, rest)):
            for t in range(len(wanted) // 2):
                out_ref[p, :, t * LANES : (t + 1) * LANES] = two_blocks(
                    tile_of(map_ref, p), wanted[2 * t], wanted[2 * t + 1]
                )


def prior_kernel(fill_ref, prior_ref, inv_ref, base_ref, own_ref):
    panels = inv_ref.shape[0]
    own_cols = own_ref.shape[1]
    row_at = lax.axis_index("row")
    for p in range(panels):
        chosen = chosen_of(fill_ref, prior_ref, p)
        picked = split(
            jnp.concatenate(
                [
                    two_blocks(tile_of(inv_ref, p), chosen[2 * t], chosen[2 * t + 1])
                    for t in range(len(chosen) // 2)
                ],
                1,
            )
        )
        base_ref[p] = mm(picked, picked, TN)
        own = inv_ref[p, :, pl.ds(pl.multiple_of(row_at * own_cols, own_cols), own_cols)]
        own_ref[p] = mm(own, inv_ref[p], TN)


def segment_kernel(row_count, *refs):
    parts = refs[:row_count]
    base_ref, links_ref, links_t_ref, whole_ref = refs[row_count:]
    panels, rows, _ = parts[0].shape
    size = base_ref.shape[1]
    row_at = lax.axis_index("row")
    for d, part in enumerate(parts):
        at = lax.rem(row_at + (row_count - d), row_count) * rows
        links_ref[:, pl.ds(pl.multiple_of(at, rows), rows), :] = part[...]
    cov = base_ref[panels - 1]
    link_t = links_ref[panels - 1].T
    links_t_ref[panels - 1] = link_t
    for p in range(panels - 2, -1, -1):
        own_t = links_ref[p].T
        links_t_ref[p] = own_t
        own_t = split(own_t)
        cov = carry(own_t, cov, base_ref[p])
        link_t = mm(own_t, link_t)
    whole_ref[:size] = link_t
    whole_ref[size:] = cov


def chip_kernel(own_ref, other_ref, link_t_ref, cov_ref, packed_ref, half_t_ref):
    size = cov_ref.shape[0]
    lower = is_lower()
    own, other = own_ref[...], other_ref[...]
    down = jnp.where(lower, own, other)
    up = jnp.where(lower, other, own)
    down_t = split(down[:size])
    cov = carry(down_t, up[size:], down[size:])
    link_t = mm(down_t, up[:size])
    link_t_ref[...] = link_t
    cov_ref[...] = cov
    packed_ref[...] = own_half(pack(cov))
    half_t_ref[...] = own_half(link_t)


def extend_kernel(link_t_ref, cov_ref, own_ref, other_ref, packed_ref):
    after = unpack(from_halves(own_ref[...], other_ref[...]))
    packed_ref[...] = pack(carry(link_t_ref[...], after, cov_ref[...]))


def extend_link_kernel(link_t_ref, own_t_ref, other_t_ref, out_ref):
    out_ref[...] = mm(link_t_ref[...], from_halves(own_t_ref[...], other_t_ref[...]))


def join_kernel(level, *refs):
    past_t, past, link_t, cov = (
        joined_cores(refs[2 * i][...], refs[2 * i + 1][...], i < 2) for i in range(4)
    )
    chip = lax.axis_index("seg") // 2
    below = (lax.shift_right_logical(chip, level) & 1) == 0
    known = (chip & ((1 << level) - 1)) != (1 << level) - 1
    past_parts = split(past_t)
    joined = pack(carry(past_parts, unpack(cov), unpack(past)))
    joined_t = mm(past_parts, link_t)
    out_t = jnp.where(below, jnp.where(known, joined_t, link_t), past_t)
    out = jnp.where(below, jnp.where(known, joined, cov), past)
    for ref, whole in zip(refs[8:], (out_t, out_t, out, out)):
        ref[...] = own_half(whole)
    for ref, whole in ((refs[9], out_t), (refs[11], out)):
        half = whole.shape[0] // 2
        ref[...] = jnp.where(is_lower(), whole[half:], whole[:half])


def prepare_kernel(
    has_past, row_count, fill_ref, prior_ref, links_ref, links_t_ref, *refs
):
    rest_refs, (base_ref, own_ref, other_ref), refs = (
        refs[:row_count], refs[row_count : row_count + 3], refs[row_count + 3 :]
    )
    if has_past:
        past_refs = refs[:4]
        refs = refs[4:]
    left_ref, right_ref, const_ref, scratch = refs
    panels, size, _ = links_ref.shape
    own_cols = own_ref.shape[1]
    width = own_ref.shape[2]
    blocks = width // BLOCK
    row_at = lax.axis_index("row")
    rows = size // row_count
    seg_at = lax.axis_index("seg")
    chip_last = lax.axis_size("seg") // 2 - 1
    top = 1 << max(chip_last.bit_length() - 1, 0)
    at_row = lax.broadcasted_iota(jnp.int32, (size, size), 0)
    at_col = lax.broadcasted_iota(jnp.int32, (size, size), 1)
    eye = (at_row == at_col).astype(F32)
    if has_past:
        chip = seg_at // 2
        known = (chip & (top - 1)) != top - 1
        to_t = jnp.where(known, from_halves(past_refs[0][...], past_refs[1][...]), eye)
        gain = unpack(from_halves(past_refs[2][...], past_refs[3][...]))
    else:
        to_t = eye
        gain = jnp.zeros((size, size), F32)
    lower = (seg_at & 1) == 0
    other_t = split(other_ref[:size, :])
    to_t = jnp.where(lower, mm(other_t, to_t), to_t)
    gain = jnp.where(lower, carry(other_t, gain, other_ref[size:, :]), gain)
    for p in range(panels - 1, -1, -1):
        chosen = chosen_of(fill_ref, prior_ref, p)
        _, place = order_of(chosen, blocks)
        scratch[:, :size] = links_ref[p]
        for d, part in enumerate(rest_refs):
            at = lax.rem(row_at + (row_count - d), row_count) * rows
            scratch[pl.ds(pl.multiple_of(at, rows), rows), size:] = part[p]
        whole = jnp.concatenate(
            [
                two_blocks(tile_of(scratch), place[2 * t], place[2 * t + 1])
                for t in range(blocks // 2)
            ],
            1,
        )
        scratch[...] = whole
        own_map = scratch[:, pl.ds(pl.multiple_of(row_at * own_cols, own_cols), own_cols)]
        own_t = split(own_map.T)
        whole = split(whole)
        scratch[:, :size] = to_t
        scratch[:, size:] = gain
        own_rows = pl.ds(pl.multiple_of(row_at * rows, rows), rows)
        to_parts = split(to_t)
        left_ref[p, :rows, :] = scratch[own_rows, :size]
        left_ref[p, rows:, :] = mm(own_t, to_parts)
        right_ref[p] = mm(to_parts, whole, TN)
        gains = jnp.concatenate([scratch[own_rows, size:], mm(own_t, gain)], 0)
        const = mm(gains, whole)
        const_ref[p, :rows, :] = const[:rows]
        const_ref[p, rows:, :] = const[rows:] + own_ref[p]
        if p > 0:
            link_t = split(links_t_ref[p])
            to_t = mm(link_t, to_t)
            gain = carry(link_t, gain, base_ref[p])


def finish_kernel(halves, mask_ref, after_ref, after_other_ref, left_ref, right_ref, const_ref, diag_ref, off_ref):
    panels, total, _ = left_ref.shape
    rows = off_ref.shape[1]
    slots = rows // BLOCK
    row_at = lax.axis_index("row")
    after = split(unpack(joined_cores(after_ref[...], after_other_ref[...], halves)))
    for p in range(panels):
        result = mm(mm(left_ref[p], after), right_ref[p]) + const_ref[p]
        diag_ref[p] = result[rows:]
        for s in range(slots):
            keep = mask_ref[p, row_at * slots + s].astype(F32)
            off_ref[p, s * BLOCK : (s + 1) * BLOCK, :] = -result[s * BLOCK : (s + 1) * BLOCK] * keep


def body(fill_blocks, fill_mask, inv_diag, factor_off):
    panels, width, _ = inv_diag.shape
    rows = factor_off.shape[1]
    seg_count = lax.axis_size("seg")
    row_count = lax.axis_size("row")
    size = rows * row_count
    own_cols = width // row_count
    slots = fill_blocks.shape[1]
    chosen_cols = slots * BLOCK
    rest_cols = width - chosen_cols
    chips = seg_count // 2

    prior_fill = lax.ppermute(
        fill_blocks, "seg", [(i, i + 1) for i in range(seg_count - 1)]
    )
    (local_map,) = call(
        local_map_kernel,
        [shape(panels, rows, width)],
        [],
        [],
        far=[fill_mask, factor_off, inv_diag],
        scratch=[
            pltpu.SMEM(fill_mask.shape, jnp.int32),
            pltpu.VMEM(factor_off.shape, F32),
            pltpu.VMEM(inv_diag.shape, F32),
            pltpu.SemaphoreType.DMA((panels + 1, 3)),
        ],
        flops=6 * panels * rows * width * width,
        name="local_map",
    )
    link_own, rest_own = call(
        column_split_kernel,
        [shape(panels, rows, chosen_cols), shape(panels, rows, rest_cols)],
        [fill_blocks, prior_fill],
        [local_map],
        name="column_split",
    )
    parts = [link_own] + [
        lax.ppermute(link_own, "row", [(i, (i + d) % row_count) for i in range(row_count)])
        for d in range(1, row_count)
    ]
    base, own_prior = call(
        prior_kernel,
        [shape(panels, chosen_cols, chosen_cols), shape(panels, own_cols, width)],
        [fill_blocks, prior_fill],
        [inv_diag],
        flops=6 * panels * width * (chosen_cols * chosen_cols + own_cols * width),
        mib=24,
        name="prior",
    )
    links, links_t, own_whole, rest_own = call(
        functools.partial(segment_kernel, row_count),
        [shape(panels, size, size), shape(panels, size, size), shape(2 * size, size)],
        [],
        parts + [base],
        through=[rest_own],
        flops=18 * (panels - 1) * size**3,
        name="segment",
    )
    swap = [(i, i ^ 1) for i in range(seg_count)]
    other_whole = lax.ppermute(own_whole, "seg", swap)
    rests = [rest_own]
    for _ in range(1, row_count):
        ring = [(i, (i + 1) % row_count) for i in range(row_count)]
        rests.append(lax.ppermute(rests[-1], "row", ring))
    half = size // 2
    half_packed = shape(3 * half // 2, half)
    half_link = shape(half, size)
    link_t, cov, send, send_t = call(
        chip_kernel,
        [shape(size, size), shape(size, size), half_packed, half_link],
        [],
        [own_whole, other_whole],
        flops=18 * size**3,
        name="chip",
    )
    past = None
    after = (jnp.zeros(half_packed.shape, F32),) * 2
    levels = (chips - 1).bit_length()
    for level in range(levels):
        bit = 1 << level
        if level > 0:
            (send,) = call(
                extend_kernel, [shape(3 * half, half)], [], [link_t, cov, *past[2:]],
                flops=12 * size**3, name="extend",
            )
            if level < levels - 1:
                (send_t,) = call(
                    extend_link_kernel, [shape(size, size)], [], [link_t, *past[:2]],
                    flops=6 * size**3, name="extend_link",
                )
        got = got_t = None
        for step in range(max(bit // 2, 1)):
            route = [
                (2 * (base_chip + bit) + core, 2 * (base_chip + min(2 * step + core, bit - 1)) + core)
                for base_chip in range(0, chips, 2 * bit)
                for core in range(2)
            ]
            piece = lax.ppermute(send, "seg", route)
            got = piece if got is None else got + piece
            if level < levels - 1:
                piece_t = lax.ppermute(send_t, "seg", route)
                got_t = piece_t if got_t is None else got_t + piece_t
        got = (got, lax.ppermute(got, "seg", swap))
        if level == levels - 1:
            after = got
            continue
        got = (got_t, lax.ppermute(got_t, "seg", swap), *got)
        if past is None:
            past = got
        else:
            past = call(
                functools.partial(join_kernel, level),
                [half_link, half_link, half_packed, half_packed],
                [],
                [*past, *got],
                flops=18 * size**3,
                name="join",
            )
    total = rows + own_cols
    left, right, const = call(
        functools.partial(prepare_kernel, past is not None, row_count),
        [shape(panels, total, size), shape(panels, size, width), shape(panels, total, width)],
        [fill_blocks, prior_fill],
        [links, links_t, *rests, base, own_prior, other_whole, *(past or ())],
        scratch=[pltpu.VMEM((size, width), F32)],
        flops=6 * panels * size * (total * size + size * width + total * width + 3 * size * size),
        mib=24,
        name="prepare",
    )
    diag, off = call(
        functools.partial(finish_kernel, levels < 2),
        [shape(panels, own_cols, width), shape(panels, rows, width)],
        [fill_mask],
        [*after, left, right, const],
        flops=6 * panels * total * size * (size + width),
        name="finish",
    )
    return diag, off


def solution(mesh):
    placed = (P("seg", None), P("seg", None), P("seg", None, None), P("seg", "row", None))
    return jax.shard_map(
        body,
        mesh=mesh,
        in_specs=placed,
        out_specs=(P("seg", "row", None), P("seg", "row", None)),
        check_vma=False,
    )
```

```python
import functools

import jax
import jax.numpy as jnp
from jax import lax
from jax.experimental import pallas as pl
from jax.experimental.pallas import tpu as pltpu
from jax.sharding import PartitionSpec as P

BLOCK = 64
LANES = 128
F32 = jnp.float32
BF16 = jnp.bfloat16
NN = (((1,), (0,)), ((), ()))
NT = (((1,), (1,)), ((), ()))
TN = (((0,), (0,)), ((), ()))


def split(x):
    high = x.astype(BF16)
    return high, (x - high.astype(F32)).astype(BF16)


def mm(a, b, dims=NN):
    a = a if isinstance(a, tuple) else split(a)
    b = b if isinstance(b, tuple) else split(b)
    dot = functools.partial(lax.dot_general, dimension_numbers=dims, preferred_element_type=F32)
    return dot(a[0], b[0]) + (dot(a[0], b[1]) + dot(a[1], b[0]))


def carry(link_t, cov, base):
    link_t = link_t if isinstance(link_t, tuple) else split(link_t)
    return mm(mm(link_t, cov), link_t, NT) + base


def pack(cov):
    half = cov.shape[0] // 2
    return jnp.concatenate([cov[:half, :half], cov[:half, half:], cov[half:, half:]], 0)


def unpack(packed):
    half = packed.shape[0] // 3
    first, cross, second = packed[:half], packed[half : 2 * half], packed[2 * half :]
    top = jnp.concatenate([first, cross], 1)
    bottom = jnp.concatenate([cross.T, second], 1)
    return jnp.concatenate([top, bottom], 0)


def is_lower():
    return (lax.axis_index("seg") & 1) == 0


def from_halves(own, other):
    lower = is_lower()
    return jnp.concatenate([jnp.where(lower, own, other), jnp.where(lower, other, own)], 0)


def joined_cores(own, other, halves):
    if halves:
        return from_halves(own, other)
    seg_at = lax.axis_index("seg")
    return jnp.where(((seg_at // 2) & 1) == (seg_at & 1), own, other)


def own_half(whole):
    half = whole.shape[0] // 2
    return jnp.where(is_lower(), whole[:half], whole[half:])


def two_blocks(load, left, right):
    def placed(block, half):
        slab = load(lax.shift_right_logical(block, 1))
        return jnp.where((block & 1) == half, slab, pltpu.roll(slab, BLOCK, 1))

    a, b = placed(left, 0), placed(right, 1)
    lane = lax.broadcasted_iota(jnp.int32, a.shape, 1)
    return jnp.where(lane < BLOCK, a, b)


def tile_of(ref, *lead):
    def load(tile):
        return ref[(*lead, slice(None), pl.ds(pl.multiple_of(tile * LANES, LANES), LANES))]

    return load


def chosen_of(fill_ref, prior_ref, panel):
    slots = fill_ref.shape[1]
    if panel > 0:
        return [fill_ref[panel - 1, j] for j in range(slots)]
    first = lax.axis_index("seg") == 0
    return [jnp.where(first, fill_ref[0, j], prior_ref[prior_ref.shape[0] - 1, j]) for j in range(slots)]


def vmem(count):
    return [pl.BlockSpec(memory_space=pltpu.VMEM)] * count


def smem(count):
    return [pl.BlockSpec(memory_space=pltpu.SMEM)] * count


def call(kernel, outs, scalars, arrays, far=(), through=(), scratch=(), flops=0, mib=16, name=None):
    moved = sum(a.size * 4 for a in (*arrays, *far)) + sum(o.size * 4 for o in outs)
    first = len(scalars) + len(arrays) + len(far)
    count = len(through)

    def inner(*refs):
        kernel(*refs[:first], *refs[first + count : first + count + len(outs)], *refs[first + 2 * count + len(outs) :])

    return pl.pallas_call(
        inner,
        out_shape=[*outs, *(jax.ShapeDtypeStruct(a.shape, a.dtype) for a in through)],
        in_specs=smem(len(scalars))
        + vmem(len(arrays))
        + [pl.BlockSpec(memory_space=pltpu.HBM)] * len(far)
        + [pl.BlockSpec(memory_space=pl.ANY)] * count,
        out_specs=vmem(len(outs)) + [pl.BlockSpec(memory_space=pl.ANY)] * count,
        scratch_shapes=list(scratch),
        input_output_aliases={first + i: len(outs) + i for i in range(count)},
        cost_estimate=pl.CostEstimate(flops=flops, bytes_accessed=moved, transcendentals=0),
        compiler_params=pltpu.CompilerParams(vmem_limit_bytes=mib << 20),
        name=name,
    )(*scalars, *arrays, *(pltpu.with_memory_space_constraint(a, pltpu.HBM) for a in far), *through)


def shape(*dims):
    return jax.ShapeDtypeStruct(dims, F32)


def kept_rows(mask_ref, panel, slot, rows):
    alive = lax.axis_index("seg") * mask_ref.shape[0] + panel < (
        lax.axis_size("seg") * mask_ref.shape[0] - 1
    )
    return rows * (mask_ref[panel, slot].astype(F32) * alive.astype(F32))


def triangular_mm(left, lower):
    cut = left.shape[1] // 2
    first, second = split(left[:, :cut]), split(left[:, cut:])
    below = split(lower[cut:, :])
    return jnp.concatenate(
        [
            mm(second, (below[0][:, :cut], below[1][:, :cut])) + mm(first, lower[:cut, :cut]),
            mm(second, (below[0][:, cut:], below[1][:, cut:])),
        ],
        1,
    )


def prior_kernel(
    fill_ref, prior_ref, inv_ref, base_ref, own_ref, pick_high_ref, pick_low_ref, token_ref
):
    panels = inv_ref.shape[0]
    own_cols = own_ref.shape[1]
    row_at = lax.axis_index("row")
    token_ref[...] = jnp.zeros_like(token_ref)
    for p in range(panels):
        chosen = chosen_of(fill_ref, prior_ref, p)
        picked = split(
            jnp.concatenate(
                [
                    two_blocks(tile_of(inv_ref, p), chosen[2 * t], chosen[2 * t + 1])
                    for t in range(len(chosen) // 2)
                ],
                1,
            )
        )
        pick_high_ref[p], pick_low_ref[p] = picked
        base_ref[p] = mm(picked, picked, TN)
        own = inv_ref[p, :, pl.ds(pl.multiple_of(row_at * own_cols, own_cols), own_cols)]
        own_ref[p] = mm(own, inv_ref[p], TN)


def put_rows(mask_ref, panel, distance, part, take):
    row_count = lax.axis_size("row")
    rows = part.shape[1]
    owner = lax.rem(lax.axis_index("row") + (row_count - distance), row_count)
    for s in range(rows // BLOCK):
        slot = owner * (rows // BLOCK) + s
        kept = kept_rows(mask_ref, panel, slot, part[panel, s * BLOCK : (s + 1) * BLOCK, :])
        take(kept, pl.ds(pl.multiple_of(slot * BLOCK, BLOCK), BLOCK))


def links_kernel(distances, mask_ref, *refs):
    parts, (pick_high_ref, pick_low_ref, links_ref) = refs[: len(distances)], refs[len(distances) :]
    for p in range(links_ref.shape[0]):
        pick = (pick_high_ref[p], pick_low_ref[p])

        def take(kept, at):
            links_ref[p, at, :] = mm(kept, pick)

        for d, part in zip(distances, parts):
            put_rows(mask_ref, p, d, part, take)


def segment_kernel(
    distance, mask_ref, part, pick_high_ref, pick_low_ref, early_ref, base_ref,
    links_t_ref, whole_ref, links_ref
):
    panels, size, _ = base_ref.shape
    cov = link_t = None
    for p in range(panels - 1, -1, -1):
        pick = (pick_high_ref[p], pick_low_ref[p])
        links_ref[...] = early_ref[p]

        def take(kept, at):
            links_ref[at, :] = mm(kept, pick)

        put_rows(mask_ref, p, distance, part, take)
        own_t = links_ref[...].T
        links_t_ref[p] = own_t
        if cov is None:
            cov, link_t = base_ref[p], own_t
        else:
            own_t = split(own_t)
            cov = carry(own_t, cov, base_ref[p])
            link_t = mm(own_t, link_t)
    whole_ref[:size] = link_t
    whole_ref[size:] = cov


def maps_kernel(mask_ref, inv_ref, *refs):
    *parts, maps_ref, token_ref, rows_ref = refs
    token_ref[...] = jnp.zeros_like(token_ref)
    for p in range(inv_ref.shape[0]):

        def take(kept, at):
            rows_ref[at, :] = kept

        for d, part in enumerate(parts):
            put_rows(mask_ref, p, d, part, take)
        maps_ref[p] = triangular_mm(rows_ref[...], inv_ref[p])


def chip_kernel(own_ref, other_ref, link_t_ref, cov_ref, packed_ref, half_t_ref):
    size = cov_ref.shape[0]
    lower = is_lower()
    own, other = own_ref[...], other_ref[...]
    down = jnp.where(lower, own, other)
    up = jnp.where(lower, other, own)
    down_t = split(down[:size])
    cov = carry(down_t, up[size:], down[size:])
    link_t = mm(down_t, up[:size])
    link_t_ref[...] = link_t
    cov_ref[...] = cov
    packed_ref[...] = own_half(pack(cov))
    half_t_ref[...] = own_half(link_t)


def extend_kernel(link_t_ref, cov_ref, own_ref, other_ref, packed_ref):
    after = unpack(from_halves(own_ref[...], other_ref[...]))
    packed_ref[...] = pack(carry(link_t_ref[...], after, cov_ref[...]))


def extend_link_kernel(link_t_ref, own_t_ref, other_t_ref, out_ref):
    out_ref[...] = mm(link_t_ref[...], from_halves(own_t_ref[...], other_t_ref[...]))


def join_kernel(level, *refs):
    past_t, past, link_t, cov = (
        joined_cores(refs[2 * i][...], refs[2 * i + 1][...], i < 2) for i in range(4)
    )
    chip = lax.axis_index("seg") // 2
    below = (lax.shift_right_logical(chip, level) & 1) == 0
    known = (chip & ((1 << level) - 1)) != (1 << level) - 1
    past_parts = split(past_t)
    joined = pack(carry(past_parts, unpack(cov), unpack(past)))
    joined_t = mm(past_parts, link_t)
    out_t = jnp.where(below, jnp.where(known, joined_t, link_t), past_t)
    out = jnp.where(below, jnp.where(known, joined, cov), past)
    for ref, whole in zip(refs[8:], (out_t, out_t, out, out)):
        ref[...] = own_half(whole)
    for ref, whole in ((refs[9], out_t), (refs[11], out)):
        half = whole.shape[0] // 2
        ref[...] = jnp.where(is_lower(), whole[half:], whole[:half])


def prepare_kernel(base_ref, own_ref, other_ref, maps_ref, links_t_ref, *refs):
    left_ref, right_ref, const_ref, token_ref, scratch = refs
    token_ref[...] = jnp.zeros_like(token_ref)
    panels, own_cols, _ = own_ref.shape
    size = base_ref.shape[1]
    row_at = lax.axis_index("row")
    rows = left_ref.shape[1] - own_cols
    at_row = lax.broadcasted_iota(jnp.int32, (size, size), 0)
    at_col = lax.broadcasted_iota(jnp.int32, (size, size), 1)
    lower = is_lower()
    to_t = jnp.where(lower, other_ref[:size, :], (at_row == at_col).astype(F32))
    gain = jnp.where(lower, other_ref[size:, :], 0.0)
    own_at = pl.ds(pl.multiple_of(row_at * own_cols, own_cols), own_cols)
    own_rows = pl.ds(pl.multiple_of(row_at * rows, rows), rows)
    for p in range(panels - 1, -1, -1):
        whole = split(maps_ref[p])
        own_t = split(maps_ref[p, :, own_at].T)
        scratch[:, :size] = to_t
        scratch[:, size:] = gain
        to_parts = split(to_t)
        left_ref[p, :rows, :] = scratch[own_rows, :size]
        left_ref[p, rows:, :] = mm(own_t, to_parts)
        right_ref[p] = mm(to_parts, whole, TN)
        gains = jnp.concatenate([scratch[own_rows, size:], mm(own_t, gain)], 0)
        const = mm(gains, whole)
        const_ref[p, :rows, :] = const[:rows]
        const_ref[p, rows:, :] = const[rows:] + own_ref[p]
        if p > 0:
            link_t = split(links_t_ref[p])
            to_t = mm(link_t, to_t)
            gain = carry(link_t, gain, base_ref[p])


def finish_kernel(levels, mask_ref, after_ref, after_other_ref, *refs):
    past_refs, refs = refs[: 4 * (levels > 1)], refs[4 * (levels > 1) :]
    left_ref, right_ref, const_ref, diag_ref, off_ref = refs
    panels = left_ref.shape[0]
    rows = off_ref.shape[1]
    row_at = lax.axis_index("row")
    chip = lax.axis_index("seg") // 2
    top = (1 << levels) // 2
    after = joined_cores(after_ref[...], after_other_ref[...], levels < 2)
    after = unpack(jnp.where((chip & top) == 0, after, 0.0))
    if past_refs:
        past_t = from_halves(past_refs[0][...], past_refs[1][...])
        past = unpack(from_halves(past_refs[2][...], past_refs[3][...]))
        after = jnp.where((chip & (top - 1)) != top - 1, carry(past_t, after, past), after)
    after = split(after)
    for p in range(panels):
        result = mm(mm(left_ref[p], after), right_ref[p]) + const_ref[p]
        diag_ref[p] = result[rows:]
        for s in range(rows // BLOCK):
            keep = mask_ref[p, row_at * (rows // BLOCK) + s].astype(F32)
            off_ref[p, s * BLOCK : (s + 1) * BLOCK, :] = -result[s * BLOCK : (s + 1) * BLOCK] * keep


def body(fill_blocks, fill_mask, inv_diag, factor_off):
    panels, width, _ = inv_diag.shape
    rows = factor_off.shape[1]
    seg_count = lax.axis_size("seg")
    row_count = lax.axis_size("row")
    size = rows * row_count
    own_cols = width // row_count
    slots = fill_blocks.shape[1]
    chosen_cols = slots * BLOCK
    chips = seg_count // 2
    half_cols = size // 2

    def turn(x, axis, distance):
        count = lax.axis_size(axis)
        return lax.ppermute(x, axis, [(i, (i + distance) % count) for i in range(count)])

    ups = [factor_off]
    for _ in range(row_count // 2):
        ups.append(turn(ups[-1], "row", 1))
    prior_fill = turn(fill_blocks, "seg", 1)
    pick = jax.ShapeDtypeStruct((panels, width, chosen_cols), BF16)
    token = shape(1, 1, width)
    base, own_prior, pick_high, pick_low, prior_token = call(
        prior_kernel,
        [shape(panels, chosen_cols, chosen_cols), shape(panels, own_cols, width), pick, pick, token],
        [fill_blocks, prior_fill],
        [inv_diag],
        flops=6 * panels * width * (chosen_cols * chosen_cols + own_cols * width),
        mib=24,
        name="prior",
    )
    downs = [factor_off + prior_token]
    for _ in range((row_count - 1) // 2):
        downs.append(turn(downs[-1], "row", -1))
    parts = ups + downs[:0:-1]
    last = len(ups) - 1
    early = [d for d in range(row_count) if d != last]
    (links,) = call(
        functools.partial(links_kernel, early),
        [shape(panels, size, size)],
        [fill_mask],
        [*(parts[d] for d in early), pick_high, pick_low],
        flops=6 * panels * size * size * width,
        name="links",
    )
    links_t, own_whole = call(
        functools.partial(segment_kernel, last),
        [shape(panels, size, size), shape(2 * size, size)],
        [fill_mask],
        [parts[last], pick_high, pick_low, links, base],
        scratch=[pltpu.VMEM((size, size), F32)],
        flops=6 * panels * rows * size * width + 18 * (panels - 1) * size**3,
        name="segment",
    )
    maps, maps_token = call(
        maps_kernel,
        [shape(panels, size, width), shape(1, half_cols)],
        [fill_mask],
        [inv_diag, *parts],
        scratch=[pltpu.VMEM((size, width), F32)],
        flops=6 * panels * size * width * width,
        mib=24,
        name="maps",
    )
    swap = [(i, i ^ 1) for i in range(seg_count)]
    other_whole = lax.ppermute(own_whole, "seg", swap)
    half = size // 2
    half_packed = shape(3 * half // 2, half)
    half_link = shape(half, size)
    link_t, cov, send, send_t = call(
        chip_kernel,
        [shape(size, size), shape(size, size), half_packed, half_link],
        [],
        [own_whole, other_whole],
        flops=18 * size**3,
        name="chip",
    )
    total = rows + own_cols
    left, right, const, prepare_token = call(
        prepare_kernel,
        [
            shape(panels, total, size),
            shape(panels, size, width),
            shape(panels, total, width),
            shape(1, half_cols),
        ],
        [],
        [base, own_prior, other_whole, maps, links_t],
        scratch=[pltpu.VMEM((size, width), F32)],
        flops=6 * panels * size * (total * size + size * width + total * width + 3 * size * size),
        mib=24,
        name="prepare",
    )
    past = None
    after = (jnp.zeros(half_packed.shape, F32),) * 2
    levels = (chips - 1).bit_length()
    for level in range(levels):
        bit = 1 << level
        if level > 0:
            (send,) = call(
                extend_kernel, [shape(3 * half, half)], [], [link_t, cov, *past[2:]],
                flops=12 * size**3, name="extend",
            )
            if level < levels - 1:
                (send_t,) = call(
                    extend_link_kernel, [shape(size, size)], [], [link_t, *past[:2]],
                    flops=6 * size**3, name="extend_link",
                )
        got = got_t = None
        for step in range(max(bit // 2, 1)):
            route = list(range(seg_count))
            for base_chip in range(0, chips, 2 * bit):
                for core in range(2):
                    upper_at = 2 * (base_chip + bit) + core
                    lower_at = 2 * (base_chip + (2 * step + core) % bit) + core
                    route[upper_at], route[lower_at] = lower_at, upper_at
            route = list(enumerate(route))
            here = ((lax.axis_index("seg") // 2) & (bit - 1)) // 2 == step
            piece = lax.ppermute(send, "seg", route)
            got = piece if step == 0 else jnp.where(here, piece, got)
            if level < levels - 1:
                piece_t = lax.ppermute(send_t, "seg", route)
                got_t = piece_t if step == 0 else jnp.where(here, piece_t, got_t)
        if level == levels - 1:
            got = got + prepare_token
        elif level == 0:
            got = got + maps_token
        got = (got, lax.ppermute(got, "seg", swap))
        if level == levels - 1:
            after = got
            continue
        got = (got_t, lax.ppermute(got_t, "seg", swap), *got)
        if past is None:
            past = got
        else:
            past = call(
                functools.partial(join_kernel, level),
                [half_link, half_link, half_packed, half_packed],
                [],
                [*past, *got],
                flops=18 * size**3,
                name="join",
            )
    diag, off = call(
        functools.partial(finish_kernel, levels),
        [shape(panels, own_cols, width), shape(panels, rows, width)],
        [fill_mask],
        [*after, *(past or ()), left, right, const],
        flops=6 * panels * total * size * (size + width),
        name="finish",
    )
    return diag, off


def solution(mesh):
    placed = (P("seg", None), P("seg", None), P("seg", None, None), P("seg", "row", None))
    return jax.shard_map(
        body,
        mesh=mesh,
        in_specs=placed,
        out_specs=(P("seg", "row", None), P("seg", "row", None)),
        check_vma=False,
    )
```

```python
import functools

import jax
import jax.numpy as jnp
from jax import lax
from jax.experimental import pallas as pl
from jax.experimental.pallas import tpu as pltpu
from jax.sharding import PartitionSpec as P

BLOCK = 64
LANES = 128
F32 = jnp.float32
BF16 = jnp.bfloat16
NN = (((1,), (0,)), ((), ()))
NT = (((1,), (1,)), ((), ()))
TN = (((0,), (0,)), ((), ()))


def split(x):
    high = x.astype(BF16)
    return high, (x - high.astype(F32)).astype(BF16)


def mm(a, b, dims=NN):
    a = a if isinstance(a, tuple) else split(a)
    b = b if isinstance(b, tuple) else split(b)
    dot = functools.partial(lax.dot_general, dimension_numbers=dims, preferred_element_type=F32)
    return dot(a[0], b[0]) + (dot(a[0], b[1]) + dot(a[1], b[0]))


def carry(link_t, cov, base):
    link_t = link_t if isinstance(link_t, tuple) else split(link_t)
    return mm(mm(link_t, cov), link_t, NT) + base


def pack(cov):
    half = cov.shape[0] // 2
    return jnp.concatenate([cov[:half, :half], cov[:half, half:], cov[half:, half:]], 0)


def unpack(packed):
    half = packed.shape[0] // 3
    first, cross, second = packed[:half], packed[half : 2 * half], packed[2 * half :]
    top = jnp.concatenate([first, cross], 1)
    bottom = jnp.concatenate([cross.T, second], 1)
    return jnp.concatenate([top, bottom], 0)


def is_lower():
    return (lax.axis_index("seg") & 1) == 0


def from_halves(own, other):
    lower = is_lower()
    return jnp.concatenate([jnp.where(lower, own, other), jnp.where(lower, other, own)], 0)


def own_half(whole):
    half = whole.shape[0] // 2
    return jnp.where(is_lower(), whole[:half], whole[half:])


def two_blocks(load, left, right):
    def placed(block, half):
        slab = load(lax.shift_right_logical(block, 1))
        return jnp.where((block & 1) == half, slab, pltpu.roll(slab, BLOCK, 1))

    a, b = placed(left, 0), placed(right, 1)
    lane = lax.broadcasted_iota(jnp.int32, a.shape, 1)
    return jnp.where(lane < BLOCK, a, b)


def tile_of(ref, *lead):
    def load(tile):
        return ref[(*lead, slice(None), pl.ds(pl.multiple_of(tile * LANES, LANES), LANES))]

    return load


def chosen_of(panel, fill_ref, prior_ref=None):
    slots = fill_ref.shape[1]
    if panel > 0:
        return [fill_ref[panel - 1, j] for j in range(slots)]
    first = lax.axis_index("seg") == 0
    last = prior_ref.shape[0] - 1
    return [jnp.where(first, fill_ref[0, j], prior_ref[last, j]) for j in range(slots)]


def vmem(count):
    return [pl.BlockSpec(memory_space=pltpu.VMEM)] * count


def smem(count):
    return [pl.BlockSpec(memory_space=pltpu.SMEM)] * count


def call(kernel, outs, scalars, arrays, far=(), through=(), scratch=(), flops=0, mib=16, name=None):
    moved = sum(a.size * 4 for a in (*arrays, *far)) + sum(o.size * 4 for o in outs)
    first = len(scalars) + len(arrays) + len(far)
    count = len(through)

    def inner(*refs):
        kernel(*refs[:first], *refs[first + count : first + count + len(outs)], *refs[first + 2 * count + len(outs) :])

    return pl.pallas_call(
        inner,
        out_shape=[*outs, *(jax.ShapeDtypeStruct(a.shape, a.dtype) for a in through)],
        in_specs=smem(len(scalars))
        + vmem(len(arrays))
        + [pl.BlockSpec(memory_space=pltpu.HBM)] * len(far)
        + [pl.BlockSpec(memory_space=pl.ANY)] * count,
        out_specs=vmem(len(outs)) + [pl.BlockSpec(memory_space=pl.ANY)] * count,
        scratch_shapes=list(scratch),
        input_output_aliases={first + i: len(outs) + i for i in range(count)},
        cost_estimate=pl.CostEstimate(flops=flops, bytes_accessed=moved, transcendentals=0),
        compiler_params=pltpu.CompilerParams(vmem_limit_bytes=mib << 20),
        name=name,
    )(*scalars, *arrays, *(pltpu.with_memory_space_constraint(a, pltpu.HBM) for a in far), *through)


def shape(*dims):
    return jax.ShapeDtypeStruct(dims, F32)


def kept_rows(mask_ref, panel, slot, rows):
    alive = lax.axis_index("seg") * mask_ref.shape[0] + panel < (
        lax.axis_size("seg") * mask_ref.shape[0] - 1
    )
    return rows * (mask_ref[panel, slot].astype(F32) * alive.astype(F32))


def triangular_mm(left, lower):
    cut = left.shape[1] // 2
    first, second = split(left[:, :cut]), split(left[:, cut:])
    below = split(lower[cut:, :])
    return jnp.concatenate(
        [
            mm(second, (below[0][:, :cut], below[1][:, :cut])) + mm(first, lower[:cut, :cut]),
            mm(second, (below[0][:, cut:], below[1][:, cut:])),
        ],
        1,
    )


def prior_kernel(panel, *refs):
    *scalar_refs, inv_hbm, base_ref, own_ref, pick_high_ref, pick_low_ref = refs[:-2]
    inv_ref, sem = refs[-2:]
    copy = pltpu.make_async_copy(inv_hbm.at[panel], inv_ref, sem)
    copy.start()
    chosen = chosen_of(panel, *scalar_refs)
    own_cols = own_ref.shape[0]
    own_at = pl.ds(pl.multiple_of(lax.axis_index("row") * own_cols, own_cols), own_cols)
    copy.wait()
    picked_t = split(
        jnp.concatenate(
            [
                two_blocks(tile_of(inv_ref), chosen[2 * t], chosen[2 * t + 1]).T
                for t in range(len(chosen) // 2)
            ],
            0,
        )
    )
    pick_high_ref[...], pick_low_ref[...] = picked_t
    base_ref[...] = mm(picked_t, picked_t, NT)
    own_ref[...] = mm(inv_ref[:, own_at].T, inv_ref[...])


def put_rows(mask_ref, panel, distance, part, take):
    row_count = lax.axis_size("row")
    rows = part.shape[1]
    owner = lax.rem(lax.axis_index("row") + (row_count - distance), row_count)
    for s in range(rows // BLOCK):
        slot = owner * (rows // BLOCK) + s
        kept = kept_rows(mask_ref, panel, slot, part[panel, s * BLOCK : (s + 1) * BLOCK, :])
        take(kept, pl.ds(pl.multiple_of(slot * BLOCK, BLOCK), BLOCK))


def links_kernel(distances, missing, mask_ref, *refs):
    parts, refs = refs[: len(distances)], refs[len(distances) :]
    *pick_refs, links_t_ref, rows_ref = refs
    for p in range(links_t_ref.shape[0]):

        def take(kept, at):
            rows_ref[at, :] = kept

        for d, part in zip(distances, parts):
            put_rows(mask_ref, p, d, part, take)
        put_rows(mask_ref, p, missing, parts[0], lambda kept, at: take(jnp.zeros_like(kept), at))
        pick = (pick_refs[2 * p][...], pick_refs[2 * p + 1][...])
        links_t_ref[p] = mm(pick, rows_ref[...], NT)


def segment_kernel(distance, panels, mask_ref, part, early_ref, *refs):
    pick_refs, base_refs = refs[: 2 * panels], refs[2 * panels : 3 * panels]
    links_t_ref, whole_ref = refs[3 * panels :]
    size = links_t_ref.shape[1]
    lane = lax.broadcasted_iota(jnp.int32, (size, size), 1) // BLOCK
    cov = link_t = None
    for p in range(panels - 1, -1, -1):
        pick = (pick_refs[2 * p][...], pick_refs[2 * p + 1][...])
        pieces = [early_ref[p]]

        def take(kept, at):
            late = mm(pick, jnp.concatenate([kept] * (size // BLOCK), 0), NT)
            pieces.append(jnp.where(lane == at.start // BLOCK, late, pieces[-1]))

        put_rows(mask_ref, p, distance, part, take)
        own_t = pieces[-1]
        links_t_ref[p] = own_t
        if cov is None:
            cov, link_t = base_refs[p][...], own_t
        else:
            own_t = split(own_t)
            cov = carry(own_t, cov, base_refs[p][...])
            link_t = mm(own_t, link_t)
    whole_ref[:size] = link_t
    whole_ref[size:] = cov


def maps_kernel(mask_ref, inv_ref, *refs):
    *parts, maps_ref, token_ref, rows_ref = refs
    token_ref[...] = jnp.zeros_like(token_ref)
    for p in range(inv_ref.shape[0]):

        def take(kept, at):
            rows_ref[at, :] = kept

        for d, part in enumerate(parts):
            put_rows(mask_ref, p, d, part, take)
        maps_ref[p] = triangular_mm(rows_ref[...], inv_ref[p])


def chip_kernel(own_ref, other_ref, link_t_ref, cov_ref, packed_ref, half_t_ref):
    size = cov_ref.shape[0]
    lower = is_lower()
    own, other = own_ref[...], other_ref[...]
    down = jnp.where(lower, own, other)
    up = jnp.where(lower, other, own)
    down_t = split(down[:size])
    cov = carry(down_t, up[size:], down[size:])
    link_t = mm(down_t, up[:size])
    link_t_ref[...] = link_t
    cov_ref[...] = cov
    packed_ref[...] = own_half(pack(cov))
    half_t_ref[...] = own_half(link_t)


def merge_kernel(level, link_t_ref, cov_ref, *refs):
    got_t = from_halves(refs[0][...], refs[1][...])
    got = unpack(from_halves(refs[2][...], refs[3][...]))
    own_t, own = link_t_ref[...], cov_ref[...]
    lower = (lax.shift_right_logical(lax.axis_index("seg") // 2, level) & 1) == 0
    down_t = split(jnp.where(lower, own_t, got_t))
    cov = carry(down_t, jnp.where(lower, got, own), jnp.where(lower, own, got))
    refs[4][...] = own_half(pack(cov))
    if len(refs) > 5:
        link_t = mm(down_t, jnp.where(lower, got_t, own_t))
        refs[5][...] = own_half(link_t)
        refs[6][...] = link_t
        refs[7][...] = cov


def join_kernel(level, *refs):
    past_t, past, link_t, cov = (
        from_halves(refs[2 * i][...], refs[2 * i + 1][...]) for i in range(4)
    )
    chip = lax.axis_index("seg") // 2
    below = (lax.shift_right_logical(chip, level) & 1) == 0
    known = (chip & ((1 << level) - 1)) != (1 << level) - 1
    past_parts = split(past_t)
    joined = pack(carry(past_parts, unpack(cov), unpack(past)))
    joined_t = mm(past_parts, link_t)
    out_t = jnp.where(below, jnp.where(known, joined_t, link_t), past_t)
    out = jnp.where(below, jnp.where(known, joined, cov), past)
    for i, whole in enumerate((out_t, out)):
        half = whole.shape[0] // 2
        refs[8 + 2 * i][...] = own_half(whole)
        refs[9 + 2 * i][...] = jnp.where(is_lower(), whole[half:], whole[:half])


def prepare_kernel(levels, panels, *refs):
    base_refs, own_refs, refs = refs[:panels], refs[panels : 2 * panels], refs[2 * panels :]
    (other_ref, maps_ref, links_t_ref), refs = refs[:3], refs[3:]
    past_refs, refs = refs[: 4 * (levels > 1)], refs[4 * (levels > 1) :]
    left_high, left_low, right_high, right_low, const_ref, token_ref, scratch = refs
    token_ref[...] = jnp.zeros_like(token_ref)
    own_cols = own_refs[0].shape[0]
    size = base_refs[0].shape[0]
    row_at = lax.axis_index("row")
    rows = left_high.shape[1] - own_cols
    at_row = lax.broadcasted_iota(jnp.int32, (size, size), 0)
    at_col = lax.broadcasted_iota(jnp.int32, (size, size), 1)
    eye = (at_row == at_col).astype(F32)
    lower = is_lower()
    if past_refs:
        chip = lax.axis_index("seg") // 2
        low = (1 << (levels - 1)) - 1
        known = (chip & low) != low
        past_t = from_halves(past_refs[0][...], past_refs[1][...])
        past = unpack(from_halves(past_refs[2][...], past_refs[3][...]))
        to_t = jnp.where(known, past_t, eye)
        gain = jnp.where(known, past, 0.0)
        other_t = split(other_ref[:size, :])
        to_t = jnp.where(lower, mm(other_t, to_t), to_t)
        gain = jnp.where(lower, carry(other_t, gain, other_ref[size:, :]), gain)
    else:
        to_t = jnp.where(lower, other_ref[:size, :], eye)
        gain = jnp.where(lower, other_ref[size:, :], 0.0)
    own_at = pl.ds(pl.multiple_of(row_at * own_cols, own_cols), own_cols)
    own_rows = pl.ds(pl.multiple_of(row_at * rows, rows), rows)
    for p in range(panels - 1, -1, -1):
        whole = split(maps_ref[p])
        own_t = split(maps_ref[p, :, own_at].T)
        scratch[:, :size] = to_t
        scratch[:, size:] = gain
        to_parts = split(to_t)
        left = jnp.concatenate([scratch[own_rows, :size], mm(own_t, to_parts)], 0)
        left_high[p], left_low[p] = split(left)
        right_high[p], right_low[p] = split(mm(to_parts, whole, TN))
        gains = jnp.concatenate([scratch[own_rows, size:], mm(own_t, gain)], 0)
        const = mm(gains, whole)
        const_ref[p, :rows, :] = const[:rows]
        const_ref[p, rows:, :] = const[rows:] + own_refs[p][...]
        if p > 0:
            link_t = split(links_t_ref[p])
            to_t = mm(link_t, to_t)
            gain = carry(link_t, gain, base_refs[p][...])


def finish_kernel(levels, mask_ref, after_ref, after_other_ref, *refs):
    left_high, left_low, right_high, right_low, const_ref, diag_ref, off_ref = refs
    rows = off_ref.shape[1]
    row_at = lax.axis_index("row")
    chip = lax.axis_index("seg") // 2
    after = from_halves(after_ref[...], after_other_ref[...])
    after = split(unpack(jnp.where((chip & ((1 << levels) // 2)) == 0, after, 0.0)))
    for p in range(const_ref.shape[0]):
        left = (left_high[p], left_low[p])
        right = (right_high[p], right_low[p])
        result = mm(mm(left, after), right) + const_ref[p]
        diag_ref[p] = result[rows:]
        for s in range(rows // BLOCK):
            keep = mask_ref[p, row_at * (rows // BLOCK) + s].astype(F32)
            off_ref[p, s * BLOCK : (s + 1) * BLOCK, :] = -result[s * BLOCK : (s + 1) * BLOCK] * keep


def body(fill_blocks, fill_mask, inv_diag, factor_off):
    panels, width, _ = inv_diag.shape
    rows = factor_off.shape[1]
    seg_count = lax.axis_size("seg")
    row_count = lax.axis_size("row")
    size = rows * row_count
    own_cols = width // row_count
    slots = fill_blocks.shape[1]
    chosen_cols = slots * BLOCK
    chips = seg_count // 2
    half_cols = size // 2

    def turn(x, axis, distance):
        count = lax.axis_size(axis)
        return lax.ppermute(x, axis, [(i, (i + distance) % count) for i in range(count)])

    ups = [factor_off]
    for _ in range(row_count // 2):
        ups.append(turn(ups[-1], "row", 1))
    prior_fill = turn(fill_blocks, "seg", 1)
    pick = jax.ShapeDtypeStruct((chosen_cols, width), BF16)
    bases, priors, picks = [], [], []
    for p in range(panels):
        base, own_prior, *high_low = call(
            functools.partial(prior_kernel, p),
            [shape(chosen_cols, chosen_cols), shape(own_cols, width), pick, pick],
            [fill_blocks] if p else [fill_blocks, prior_fill],
            [],
            far=[inv_diag],
            scratch=[pltpu.VMEM((width, width), F32), pltpu.SemaphoreType.DMA],
            flops=6 * width * (chosen_cols * chosen_cols + own_cols * width),
            name="prior",
        )
        bases.append(base)
        priors.append(own_prior)
        picks += high_low
    downs = [factor_off + jnp.minimum(prior_fill[-1:, -1:], 0).astype(F32)]
    for _ in range((row_count - 1) // 2):
        downs.append(turn(downs[-1], "row", -1))
    parts = ups + downs[:0:-1]
    last = len(ups) - 1
    early = [d for d in range(row_count) if d != last]
    (links,) = call(
        functools.partial(links_kernel, early, last),
        [shape(panels, size, size)],
        [fill_mask],
        [*(parts[d] for d in early), *picks],
        scratch=[pltpu.VMEM((size, width), F32)],
        flops=6 * panels * size * size * width,
        name="links",
    )
    links_t, own_whole = call(
        functools.partial(segment_kernel, last, panels),
        [shape(panels, size, size), shape(2 * size, size)],
        [fill_mask],
        [parts[last], links, *picks, *bases],
        flops=6 * panels * size * size * width + 18 * (panels - 1) * size**3,
        name="segment",
    )
    maps, maps_token = call(
        maps_kernel,
        [shape(panels, size, width), shape(1, half_cols)],
        [fill_mask],
        [inv_diag, *parts],
        scratch=[pltpu.VMEM((size, width), F32)],
        flops=6 * panels * size * width * width,
        mib=24,
        name="maps",
    )
    swap = [(i, i ^ 1) for i in range(seg_count)]
    other_whole = lax.ppermute(own_whole, "seg", swap)
    half = size // 2
    half_packed = shape(3 * half // 2, half)
    half_link = shape(half, size)
    link_t, cov, send, send_t = call(
        chip_kernel,
        [shape(size, size), shape(size, size), half_packed, half_link],
        [],
        [own_whole, other_whole],
        flops=18 * size**3,
        name="chip",
    )
    past = None
    after = (jnp.zeros(half_packed.shape, F32),) * 2
    levels = (chips - 1).bit_length()
    prepared = None

    def prepare():
        total = rows + own_cols
        left = jax.ShapeDtypeStruct((panels, total, size), BF16)
        right = jax.ShapeDtypeStruct((panels, size, width), BF16)
        return call(
            functools.partial(prepare_kernel, levels, panels),
            [left, left, right, right, shape(panels, total, width), shape(1, half_cols)],
            [],
            [*bases, *priors, other_whole, maps, links_t, *(past or ())],
            scratch=[pltpu.VMEM((size, width), F32)],
            flops=6 * panels * size * (total * size + size * width + total * width + 3 * size * size),
            mib=24,
            name="prepare",
        )

    for level in range(levels):
        partner = [(i, i ^ (2 << level)) for i in range(seg_count)]
        got = lax.ppermute(send, "seg", partner)
        if level == levels - 1:
            *prepared, token = prepare()
            got = got + token
            after = (got, lax.ppermute(got, "seg", swap))
            break
        got_t = lax.ppermute(send_t, "seg", partner)
        if level == 0:
            got = got + maps_token
        got = (got_t, lax.ppermute(got_t, "seg", swap), got, lax.ppermute(got, "seg", swap))
        outs = [half_packed]
        if level < levels - 2:
            outs += [half_link, shape(size, size), shape(size, size)]
        send, *more = call(
            functools.partial(merge_kernel, level), outs, [], [link_t, cov, *got],
            flops=18 * size**3, name="merge",
        )
        if more:
            send_t, link_t, cov = more
        if past is None:
            past = got
        else:
            past = call(
                functools.partial(join_kernel, level),
                [half_link, half_link, half_packed, half_packed],
                [],
                [*past, *got],
                flops=18 * size**3,
                name="join",
            )
    if prepared is None:
        *prepared, _ = prepare()
    diag, off = call(
        functools.partial(finish_kernel, levels),
        [shape(panels, own_cols, width), shape(panels, rows, width)],
        [fill_mask],
        [*after, *prepared],
        flops=6 * panels * (rows + own_cols) * size * (size + width),
        name="finish",
    )
    return diag, off


def solution(mesh):
    placed = (P("seg", None), P("seg", None), P("seg", None, None), P("seg", "row", None))
    return jax.shard_map(
        body,
        mesh=mesh,
        in_specs=placed,
        out_specs=(P("seg", "row", None), P("seg", "row", None)),
        check_vma=False,
    )
```

```python
import functools

import jax
import jax.numpy as jnp
from jax import lax
from jax.experimental import pallas as pl
from jax.experimental.pallas import tpu as pltpu
from jax.sharding import PartitionSpec as P

BLOCK = 64
LANES = 128
F32 = jnp.float32
BF16 = jnp.bfloat16
NN = (((1,), (0,)), ((), ()))
NT = (((1,), (1,)), ((), ()))
TN = (((0,), (0,)), ((), ()))


def split(x):
    high = x.astype(BF16)
    return high, (x - high.astype(F32)).astype(BF16)


def mm(a, b, dims=NN):
    a = a if isinstance(a, tuple) else split(a)
    b = b if isinstance(b, tuple) else split(b)
    dot = functools.partial(lax.dot_general, dimension_numbers=dims, preferred_element_type=F32)
    return dot(a[0], b[0]) + (dot(a[0], b[1]) + dot(a[1], b[0]))


def carry(link_t, cov, base):
    link_t = link_t if isinstance(link_t, tuple) else split(link_t)
    return mm(mm(link_t, cov), link_t, NT) + base


def pack(cov):
    half = cov.shape[0] // 2
    return jnp.concatenate([cov[:half, :half], cov[:half, half:], cov[half:, half:]], 0)


def unpack(packed):
    half = packed.shape[0] // 3
    first, cross, second = packed[:half], packed[half : 2 * half], packed[2 * half :]
    top = jnp.concatenate([first, cross], 1)
    bottom = jnp.concatenate([cross.T, second], 1)
    return jnp.concatenate([top, bottom], 0)


def is_lower():
    return (lax.axis_index("seg") & 1) == 0


def from_halves(own, other):
    lower = is_lower()
    return jnp.concatenate([jnp.where(lower, own, other), jnp.where(lower, other, own)], 0)


def own_half(whole):
    half = whole.shape[0] // 2
    return jnp.where(is_lower(), whole[:half], whole[half:])


def two_blocks(load, left, right):
    def placed(block, half):
        slab = load(lax.shift_right_logical(block, 1))
        return jnp.where((block & 1) == half, slab, pltpu.roll(slab, BLOCK, 1))

    a, b = placed(left, 0), placed(right, 1)
    lane = lax.broadcasted_iota(jnp.int32, a.shape, 1)
    return jnp.where(lane < BLOCK, a, b)


def tile_of(ref, *lead):
    def load(tile):
        return ref[(*lead, slice(None), pl.ds(pl.multiple_of(tile * LANES, LANES), LANES))]

    return load


def chosen_of(panel, fill_ref, prior_ref=None):
    slots = fill_ref.shape[1]
    if panel > 0:
        return [fill_ref[panel - 1, j] for j in range(slots)]
    first = lax.axis_index("seg") == 0
    last = prior_ref.shape[0] - 1
    return [jnp.where(first, fill_ref[0, j], prior_ref[last, j]) for j in range(slots)]


def vmem(count):
    return [pl.BlockSpec(memory_space=pltpu.VMEM)] * count


def smem(count):
    return [pl.BlockSpec(memory_space=pltpu.SMEM)] * count


def call(kernel, outs, scalars, arrays, far=(), through=(), scratch=(), flops=0, mib=16, name=None):
    moved = sum(a.size * 4 for a in (*arrays, *far)) + sum(o.size * 4 for o in outs)
    first = len(scalars) + len(arrays) + len(far)
    count = len(through)

    def inner(*refs):
        kernel(*refs[:first], *refs[first + count : first + count + len(outs)], *refs[first + 2 * count + len(outs) :])

    return pl.pallas_call(
        inner,
        out_shape=[*outs, *(jax.ShapeDtypeStruct(a.shape, a.dtype) for a in through)],
        in_specs=smem(len(scalars))
        + vmem(len(arrays))
        + [pl.BlockSpec(memory_space=pltpu.HBM)] * len(far)
        + [pl.BlockSpec(memory_space=pl.ANY)] * count,
        out_specs=vmem(len(outs)) + [pl.BlockSpec(memory_space=pl.ANY)] * count,
        scratch_shapes=list(scratch),
        input_output_aliases={first + i: len(outs) + i for i in range(count)},
        cost_estimate=pl.CostEstimate(flops=flops, bytes_accessed=moved, transcendentals=0),
        compiler_params=pltpu.CompilerParams(vmem_limit_bytes=mib << 20),
        name=name,
    )(*scalars, *arrays, *(pltpu.with_memory_space_constraint(a, pltpu.HBM) for a in far), *through)


def shape(*dims):
    return jax.ShapeDtypeStruct(dims, F32)


def kept_rows(mask_ref, panel, slot, rows):
    alive = lax.axis_index("seg") * mask_ref.shape[0] + panel < (
        lax.axis_size("seg") * mask_ref.shape[0] - 1
    )
    return rows * (mask_ref[panel, slot].astype(F32) * alive.astype(F32))


def triangular_mm(left, lower):
    cut = left.shape[1] // 2
    first, second = split(left[:, :cut]), split(left[:, cut:])
    below = split(lower[cut:, :])
    return jnp.concatenate(
        [
            mm(second, (below[0][:, :cut], below[1][:, :cut])) + mm(first, lower[:cut, :cut]),
            mm(second, (below[0][:, cut:], below[1][:, cut:])),
        ],
        1,
    )


def prior_kernel(panel, *refs):
    *scalar_refs, inv_hbm, base_ref, own_ref, pick_high_ref, pick_low_ref, token_ref = refs[:-2]
    inv_ref, sem = refs[-2:]
    copy = pltpu.make_async_copy(inv_hbm.at[panel], inv_ref, sem)
    copy.start()
    token_ref[...] = jnp.zeros_like(token_ref)
    chosen = chosen_of(panel, *scalar_refs)
    own_cols = own_ref.shape[0]
    own_at = pl.ds(pl.multiple_of(lax.axis_index("row") * own_cols, own_cols), own_cols)
    copy.wait()
    picked_t = split(
        jnp.concatenate(
            [
                two_blocks(tile_of(inv_ref), chosen[2 * t], chosen[2 * t + 1]).T
                for t in range(len(chosen) // 2)
            ],
            0,
        )
    )
    pick_high_ref[...], pick_low_ref[...] = picked_t
    base_ref[...] = mm(picked_t, picked_t, NT)
    own_ref[...] = mm(inv_ref[:, own_at].T, inv_ref[...])


def put_rows(mask_ref, panel, distance, part, take):
    row_count = lax.axis_size("row")
    rows = part.shape[1]
    owner = lax.rem(lax.axis_index("row") + (row_count - distance), row_count)
    for s in range(rows // BLOCK):
        slot = owner * (rows // BLOCK) + s
        kept = kept_rows(mask_ref, panel, slot, part[panel, s * BLOCK : (s + 1) * BLOCK, :])
        take(kept, pl.ds(pl.multiple_of(slot * BLOCK, BLOCK), BLOCK))


def links_kernel(distances, missing, mask_ref, *refs):
    parts, refs = refs[: len(distances)], refs[len(distances) :]
    *pick_refs, links_t_ref, rows_ref = refs
    for p in range(links_t_ref.shape[0]):

        def take(kept, at):
            rows_ref[at, :] = kept

        for d, part in zip(distances, parts):
            put_rows(mask_ref, p, d, part, take)
        put_rows(mask_ref, p, missing, parts[0], lambda kept, at: take(jnp.zeros_like(kept), at))
        pick = (pick_refs[2 * p][...], pick_refs[2 * p + 1][...])
        links_t_ref[p] = mm(pick, rows_ref[...], NT)


def segment_kernel(distance, panels, mask_ref, part, early_ref, *refs):
    pick_refs, base_refs = refs[: 2 * panels], refs[2 * panels : 3 * panels]
    links_t_ref, whole_ref = refs[3 * panels :]
    size = links_t_ref.shape[1]
    lane = lax.broadcasted_iota(jnp.int32, (size, size), 1) // BLOCK
    cov = link_t = None
    for p in range(panels - 1, -1, -1):
        pick = (pick_refs[2 * p][...], pick_refs[2 * p + 1][...])
        pieces = [early_ref[p]]

        def take(kept, at):
            late = mm(pick, jnp.concatenate([kept] * (size // BLOCK), 0), NT)
            pieces.append(jnp.where(lane == at.start // BLOCK, late, pieces[-1]))

        put_rows(mask_ref, p, distance, part, take)
        own_t = pieces[-1]
        links_t_ref[p] = own_t
        if cov is None:
            cov, link_t = base_refs[p][...], own_t
        else:
            own_t = split(own_t)
            cov = carry(own_t, cov, base_refs[p][...])
            link_t = mm(own_t, link_t)
    whole_ref[:size] = link_t
    whole_ref[size:] = cov


def maps_kernel(mask_ref, inv_ref, *refs):
    *parts, maps_ref, token_ref, rows_ref = refs
    token_ref[...] = jnp.zeros_like(token_ref)
    for p in range(inv_ref.shape[0]):

        def take(kept, at):
            rows_ref[at, :] = kept

        for d, part in enumerate(parts):
            put_rows(mask_ref, p, d, part, take)
        maps_ref[p] = triangular_mm(rows_ref[...], inv_ref[p])


def chip_kernel(own_ref, other_ref, link_t_ref, cov_ref, packed_ref, half_t_ref):
    size = cov_ref.shape[0]
    lower = is_lower()
    own, other = own_ref[...], other_ref[...]
    down = jnp.where(lower, own, other)
    up = jnp.where(lower, other, own)
    down_t = split(down[:size])
    cov = carry(down_t, up[size:], down[size:])
    link_t = mm(down_t, up[:size])
    link_t_ref[...] = link_t
    cov_ref[...] = cov
    packed_ref[...] = own_half(pack(cov))
    half_t_ref[...] = own_half(link_t)


def merge_kernel(level, link_t_ref, cov_ref, *refs):
    got_t = from_halves(refs[0][...], refs[1][...])
    got = unpack(from_halves(refs[2][...], refs[3][...]))
    own_t, own = link_t_ref[...], cov_ref[...]
    lower = (lax.shift_right_logical(lax.axis_index("seg") // 2, level) & 1) == 0
    down_t = split(jnp.where(lower, own_t, got_t))
    cov = carry(down_t, jnp.where(lower, got, own), jnp.where(lower, own, got))
    refs[4][...] = own_half(pack(cov))
    if len(refs) > 5:
        link_t = mm(down_t, jnp.where(lower, got_t, own_t))
        refs[5][...] = own_half(link_t)
        refs[6][...] = link_t
        refs[7][...] = cov


def join_kernel(level, *refs):
    past_t, past, link_t, cov = (
        from_halves(refs[2 * i][...], refs[2 * i + 1][...]) for i in range(4)
    )
    chip = lax.axis_index("seg") // 2
    below = (lax.shift_right_logical(chip, level) & 1) == 0
    known = (chip & ((1 << level) - 1)) != (1 << level) - 1
    past_parts = split(past_t)
    joined = pack(carry(past_parts, unpack(cov), unpack(past)))
    joined_t = mm(past_parts, link_t)
    out_t = jnp.where(below, jnp.where(known, joined_t, link_t), past_t)
    out = jnp.where(below, jnp.where(known, joined, cov), past)
    for i, whole in enumerate((out_t, out)):
        half = whole.shape[0] // 2
        refs[8 + 2 * i][...] = own_half(whole)
        refs[9 + 2 * i][...] = jnp.where(is_lower(), whole[half:], whole[:half])


def prepare_kernel(levels, panels, *refs):
    base_refs, own_refs, refs = refs[:panels], refs[panels : 2 * panels], refs[2 * panels :]
    (other_ref, maps_ref, links_t_ref), refs = refs[:3], refs[3:]
    past_refs, refs = refs[: 4 * (levels > 1)], refs[4 * (levels > 1) :]
    left_high, left_low, right_high, right_low, const_ref, token_ref, scratch = refs
    token_ref[...] = jnp.zeros_like(token_ref)
    own_cols = own_refs[0].shape[0]
    size = base_refs[0].shape[0]
    row_at = lax.axis_index("row")
    rows = left_high.shape[1] - own_cols
    at_row = lax.broadcasted_iota(jnp.int32, (size, size), 0)
    at_col = lax.broadcasted_iota(jnp.int32, (size, size), 1)
    eye = (at_row == at_col).astype(F32)
    lower = is_lower()
    if past_refs:
        chip = lax.axis_index("seg") // 2
        low = (1 << (levels - 1)) - 1
        known = (chip & low) != low
        past_t = from_halves(past_refs[0][...], past_refs[1][...])
        past = unpack(from_halves(past_refs[2][...], past_refs[3][...]))
        to_t = jnp.where(known, past_t, eye)
        gain = jnp.where(known, past, 0.0)
        other_t = split(other_ref[:size, :])
        to_t = jnp.where(lower, mm(other_t, to_t), to_t)
        gain = jnp.where(lower, carry(other_t, gain, other_ref[size:, :]), gain)
    else:
        to_t = jnp.where(lower, other_ref[:size, :], eye)
        gain = jnp.where(lower, other_ref[size:, :], 0.0)
    own_at = pl.ds(pl.multiple_of(row_at * own_cols, own_cols), own_cols)
    own_rows = pl.ds(pl.multiple_of(row_at * rows, rows), rows)
    for p in range(panels - 1, -1, -1):
        whole = split(maps_ref[p])
        own_t = split(maps_ref[p, :, own_at].T)
        scratch[:, :size] = to_t
        scratch[:, size:] = gain
        to_parts = split(to_t)
        left = jnp.concatenate([scratch[own_rows, :size], mm(own_t, to_parts)], 0)
        left_high[p], left_low[p] = split(left)
        right_high[p], right_low[p] = split(mm(to_parts, whole, TN))
        gains = jnp.concatenate([scratch[own_rows, size:], mm(own_t, gain)], 0)
        const = mm(gains, whole)
        const_ref[p, :rows, :] = const[:rows]
        const_ref[p, rows:, :] = const[rows:] + own_refs[p][...]
        if p > 0:
            link_t = split(links_t_ref[p])
            to_t = mm(link_t, to_t)
            gain = carry(link_t, gain, base_refs[p][...])


def finish_kernel(levels, mask_ref, after_ref, after_other_ref, *refs):
    left_high, left_low, right_high, right_low, const_ref, diag_ref, off_ref = refs
    rows = off_ref.shape[1]
    row_at = lax.axis_index("row")
    chip = lax.axis_index("seg") // 2
    after = from_halves(after_ref[...], after_other_ref[...])
    after = split(unpack(jnp.where((chip & ((1 << levels) // 2)) == 0, after, 0.0)))
    for p in range(const_ref.shape[0]):
        left = (left_high[p], left_low[p])
        right = (right_high[p], right_low[p])
        result = mm(mm(left, after), right) + const_ref[p]
        diag_ref[p] = result[rows:]
        for s in range(rows // BLOCK):
            keep = mask_ref[p, row_at * (rows // BLOCK) + s].astype(F32)
            off_ref[p, s * BLOCK : (s + 1) * BLOCK, :] = -result[s * BLOCK : (s + 1) * BLOCK] * keep


def body(fill_blocks, fill_mask, inv_diag, factor_off):
    panels, width, _ = inv_diag.shape
    rows = factor_off.shape[1]
    seg_count = lax.axis_size("seg")
    row_count = lax.axis_size("row")
    size = rows * row_count
    own_cols = width // row_count
    slots = fill_blocks.shape[1]
    chosen_cols = slots * BLOCK
    chips = seg_count // 2
    half_cols = size // 2

    def turn(x, axis, distance):
        count = lax.axis_size(axis)
        return lax.ppermute(x, axis, [(i, (i + distance) % count) for i in range(count)])

    prior_fill = turn(fill_blocks, "seg", 1)
    ups = [factor_off, turn(factor_off, "row", 1)]
    for _ in range(1, row_count // 2):
        ups.append(turn(ups[-1] + jnp.minimum(jnp.min(prior_fill), 0).astype(F32), "row", 1))
    pick = jax.ShapeDtypeStruct((chosen_cols, width), BF16)
    bases, priors, picks, tokens = [], [], [], []
    for p in range(panels):
        base, own_prior, *high_low, token = call(
            functools.partial(prior_kernel, p),
            [shape(chosen_cols, chosen_cols), shape(own_cols, width), pick, pick, shape(1, 1, width)],
            [fill_blocks] if p else [fill_blocks, prior_fill],
            [],
            far=[inv_diag],
            scratch=[pltpu.VMEM((width, width), F32), pltpu.SemaphoreType.DMA],
            flops=6 * width * (chosen_cols * chosen_cols + own_cols * width),
            name="prior",
        )
        bases.append(base)
        priors.append(own_prior)
        picks += high_low
        tokens.append(token)
    downs = [factor_off + tokens[-1]]
    for _ in range((row_count - 1) // 2):
        downs.append(turn(downs[-1], "row", -1))
    parts = ups + downs[:0:-1]
    last = len(ups) - 1
    early = [d for d in range(row_count) if d != last]
    (links,) = call(
        functools.partial(links_kernel, early, last),
        [shape(panels, size, size)],
        [fill_mask],
        [*(parts[d] for d in early), *picks],
        scratch=[pltpu.VMEM((size, width), F32)],
        flops=6 * panels * size * size * width,
        name="links",
    )
    links_t, own_whole = call(
        functools.partial(segment_kernel, last, panels),
        [shape(panels, size, size), shape(2 * size, size)],
        [fill_mask],
        [parts[last], links, *picks, *bases],
        flops=6 * panels * size * size * width + 18 * (panels - 1) * size**3,
        name="segment",
    )
    maps, maps_token = call(
        maps_kernel,
        [shape(panels, size, width), shape(1, half_cols)],
        [fill_mask],
        [inv_diag, *parts],
        scratch=[pltpu.VMEM((size, width), F32)],
        flops=6 * panels * size * width * width,
        mib=24,
        name="maps",
    )
    swap = [(i, i ^ 1) for i in range(seg_count)]
    other_whole = lax.ppermute(own_whole, "seg", swap)
    half = size // 2
    half_packed = shape(3 * half // 2, half)
    half_link = shape(half, size)
    link_t, cov, send, send_t = call(
        chip_kernel,
        [shape(size, size), shape(size, size), half_packed, half_link],
        [],
        [own_whole, other_whole],
        flops=18 * size**3,
        name="chip",
    )
    past = None
    after = (jnp.zeros(half_packed.shape, F32),) * 2
    levels = (chips - 1).bit_length()
    prepared = None

    def prepare():
        total = rows + own_cols
        left = jax.ShapeDtypeStruct((panels, total, size), BF16)
        right = jax.ShapeDtypeStruct((panels, size, width), BF16)
        return call(
            functools.partial(prepare_kernel, levels, panels),
            [left, left, right, right, shape(panels, total, width), shape(1, half_cols)],
            [],
            [*bases, *priors, other_whole, maps, links_t, *(past or ())],
            scratch=[pltpu.VMEM((size, width), F32)],
            flops=6 * panels * size * (total * size + size * width + total * width + 3 * size * size),
            mib=24,
            name="prepare",
        )

    for level in range(levels):
        partner = [(i, i ^ (2 << level)) for i in range(seg_count)]
        got = lax.ppermute(send, "seg", partner)
        if level == levels - 1:
            *prepared, token = prepare()
            got = got + token
            after = (got, lax.ppermute(got, "seg", swap))
            break
        got_t = lax.ppermute(send_t, "seg", partner)
        if level == 0:
            got = got + maps_token
        got = (got_t, lax.ppermute(got_t, "seg", swap), got, lax.ppermute(got, "seg", swap))
        outs = [half_packed]
        if level < levels - 2:
            outs += [half_link, shape(size, size), shape(size, size)]
        send, *more = call(
            functools.partial(merge_kernel, level), outs, [], [link_t, cov, *got],
            flops=18 * size**3, name="merge",
        )
        if more:
            send_t, link_t, cov = more
        if past is None:
            past = got
        else:
            past = call(
                functools.partial(join_kernel, level),
                [half_link, half_link, half_packed, half_packed],
                [],
                [*past, *got],
                flops=18 * size**3,
                name="join",
            )
    if prepared is None:
        *prepared, _ = prepare()
    diag, off = call(
        functools.partial(finish_kernel, levels),
        [shape(panels, own_cols, width), shape(panels, rows, width)],
        [fill_mask],
        [*after, *prepared],
        flops=6 * panels * (rows + own_cols) * size * (size + width),
        name="finish",
    )
    return diag, off


def solution(mesh):
    placed = (P("seg", None), P("seg", None), P("seg", None, None), P("seg", "row", None))
    return jax.shard_map(
        body,
        mesh=mesh,
        in_specs=placed,
        out_specs=(P("seg", "row", None), P("seg", "row", None)),
        check_vma=False,
    )
```

```python
import functools

import jax
import jax.numpy as jnp
from jax import lax
from jax.experimental import pallas as pl
from jax.experimental.pallas import tpu as pltpu
from jax.sharding import PartitionSpec as P

BLOCK = 64
LANES = 128
F32 = jnp.float32
BF16 = jnp.bfloat16
NN = (((1,), (0,)), ((), ()))
NT = (((1,), (1,)), ((), ()))
TN = (((0,), (0,)), ((), ()))


def split(x):
    high = x.astype(BF16)
    return high, (x - high.astype(F32)).astype(BF16)


def mm(a, b, dims=NN):
    a = a if isinstance(a, tuple) else split(a)
    b = b if isinstance(b, tuple) else split(b)
    dot = functools.partial(lax.dot_general, dimension_numbers=dims, preferred_element_type=F32)
    return dot(a[0], b[0]) + (dot(a[0], b[1]) + dot(a[1], b[0]))


def carry(link_t, cov, base):
    link_t = link_t if isinstance(link_t, tuple) else split(link_t)
    return mm(mm(link_t, cov), link_t, NT) + base


def pack(cov):
    half = cov.shape[0] // 2
    return jnp.concatenate([cov[:half, :half], cov[:half, half:], cov[half:, half:]], 0)


def unpack(packed):
    half = packed.shape[0] // 3
    first, cross, second = packed[:half], packed[half : 2 * half], packed[2 * half :]
    top = jnp.concatenate([first, cross], 1)
    bottom = jnp.concatenate([cross.T, second], 1)
    return jnp.concatenate([top, bottom], 0)


def is_lower():
    return (lax.axis_index("seg") & 1) == 0


def from_halves(own, other):
    lower = is_lower()
    return jnp.concatenate([jnp.where(lower, own, other), jnp.where(lower, other, own)], 0)


def joined_cores(own, other, halves):
    if halves:
        return from_halves(own, other)
    seg_at = lax.axis_index("seg")
    return jnp.where(((seg_at // 2) & 1) == (seg_at & 1), own, other)


def own_half(whole):
    half = whole.shape[0] // 2
    return jnp.where(is_lower(), whole[:half], whole[half:])


def two_blocks(load, left, right):
    def placed(block, half):
        slab = load(lax.shift_right_logical(block, 1))
        return jnp.where((block & 1) == half, slab, pltpu.roll(slab, BLOCK, 1))

    a, b = placed(left, 0), placed(right, 1)
    lane = lax.broadcasted_iota(jnp.int32, a.shape, 1)
    return jnp.where(lane < BLOCK, a, b)


def tile_of(ref, *lead):
    def load(tile):
        return ref[(*lead, slice(None), pl.ds(pl.multiple_of(tile * LANES, LANES), LANES))]

    return load


def chosen_of(panel, fill_ref, prior_ref=None):
    slots = fill_ref.shape[1]
    if panel > 0:
        return [fill_ref[panel - 1, j] for j in range(slots)]
    first = lax.axis_index("seg") == 0
    last = prior_ref.shape[0] - 1
    return [jnp.where(first, fill_ref[0, j], prior_ref[last, j]) for j in range(slots)]


def vmem(count):
    return [pl.BlockSpec(memory_space=pltpu.VMEM)] * count


def smem(count):
    return [pl.BlockSpec(memory_space=pltpu.SMEM)] * count


def call(kernel, outs, scalars, arrays, far=(), through=(), scratch=(), flops=0, mib=16, name=None):
    moved = sum(a.size * 4 for a in (*arrays, *far)) + sum(o.size * 4 for o in outs)
    first = len(scalars) + len(arrays) + len(far)
    count = len(through)

    def inner(*refs):
        kernel(*refs[:first], *refs[first + count : first + count + len(outs)], *refs[first + 2 * count + len(outs) :])

    return pl.pallas_call(
        inner,
        out_shape=[*outs, *(jax.ShapeDtypeStruct(a.shape, a.dtype) for a in through)],
        in_specs=smem(len(scalars))
        + vmem(len(arrays))
        + [pl.BlockSpec(memory_space=pltpu.HBM)] * len(far)
        + [pl.BlockSpec(memory_space=pl.ANY)] * count,
        out_specs=vmem(len(outs)) + [pl.BlockSpec(memory_space=pl.ANY)] * count,
        scratch_shapes=list(scratch),
        input_output_aliases={first + i: len(outs) + i for i in range(count)},
        cost_estimate=pl.CostEstimate(flops=flops, bytes_accessed=moved, transcendentals=0),
        compiler_params=pltpu.CompilerParams(vmem_limit_bytes=mib << 20),
        name=name,
    )(*scalars, *arrays, *(pltpu.with_memory_space_constraint(a, pltpu.HBM) for a in far), *through)


def shape(*dims):
    return jax.ShapeDtypeStruct(dims, F32)


def kept_rows(mask_ref, panel, slot, rows):
    alive = lax.axis_index("seg") * mask_ref.shape[0] + panel < (
        lax.axis_size("seg") * mask_ref.shape[0] - 1
    )
    return rows * (mask_ref[panel, slot].astype(F32) * alive.astype(F32))


def triangular_mm(left, lower):
    cut = left.shape[1] // 2
    first, second = split(left[:, :cut]), split(left[:, cut:])
    below = split(lower[cut:, :])
    return jnp.concatenate(
        [
            mm(second, (below[0][:, :cut], below[1][:, :cut])) + mm(first, lower[:cut, :cut]),
            mm(second, (below[0][:, cut:], below[1][:, cut:])),
        ],
        1,
    )


def raw_kernel(factor_hbm, first_ref, upper_ref, sems):
    copies = [
        pltpu.make_async_copy(factor_hbm.at[1:], upper_ref, sems.at[0]),
        pltpu.make_async_copy(factor_hbm.at[:1], first_ref, sems.at[1]),
    ]
    for copy in copies:
        copy.start()
    for copy in copies:
        copy.wait()


def prior_kernel(panel, *refs):
    *scalar_refs, inv_hbm, factor_hbm, base_ref, own_ref, pick_high_ref, pick_low_ref = refs[:-5]
    first_ref, upper_ref, inv_ref, sem, raw_sems = refs[-5:]
    copy = pltpu.make_async_copy(inv_hbm.at[panel], inv_ref, sem)
    copy.start()
    raw_copies = (
        pltpu.make_async_copy(factor_hbm.at[1:], upper_ref, raw_sems.at[0]),
        pltpu.make_async_copy(factor_hbm.at[:1], first_ref, raw_sems.at[1]),
    )
    for raw_copy in raw_copies:
        raw_copy.start()
    chosen = chosen_of(panel, *scalar_refs)
    own_cols = own_ref.shape[0]
    own_at = pl.ds(pl.multiple_of(lax.axis_index("row") * own_cols, own_cols), own_cols)
    copy.wait()
    picked = split(
        jnp.concatenate(
            [
                two_blocks(tile_of(inv_ref), chosen[2 * t], chosen[2 * t + 1])
                for t in range(len(chosen) // 2)
            ],
            1,
        )
    )
    pick_high_ref[...], pick_low_ref[...] = picked
    base_ref[...] = mm(picked, picked, TN)
    own_ref[...] = mm(inv_ref[:, own_at], inv_ref[...], TN)
    for raw_copy in raw_copies:
        raw_copy.wait()


def put_rows(mask_ref, panel, distance, part, take):
    row_count = lax.axis_size("row")
    rows = part.shape[0]
    owner = lax.rem(lax.axis_index("row") + (row_count - distance), row_count)
    for s in range(rows // BLOCK):
        slot = owner * (rows // BLOCK) + s
        kept = kept_rows(mask_ref, panel, slot, part[s * BLOCK : (s + 1) * BLOCK, :])
        take(kept, pl.ds(pl.multiple_of(slot * BLOCK, BLOCK), BLOCK))


def links_kernel(first, distances, mask_ref, *refs):
    parts, refs = refs[: len(distances)], refs[len(distances) :]
    *pick_refs, links_t_ref, rows_ref = refs
    rows_ref[...] = jnp.zeros_like(rows_ref)
    for p in range(links_t_ref.shape[0]):
        pick = (pick_refs[2 * p][...], pick_refs[2 * p + 1][...])

        def take(kept, at):
            rows_ref[at, :] = mm(kept, pick)

        for d, part in zip(distances, parts):
            put_rows(mask_ref, first + p, d, part[p], take)
        links_t_ref[p] = rows_ref[...].T


def early_kernel(distances, mask_ref, raw_ref, *refs):
    *refs, raw_out_ref, rows_ref = refs
    raw_out_ref[...] = raw_ref[...]
    links_kernel(0, distances, mask_ref, *refs, rows_ref)


def late_kernel(distances, mask_ref, first_t_ref, *refs):
    *in_refs, _, links_t_ref, top_ref, bottom_ref, rows_ref = refs
    links_kernel(1, distances, mask_ref, *in_refs, links_t_ref, rows_ref)
    link_t = links_t_ref[links_t_ref.shape[0] - 1]
    for p in range(links_t_ref.shape[0] - 2, -1, -1):
        link_t = mm(links_t_ref[p], link_t)
    whole = mm(first_t_ref[0], link_t)
    top_ref[...] = whole[: top_ref.shape[0]]
    bottom_ref[...] = whole[top_ref.shape[0] :]


def segment_kernel(distance, panels, mask_ref, *refs):
    first_part, first_early, upper_part, upper_early = refs[:4]
    pick_refs, base_refs = refs[4 : 4 + 2 * panels], refs[4 + 2 * panels : 4 + 3 * panels]
    first_t_ref, upper_t_ref, whole_ref = refs[4 + 3 * panels :]
    size = base_refs[0].shape[0]
    lane = lax.broadcasted_iota(jnp.int32, (size, size), 1) // BLOCK
    cov = link_t = None
    for p in range(panels - 1, -1, -1):
        pick = (pick_refs[2 * p][...], pick_refs[2 * p + 1][...])
        part, early = (upper_part[p - 1], upper_early[p - 1]) if p else (first_part[0], first_early[0])
        pieces = [early]

        def take(kept, at):
            late = jnp.concatenate([mm(kept, pick)] * (size // BLOCK), 0).T
            pieces.append(jnp.where(lane == at.start // BLOCK, late, pieces[-1]))

        put_rows(mask_ref, p, distance, part, take)
        own_t = pieces[-1]
        if p:
            upper_t_ref[p - 1] = own_t
        else:
            first_t_ref[0] = own_t
        if cov is None:
            cov, link_t = base_refs[p][...], own_t
        else:
            own_t = split(own_t)
            cov = carry(own_t, cov, base_refs[p][...])
            link_t = mm(own_t, link_t)
    whole_ref[:size] = link_t
    whole_ref[size:] = cov


def maps_kernel(row_count, mask_ref, inv_ref, *refs):
    firsts, lowers, uppers = (refs[i * row_count : (i + 1) * row_count] for i in range(3))
    maps_ref, rows_ref = refs[3 * row_count :]
    lower = is_lower()

    def take(kept, at):
        rows_ref[at, :] = kept

    for p in range(inv_ref.shape[0]):
        for d in range(row_count):
            part = jnp.where(lower, lowers[d][p - 1], uppers[d][p - 1]) if p else firsts[d][0]
            put_rows(mask_ref, p, d, part, take)
        maps_ref[p] = triangular_mm(rows_ref[...], inv_ref[p])


def chip_kernel(own_ref, other_ref, cov_ref, packed_ref):
    size = cov_ref.shape[0]
    lower = is_lower()
    own, other = own_ref[...], other_ref[...]
    down_t = jnp.where(lower, own[:size], other[:size])
    up = jnp.where(lower, other[size:], own[size:])
    cov = carry(down_t, up, jnp.where(lower, own[size:], other[size:]))
    cov_ref[...] = cov
    packed_ref[...] = own_half(pack(cov))


def chip_link_kernel(own_ref, other_ref, *refs):
    link_t_ref, half_t_ref = refs[5:]
    size = link_t_ref.shape[0]
    lower = is_lower()
    down_t = jnp.where(lower, own_ref[:size, :], other_ref[:size, :])
    late_t, other_late_t = (jnp.concatenate([a[...], b[...]], 0) for a, b in (refs[:2], refs[2:4]))
    link_t = mm(down_t, jnp.where(lower, other_late_t, late_t))
    link_t_ref[...] = link_t
    half_t_ref[...] = own_half(link_t)


def extend_kernel(link_t_ref, cov_ref, own_ref, other_ref, packed_ref):
    after = unpack(from_halves(own_ref[...], other_ref[...]))
    packed_ref[...] = pack(carry(link_t_ref[...], after, cov_ref[...]))


def extend_link_kernel(link_t_ref, own_t_ref, other_t_ref, out_ref):
    out_ref[...] = mm(link_t_ref[...], from_halves(own_t_ref[...], other_t_ref[...]))


def join_kernel(level, *refs):
    past_t, past, link_t, cov = (
        joined_cores(refs[2 * i][...], refs[2 * i + 1][...], i < 2) for i in range(4)
    )
    chip = lax.axis_index("seg") // 2
    below = (lax.shift_right_logical(chip, level) & 1) == 0
    known = (chip & ((1 << level) - 1)) != (1 << level) - 1
    past_parts = split(past_t)
    joined = pack(carry(past_parts, unpack(cov), unpack(past)))
    joined_t = mm(past_parts, link_t)
    out_t = jnp.where(below, jnp.where(known, joined_t, link_t), past_t)
    out = jnp.where(below, jnp.where(known, joined, cov), past)
    for ref, whole in zip(refs[8:], (out_t, out_t, out, out)):
        ref[...] = own_half(whole)
    for ref, whole in ((refs[9], out_t), (refs[11], out)):
        half = whole.shape[0] // 2
        ref[...] = jnp.where(is_lower(), whole[half:], whole[:half])


def prepare_kernel(panels, *refs):
    base_refs, own_refs, refs = refs[:panels], refs[panels : 2 * panels], refs[2 * panels :]
    (other_ref, top_ref, bottom_ref, maps_ref, lower_t_ref, upper_t_ref), refs = refs[:6], refs[6:]
    left_high, left_low, right_high, right_low, const_ref, token_ref, scratch = refs
    token_ref[...] = jnp.zeros_like(token_ref)
    own_cols = own_refs[0].shape[0]
    size = base_refs[0].shape[0]
    row_at = lax.axis_index("row")
    rows = left_high.shape[1] - own_cols
    at_row = lax.broadcasted_iota(jnp.int32, (size, size), 0)
    at_col = lax.broadcasted_iota(jnp.int32, (size, size), 1)
    eye = (at_row == at_col).astype(F32)
    lower = is_lower()
    to_t = jnp.where(lower, jnp.concatenate([top_ref[...], bottom_ref[...]], 0), eye)
    gain = jnp.where(lower, other_ref[size:, :], 0.0)
    own_at = pl.ds(pl.multiple_of(row_at * own_cols, own_cols), own_cols)
    own_rows = pl.ds(pl.multiple_of(row_at * rows, rows), rows)
    for p in range(panels - 1, -1, -1):
        whole = split(maps_ref[p])
        own_t = split(maps_ref[p, :, own_at].T)
        scratch[:, :size] = to_t
        scratch[:, size:] = gain
        to_parts = split(to_t)
        left = jnp.concatenate([scratch[own_rows, :size], mm(own_t, to_parts)], 0)
        left_high[p], left_low[p] = split(left)
        right_high[p], right_low[p] = split(mm(to_parts, whole, TN))
        gains = jnp.concatenate([scratch[own_rows, size:], mm(own_t, gain)], 0)
        const = mm(gains, whole)
        const_ref[p, :rows, :] = const[:rows]
        const_ref[p, rows:, :] = const[rows:] + own_refs[p][...]
        if p > 0:
            link_t = split(jnp.where(lower, lower_t_ref[p - 1], upper_t_ref[p - 1]))
            to_t = mm(link_t, to_t)
            gain = carry(link_t, gain, base_refs[p][...])


def finish_kernel(levels, mask_ref, after_ref, after_other_ref, *refs):
    past_refs, refs = refs[: 4 * (levels > 1)], refs[4 * (levels > 1) :]
    left_high, left_low, right_high, right_low, const_ref, diag_ref, off_ref = refs
    rows = off_ref.shape[1]
    row_at = lax.axis_index("row")
    chip = lax.axis_index("seg") // 2
    after = joined_cores(after_ref[...], after_other_ref[...], levels < 2)
    top = (1 << levels) // 2
    after = unpack(jnp.where((chip & top) == 0, after, 0.0))
    if past_refs:
        past_t = from_halves(past_refs[0][...], past_refs[1][...])
        past = unpack(from_halves(past_refs[2][...], past_refs[3][...]))
        after = jnp.where((chip & (top - 1)) != top - 1, carry(past_t, after, past), after)
    after = split(after)
    for p in range(const_ref.shape[0]):
        left = (left_high[p], left_low[p])
        right = (right_high[p], right_low[p])
        result = mm(mm(left, after), right) + const_ref[p]
        diag_ref[p] = result[rows:]
        for s in range(rows // BLOCK):
            keep = mask_ref[p, row_at * (rows // BLOCK) + s].astype(F32)
            off_ref[p, s * BLOCK : (s + 1) * BLOCK, :] = -result[s * BLOCK : (s + 1) * BLOCK] * keep


def body(fill_blocks, fill_mask, inv_diag, factor_off):
    panels, width, _ = inv_diag.shape
    rows = factor_off.shape[1]
    seg_count = lax.axis_size("seg")
    row_count = lax.axis_size("row")
    size = rows * row_count
    own_cols = width // row_count
    slots = fill_blocks.shape[1]
    chosen_cols = slots * BLOCK
    chips = seg_count // 2
    half_cols = size // 2

    def turn_seg(x):
        return lax.ppermute(x, "seg", [(i, (i + 1) % seg_count) for i in range(seg_count)])

    def turn(x, distance, core=None):
        route = []
        for i in range(seg_count):
            for j in range(row_count):
                moves = distance if core is None or i % 2 == core else 0
                route.append((i * row_count + j, i * row_count + (j + moves) % row_count))
        return lax.ppermute(x, ("seg", "row"), route)

    def gather(x, x_down, core, gate):
        ups, downs = [x, turn(x, 1, core)], [x_down]
        for _ in range(1, row_count // 2):
            ups.append(turn(ups[-1] + gate, 1, core))
        for _ in range((row_count - 1) // 2):
            downs.append(turn(downs[-1], -1, core))
        return ups + downs[:0:-1]

    prior_fill = turn_seg(fill_blocks)
    pick = jax.ShapeDtypeStruct((width, chosen_cols), BF16)
    raw_shapes = [shape(1, rows, width), shape(panels - 1, rows, width)]
    bases, priors, picks, raws = [], [], [], []
    for p in range(panels):
        base, own_prior, *high_low, raw_first, raw_upper = call(
            functools.partial(prior_kernel, p),
            [shape(chosen_cols, chosen_cols), shape(own_cols, width), pick, pick, *raw_shapes],
            [fill_blocks] if p else [fill_blocks, prior_fill],
            [],
            far=[inv_diag, factor_off],
            scratch=[
                pltpu.VMEM((width, width), F32),
                pltpu.SemaphoreType.DMA,
                pltpu.SemaphoreType.DMA((2,)),
            ],
            flops=6 * width * (chosen_cols * chosen_cols + own_cols * width),
            name="prior",
        )
        bases.append(base)
        priors.append(own_prior)
        picks += high_low
        raws.append((raw_first, raw_upper))
    index_gate = jnp.minimum(jnp.min(prior_fill), 0).astype(F32)
    raw_first, raw_upper = call(
        raw_kernel,
        raw_shapes,
        [],
        [],
        far=[factor_off],
        scratch=[pltpu.SemaphoreType.DMA((2,))],
        name="raw",
    )
    firsts = gather(raw_first, raws[-1][0], None, index_gate)
    lowers = gather(raw_upper, raws[-1][1], 0, index_gate)
    last = row_count // 2
    early = [d for d in range(row_count) if d != last]
    first_early, raw_late = call(
        functools.partial(early_kernel, early),
        [shape(1, size, size), raw_shapes[1]],
        [fill_mask],
        [raws[-1][1], *(firsts[d] for d in early), *picks[:2]],
        scratch=[pltpu.VMEM((size, chosen_cols), F32)],
        flops=6 * size * size * width,
        name="early",
    )
    uppers = gather(raw_late, raw_late, 1, index_gate)
    (upper_early,) = call(
        functools.partial(links_kernel, 1, early),
        [shape(panels - 1, size, size)],
        [fill_mask],
        [*(lowers[d] for d in early), *picks[2:]],
        scratch=[pltpu.VMEM((size, chosen_cols), F32)],
        flops=6 * (panels - 1) * size * size * width,
        name="links",
    )
    first_t, lower_t, own_whole = call(
        functools.partial(segment_kernel, last, panels),
        [shape(1, size, size), shape(panels - 1, size, size), shape(2 * size, size)],
        [fill_mask],
        [firsts[last], first_early, lowers[last], upper_early, *picks, *bases],
        flops=6 * panels * rows * size * width + 18 * (panels - 1) * size**3,
        name="segment",
    )
    (maps,) = call(
        functools.partial(maps_kernel, row_count),
        [shape(panels, size, width)],
        [fill_mask],
        [inv_diag, *firsts, *lowers, *uppers],
        scratch=[pltpu.VMEM((size, width), F32)],
        flops=6 * panels * size * width * width,
        mib=24,
        name="maps",
    )
    swap = [(i, i ^ 1) for i in range(seg_count)]
    late_gate = uppers[1][0, :1, :size] * 0.0
    other_whole = lax.ppermute(own_whole + late_gate, "seg", swap)
    half = size // 2
    half_packed = shape(3 * half // 2, half)
    half_link = shape(half, size)
    cov, send = call(
        chip_kernel, [shape(size, size), half_packed], [], [own_whole, other_whole],
        flops=12 * size**3, name="chip",
    )
    upper_t, *own_late = call(
        functools.partial(late_kernel, list(range(row_count))),
        [shape(panels - 1, size, size), half_link, half_link],
        [fill_mask],
        [first_t, *uppers, *picks[2:], send],
        scratch=[pltpu.VMEM((size, chosen_cols), F32)],
        flops=6 * (panels - 1) * size * size * width + 6 * (panels - 1) * size**3,
        name="late",
    )
    other_late = [lax.ppermute(x, "seg", swap) for x in own_late]
    past = None
    after = (jnp.zeros(half_packed.shape, F32),) * 2
    levels = (chips - 1).bit_length()
    prepared = None

    def prepare():
        total = rows + own_cols
        left = jax.ShapeDtypeStruct((panels, total, size), BF16)
        right = jax.ShapeDtypeStruct((panels, size, width), BF16)
        return call(
            functools.partial(prepare_kernel, panels),
            [left, left, right, right, shape(panels, total, width), shape(1, half_cols)],
            [],
            [*bases, *priors, other_whole, *other_late, maps, lower_t, upper_t],
            scratch=[pltpu.VMEM((size, width), F32)],
            flops=6 * panels * size * (total * size + size * width + total * width + 3 * size * size),
            mib=24,
            name="prepare",
        )

    for level in range(levels):
        bit = 1 << level
        if level > 0:
            (send,) = call(
                extend_kernel, [shape(3 * half, half)], [], [link_t, cov, *past[2:]],
                flops=12 * size**3, name="extend",
            )
            if level < levels - 1:
                (send_t,) = call(
                    extend_link_kernel, [shape(size, size)], [], [link_t, *past[:2]],
                    flops=6 * size**3, name="extend_link",
                )
        got = got_t = None
        for step in range(max(bit // 2, 1)):
            route = list(range(seg_count))
            for base_chip in range(0, chips, 2 * bit):
                for core in range(2):
                    upper_at = 2 * (base_chip + bit) + core
                    lower_at = 2 * (base_chip + (2 * step + core) % bit) + core
                    route[upper_at], route[lower_at] = lower_at, upper_at
            route = list(enumerate(route))
            here = ((lax.axis_index("seg") // 2) & (bit - 1)) // 2 == step
            piece = lax.ppermute(send, "seg", route)
            got = piece if step == 0 else jnp.where(here, piece, got)
            if level == 0 and levels > 1:
                link_t, send_t = call(
                    chip_link_kernel, [shape(size, size), half_link], [],
                    [own_whole, other_whole, *own_late, *other_late, piece],
                    flops=6 * size**3, name="chip_link",
                )
            if level < levels - 1:
                piece_t = lax.ppermute(send_t, "seg", route)
                got_t = piece_t if step == 0 else jnp.where(here, piece_t, got_t)
        if level == levels - 1:
            *prepared, token = prepare()
            got = got + token
            after = (got, lax.ppermute(got, "seg", swap))
            break
        got = (got_t, lax.ppermute(got_t, "seg", swap), got, lax.ppermute(got, "seg", swap))
        if past is None:
            past = got
        else:
            past = call(
                functools.partial(join_kernel, level),
                [half_link, half_link, half_packed, half_packed],
                [],
                [*past, *got],
                flops=18 * size**3,
                name="join",
            )
    if prepared is None:
        *prepared, _ = prepare()
    diag, off = call(
        functools.partial(finish_kernel, levels),
        [shape(panels, own_cols, width), shape(panels, rows, width)],
        [fill_mask],
        [*after, *(past or ()), *prepared],
        flops=6 * panels * (rows + own_cols) * size * (size + width),
        name="finish",
    )
    return diag, off


def solution(mesh):
    placed = (P("seg", None), P("seg", None), P("seg", None, None), P("seg", "row", None))
    return jax.shard_map(
        body,
        mesh=mesh,
        in_specs=placed,
        out_specs=(P("seg", "row", None), P("seg", "row", None)),
        check_vma=False,
    )
```

```python
import functools

import jax
import jax.numpy as jnp
from jax import lax
from jax.experimental import pallas as pl
from jax.experimental.pallas import tpu as pltpu
from jax.sharding import PartitionSpec as P

BLOCK = 64
LANES = 128
F32 = jnp.float32
BF16 = jnp.bfloat16
NN = (((1,), (0,)), ((), ()))
NT = (((1,), (1,)), ((), ()))
TN = (((0,), (0,)), ((), ()))


def split(x):
    high = x.astype(BF16)
    return high, (x - high.astype(F32)).astype(BF16)


def mm(a, b, dims=NN):
    a = a if isinstance(a, tuple) else split(a)
    b = b if isinstance(b, tuple) else split(b)
    dot = functools.partial(lax.dot_general, dimension_numbers=dims, preferred_element_type=F32)
    return dot(a[0], b[0]) + (dot(a[0], b[1]) + dot(a[1], b[0]))


def carry(link_t, cov, base):
    link_t = link_t if isinstance(link_t, tuple) else split(link_t)
    return mm(mm(link_t, cov), link_t, NT) + base


def pack(cov):
    half = cov.shape[0] // 2
    part = half // 2
    first, second = cov[:half, :half], cov[half:, half:]
    lane = lax.broadcasted_iota(jnp.int32, (part, half), 1)
    last = jnp.where(lane < part, pltpu.roll(first[part:], part, 1), second[part:])
    return jnp.concatenate([cov[:half, half:], first[:part], second[:part], last], 0)


def unpack(packed):
    half = packed.shape[1]
    part = half // 2
    cross, last = packed[:half], packed[2 * half :]
    row = lax.broadcasted_iota(jnp.int32, (half, half), 0)
    lane = lax.broadcasted_iota(jnp.int32, (half, half), 1)

    def symmetric(top, bottom):
        upper = jnp.concatenate([top, bottom], 0)
        return jnp.where((row < part) | (lane >= part), upper, upper.T)

    first = symmetric(packed[half : half + part], pltpu.roll(last, part, 1))
    second = symmetric(packed[half + part : 2 * half], last)
    top = jnp.concatenate([first, cross], 1)
    bottom = jnp.concatenate([cross.T, second], 1)
    return jnp.concatenate([top, bottom], 0)


def is_lower():
    return (lax.axis_index("seg") & 1) == 0


def from_halves(own, other):
    lower = is_lower()
    return jnp.concatenate([jnp.where(lower, own, other), jnp.where(lower, other, own)], 0)


def own_half(whole):
    half = whole.shape[0] // 2
    return jnp.where(is_lower(), whole[:half], whole[half:])


def two_blocks(load, left, right):
    def placed(block, half):
        slab = load(lax.shift_right_logical(block, 1))
        return jnp.where((block & 1) == half, slab, pltpu.roll(slab, BLOCK, 1))

    a, b = placed(left, 0), placed(right, 1)
    lane = lax.broadcasted_iota(jnp.int32, a.shape, 1)
    return jnp.where(lane < BLOCK, a, b)


def tile_of(ref, *lead):
    def load(tile):
        return ref[(*lead, slice(None), pl.ds(pl.multiple_of(tile * LANES, LANES), LANES))]

    return load


def chosen_of(panel, fill_ref, prior_ref=None):
    slots = fill_ref.shape[1]
    if panel > 0:
        return [fill_ref[panel - 1, j] for j in range(slots)]
    first = lax.axis_index("seg") == 0
    last = prior_ref.shape[0] - 1
    return [jnp.where(first, fill_ref[0, j], prior_ref[last, j]) for j in range(slots)]


def order_of(chosen, blocks):
    slots = len(chosen)
    rest = [jnp.int32(0)] * (blocks - slots)
    place = []
    seen = jnp.int32(0)
    for b in range(blocks):
        hit = jnp.int32(0)
        where = jnp.int32(0)
        for j in range(slots):
            same = (chosen[j] == b).astype(jnp.int32)
            hit = hit + same
            where = where + same * j
        free = 1 - hit
        for q in range(blocks - slots):
            rest[q] = rest[q] + jnp.where(seen == q, free * b, 0)
        place.append(jnp.where(hit > 0, where, slots + seen))
        seen = seen + free
    return rest, place


def vmem(count):
    return [pl.BlockSpec(memory_space=pltpu.VMEM)] * count


def smem(count):
    return [pl.BlockSpec(memory_space=pltpu.SMEM)] * count


def call(kernel, outs, scalars, arrays, far=(), through=(), scratch=(), flops=0, mib=16, name=None):
    moved = sum(a.size * 4 for a in (*arrays, *far)) + sum(o.size * 4 for o in outs)
    first = len(scalars) + len(arrays) + len(far)
    count = len(through)

    def inner(*refs):
        kernel(*refs[:first], *refs[first + count : first + count + len(outs)], *refs[first + 2 * count + len(outs) :])

    return pl.pallas_call(
        inner,
        out_shape=[*outs, *(jax.ShapeDtypeStruct(a.shape, a.dtype) for a in through)],
        in_specs=smem(len(scalars))
        + vmem(len(arrays))
        + [pl.BlockSpec(memory_space=pltpu.HBM)] * len(far)
        + [pl.BlockSpec(memory_space=pl.ANY)] * count,
        out_specs=vmem(len(outs)) + [pl.BlockSpec(memory_space=pl.ANY)] * count,
        scratch_shapes=list(scratch),
        input_output_aliases={first + i: len(outs) + i for i in range(count)},
        cost_estimate=pl.CostEstimate(flops=flops, bytes_accessed=moved, transcendentals=0),
        compiler_params=pltpu.CompilerParams(vmem_limit_bytes=mib << 20),
        name=name,
    )(*scalars, *arrays, *(pltpu.with_memory_space_constraint(a, pltpu.HBM) for a in far), *through)


def shape(*dims):
    return jax.ShapeDtypeStruct(dims, F32)


def kept_rows(mask_ref, panel, slot, rows):
    alive = lax.axis_index("seg") * mask_ref.shape[0] + panel < (
        lax.axis_size("seg") * mask_ref.shape[0] - 1
    )
    return rows * (mask_ref[panel, slot].astype(F32) * alive.astype(F32))


def triangular_mm(left, lower):
    cut = left.shape[1] // 2
    first, second = split(left[:, :cut]), split(left[:, cut:])
    below = split(lower[cut:, :])
    return jnp.concatenate(
        [
            mm(second, (below[0][:, :cut], below[1][:, :cut])) + mm(first, lower[:cut, :cut]),
            mm(second, (below[0][:, cut:], below[1][:, cut:])),
        ],
        1,
    )


def prior_kernel(panel, *refs):
    *scalar_refs, inv_hbm, base_ref, own_ref, pick_high_ref, pick_low_ref, token_ref = refs[:-2]
    inv_ref, sem = refs[-2:]
    copy = pltpu.make_async_copy(inv_hbm.at[panel], inv_ref, sem)
    copy.start()
    token_ref[...] = jnp.zeros_like(token_ref)
    chosen = chosen_of(panel, *scalar_refs)
    own_cols = own_ref.shape[0]
    own_at = pl.ds(pl.multiple_of(lax.axis_index("row") * own_cols, own_cols), own_cols)
    copy.wait()
    picked = split(
        jnp.concatenate(
            [
                two_blocks(tile_of(inv_ref), chosen[2 * t], chosen[2 * t + 1])
                for t in range(len(chosen) // 2)
            ],
            1,
        )
    )
    pick_high_ref[...], pick_low_ref[...] = picked
    base_ref[...] = mm(picked, picked, TN)
    own_ref[...] = mm(inv_ref[:, own_at], inv_ref[...], TN)


def send_kernel(
    mask_hbm, fill_hbm, factor_hbm, inv_hbm, sent_ref, rest_ref,
    mask_ref, fill_ref, factor_ref, inv_ref, map_ref, sems
):
    panels, rows, width = factor_ref.shape
    cut = width // 2
    row_at = lax.axis_index("row")
    small = [
        pltpu.make_async_copy(mask_hbm, mask_ref, sems.at[0, 0]),
        pltpu.make_async_copy(fill_hbm, fill_ref, sems.at[0, 1]),
        pltpu.make_async_copy(factor_hbm, factor_ref, sems.at[0, 2]),
    ]
    large = [
        (
            pltpu.make_async_copy(inv_hbm.at[p, cut:, :], inv_ref.at[p - 1, cut:, :], sems.at[p, 0]),
            pltpu.make_async_copy(
                inv_hbm.at[p, :cut, :cut], inv_ref.at[p - 1, :cut, :cut], sems.at[p, 1]
            ),
        )
        for p in range(1, panels)
    ]
    for copy in (*small, *(copy for pair in large for copy in pair)):
        copy.start()
    for copy in small:
        copy.wait()

    def kept_own(p):
        return jnp.concatenate(
            [
                kept_rows(
                    mask_ref, p, row_at * (rows // BLOCK) + s,
                    factor_ref[p, s * BLOCK : (s + 1) * BLOCK, :],
                )
                for s in range(rows // BLOCK)
            ],
            0,
        )

    sent_ref[:, :width] = kept_own(0)
    for p in range(1, panels):
        chosen = chosen_of(p, fill_ref)
        rest, _ = order_of(chosen, width // BLOCK)
        kept = kept_own(p)
        for copy in large[p - 1]:
            copy.wait()
        map_ref[...] = triangular_mm(kept, inv_ref[p - 1])
        for ref, wanted, at in (
            (sent_ref, chosen, width + (p - 1) * len(chosen) * BLOCK),
            (rest_ref, rest, (p - 1) * len(rest) * BLOCK),
        ):
            for t in range(len(wanted) // 2):
                ref[:, at + t * LANES : at + (t + 1) * LANES] = two_blocks(
                    tile_of(map_ref), wanted[2 * t], wanted[2 * t + 1]
                )


def rows_from(distance, rows):
    row_count = lax.axis_size("row")
    owner = lax.rem(lax.axis_index("row") + (row_count - distance), row_count)
    return pl.ds(pl.multiple_of(owner * rows, rows), rows)


def links_kernel(distances, panels, *refs):
    parts, (high_ref, low_ref, links_t_ref, rows_ref) = refs[: len(distances)], refs[len(distances) :]
    width = high_ref.shape[0]
    size = rows_ref.shape[0]
    pick = (high_ref[...], low_ref[...])
    rows_ref[...] = jnp.zeros_like(rows_ref)
    for p in range(panels):
        for d, part in zip(distances, parts):
            at = rows_from(d, part.shape[0])
            if p == 0:
                rows_ref[at, :] = mm(part[:, :width], pick)
            else:
                rows_ref[at, :] = part[:, width + (p - 1) * size : width + p * size]
        links_t_ref[p] = rows_ref[...].T


def segment_kernel(distance, panels, part, high_ref, low_ref, early_ref, *refs):
    base_refs, (links_t_ref, whole_ref) = refs[:panels], refs[panels:]
    rows = part.shape[0]
    width, size = high_ref.shape
    lane = lax.broadcasted_iota(jnp.int32, (size, size), 1) // rows
    here = lane == rows_from(distance, rows).start // rows
    link_t = cov = None
    for p in range(panels - 1, -1, -1):
        if p == 0:
            late = mm(part[:, :width], (high_ref[...], low_ref[...]))
        else:
            late = part[:, width + (p - 1) * size : width + p * size]
        late_t = jnp.concatenate([late] * (size // rows), 0).T
        own_t = jnp.where(here, late_t, early_ref[p])
        links_t_ref[p] = own_t
        if cov is None:
            cov, link_t = base_refs[p][...], own_t
        else:
            own_t = split(own_t)
            cov = carry(own_t, cov, base_refs[p][...])
            link_t = mm(own_t, link_t)
    whole_ref[:size] = link_t
    whole_ref[size:] = cov


def first_map_kernel(inv_ref, *refs):
    *parts, _, map_ref, token_ref, rows_ref = refs
    width = map_ref.shape[1]
    token_ref[...] = jnp.zeros_like(token_ref)
    for d, part in enumerate(parts):
        rows_ref[rows_from(d, part.shape[0]), :] = part[:, :width]
    map_ref[...] = triangular_mm(rows_ref[...], inv_ref[0])


def chip_kernel(own_ref, other_ref, link_t_ref, cov_ref, packed_ref, half_t_ref):
    size = cov_ref.shape[0]
    lower = is_lower()
    own, other = own_ref[...], other_ref[...]
    down = jnp.where(lower, own, other)
    up = jnp.where(lower, other, own)
    down_t = split(down[:size])
    cov = carry(down_t, up[size:], down[size:])
    link_t = mm(down_t, up[:size])
    link_t_ref[...] = link_t
    cov_ref[...] = cov
    packed_ref[...] = own_half(pack(cov))
    half_t_ref[...] = own_half(link_t)


def merge_kernel(level, link_t_ref, cov_ref, *refs):
    got_t = from_halves(refs[0][...], refs[1][...])
    got = unpack(from_halves(refs[2][...], refs[3][...]))
    own_t, own = link_t_ref[...], cov_ref[...]
    lower = (lax.shift_right_logical(lax.axis_index("seg") // 2, level) & 1) == 0
    down_t = split(jnp.where(lower, own_t, got_t))
    cov = carry(down_t, jnp.where(lower, got, own), jnp.where(lower, own, got))
    refs[4][...] = own_half(pack(cov))
    if len(refs) > 5:
        link_t = mm(down_t, jnp.where(lower, got_t, own_t))
        refs[5][...] = own_half(link_t)
        refs[6][...] = link_t
        refs[7][...] = cov


def join_kernel(level, *refs):
    past_t, past, link_t, cov = (
        from_halves(refs[2 * i][...], refs[2 * i + 1][...]) for i in range(4)
    )
    chip = lax.axis_index("seg") // 2
    below = (lax.shift_right_logical(chip, level) & 1) == 0
    known = (chip & ((1 << level) - 1)) != (1 << level) - 1
    past_parts = split(past_t)
    joined = pack(carry(past_parts, unpack(cov), unpack(past)))
    joined_t = mm(past_parts, link_t)
    out_t = jnp.where(below, jnp.where(known, joined_t, link_t), past_t)
    out = jnp.where(below, jnp.where(known, joined, cov), past)
    for i, whole in enumerate((out_t, out)):
        half = whole.shape[0] // 2
        refs[8 + 2 * i][...] = own_half(whole)
        refs[9 + 2 * i][...] = jnp.where(is_lower(), whole[half:], whole[:half])


def prepare_kernel(levels, panels, row_count, fill_ref, *refs):
    base_refs, own_refs, refs = refs[:panels], refs[panels : 2 * panels], refs[2 * panels :]
    (other_ref, first_map_ref, links_t_ref), refs = refs[:3], refs[3:]
    parts, rests, refs = refs[:row_count], refs[row_count : 2 * row_count], refs[2 * row_count :]
    past_refs, refs = refs[: 4 * (levels > 1)], refs[4 * (levels > 1) :]
    left_high, left_low, right_high, right_low, const_ref, token_ref, scratch, order_ref = refs
    token_ref[...] = jnp.zeros_like(token_ref)
    own_cols, width = own_refs[0].shape
    size = base_refs[0].shape[0]
    row_at = lax.axis_index("row")
    rows = left_high.shape[1] - own_cols
    at_row = lax.broadcasted_iota(jnp.int32, (size, size), 0)
    at_col = lax.broadcasted_iota(jnp.int32, (size, size), 1)
    eye = (at_row == at_col).astype(F32)
    lower = is_lower()
    if past_refs:
        chip = lax.axis_index("seg") // 2
        low = (1 << (levels - 1)) - 1
        known = (chip & low) != low
        past_t = from_halves(past_refs[0][...], past_refs[1][...])
        past = unpack(from_halves(past_refs[2][...], past_refs[3][...]))
        to_t = jnp.where(known, past_t, eye)
        gain = jnp.where(known, past, 0.0)
        other_t = split(other_ref[:size, :])
        to_t = jnp.where(lower, mm(other_t, to_t), to_t)
        gain = jnp.where(lower, carry(other_t, gain, other_ref[size:, :]), gain)
    else:
        to_t = jnp.where(lower, other_ref[:size, :], eye)
        gain = jnp.where(lower, other_ref[size:, :], 0.0)
    own_at = pl.ds(pl.multiple_of(row_at * own_cols, own_cols), own_cols)
    own_rows = pl.ds(pl.multiple_of(row_at * rows, rows), rows)
    for p in range(panels - 1, -1, -1):
        if p == 0:
            whole, own_map = first_map_ref[...], first_map_ref[:, own_at]
        else:
            _, place = order_of(chosen_of(p, fill_ref), width // BLOCK)
            chosen_at, rest_at = width + (p - 1) * size, (p - 1) * (width - size)
            for d in range(row_count):
                at = rows_from(d, rows)
                order_ref[at, :size] = parts[d][:, chosen_at : chosen_at + size]
                order_ref[at, size:] = rests[d][:, rest_at : rest_at + width - size]
            whole = jnp.concatenate(
                [
                    two_blocks(tile_of(order_ref), place[2 * t], place[2 * t + 1])
                    for t in range(len(place) // 2)
                ],
                1,
            )
            order_ref[...] = whole
            own_map = order_ref[:, own_at]
        whole, own_t = split(whole), split(own_map.T)
        scratch[:, :size] = to_t
        scratch[:, size:] = gain
        to_parts = split(to_t)
        left = jnp.concatenate([scratch[own_rows, :size], mm(own_t, to_parts)], 0)
        left_high[p], left_low[p] = split(left)
        right_high[p], right_low[p] = split(mm(to_parts, whole, TN))
        gains = jnp.concatenate([scratch[own_rows, size:], mm(own_t, gain)], 0)
        const = mm(gains, whole)
        const_ref[p, :rows, :] = const[:rows]
        const_ref[p, rows:, :] = const[rows:] + own_refs[p][...]
        if p > 0:
            link_t = split(links_t_ref[p])
            to_t = mm(link_t, to_t)
            gain = carry(link_t, gain, base_refs[p][...])


def finish_kernel(levels, mask_ref, after_ref, after_other_ref, *refs):
    left_high, left_low, right_high, right_low, const_ref, diag_ref, off_ref = refs
    rows = off_ref.shape[1]
    row_at = lax.axis_index("row")
    chip = lax.axis_index("seg") // 2
    after = from_halves(after_ref[...], after_other_ref[...])
    after = split(unpack(jnp.where((chip & ((1 << levels) // 2)) == 0, after, 0.0)))
    for p in range(const_ref.shape[0]):
        left = (left_high[p], left_low[p])
        right = (right_high[p], right_low[p])
        result = mm(mm(left, after), right) + const_ref[p]
        diag_ref[p] = result[rows:]
        for s in range(rows // BLOCK):
            keep = mask_ref[p, row_at * (rows // BLOCK) + s].astype(F32)
            off_ref[p, s * BLOCK : (s + 1) * BLOCK, :] = -result[s * BLOCK : (s + 1) * BLOCK] * keep


def body(fill_blocks, fill_mask, inv_diag, factor_off):
    panels, width, _ = inv_diag.shape
    rows = factor_off.shape[1]
    seg_count = lax.axis_size("seg")
    row_count = lax.axis_size("row")
    size = rows * row_count
    own_cols = width // row_count
    slots = fill_blocks.shape[1]
    chosen_cols = slots * BLOCK
    rest_cols = width - chosen_cols
    chips = seg_count // 2
    half_cols = size // 2

    def turn(x, axis, distance):
        count = lax.axis_size(axis)
        return lax.ppermute(x, axis, [(i, (i + distance) % count) for i in range(count)])

    sent, rest = call(
        send_kernel,
        [shape(rows, width + (panels - 1) * chosen_cols), shape(rows, (panels - 1) * rest_cols)],
        [],
        [],
        far=[fill_mask, fill_blocks, factor_off, inv_diag],
        scratch=[
            pltpu.SMEM(fill_mask.shape, jnp.int32),
            pltpu.SMEM(fill_blocks.shape, jnp.int32),
            pltpu.VMEM(factor_off.shape, F32),
            pltpu.VMEM((panels - 1, width, width), F32),
            pltpu.VMEM((rows, width), F32),
            pltpu.SemaphoreType.DMA((panels, 3)),
        ],
        flops=6 * (panels - 1) * rows * width * width,
        name="send",
    )

    def zero_of(x):
        return jnp.minimum(jnp.abs(x), 0.0)

    prior_fill = turn(fill_blocks, "seg", 1)
    ups = [sent, turn(sent, "row", 1)]
    for _ in range(1, row_count // 2):
        ups.append(turn(ups[-1] + jnp.minimum(jnp.min(prior_fill), 0).astype(F32), "row", 1))
    pick = jax.ShapeDtypeStruct((width, chosen_cols), BF16)
    bases, priors, picks, tokens = [], [], [], []
    for p in range(panels):
        base, own_prior, *high_low, token = call(
            functools.partial(prior_kernel, p),
            [shape(chosen_cols, chosen_cols), shape(own_cols, width), pick, pick, shape(1, sent.shape[1])],
            [fill_blocks] if p else [fill_blocks, prior_fill],
            [],
            far=[inv_diag],
            scratch=[pltpu.VMEM((width, width), F32), pltpu.SemaphoreType.DMA],
            flops=6 * width * (chosen_cols * chosen_cols + own_cols * width),
            name="prior",
        )
        bases.append(base)
        priors.append(own_prior)
        picks += high_low
        tokens.append(token)
    downs = [sent + tokens[-1]]
    for _ in range((row_count - 1) // 2):
        downs.append(turn(downs[-1], "row", -1))
    parts = ups + downs[:0:-1]
    last = len(ups) - 1
    early = [d for d in range(row_count) if d != last]
    (links,) = call(
        functools.partial(links_kernel, early, panels),
        [shape(panels, size, size)],
        [],
        [*(parts[d] for d in early), *picks[:2]],
        scratch=[pltpu.VMEM((size, size), F32)],
        flops=6 * size * size * width,
        name="links",
    )
    links_t, own_whole = call(
        functools.partial(segment_kernel, last, panels),
        [shape(panels, size, size), shape(2 * size, size)],
        [],
        [parts[last], *picks[:2], links, *bases],
        flops=6 * rows * size * width + 18 * (panels - 1) * size**3,
        name="segment",
    )
    rest = rest + zero_of(ups[1][:1, : rest.shape[1]])
    rest_ups, rest_downs = [rest, turn(rest, "row", 1)], [rest]
    for _ in range(1, row_count // 2):
        rest_ups.append(turn(rest_ups[-1], "row", 1))
    for _ in range((row_count - 1) // 2):
        rest_downs.append(turn(rest_downs[-1], "row", -1))
    rests = rest_ups + rest_downs[:0:-1]
    swap_gate = zero_of(rest_ups[1][:1, :size] + own_whole[:1])
    swap = [(i, i ^ 1) for i in range(seg_count)]
    other_whole = lax.ppermute(own_whole + swap_gate, "seg", swap)
    half = size // 2
    half_packed = shape(5 * half // 4, half)
    half_link = shape(half, size)
    link_t, cov, send, send_t = call(
        chip_kernel,
        [shape(size, size), shape(size, size), half_packed, half_link],
        [],
        [own_whole, other_whole],
        flops=18 * size**3,
        name="chip",
    )
    first_map, map_token = call(
        first_map_kernel,
        [shape(size, width), shape(1, half_cols)],
        [],
        [inv_diag, *parts, send],
        scratch=[pltpu.VMEM((size, width), F32)],
        flops=6 * size * width * width,
        name="first_map",
    )
    level_gate = map_token + zero_of(rest_ups[-1][:1, :half_cols] + rest_downs[-1][:1, :half_cols])
    past = None
    after = (jnp.zeros(half_packed.shape, F32),) * 2
    levels = (chips - 1).bit_length()
    prepared = None

    def prepare():
        total = rows + own_cols
        left = jax.ShapeDtypeStruct((panels, total, size), BF16)
        right = jax.ShapeDtypeStruct((panels, size, width), BF16)
        return call(
            functools.partial(prepare_kernel, levels, panels, row_count),
            [left, left, right, right, shape(panels, total, width), shape(1, half_cols)],
            [fill_blocks],
            [*bases, *priors, other_whole, first_map, links_t, *parts, *rests, *(past or ())],
            scratch=[pltpu.VMEM((size, width), F32), pltpu.VMEM((size, width), F32)],
            flops=6 * panels * size * (total * size + size * width + total * width + 3 * size * size),
            mib=24,
            name="prepare",
        )

    for level in range(levels):
        partner = [(i, i ^ (2 << level)) for i in range(seg_count)]
        got = lax.ppermute(send, "seg", partner)
        if level == levels - 1:
            *prepared, token = prepare()
            got = got + token
            after = (got, lax.ppermute(got, "seg", swap))
            break
        got_t = lax.ppermute(send_t, "seg", partner)
        if level == 0:
            got = got + level_gate
        got = (got_t, lax.ppermute(got_t, "seg", swap), got, lax.ppermute(got, "seg", swap))
        outs = [half_packed]
        if level < levels - 2:
            outs += [half_link, shape(size, size), shape(size, size)]
        send, *more = call(
            functools.partial(merge_kernel, level), outs, [], [link_t, cov, *got],
            flops=18 * size**3, name="merge",
        )
        if more:
            send_t, link_t, cov = more
        if past is None:
            past = got
        else:
            past = call(
                functools.partial(join_kernel, level),
                [half_link, half_link, half_packed, half_packed],
                [],
                [*past, *got],
                flops=18 * size**3,
                name="join",
            )
    if prepared is None:
        *prepared, _ = prepare()
    diag, off = call(
        functools.partial(finish_kernel, levels),
        [shape(panels, own_cols, width), shape(panels, rows, width)],
        [fill_mask],
        [*after, *prepared],
        flops=6 * panels * (rows + own_cols) * size * (size + width),
        name="finish",
    )
    return diag, off


def solution(mesh):
    placed = (P("seg", None), P("seg", None), P("seg", None, None), P("seg", "row", None))
    return jax.shard_map(
        body,
        mesh=mesh,
        in_specs=placed,
        out_specs=(P("seg", "row", None), P("seg", "row", None)),
        check_vma=False,
    )
```

```python
import functools

import jax
import jax.numpy as jnp
from jax import lax
from jax.experimental import pallas as pl
from jax.experimental.pallas import tpu as pltpu
from jax.sharding import PartitionSpec as P

BLOCK = 64
LANES = 128
F32 = jnp.float32
BF16 = jnp.bfloat16
NN = (((1,), (0,)), ((), ()))
NT = (((1,), (1,)), ((), ()))
TN = (((0,), (0,)), ((), ()))


def split(x):
    high = x.astype(BF16)
    return high, (x - high.astype(F32)).astype(BF16)


def mm(a, b, dims=NN):
    a = a if isinstance(a, tuple) else split(a)
    b = b if isinstance(b, tuple) else split(b)
    dot = functools.partial(lax.dot_general, dimension_numbers=dims, preferred_element_type=F32)
    return dot(a[0], b[0]) + (dot(a[0], b[1]) + dot(a[1], b[0]))


def carry(link_t, cov, base):
    link_t = link_t if isinstance(link_t, tuple) else split(link_t)
    return mm(mm(link_t, cov), link_t, NT) + base


def pack(cov):
    half = cov.shape[0] // 2
    part = half // 2
    first, second = cov[:half, :half], cov[half:, half:]
    lane = lax.broadcasted_iota(jnp.int32, (part, half), 1)
    last = jnp.where(lane < part, pltpu.roll(first[part:], part, 1), second[part:])
    return jnp.concatenate([cov[:half, half:], first[:part], second[:part], last], 0)


def unpack(packed):
    half = packed.shape[1]
    part = half // 2
    cross, last = packed[:half], packed[2 * half :]
    row = lax.broadcasted_iota(jnp.int32, (half, half), 0)
    lane = lax.broadcasted_iota(jnp.int32, (half, half), 1)

    def symmetric(top, bottom):
        upper = jnp.concatenate([top, bottom], 0)
        return jnp.where((row < part) | (lane >= part), upper, upper.T)

    first = symmetric(packed[half : half + part], pltpu.roll(last, part, 1))
    second = symmetric(packed[half + part : 2 * half], last)
    top = jnp.concatenate([first, cross], 1)
    bottom = jnp.concatenate([cross.T, second], 1)
    return jnp.concatenate([top, bottom], 0)


def is_lower():
    return (lax.axis_index("seg") & 1) == 0


def from_halves(own, other):
    lower = is_lower()
    return jnp.concatenate([jnp.where(lower, own, other), jnp.where(lower, other, own)], 0)


def own_half(whole):
    half = whole.shape[0] // 2
    return jnp.where(is_lower(), whole[:half], whole[half:])


def two_blocks(load, left, right):
    def placed(block, half):
        slab = load(lax.shift_right_logical(block, 1))
        return jnp.where((block & 1) == half, slab, pltpu.roll(slab, BLOCK, 1))

    a, b = placed(left, 0), placed(right, 1)
    lane = lax.broadcasted_iota(jnp.int32, a.shape, 1)
    return jnp.where(lane < BLOCK, a, b)


def tile_of(ref, *lead):
    def load(tile):
        return ref[(*lead, slice(None), pl.ds(pl.multiple_of(tile * LANES, LANES), LANES))]

    return load


def chosen_of(panel, fill_ref, prior_ref=None):
    slots = fill_ref.shape[1]
    if panel > 0:
        return [fill_ref[panel - 1, j] for j in range(slots)]
    first = lax.axis_index("seg") == 0
    last = prior_ref.shape[0] - 1
    return [jnp.where(first, fill_ref[0, j], prior_ref[last, j]) for j in range(slots)]


def vmem(count):
    return [pl.BlockSpec(memory_space=pltpu.VMEM)] * count


def smem(count):
    return [pl.BlockSpec(memory_space=pltpu.SMEM)] * count


def call(
    kernel, outs, scalars, arrays, far=(), out_far=False, through=(), scratch=(), flops=0, mib=16, name=None
):
    moved = sum(a.size * 4 for a in (*arrays, *far)) + sum(o.size * 4 for o in outs)
    first = len(scalars) + len(arrays) + len(far)
    count = len(through)

    def inner(*refs):
        kernel(*refs[:first], *refs[first + count : first + count + len(outs)], *refs[first + 2 * count + len(outs) :])

    return pl.pallas_call(
        inner,
        out_shape=[*outs, *(jax.ShapeDtypeStruct(a.shape, a.dtype) for a in through)],
        in_specs=smem(len(scalars))
        + vmem(len(arrays))
        + [pl.BlockSpec(memory_space=pltpu.HBM)] * len(far)
        + [pl.BlockSpec(memory_space=pl.ANY)] * count,
        out_specs=([pl.BlockSpec(memory_space=pltpu.HBM)] * len(outs) if out_far else vmem(len(outs)))
        + [pl.BlockSpec(memory_space=pl.ANY)] * count,
        scratch_shapes=list(scratch),
        input_output_aliases={first + i: len(outs) + i for i in range(count)},
        cost_estimate=pl.CostEstimate(flops=flops, bytes_accessed=moved, transcendentals=0),
        compiler_params=pltpu.CompilerParams(vmem_limit_bytes=mib << 20),
        name=name,
    )(*scalars, *arrays, *(pltpu.with_memory_space_constraint(a, pltpu.HBM) for a in far), *through)


def shape(*dims):
    return jax.ShapeDtypeStruct(dims, F32)


def kept_rows(mask_ref, panel, slot, rows):
    alive = lax.axis_index("seg") * mask_ref.shape[0] + panel < (
        lax.axis_size("seg") * mask_ref.shape[0] - 1
    )
    return rows * (mask_ref[panel, slot].astype(F32) * alive.astype(F32))


def triangular_mm(left, lower):
    cut = left.shape[1] // 2
    first, second = split(left[:, :cut]), split(left[:, cut:])
    below = split(lower[cut:, :])
    return jnp.concatenate(
        [
            mm(second, (below[0][:, :cut], below[1][:, :cut])) + mm(first, lower[:cut, :cut]),
            mm(second, (below[0][:, cut:], below[1][:, cut:])),
        ],
        1,
    )


def prior_kernel(panel, *refs):
    *scalar_refs, inv_hbm, base_ref, own_ref, pick_high_ref, pick_low_ref, token_ref = refs[:-2]
    inv_ref, sem = refs[-2:]
    copy = pltpu.make_async_copy(inv_hbm.at[panel], inv_ref, sem)
    copy.start()
    token_ref[...] = jnp.zeros_like(token_ref)
    chosen = chosen_of(panel, *scalar_refs)
    own_cols = own_ref.shape[0]
    own_at = pl.ds(pl.multiple_of(lax.axis_index("row") * own_cols, own_cols), own_cols)
    copy.wait()
    picked = split(
        jnp.concatenate(
            [
                two_blocks(tile_of(inv_ref), chosen[2 * t], chosen[2 * t + 1])
                for t in range(len(chosen) // 2)
            ],
            1,
        )
    )
    pick_high_ref[...], pick_low_ref[...] = picked
    base_ref[...] = mm(picked, picked, TN)
    own_ref[...] = mm(inv_ref[:, own_at], inv_ref[...], TN)


def put_rows(mask_ref, panel, distance, part, take):
    row_count = lax.axis_size("row")
    rows = part.shape[1]
    owner = lax.rem(lax.axis_index("row") + (row_count - distance), row_count)
    for s in range(rows // BLOCK):
        slot = owner * (rows // BLOCK) + s
        kept = kept_rows(mask_ref, panel, slot, part[panel, s * BLOCK : (s + 1) * BLOCK, :])
        take(kept, pl.ds(pl.multiple_of(slot * BLOCK, BLOCK), BLOCK))


def links_kernel(distances, mask_ref, *refs):
    parts, refs = refs[: len(distances)], refs[len(distances) :]
    *pick_refs, links_t_ref, rows_ref = refs
    rows_ref[...] = jnp.zeros_like(rows_ref)
    for p in range(links_t_ref.shape[0]):
        pick = (pick_refs[2 * p][...], pick_refs[2 * p + 1][...])

        def take(kept, at):
            rows_ref[at, :] = mm(kept, pick)

        for d, part in zip(distances, parts):
            put_rows(mask_ref, p, d, part, take)
        links_t_ref[p] = rows_ref[...].T


def segment_kernel(distance, panels, mask_ref, part, early_ref, *refs):
    pick_refs, base_refs = refs[: 2 * panels], refs[2 * panels : 3 * panels]
    links_t_ref, whole_ref = refs[3 * panels :]
    size = links_t_ref.shape[1]
    lane = lax.broadcasted_iota(jnp.int32, (size, size), 1) // BLOCK
    cov = link_t = None
    for p in range(panels - 1, -1, -1):
        pick = (pick_refs[2 * p][...], pick_refs[2 * p + 1][...])
        pieces = [early_ref[p]]

        def take(kept, at):
            late_t = jnp.concatenate([mm(kept, pick)] * (size // BLOCK), 0).T
            pieces.append(jnp.where(lane == at.start // BLOCK, late_t, pieces[-1]))

        put_rows(mask_ref, p, distance, part, take)
        own_t = pieces[-1]
        links_t_ref[p] = own_t
        if cov is None:
            cov, link_t = base_refs[p][...], own_t
        else:
            own_t = split(own_t)
            cov = carry(own_t, cov, base_refs[p][...])
            link_t = mm(own_t, link_t)
    whole_ref[:size] = link_t
    whole_ref[size:] = cov


def maps_kernel(mask_ref, inv_ref, *refs):
    *parts, maps_ref, token_ref, rows_ref = refs
    token_ref[...] = jnp.zeros_like(token_ref)
    for p in range(inv_ref.shape[0]):

        def take(kept, at):
            rows_ref[at, :] = kept

        for d, part in enumerate(parts):
            put_rows(mask_ref, p, d, part, take)
        maps_ref[p] = triangular_mm(rows_ref[...], inv_ref[p])


def chip_kernel(own_ref, other_ref, link_t_ref, cov_ref, packed_ref, half_t_ref):
    size = cov_ref.shape[0]
    lower = is_lower()
    own, other = own_ref[...], other_ref[...]
    down = jnp.where(lower, own, other)
    up = jnp.where(lower, other, own)
    down_t = split(down[:size])
    cov = carry(down_t, up[size:], down[size:])
    link_t = mm(down_t, up[:size])
    link_t_ref[...] = link_t
    cov_ref[...] = cov
    packed_ref[...] = own_half(pack(cov))
    half_t_ref[...] = own_half(link_t)


def merge_kernel(level, link_t_ref, cov_ref, *refs):
    got_t = from_halves(refs[0][...], refs[1][...])
    got = unpack(from_halves(refs[2][...], refs[3][...]))
    own_t, own = link_t_ref[...], cov_ref[...]
    lower = (lax.shift_right_logical(lax.axis_index("seg") // 2, level) & 1) == 0
    down_t = split(jnp.where(lower, own_t, got_t))
    cov = carry(down_t, jnp.where(lower, got, own), jnp.where(lower, own, got))
    refs[4][...] = own_half(pack(cov))
    if len(refs) > 5:
        link_t = mm(down_t, jnp.where(lower, got_t, own_t))
        refs[5][...] = own_half(link_t)
        refs[6][...] = link_t
        refs[7][...] = cov


def join_kernel(level, *refs):
    past_t, past, link_t, cov = (
        from_halves(refs[2 * i][...], refs[2 * i + 1][...]) for i in range(4)
    )
    chip = lax.axis_index("seg") // 2
    below = (lax.shift_right_logical(chip, level) & 1) == 0
    known = (chip & ((1 << level) - 1)) != (1 << level) - 1
    past_parts = split(past_t)
    joined = pack(carry(past_parts, unpack(cov), unpack(past)))
    joined_t = mm(past_parts, link_t)
    out_t = jnp.where(below, jnp.where(known, joined_t, link_t), past_t)
    out = jnp.where(below, jnp.where(known, joined, cov), past)
    for i, whole in enumerate((out_t, out)):
        half = whole.shape[0] // 2
        refs[8 + 2 * i][...] = own_half(whole)
        refs[9 + 2 * i][...] = jnp.where(is_lower(), whole[half:], whole[:half])


def prepare_kernel(levels, panels, *refs):
    base_refs, own_refs, refs = refs[:panels], refs[panels : 2 * panels], refs[2 * panels :]
    (other_ref, maps_ref, links_t_ref), refs = refs[:3], refs[3:]
    past_refs, refs = refs[: 4 * (levels > 1)], refs[4 * (levels > 1) :]
    left_high, left_low, right_high, right_low, const_ref, token_ref, scratch = refs
    token_ref[...] = jnp.zeros_like(token_ref)
    own_cols = own_refs[0].shape[0]
    size = base_refs[0].shape[0]
    row_at = lax.axis_index("row")
    rows = left_high.shape[0] // panels - own_cols
    at_row = lax.broadcasted_iota(jnp.int32, (size, size), 0)
    at_col = lax.broadcasted_iota(jnp.int32, (size, size), 1)
    eye = (at_row == at_col).astype(F32)
    lower = is_lower()
    if past_refs:
        chip = lax.axis_index("seg") // 2
        low = (1 << (levels - 1)) - 1
        known = (chip & low) != low
        past_t = from_halves(past_refs[0][...], past_refs[1][...])
        past = unpack(from_halves(past_refs[2][...], past_refs[3][...]))
        to_t = jnp.where(known, past_t, eye)
        gain = jnp.where(known, past, 0.0)
        other_t = split(other_ref[:size, :])
        to_t = jnp.where(lower, mm(other_t, to_t), to_t)
        gain = jnp.where(lower, carry(other_t, gain, other_ref[size:, :]), gain)
    else:
        to_t = jnp.where(lower, other_ref[:size, :], eye)
        gain = jnp.where(lower, other_ref[size:, :], 0.0)
    own_at = pl.ds(pl.multiple_of(row_at * own_cols, own_cols), own_cols)
    own_rows = pl.ds(pl.multiple_of(row_at * rows, rows), rows)
    for p in range(panels - 1, -1, -1):
        whole = split(maps_ref[p])
        own_t = split(maps_ref[p, :, own_at].T)
        scratch[:, :size] = to_t
        scratch[:, size:] = gain
        to_parts = split(to_t)
        left = jnp.concatenate([scratch[own_rows, :size], mm(own_t, to_parts)], 0)
        part = slice(p * left.shape[0], (p + 1) * left.shape[0])
        left_high[part, :], left_low[part, :] = split(left)
        right_high[p], right_low[p] = split(mm(to_parts, whole, TN))
        gains = jnp.concatenate([scratch[own_rows, size:], mm(own_t, gain)], 0)
        const = mm(gains, whole)
        const_ref[p, :rows, :] = const[:rows]
        const_ref[p, rows:, :] = const[rows:] + own_refs[p][...]
        if p > 0:
            link_t = split(links_t_ref[p])
            to_t = mm(link_t, to_t)
            gain = carry(link_t, gain, base_refs[p][...])


def finish_kernel(levels, mask_ref, after_ref, after_other_ref, *refs):
    left_high, left_low, right_high, right_low, const_ref, diag_hbm, off_hbm = refs[:7]
    diag_ref, off_ref, sems = refs[7:]
    panels, total, _ = const_ref.shape
    rows = off_ref.shape[1]
    row_at = lax.axis_index("row")
    chip = lax.axis_index("seg") // 2
    after = from_halves(after_ref[...], after_other_ref[...])
    after = unpack(jnp.where((chip & ((1 << levels) // 2)) == 0, after, 0.0))
    inner = split(mm((left_high[...], left_low[...]), after))
    copies = []
    for p in range(panels):
        part = slice(p * total, (p + 1) * total)
        right = (right_high[p], right_low[p])
        result = mm((inner[0][part], inner[1][part]), right) + const_ref[p]
        diag_ref[p] = result[rows:]
        for s in range(rows // BLOCK):
            keep = mask_ref[p, row_at * (rows // BLOCK) + s].astype(F32)
            off_ref[p, s * BLOCK : (s + 1) * BLOCK, :] = -result[s * BLOCK : (s + 1) * BLOCK] * keep
        copies.append(pltpu.make_async_copy(diag_ref.at[p], diag_hbm.at[p], sems.at[p, 0]))
        copies.append(pltpu.make_async_copy(off_ref.at[p], off_hbm.at[p], sems.at[p, 1]))
        copies[-2].start()
        copies[-1].start()
    for copy in copies:
        copy.wait()


def body(fill_blocks, fill_mask, inv_diag, factor_off):
    panels, width, _ = inv_diag.shape
    rows = factor_off.shape[1]
    seg_count = lax.axis_size("seg")
    row_count = lax.axis_size("row")
    size = rows * row_count
    own_cols = width // row_count
    slots = fill_blocks.shape[1]
    chosen_cols = slots * BLOCK
    chips = seg_count // 2
    half_cols = size // 2

    def turn(x, axis, distance):
        count = lax.axis_size(axis)
        return lax.ppermute(x, axis, [(i, (i + distance) % count) for i in range(count)])

    prior_fill = turn(fill_blocks, "seg", 1)
    ups = [factor_off, turn(factor_off, "row", 1)]
    for _ in range(1, row_count // 2):
        ups.append(turn(ups[-1] + jnp.minimum(jnp.min(prior_fill), 0).astype(F32), "row", 1))
    pick = jax.ShapeDtypeStruct((width, chosen_cols), BF16)
    bases, priors, picks, tokens = [], [], [], []
    for p in range(panels):
        base, own_prior, *high_low, token = call(
            functools.partial(prior_kernel, p),
            [shape(chosen_cols, chosen_cols), shape(own_cols, width), pick, pick, shape(1, 1, width)],
            [fill_blocks] if p else [fill_blocks, prior_fill],
            [],
            far=[inv_diag],
            scratch=[pltpu.VMEM((width, width), F32), pltpu.SemaphoreType.DMA],
            flops=6 * width * (chosen_cols * chosen_cols + own_cols * width),
            name="prior",
        )
        bases.append(base)
        priors.append(own_prior)
        picks += high_low
        tokens.append(token)
    downs = [factor_off + tokens[-1]]
    for _ in range((row_count - 1) // 2):
        downs.append(turn(downs[-1], "row", -1))
    parts = ups + downs[:0:-1]
    last = len(ups) - 1
    early = [d for d in range(row_count) if d != last]
    (links,) = call(
        functools.partial(links_kernel, early),
        [shape(panels, size, size)],
        [fill_mask],
        [*(parts[d] for d in early), *picks],
        scratch=[pltpu.VMEM((size, chosen_cols), F32)],
        flops=6 * panels * size * size * width,
        name="links",
    )
    links_t, own_whole = call(
        functools.partial(segment_kernel, last, panels),
        [shape(panels, size, size), shape(2 * size, size)],
        [fill_mask],
        [parts[last], links, *picks, *bases],
        flops=6 * panels * rows * size * width + 18 * (panels - 1) * size**3,
        name="segment",
    )
    maps, maps_token = call(
        maps_kernel,
        [shape(panels, size, width), shape(1, half_cols)],
        [fill_mask],
        [inv_diag, *parts],
        scratch=[pltpu.VMEM((size, width), F32)],
        flops=6 * panels * size * width * width,
        mib=24,
        name="maps",
    )
    swap = [(i, i ^ 1) for i in range(seg_count)]
    other_whole = lax.ppermute(own_whole, "seg", swap)
    half = size // 2
    half_packed = shape(5 * half // 4, half)
    half_link = shape(half, size)
    link_t, cov, send, send_t = call(
        chip_kernel,
        [shape(size, size), shape(size, size), half_packed, half_link],
        [],
        [own_whole, other_whole],
        flops=18 * size**3,
        name="chip",
    )
    past = None
    after = (jnp.zeros(half_packed.shape, F32),) * 2
    levels = (chips - 1).bit_length()
    prepared = None

    def prepare():
        total = rows + own_cols
        left = jax.ShapeDtypeStruct((panels * total, size), BF16)
        right = jax.ShapeDtypeStruct((panels, size, width), BF16)
        return call(
            functools.partial(prepare_kernel, levels, panels),
            [left, left, right, right, shape(panels, total, width), shape(1, half_cols)],
            [],
            [*bases, *priors, other_whole, maps, links_t, *(past or ())],
            scratch=[pltpu.VMEM((size, width), F32)],
            flops=6 * panels * size * (total * size + size * width + total * width + 3 * size * size),
            mib=24,
            name="prepare",
        )

    for level in range(levels):
        partner = [(i, i ^ (2 << level)) for i in range(seg_count)]
        got = lax.ppermute(send, "seg", partner)
        if level == levels - 1:
            *prepared, token = prepare()
            got = got + token
            after = (got, lax.ppermute(got, "seg", swap))
            break
        got_t = lax.ppermute(send_t, "seg", partner)
        if level == 0:
            got = got + maps_token
        got = (got_t, lax.ppermute(got_t, "seg", swap), got, lax.ppermute(got, "seg", swap))
        outs = [half_packed]
        if level < levels - 2:
            outs += [half_link, shape(size, size), shape(size, size)]
        send, *more = call(
            functools.partial(merge_kernel, level), outs, [], [link_t, cov, *got],
            flops=18 * size**3, name="merge",
        )
        if more:
            send_t, link_t, cov = more
        if past is None:
            past = got
        else:
            past = call(
                functools.partial(join_kernel, level),
                [half_link, half_link, half_packed, half_packed],
                [],
                [*past, *got],
                flops=18 * size**3,
                name="join",
            )
    if prepared is None:
        *prepared, _ = prepare()
    diag, off = call(
        functools.partial(finish_kernel, levels),
        [shape(panels, own_cols, width), shape(panels, rows, width)],
        [fill_mask],
        [*after, *prepared],
        out_far=True,
        scratch=[
            pltpu.VMEM((panels, own_cols, width), F32),
            pltpu.VMEM((panels, rows, width), F32),
            pltpu.SemaphoreType.DMA((panels, 2)),
        ],
        flops=6 * panels * (rows + own_cols) * size * (size + width),
        name="finish",
    )
    return diag, off


def solution(mesh):
    placed = (P("seg", None), P("seg", None), P("seg", None, None), P("seg", "row", None))
    return jax.shard_map(
        body,
        mesh=mesh,
        in_specs=placed,
        out_specs=(P("seg", "row", None), P("seg", "row", None)),
        check_vma=False,
    )
```

```python
import functools
from typing import NamedTuple

import jax
import jax.numpy as jnp
from jax import lax
from jax.experimental import pallas as pl
from jax.experimental.pallas import tpu as pltpu
from jax.sharding import PartitionSpec as P

BLOCK = 64
LANES = 128
F32 = jnp.float32
BF16 = jnp.bfloat16
NN = (((1,), (0,)), ((), ()))
NT = (((1,), (1,)), ((), ()))
TN = (((0,), (0,)), ((), ()))


def split(x):
    high = x.astype(BF16)
    return high, (x - high.astype(F32)).astype(BF16)


def mm(a, b, dims=NN):
    a = a if isinstance(a, tuple) else split(a)
    b = b if isinstance(b, tuple) else split(b)
    dot = functools.partial(lax.dot_general, dimension_numbers=dims, preferred_element_type=F32)
    return dot(a[0], b[0]) + (dot(a[0], b[1]) + dot(a[1], b[0]))


def carry(link_t, cov, base):
    link_t = link_t if isinstance(link_t, tuple) else split(link_t)
    return mm(mm(link_t, cov), link_t, NT) + base


def pack(cov):
    half = cov.shape[0] // 2
    part = half // 2
    first, second = cov[:half, :half], cov[half:, half:]
    lane = lax.broadcasted_iota(jnp.int32, (part, half), 1)
    last = jnp.where(lane < part, pltpu.roll(first[part:], part, 1), second[part:])
    return jnp.concatenate([cov[:half, half:], first[:part], second[:part], last], 0)


def unpack(packed):
    half = packed.shape[1]
    part = half // 2
    cross, last = packed[:half], packed[2 * half :]
    row = lax.broadcasted_iota(jnp.int32, (half, half), 0)
    lane = lax.broadcasted_iota(jnp.int32, (half, half), 1)

    def symmetric(top, bottom):
        upper = jnp.concatenate([top, bottom], 0)
        return jnp.where((row < part) | (lane >= part), upper, upper.T)

    first = symmetric(packed[half : half + part], pltpu.roll(last, part, 1))
    second = symmetric(packed[half + part : 2 * half], last)
    top = jnp.concatenate([first, cross], 1)
    bottom = jnp.concatenate([cross.T, second], 1)
    return jnp.concatenate([top, bottom], 0)


def is_lower():
    return (lax.axis_index("seg") & 1) == 0


def from_halves(own, other):
    lower = is_lower()
    return jnp.concatenate([jnp.where(lower, own, other), jnp.where(lower, other, own)], 0)


def own_half(whole):
    half = whole.shape[0] // 2
    return jnp.where(is_lower(), whole[:half], whole[half:])


def two_blocks(load, left, right):
    def placed(block, half):
        slab = load(lax.shift_right_logical(block, 1))
        return jnp.where((block & 1) == half, slab, pltpu.roll(slab, BLOCK, 1))

    a, b = placed(left, 0), placed(right, 1)
    lane = lax.broadcasted_iota(jnp.int32, a.shape, 1)
    return jnp.where(lane < BLOCK, a, b)


def tile_of(ref, *lead):
    def load(tile):
        return ref[(*lead, slice(None), pl.ds(pl.multiple_of(tile * LANES, LANES), LANES))]

    return load


def chosen_of(panel, fill_ref, prior_ref=None):
    slots = fill_ref.shape[1]
    if panel > 0:
        return [fill_ref[panel - 1, j] for j in range(slots)]
    first = lax.axis_index("seg") == 0
    last = prior_ref.shape[0] - 1
    return [jnp.where(first, fill_ref[0, j], prior_ref[last, j]) for j in range(slots)]


def vmem(count):
    return [pl.BlockSpec(memory_space=pltpu.VMEM)] * count


def smem(count):
    return [pl.BlockSpec(memory_space=pltpu.SMEM)] * count


def call(
    kernel, outs, scalars, arrays, far=(), out_far=False, through=(), scratch=(), flops=0, mib=16, name=None
):
    moved = sum(a.size * 4 for a in (*arrays, *far)) + sum(o.size * 4 for o in outs)
    first = len(scalars) + len(arrays) + len(far)
    count = len(through)

    def inner(*refs):
        kernel(*refs[:first], *refs[first + count : first + count + len(outs)], *refs[first + 2 * count + len(outs) :])

    return pl.pallas_call(
        inner,
        out_shape=[*outs, *(jax.ShapeDtypeStruct(a.shape, a.dtype) for a in through)],
        in_specs=smem(len(scalars))
        + vmem(len(arrays))
        + [pl.BlockSpec(memory_space=pltpu.HBM)] * len(far)
        + [pl.BlockSpec(memory_space=pl.ANY)] * count,
        out_specs=([pl.BlockSpec(memory_space=pltpu.HBM)] * len(outs) if out_far else vmem(len(outs)))
        + [pl.BlockSpec(memory_space=pl.ANY)] * count,
        scratch_shapes=list(scratch),
        input_output_aliases={first + i: len(outs) + i for i in range(count)},
        cost_estimate=pl.CostEstimate(flops=flops, bytes_accessed=moved, transcendentals=0),
        compiler_params=pltpu.CompilerParams(vmem_limit_bytes=mib << 20),
        name=name,
    )(*scalars, *arrays, *(pltpu.with_memory_space_constraint(a, pltpu.HBM) for a in far), *through)


def shape(*dims):
    return jax.ShapeDtypeStruct(dims, F32)


def kept_rows(mask_ref, panel, slot, rows):
    alive = lax.axis_index("seg") * mask_ref.shape[0] + panel < (
        lax.axis_size("seg") * mask_ref.shape[0] - 1
    )
    return rows * (mask_ref[panel, slot].astype(F32) * alive.astype(F32))


def triangular_mm(left, lower):
    cut = left.shape[1] // 2
    first, second = split(left[:, :cut]), split(left[:, cut:])
    below = split(lower[cut:, :])
    return jnp.concatenate(
        [
            mm(second, (below[0][:, :cut], below[1][:, :cut])) + mm(first, lower[:cut, :cut]),
            mm(second, (below[0][:, cut:], below[1][:, cut:])),
        ],
        1,
    )


def prior_kernel(panel, *refs):
    *scalar_refs, inv_hbm, base_ref, own_ref, pick_high_ref, pick_low_ref, token_ref = refs[:-2]
    inv_ref, sem = refs[-2:]
    copy = pltpu.make_async_copy(inv_hbm.at[panel], inv_ref, sem)
    copy.start()
    token_ref[...] = jnp.zeros_like(token_ref)
    chosen = chosen_of(panel, *scalar_refs)
    own_cols = own_ref.shape[0]
    own_at = pl.ds(pl.multiple_of(lax.axis_index("row") * own_cols, own_cols), own_cols)
    copy.wait()
    picked = split(
        jnp.concatenate(
            [
                two_blocks(tile_of(inv_ref), chosen[2 * t], chosen[2 * t + 1])
                for t in range(len(chosen) // 2)
            ],
            1,
        )
    )
    pick_high_ref[...], pick_low_ref[...] = picked
    base_ref[...] = mm(picked, picked, TN)
    own_ref[...] = mm(inv_ref[:, own_at], inv_ref[...], TN)


class Plan(NamedTuple):
    early: tuple
    late: tuple
    late_from: tuple


def at_row(table):
    value = jnp.int32(table[0])
    for i, entry in enumerate(table[1:], 1):
        value = jnp.where(lax.axis_index("row") == i, entry, value)
    return value


def slots_of(owners, rows):
    first = at_row(owners) * (rows // BLOCK)
    return [first + s for s in range(rows // BLOCK)]


def put_rows(mask_ref, panel, owners, part, out_ref, take):
    for s, slot in enumerate(slots_of(owners, part.shape[0])):
        kept = kept_rows(mask_ref, panel, slot, part[s * BLOCK : (s + 1) * BLOCK, :])
        out_ref[pl.ds(pl.multiple_of(slot * BLOCK, BLOCK), BLOCK), :] = take(kept)


def late_part(plan, refs, panel):
    part = refs[0][panel]
    for i, ref in enumerate(refs[1:], 1):
        part = jnp.where(at_row(plan.late_from) == i, ref[panel], part)
    return part


def links_kernel(plan, mask_ref, *refs):
    count = len(plan.early)
    parts, refs = refs[:count], refs[count:]
    *pick_refs, links_t_ref, late_keep_ref, rows_ref = refs
    rows_ref[...] = jnp.zeros_like(rows_ref)
    for p in range(links_t_ref.shape[0]):
        pick = (pick_refs[2 * p][...], pick_refs[2 * p + 1][...])
        for owners, part in zip(plan.early, parts):
            put_rows(mask_ref, p, owners, part[p], rows_ref, lambda kept: mm(kept, pick))
        links_t_ref[p] = rows_ref[...].T
        for s, slot in enumerate(slots_of(plan.late, late_keep_ref.shape[1])):
            block = slice(s * BLOCK, (s + 1) * BLOCK)
            ones = jnp.ones((BLOCK, late_keep_ref.shape[2]), F32)
            late_keep_ref[p, block, :] = kept_rows(mask_ref, p, slot, ones)


def segment_kernel(plan, panels, *refs):
    count = max(plan.late_from) + 1
    late_refs, (early_ref, keep_ref), refs = refs[:count], refs[count : count + 2], refs[count + 2 :]
    pick_refs, base_refs = refs[: 2 * panels], refs[2 * panels : 3 * panels]
    links_t_ref, whole_ref = refs[3 * panels :]
    size = links_t_ref.shape[1]
    rows = keep_ref.shape[1]
    here = lax.broadcasted_iota(jnp.int32, (size, size), 1) // rows == at_row(plan.late)
    cov = link_t = None
    for p in range(panels - 1, -1, -1):
        pick = (pick_refs[2 * p][...], pick_refs[2 * p + 1][...])
        late = mm(late_part(plan, late_refs, p), pick) * keep_ref[p]
        late_t = jnp.concatenate([late] * (size // rows), 0).T
        own_t = jnp.where(here, late_t, early_ref[p])
        links_t_ref[p] = own_t
        if cov is None:
            cov, link_t = base_refs[p][...], own_t
        else:
            own_t = split(own_t)
            cov = carry(own_t, cov, base_refs[p][...])
            link_t = mm(own_t, link_t)
    whole_ref[:size] = link_t
    whole_ref[size:] = cov


def maps_kernel(plan, mask_ref, inv_ref, *refs):
    count = len(plan.early)
    parts, late_refs = refs[:count], refs[count:-3]
    maps_ref, token_ref, rows_ref = refs[-3:]
    token_ref[...] = jnp.zeros_like(token_ref)
    for p in range(inv_ref.shape[0]):
        for owners, part in zip(plan.early, parts):
            put_rows(mask_ref, p, owners, part[p], rows_ref, lambda kept: kept)
        put_rows(mask_ref, p, plan.late, late_part(plan, late_refs, p), rows_ref, lambda kept: kept)
        maps_ref[p] = triangular_mm(rows_ref[...], inv_ref[p])


def chip_kernel(own_ref, other_ref, link_t_ref, cov_ref, packed_ref, half_t_ref):
    size = cov_ref.shape[0]
    lower = is_lower()
    own, other = own_ref[...], other_ref[...]
    down = jnp.where(lower, own, other)
    up = jnp.where(lower, other, own)
    down_t = split(down[:size])
    cov = carry(down_t, up[size:], down[size:])
    link_t = mm(down_t, up[:size])
    link_t_ref[...] = link_t
    cov_ref[...] = cov
    packed_ref[...] = own_half(pack(cov))
    half_t_ref[...] = own_half(link_t)


def merge_kernel(level, link_t_ref, cov_ref, *refs):
    got_t = from_halves(refs[0][...], refs[1][...])
    got = unpack(from_halves(refs[2][...], refs[3][...]))
    own_t, own = link_t_ref[...], cov_ref[...]
    lower = (lax.shift_right_logical(lax.axis_index("seg") // 2, level) & 1) == 0
    down_t = split(jnp.where(lower, own_t, got_t))
    cov = carry(down_t, jnp.where(lower, got, own), jnp.where(lower, own, got))
    refs[4][...] = own_half(pack(cov))
    if len(refs) > 5:
        link_t = mm(down_t, jnp.where(lower, got_t, own_t))
        refs[5][...] = own_half(link_t)
        refs[6][...] = link_t
        refs[7][...] = cov


def join_kernel(level, *refs):
    past_t, past, link_t, cov = (
        from_halves(refs[2 * i][...], refs[2 * i + 1][...]) for i in range(4)
    )
    chip = lax.axis_index("seg") // 2
    below = (lax.shift_right_logical(chip, level) & 1) == 0
    known = (chip & ((1 << level) - 1)) != (1 << level) - 1
    past_parts = split(past_t)
    joined = pack(carry(past_parts, unpack(cov), unpack(past)))
    joined_t = mm(past_parts, link_t)
    out_t = jnp.where(below, jnp.where(known, joined_t, link_t), past_t)
    out = jnp.where(below, jnp.where(known, joined, cov), past)
    for i, whole in enumerate((out_t, out)):
        half = whole.shape[0] // 2
        refs[8 + 2 * i][...] = own_half(whole)
        refs[9 + 2 * i][...] = jnp.where(is_lower(), whole[half:], whole[:half])


def prepare_kernel(levels, panels, mask_ref, *refs):
    base_refs, own_refs, refs = refs[:panels], refs[panels : 2 * panels], refs[2 * panels :]
    (other_ref, maps_ref, links_t_ref), refs = refs[:3], refs[3:]
    past_refs, refs = refs[: 4 * (levels > 1)], refs[4 * (levels > 1) :]
    left_high, left_low, right_high, right_low, const_ref, token_ref, scratch = refs
    token_ref[...] = jnp.zeros_like(token_ref)
    own_cols = own_refs[0].shape[0]
    size = base_refs[0].shape[0]
    row_at = lax.axis_index("row")
    rows = left_high.shape[0] // panels - own_cols
    at_row = lax.broadcasted_iota(jnp.int32, (size, size), 0)
    at_col = lax.broadcasted_iota(jnp.int32, (size, size), 1)
    eye = (at_row == at_col).astype(F32)
    lower = is_lower()
    if past_refs:
        chip = lax.axis_index("seg") // 2
        low = (1 << (levels - 1)) - 1
        known = (chip & low) != low
        past_t = from_halves(past_refs[0][...], past_refs[1][...])
        past = unpack(from_halves(past_refs[2][...], past_refs[3][...]))
        to_t = jnp.where(known, past_t, eye)
        gain = jnp.where(known, past, 0.0)
        other_t = split(other_ref[:size, :])
        to_t = jnp.where(lower, mm(other_t, to_t), to_t)
        gain = jnp.where(lower, carry(other_t, gain, other_ref[size:, :]), gain)
    else:
        to_t = jnp.where(lower, other_ref[:size, :], eye)
        gain = jnp.where(lower, other_ref[size:, :], 0.0)
    own_at = pl.ds(pl.multiple_of(row_at * own_cols, own_cols), own_cols)
    own_rows = pl.ds(pl.multiple_of(row_at * rows, rows), rows)
    for p in range(panels - 1, -1, -1):
        whole = split(maps_ref[p])
        own_t = split(maps_ref[p, :, own_at].T)
        scratch[:, :size] = to_t
        scratch[:, size:] = gain
        to_parts = split(to_t)
        cross = jnp.concatenate(
            [
                jnp.full((BLOCK, size), -mask_ref[p, slot].astype(F32))
                for slot in slots_of(tuple(range(size // rows)), rows)
            ],
            0,
        )
        left = jnp.concatenate([scratch[own_rows, :size] * cross, mm(own_t, to_parts)], 0)
        part = slice(p * left.shape[0], (p + 1) * left.shape[0])
        left_high[part, :], left_low[part, :] = split(left)
        right_high[p], right_low[p] = split(mm(to_parts, whole, TN))
        gains = jnp.concatenate([scratch[own_rows, size:] * cross, mm(own_t, gain)], 0)
        const = mm(gains, whole)
        const_ref[p, :rows, :] = const[:rows]
        const_ref[p, rows:, :] = const[rows:] + own_refs[p][...]
        if p > 0:
            link_t = split(links_t_ref[p])
            to_t = mm(link_t, to_t)
            gain = carry(link_t, gain, base_refs[p][...])


def finish_kernel(levels, after_ref, after_other_ref, *refs):
    left_high, left_low, right_high, right_low, const_ref, diag_hbm, off_hbm = refs[:7]
    diag_ref, off_ref, sems = refs[7:]
    panels, total, _ = const_ref.shape
    rows = off_ref.shape[1]
    chip = lax.axis_index("seg") // 2
    after = from_halves(after_ref[...], after_other_ref[...])
    after = unpack(jnp.where((chip & ((1 << levels) // 2)) == 0, after, 0.0))
    inner = split(mm((left_high[...], left_low[...]), after))
    copies = []
    for p in range(panels):
        part = slice(p * total, (p + 1) * total)
        right = (right_high[p], right_low[p])
        result = mm((inner[0][part], inner[1][part]), right) + const_ref[p]
        diag_ref[p] = result[rows:]
        off_ref[p] = result[:rows]
        copies.append(pltpu.make_async_copy(diag_ref.at[p], diag_hbm.at[p], sems.at[p, 0]))
        copies.append(pltpu.make_async_copy(off_ref.at[p], off_hbm.at[p], sems.at[p, 1]))
        copies[-2].start()
        copies[-1].start()
    for copy in copies:
        copy.wait()


def body(fill_blocks, fill_mask, inv_diag, factor_off):
    panels, width, _ = inv_diag.shape
    rows = factor_off.shape[1]
    seg_count = lax.axis_size("seg")
    row_count = lax.axis_size("row")
    size = rows * row_count
    own_cols = width // row_count
    slots = fill_blocks.shape[1]
    chosen_cols = slots * BLOCK
    chips = seg_count // 2
    half_cols = size // 2

    def turn(x, axis, distance):
        count = lax.axis_size(axis)
        return lax.ppermute(x, axis, [(i, (i + distance) % count) for i in range(count)])

    prior_fill = turn(fill_blocks, "seg", 1)
    pick = jax.ShapeDtypeStruct((width, chosen_cols), BF16)
    bases, priors, picks, tokens = [], [], [], []
    for p in range(panels):
        base, own_prior, *high_low, token = call(
            functools.partial(prior_kernel, p),
            [shape(chosen_cols, chosen_cols), shape(own_cols, width), pick, pick, shape(1, 1, width)],
            [fill_blocks] if p else [fill_blocks, prior_fill],
            [],
            far=[inv_diag],
            scratch=[pltpu.VMEM((width, width), F32), pltpu.SemaphoreType.DMA],
            flops=6 * width * (chosen_cols * chosen_cols + own_cols * width),
            name="prior",
        )
        bases.append(base)
        priors.append(own_prior)
        picks += high_low
        tokens.append(token)
    second = factor_off + tokens[-1]
    index_gate = jnp.minimum(jnp.min(prior_fill), 0).astype(F32)

    def step(x, targets):
        return lax.ppermute(x, "row", list(enumerate(targets)))

    if row_count == 4:
        near = step(factor_off, (2, 0, 3, 1))
        far = step(second, (1, 3, 0, 2))
        lates = [step(second, (0, 2, 1, 3)), step(near + index_gate, (1, 0, 3, 2))]
        parts = [factor_off, near, far]
        plan = Plan(((0, 1, 2, 3), (1, 3, 0, 2), (2, 0, 3, 1)), (3, 2, 1, 0), (1, 0, 0, 1))
    else:
        ups, downs = [factor_off], [second]
        for i in range(row_count // 2):
            ups.append(turn(ups[-1] + index_gate if i else ups[-1], "row", 1))
        for _ in range((row_count - 1) // 2):
            downs.append(turn(downs[-1], "row", -1))
        parts, lates = ups[:-1] + downs[:0:-1], ups[-1:]
        far_off = len(ups) - 1
        came = [d for d in range(row_count) if d != far_off]
        whose = [tuple((i - d) % row_count for i in range(row_count)) for d in (*came, far_off)]
        plan = Plan(tuple(whose[:-1]), whose[-1], (0,) * row_count)
    links, late_keep = call(
        functools.partial(links_kernel, plan),
        [shape(panels, size, size), shape(panels, rows, size)],
        [fill_mask],
        [*parts, *picks],
        scratch=[pltpu.VMEM((size, chosen_cols), F32)],
        flops=6 * panels * size * size * width,
        name="links",
    )
    links_t, own_whole = call(
        functools.partial(segment_kernel, plan, panels),
        [shape(panels, size, size), shape(2 * size, size)],
        [],
        [*lates, links, late_keep, *picks, *bases],
        flops=6 * panels * rows * size * width + 18 * (panels - 1) * size**3,
        name="segment",
    )
    maps, maps_token = call(
        functools.partial(maps_kernel, plan),
        [shape(panels, size, width), shape(1, half_cols)],
        [fill_mask],
        [inv_diag, *parts, *lates],
        scratch=[pltpu.VMEM((size, width), F32)],
        flops=6 * panels * size * width * width,
        mib=24,
        name="maps",
    )
    swap = [(i, i ^ 1) for i in range(seg_count)]
    other_whole = lax.ppermute(own_whole, "seg", swap)
    half = size // 2
    half_packed = shape(5 * half // 4, half)
    half_link = shape(half, size)
    link_t, cov, send, send_t = call(
        chip_kernel,
        [shape(size, size), shape(size, size), half_packed, half_link],
        [],
        [own_whole, other_whole],
        flops=18 * size**3,
        name="chip",
    )
    past = None
    after = (jnp.zeros(half_packed.shape, F32),) * 2
    levels = (chips - 1).bit_length()
    prepared = None

    def prepare():
        total = rows + own_cols
        left = jax.ShapeDtypeStruct((panels * total, size), BF16)
        right = jax.ShapeDtypeStruct((panels, size, width), BF16)
        return call(
            functools.partial(prepare_kernel, levels, panels),
            [left, left, right, right, shape(panels, total, width), shape(1, half_cols)],
            [fill_mask],
            [*bases, *priors, other_whole, maps, links_t, *(past or ())],
            scratch=[pltpu.VMEM((size, width), F32)],
            flops=6 * panels * size * (total * size + size * width + total * width + 3 * size * size),
            mib=24,
            name="prepare",
        )

    for level in range(levels):
        partner = [(i, i ^ (2 << level)) for i in range(seg_count)]
        got = lax.ppermute(send, "seg", partner)
        if level == levels - 1:
            *prepared, token = prepare()
            got = got + token
            after = (got, lax.ppermute(got, "seg", swap))
            break
        got_t = lax.ppermute(send_t, "seg", partner)
        if level == 0:
            got = got + maps_token
        got = (got_t, lax.ppermute(got_t, "seg", swap), got, lax.ppermute(got, "seg", swap))
        outs = [half_packed]
        if level < levels - 2:
            outs += [half_link, shape(size, size), shape(size, size)]
        send, *more = call(
            functools.partial(merge_kernel, level), outs, [], [link_t, cov, *got],
            flops=18 * size**3, name="merge",
        )
        if more:
            send_t, link_t, cov = more
        if past is None:
            past = got
        else:
            past = call(
                functools.partial(join_kernel, level),
                [half_link, half_link, half_packed, half_packed],
                [],
                [*past, *got],
                flops=18 * size**3,
                name="join",
            )
    if prepared is None:
        *prepared, _ = prepare()
    diag, off = call(
        functools.partial(finish_kernel, levels),
        [shape(panels, own_cols, width), shape(panels, rows, width)],
        [],
        [*after, *prepared],
        out_far=True,
        scratch=[
            pltpu.VMEM((panels, own_cols, width), F32),
            pltpu.VMEM((panels, rows, width), F32),
            pltpu.SemaphoreType.DMA((panels, 2)),
        ],
        flops=6 * panels * (rows + own_cols) * size * (size + width),
        name="finish",
    )
    return diag, off


def solution(mesh):
    placed = (P("seg", None), P("seg", None), P("seg", None, None), P("seg", "row", None))
    return jax.shard_map(
        body,
        mesh=mesh,
        in_specs=placed,
        out_specs=(P("seg", "row", None), P("seg", "row", None)),
        check_vma=False,
    )
```

```python
import functools
from typing import NamedTuple

import jax
import jax.numpy as jnp
from jax import lax
from jax.experimental import pallas as pl
from jax.experimental.pallas import tpu as pltpu
from jax.sharding import PartitionSpec as P

BLOCK = 64
LANES = 128
F32 = jnp.float32
BF16 = jnp.bfloat16
NN = (((1,), (0,)), ((), ()))
NT = (((1,), (1,)), ((), ()))
TN = (((0,), (0,)), ((), ()))


def split(x):
    high = x.astype(BF16)
    return high, (x - high.astype(F32)).astype(BF16)


def mm(a, b, dims=NN):
    a = a if isinstance(a, tuple) else split(a)
    b = b if isinstance(b, tuple) else split(b)
    dot = functools.partial(lax.dot_general, dimension_numbers=dims, preferred_element_type=F32)
    return dot(a[0], b[0]) + (dot(a[0], b[1]) + dot(a[1], b[0]))


def carry(link_t, cov, base):
    link_t = link_t if isinstance(link_t, tuple) else split(link_t)
    return mm(mm(link_t, cov), link_t, NT) + base


def pack(cov):
    half = cov.shape[0] // 2
    part = half // 2
    first, second = cov[:half, :half], cov[half:, half:]
    lane = lax.broadcasted_iota(jnp.int32, (part, half), 1)
    last = jnp.where(lane < part, pltpu.roll(first[part:], part, 1), second[part:])
    return jnp.concatenate([cov[:half, half:], first[:part], second[:part], last], 0)


def unpack(packed):
    half = packed.shape[1]
    part = half // 2
    cross, last = packed[:half], packed[2 * half :]
    row = lax.broadcasted_iota(jnp.int32, (half, half), 0)
    lane = lax.broadcasted_iota(jnp.int32, (half, half), 1)

    def symmetric(top, bottom):
        upper = jnp.concatenate([top, bottom], 0)
        return jnp.where((row < part) | (lane >= part), upper, upper.T)

    first = symmetric(packed[half : half + part], pltpu.roll(last, part, 1))
    second = symmetric(packed[half + part : 2 * half], last)
    top = jnp.concatenate([first, cross], 1)
    bottom = jnp.concatenate([cross.T, second], 1)
    return jnp.concatenate([top, bottom], 0)


def widen(packed):
    rows = packed.shape[0] // 2
    return jnp.concatenate([packed[:rows], packed[rows:]], 1)


def narrow(wide):
    columns = wide.shape[1] // 2
    return jnp.concatenate([wide[:, :columns], wide[:, columns:]], 0)


def is_lower():
    return (lax.axis_index("seg") & 1) == 0


def from_halves(own, other):
    lower = is_lower()
    return jnp.concatenate([jnp.where(lower, own, other), jnp.where(lower, other, own)], 0)


def own_half(whole):
    half = whole.shape[0] // 2
    return jnp.where(is_lower(), whole[:half], whole[half:])


def two_blocks(load, left, right):
    def placed(block, half):
        slab = load(lax.shift_right_logical(block, 1))
        return jnp.where((block & 1) == half, slab, pltpu.roll(slab, BLOCK, 1))

    a, b = placed(left, 0), placed(right, 1)
    lane = lax.broadcasted_iota(jnp.int32, a.shape, 1)
    return jnp.where(lane < BLOCK, a, b)


def tile_of(ref, *lead):
    def load(tile):
        return ref[(*lead, slice(None), pl.ds(pl.multiple_of(tile * LANES, LANES), LANES))]

    return load


def chosen_of(panel, fill_ref, prior_ref=None):
    slots = fill_ref.shape[1]
    if panel > 0:
        return [fill_ref[panel - 1, j] for j in range(slots)]
    first = lax.axis_index("seg") == 0
    last = prior_ref.shape[0] - 1
    return [jnp.where(first, fill_ref[0, j], prior_ref[last, j]) for j in range(slots)]


def vmem(count):
    return [pl.BlockSpec(memory_space=pltpu.VMEM)] * count


def smem(count):
    return [pl.BlockSpec(memory_space=pltpu.SMEM)] * count


def call(
    kernel, outs, scalars, arrays, far=(), out_far=False, through=(), scratch=(), flops=0, mib=16, name=None
):
    moved = sum(a.size * 4 for a in (*arrays, *far)) + sum(o.size * 4 for o in outs)
    first = len(scalars) + len(arrays) + len(far)
    count = len(through)

    def inner(*refs):
        kernel(*refs[:first], *refs[first + count : first + count + len(outs)], *refs[first + 2 * count + len(outs) :])

    return pl.pallas_call(
        inner,
        out_shape=[*outs, *(jax.ShapeDtypeStruct(a.shape, a.dtype) for a in through)],
        in_specs=smem(len(scalars))
        + vmem(len(arrays))
        + [pl.BlockSpec(memory_space=pltpu.HBM)] * len(far)
        + [pl.BlockSpec(memory_space=pl.ANY)] * count,
        out_specs=([pl.BlockSpec(memory_space=pltpu.HBM)] * len(outs) if out_far else vmem(len(outs)))
        + [pl.BlockSpec(memory_space=pl.ANY)] * count,
        scratch_shapes=list(scratch),
        input_output_aliases={first + i: len(outs) + i for i in range(count)},
        cost_estimate=pl.CostEstimate(flops=flops, bytes_accessed=moved, transcendentals=0),
        compiler_params=pltpu.CompilerParams(vmem_limit_bytes=mib << 20),
        name=name,
    )(*scalars, *arrays, *(pltpu.with_memory_space_constraint(a, pltpu.HBM) for a in far), *through)


def shape(*dims):
    return jax.ShapeDtypeStruct(dims, F32)


def kept_rows(mask_ref, panel, slot, rows):
    alive = lax.axis_index("seg") * mask_ref.shape[0] + panel < (
        lax.axis_size("seg") * mask_ref.shape[0] - 1
    )
    return rows * (mask_ref[panel, slot].astype(F32) * alive.astype(F32))


def triangular_mm(left, lower):
    cut = left.shape[1] // 2
    first, second = split(left[:, :cut]), split(left[:, cut:])
    below = split(lower[cut:, :])
    return jnp.concatenate(
        [
            mm(second, (below[0][:, :cut], below[1][:, :cut])) + mm(first, lower[:cut, :cut]),
            mm(second, (below[0][:, cut:], below[1][:, cut:])),
        ],
        1,
    )


def prior_kernel(panel, *refs):
    *scalar_refs, inv_hbm, base_ref, own_ref, pick_high_ref, pick_low_ref, token_ref = refs[:-2]
    inv_ref, sem = refs[-2:]
    copy = pltpu.make_async_copy(inv_hbm.at[panel], inv_ref, sem)
    copy.start()
    token_ref[...] = jnp.zeros_like(token_ref)
    chosen = chosen_of(panel, *scalar_refs)
    own_cols = own_ref.shape[0]
    own_at = pl.ds(pl.multiple_of(lax.axis_index("row") * own_cols, own_cols), own_cols)
    copy.wait()
    picked = split(
        jnp.concatenate(
            [
                two_blocks(tile_of(inv_ref), chosen[2 * t], chosen[2 * t + 1])
                for t in range(len(chosen) // 2)
            ],
            1,
        )
    )
    pick_high_ref[...], pick_low_ref[...] = picked
    base_ref[...] = mm(picked, picked, TN)
    own_ref[...] = mm(inv_ref[:, own_at], inv_ref[...], TN)


class Plan(NamedTuple):
    early: tuple
    late: tuple


def at_row(table):
    value = jnp.int32(table[0])
    for i, entry in enumerate(table[1:], 1):
        value = jnp.where(lax.axis_index("row") == i, entry, value)
    return value


def slots_of(owners, rows):
    first = at_row(owners) * (rows // BLOCK)
    return [first + s for s in range(rows // BLOCK)]


def put_rows(mask_ref, panel, owners, part, out_ref, take):
    for s, slot in enumerate(slots_of(owners, part.shape[0])):
        kept = kept_rows(mask_ref, panel, slot, part[s * BLOCK : (s + 1) * BLOCK, :])
        out_ref[pl.ds(pl.multiple_of(slot * BLOCK, BLOCK), BLOCK), :] = take(kept)


def links_kernel(plan, mask_ref, *refs):
    count = len(plan.early)
    parts, refs = refs[:count], refs[count:]
    *pick_refs, links_t_ref, late_keep_ref, rows_ref = refs
    rows_ref[...] = jnp.zeros_like(rows_ref)
    for p in range(links_t_ref.shape[0]):
        pick = (pick_refs[2 * p][...], pick_refs[2 * p + 1][...])
        for owners, part in zip(plan.early, parts):
            put_rows(mask_ref, p, owners, part[p], rows_ref, lambda kept: mm(kept, pick))
        links_t_ref[p] = rows_ref[...].T
        for s, slot in enumerate(slots_of(plan.late, late_keep_ref.shape[1])):
            block = slice(s * BLOCK, (s + 1) * BLOCK)
            ones = jnp.ones((BLOCK, late_keep_ref.shape[2]), F32)
            late_keep_ref[p, block, :] = kept_rows(mask_ref, p, slot, ones)


def segment_kernel(plan, panels, *refs):
    late_ref, early_ref, keep_ref, *refs = refs
    pick_refs, base_refs = refs[: 2 * panels], refs[2 * panels : 3 * panels]
    links_t_ref, whole_ref, cov_ref = refs[3 * panels :]
    size = links_t_ref.shape[1]
    rows = keep_ref.shape[1]
    here = lax.broadcasted_iota(jnp.int32, (size, size), 1) // rows == at_row(plan.late)
    cov = link_t = None
    for p in range(panels - 1, -1, -1):
        pick = (pick_refs[2 * p][...], pick_refs[2 * p + 1][...])
        late = mm(late_ref[p], pick) * keep_ref[p]
        late_t = jnp.concatenate([late] * (size // rows), 0).T
        own_t = jnp.where(here, late_t, early_ref[p])
        links_t_ref[p] = own_t
        if cov is None:
            cov, link_t = base_refs[p][...], own_t
        else:
            own_t = split(own_t)
            cov = carry(own_t, cov, base_refs[p][...])
            link_t = mm(own_t, link_t)
    whole_ref[:size] = link_t
    whole_ref[size:] = widen(pack(cov))
    cov_ref[...] = cov


def maps_kernel(plan, mask_ref, inv_ref, *refs):
    count = len(plan.early)
    parts, (late_ref, maps_ref, token_ref, rows_ref) = refs[:count], refs[count:]
    token_ref[...] = jnp.zeros_like(token_ref)
    for p in range(inv_ref.shape[0]):
        for owners, part in zip(plan.early, parts):
            put_rows(mask_ref, p, owners, part[p], rows_ref, lambda kept: kept)
        put_rows(mask_ref, p, plan.late, late_ref[p], rows_ref, lambda kept: kept)
        maps_ref[p] = triangular_mm(rows_ref[...], inv_ref[p])


def chip_kernel(own_ref, own_cov_ref, other_ref, link_t_ref, cov_ref, packed_ref, half_t_ref):
    size = cov_ref.shape[0]
    lower = is_lower()
    own_t, other_t = own_ref[:size, :], other_ref[:size, :]
    own, other = own_cov_ref[...], unpack(narrow(other_ref[size:, :]))
    down_t = split(jnp.where(lower, own_t, other_t))
    cov = carry(down_t, jnp.where(lower, other, own), jnp.where(lower, own, other))
    link_t = mm(down_t, jnp.where(lower, other_t, own_t))
    link_t_ref[...] = link_t
    cov_ref[...] = cov
    packed_ref[...] = own_half(pack(cov))
    half_t_ref[...] = own_half(link_t)


def merge_kernel(level, link_t_ref, cov_ref, *refs):
    got_t = from_halves(refs[0][...], refs[1][...])
    got = unpack(from_halves(refs[2][...], refs[3][...]))
    own_t, own = link_t_ref[...], cov_ref[...]
    lower = (lax.shift_right_logical(lax.axis_index("seg") // 2, level) & 1) == 0
    down_t = split(jnp.where(lower, own_t, got_t))
    cov = carry(down_t, jnp.where(lower, got, own), jnp.where(lower, own, got))
    refs[4][...] = own_half(pack(cov))
    if len(refs) > 5:
        link_t = mm(down_t, jnp.where(lower, got_t, own_t))
        refs[5][...] = own_half(link_t)
        refs[6][...] = link_t
        refs[7][...] = cov


def join_kernel(level, *refs):
    past_t, past, link_t, cov = (
        from_halves(refs[2 * i][...], refs[2 * i + 1][...]) for i in range(4)
    )
    chip = lax.axis_index("seg") // 2
    below = (lax.shift_right_logical(chip, level) & 1) == 0
    known = (chip & ((1 << level) - 1)) != (1 << level) - 1
    past_parts = split(past_t)
    joined = pack(carry(past_parts, unpack(cov), unpack(past)))
    joined_t = mm(past_parts, link_t)
    out_t = jnp.where(below, jnp.where(known, joined_t, link_t), past_t)
    out = jnp.where(below, jnp.where(known, joined, cov), past)
    for i, whole in enumerate((out_t, out)):
        half = whole.shape[0] // 2
        refs[8 + 2 * i][...] = own_half(whole)
        refs[9 + 2 * i][...] = jnp.where(is_lower(), whole[half:], whole[:half])


def prepare_kernel(levels, panels, mask_ref, *refs):
    base_refs, own_refs, refs = refs[:panels], refs[panels : 2 * panels], refs[2 * panels :]
    (other_ref, maps_ref, links_t_ref), refs = refs[:3], refs[3:]
    past_refs, refs = refs[: 4 * (levels > 1)], refs[4 * (levels > 1) :]
    left_high, left_low, right_high, right_low, const_ref, token_ref, scratch = refs
    token_ref[...] = jnp.zeros_like(token_ref)
    own_cols = own_refs[0].shape[0]
    size = base_refs[0].shape[0]
    row_at = lax.axis_index("row")
    rows = left_high.shape[0] // panels - own_cols
    at_row = lax.broadcasted_iota(jnp.int32, (size, size), 0)
    at_col = lax.broadcasted_iota(jnp.int32, (size, size), 1)
    eye = (at_row == at_col).astype(F32)
    other = unpack(narrow(other_ref[size:, :]))
    lower = is_lower()
    if past_refs:
        chip = lax.axis_index("seg") // 2
        low = (1 << (levels - 1)) - 1
        known = (chip & low) != low
        past_t = from_halves(past_refs[0][...], past_refs[1][...])
        past = unpack(from_halves(past_refs[2][...], past_refs[3][...]))
        to_t = jnp.where(known, past_t, eye)
        gain = jnp.where(known, past, 0.0)
        other_t = split(other_ref[:size, :])
        to_t = jnp.where(lower, mm(other_t, to_t), to_t)
        gain = jnp.where(lower, carry(other_t, gain, other), gain)
    else:
        to_t = jnp.where(lower, other_ref[:size, :], eye)
        gain = jnp.where(lower, other, 0.0)
    own_at = pl.ds(pl.multiple_of(row_at * own_cols, own_cols), own_cols)
    own_rows = pl.ds(pl.multiple_of(row_at * rows, rows), rows)
    for p in range(panels - 1, -1, -1):
        whole = split(maps_ref[p])
        own_t = split(maps_ref[p, :, own_at].T)
        scratch[:, :size] = to_t
        scratch[:, size:] = gain
        to_parts = split(to_t)
        cross = jnp.concatenate(
            [
                jnp.full((BLOCK, size), -mask_ref[p, slot].astype(F32))
                for slot in slots_of(tuple(range(size // rows)), rows)
            ],
            0,
        )
        left = jnp.concatenate([scratch[own_rows, :size] * cross, mm(own_t, to_parts)], 0)
        part = slice(p * left.shape[0], (p + 1) * left.shape[0])
        left_high[part, :], left_low[part, :] = split(left)
        right_high[p], right_low[p] = split(mm(to_parts, whole, TN))
        gains = jnp.concatenate([scratch[own_rows, size:] * cross, mm(own_t, gain)], 0)
        const = mm(gains, whole)
        const_ref[p, :rows, :] = const[:rows]
        const_ref[p, rows:, :] = const[rows:] + own_refs[p][...]
        if p > 0:
            link_t = split(links_t_ref[p])
            to_t = mm(link_t, to_t)
            gain = carry(link_t, gain, base_refs[p][...])


def finish_kernel(levels, after_ref, after_other_ref, *refs):
    left_high, left_low, right_high, right_low, const_ref, diag_hbm, off_hbm = refs[:7]
    diag_ref, off_ref, sems = refs[7:]
    panels, total, _ = const_ref.shape
    rows = off_ref.shape[1]
    chip = lax.axis_index("seg") // 2
    after = from_halves(after_ref[...], after_other_ref[...])
    after = unpack(jnp.where((chip & ((1 << levels) // 2)) == 0, after, 0.0))
    inner = split(mm((left_high[...], left_low[...]), after))
    copies = []
    for p in range(panels):
        part = slice(p * total, (p + 1) * total)
        right = (right_high[p], right_low[p])
        result = mm((inner[0][part], inner[1][part]), right) + const_ref[p]
        diag_ref[p] = result[rows:]
        off_ref[p] = result[:rows]
        copies.append(pltpu.make_async_copy(diag_ref.at[p], diag_hbm.at[p], sems.at[p, 0]))
        copies.append(pltpu.make_async_copy(off_ref.at[p], off_hbm.at[p], sems.at[p, 1]))
        copies[-2].start()
        copies[-1].start()
    for copy in copies:
        copy.wait()


def body(fill_blocks, fill_mask, inv_diag, factor_off):
    panels, width, _ = inv_diag.shape
    rows = factor_off.shape[1]
    seg_count = lax.axis_size("seg")
    row_count = lax.axis_size("row")
    size = rows * row_count
    own_cols = width // row_count
    slots = fill_blocks.shape[1]
    chosen_cols = slots * BLOCK
    chips = seg_count // 2
    half = size // 2

    def turn(x, axis, distance):
        count = lax.axis_size(axis)
        return lax.ppermute(x, axis, [(i, (i + distance) % count) for i in range(count)])

    prior_fill = turn(fill_blocks, "seg", 1)
    pick = jax.ShapeDtypeStruct((width, chosen_cols), BF16)
    bases, priors, picks, tokens = [], [], [], []
    for p in range(panels):
        base, own_prior, *high_low, token = call(
            functools.partial(prior_kernel, p),
            [shape(chosen_cols, chosen_cols), shape(own_cols, width), pick, pick, shape(1, 1, width)],
            [fill_blocks] if p else [fill_blocks, prior_fill],
            [],
            far=[inv_diag],
            scratch=[pltpu.VMEM((width, width), F32), pltpu.SemaphoreType.DMA],
            flops=6 * width * (chosen_cols * chosen_cols + own_cols * width),
            name="prior",
        )
        bases.append(base)
        priors.append(own_prior)
        picks += high_low
        tokens.append(token)
    second = factor_off + tokens[-1]
    index_gate = jnp.minimum(jnp.min(prior_fill), 0).astype(F32)

    downs, ups = [factor_off], [second]
    for i in range(row_count // 2):
        downs.append(turn(downs[-1] + index_gate if i else downs[-1], "row", -1))
    for _ in range((row_count - 1) // 2):
        ups.append(turn(ups[-1], "row", 1))
    parts, late = downs[:-1] + ups[:0:-1], downs[-1]
    far = len(downs) - 1
    came = [d for d in range(row_count) if d != far]
    whose = [tuple((i + d) % row_count for i in range(row_count)) for d in (*came, far)]
    plan = Plan(tuple(whose[:-1]), whose[-1])

    links, late_keep = call(
        functools.partial(links_kernel, plan),
        [shape(panels, size, size), shape(panels, rows, size)],
        [fill_mask],
        [*parts, *picks],
        scratch=[pltpu.VMEM((size, chosen_cols), F32)],
        flops=6 * panels * size * size * width,
        name="links",
    )
    links_t, own_whole, own_cov = call(
        functools.partial(segment_kernel, plan, panels),
        [shape(panels, size, size), shape(size + 5 * half // 4, size), shape(size, size)],
        [],
        [late, links, late_keep, *picks, *bases],
        flops=6 * panels * rows * size * width + 18 * (panels - 1) * size**3,
        name="segment",
    )
    maps, maps_token = call(
        functools.partial(maps_kernel, plan),
        [shape(panels, size, width), shape(1, half)],
        [fill_mask],
        [inv_diag, *parts, late],
        scratch=[pltpu.VMEM((size, width), F32)],
        flops=6 * panels * size * width * width,
        mib=24,
        name="maps",
    )
    swap = [(i, i ^ 1) for i in range(seg_count)]
    other_whole = lax.ppermute(own_whole, "seg", swap)
    half_packed = shape(5 * half // 4, half)
    half_link = shape(half, size)
    link_t, cov, send, send_t = call(
        chip_kernel,
        [shape(size, size), shape(size, size), half_packed, half_link],
        [],
        [own_whole, own_cov, other_whole],
        flops=18 * size**3,
        name="chip",
    )
    past = None
    after = (jnp.zeros(half_packed.shape, F32),) * 2
    levels = (chips - 1).bit_length()
    prepared = None

    def prepare():
        total = rows + own_cols
        left = jax.ShapeDtypeStruct((panels * total, size), BF16)
        right = jax.ShapeDtypeStruct((panels, size, width), BF16)
        return call(
            functools.partial(prepare_kernel, levels, panels),
            [left, left, right, right, shape(panels, total, width), shape(1, half)],
            [fill_mask],
            [*bases, *priors, other_whole, maps, links_t, *(past or ())],
            scratch=[pltpu.VMEM((size, width), F32)],
            flops=6 * panels * size * (total * size + size * width + total * width + 3 * size * size),
            mib=24,
            name="prepare",
        )

    for level in range(levels):
        partner = [(i, i ^ (2 << level)) for i in range(seg_count)]
        got = lax.ppermute(send, "seg", partner)
        if level == levels - 1:
            *prepared, token = prepare()
            got = got + token
            after = (got, lax.ppermute(got, "seg", swap))
            break
        got_t = lax.ppermute(send_t, "seg", partner)
        if level == 0:
            got = got + maps_token
        got = (got_t, lax.ppermute(got_t, "seg", swap), got, lax.ppermute(got, "seg", swap))
        outs = [half_packed]
        if level < levels - 2:
            outs += [half_link, shape(size, size), shape(size, size)]
        send, *more = call(
            functools.partial(merge_kernel, level), outs, [], [link_t, cov, *got],
            flops=18 * size**3, name="merge",
        )
        if more:
            send_t, link_t, cov = more
        if past is None:
            past = got
        else:
            past = call(
                functools.partial(join_kernel, level),
                [half_link, half_link, half_packed, half_packed],
                [],
                [*past, *got],
                flops=18 * size**3,
                name="join",
            )
    if prepared is None:
        *prepared, _ = prepare()
    diag, off = call(
        functools.partial(finish_kernel, levels),
        [shape(panels, own_cols, width), shape(panels, rows, width)],
        [],
        [*after, *prepared],
        out_far=True,
        scratch=[
            pltpu.VMEM((panels, own_cols, width), F32),
            pltpu.VMEM((panels, rows, width), F32),
            pltpu.SemaphoreType.DMA((panels, 2)),
        ],
        flops=6 * panels * (rows + own_cols) * size * (size + width),
        name="finish",
    )
    return diag, off


def solution(mesh):
    placed = (P("seg", None), P("seg", None), P("seg", None, None), P("seg", "row", None))
    return jax.shard_map(
        body,
        mesh=mesh,
        in_specs=placed,
        out_specs=(P("seg", "row", None), P("seg", "row", None)),
        check_vma=False,
    )
```

```python
import functools
from typing import NamedTuple

import jax
import jax.numpy as jnp
from jax import lax
from jax.experimental import pallas as pl
from jax.experimental.pallas import tpu as pltpu
from jax.sharding import PartitionSpec as P

BLOCK = 64
LANES = 128
F32 = jnp.float32
BF16 = jnp.bfloat16
NN = (((1,), (0,)), ((), ()))
NT = (((1,), (1,)), ((), ()))
TN = (((0,), (0,)), ((), ()))


def split(x):
    high = x.astype(BF16)
    return high, (x - high.astype(F32)).astype(BF16)


def mm(a, b, dims=NN):
    a = a if isinstance(a, tuple) else split(a)
    b = b if isinstance(b, tuple) else split(b)
    dot = functools.partial(lax.dot_general, dimension_numbers=dims, preferred_element_type=F32)
    return dot(a[0], b[0]) + (dot(a[0], b[1]) + dot(a[1], b[0]))


def carry(link_t, cov, base):
    link_t = link_t if isinstance(link_t, tuple) else split(link_t)
    return mm(mm(link_t, cov), link_t, NT) + base


def pack(cov):
    half = cov.shape[0] // 2
    part = half // 2
    first, second = cov[:half, :half], cov[half:, half:]
    lane = lax.broadcasted_iota(jnp.int32, (part, half), 1)
    last = jnp.where(lane < part, pltpu.roll(first[part:], part, 1), second[part:])
    return jnp.concatenate([cov[:half, half:], first[:part], second[:part], last], 0)


def unpack(packed):
    half = packed.shape[1]
    part = half // 2
    cross, last = packed[:half], packed[2 * half :]
    row = lax.broadcasted_iota(jnp.int32, (half, half), 0)
    lane = lax.broadcasted_iota(jnp.int32, (half, half), 1)

    def symmetric(top, bottom):
        upper = jnp.concatenate([top, bottom], 0)
        return jnp.where((row < part) | (lane >= part), upper, upper.T)

    first = symmetric(packed[half : half + part], pltpu.roll(last, part, 1))
    second = symmetric(packed[half + part : 2 * half], last)
    top = jnp.concatenate([first, cross], 1)
    bottom = jnp.concatenate([cross.T, second], 1)
    return jnp.concatenate([top, bottom], 0)


def is_lower():
    return (lax.axis_index("seg") & 1) == 0


def from_halves(own, other):
    lower = is_lower()
    return jnp.concatenate([jnp.where(lower, own, other), jnp.where(lower, other, own)], 0)


def own_half(whole):
    half = whole.shape[0] // 2
    return jnp.where(is_lower(), whole[:half], whole[half:])


def two_blocks(load, left, right):
    def placed(block, half):
        slab = load(lax.shift_right_logical(block, 1))
        return jnp.where((block & 1) == half, slab, pltpu.roll(slab, BLOCK, 1))

    a, b = placed(left, 0), placed(right, 1)
    lane = lax.broadcasted_iota(jnp.int32, a.shape, 1)
    return jnp.where(lane < BLOCK, a, b)


def tile_of(ref, *lead):
    def load(tile):
        return ref[(*lead, slice(None), pl.ds(pl.multiple_of(tile * LANES, LANES), LANES))]

    return load


def chosen_of(panel, fill_ref, prior_ref=None):
    slots = fill_ref.shape[1]
    if panel > 0:
        return [fill_ref[panel - 1, j] for j in range(slots)]
    first = lax.axis_index("seg") == 0
    last = prior_ref.shape[0] - 1
    return [jnp.where(first, fill_ref[0, j], prior_ref[last, j]) for j in range(slots)]


def vmem(count):
    return [pl.BlockSpec(memory_space=pltpu.VMEM)] * count


def smem(count):
    return [pl.BlockSpec(memory_space=pltpu.SMEM)] * count


def call(
    kernel, outs, scalars, arrays, far=(), out_far=False, through=(), scratch=(), flops=0, mib=16, name=None
):
    moved = sum(a.size * 4 for a in (*arrays, *far)) + sum(o.size * 4 for o in outs)
    first = len(scalars) + len(arrays) + len(far)
    count = len(through)

    def inner(*refs):
        kernel(*refs[:first], *refs[first + count : first + count + len(outs)], *refs[first + 2 * count + len(outs) :])

    return pl.pallas_call(
        inner,
        out_shape=[*outs, *(jax.ShapeDtypeStruct(a.shape, a.dtype) for a in through)],
        in_specs=smem(len(scalars))
        + vmem(len(arrays))
        + [pl.BlockSpec(memory_space=pltpu.HBM)] * len(far)
        + [pl.BlockSpec(memory_space=pl.ANY)] * count,
        out_specs=([pl.BlockSpec(memory_space=pltpu.HBM)] * len(outs) if out_far else vmem(len(outs)))
        + [pl.BlockSpec(memory_space=pl.ANY)] * count,
        scratch_shapes=list(scratch),
        input_output_aliases={first + i: len(outs) + i for i in range(count)},
        cost_estimate=pl.CostEstimate(flops=flops, bytes_accessed=moved, transcendentals=0),
        compiler_params=pltpu.CompilerParams(vmem_limit_bytes=mib << 20),
        name=name,
    )(*scalars, *arrays, *(pltpu.with_memory_space_constraint(a, pltpu.HBM) for a in far), *through)


def shape(*dims):
    return jax.ShapeDtypeStruct(dims, F32)


def kept_rows(mask_ref, panel, slot, rows):
    alive = lax.axis_index("seg") * mask_ref.shape[0] + panel < (
        lax.axis_size("seg") * mask_ref.shape[0] - 1
    )
    return rows * (mask_ref[panel, slot].astype(F32) * alive.astype(F32))


def triangular_mm(left, lower):
    cut = left.shape[1] // 2
    first, second = split(left[:, :cut]), split(left[:, cut:])
    below = split(lower[cut:, :])
    return jnp.concatenate(
        [
            mm(second, (below[0][:, :cut], below[1][:, :cut])) + mm(first, lower[:cut, :cut]),
            mm(second, (below[0][:, cut:], below[1][:, cut:])),
        ],
        1,
    )


def prior_kernel(panel, *refs):
    *scalar_refs, inv_hbm, base_ref, own_ref, pick_high_ref, pick_low_ref, token_ref = refs[:-2]
    inv_ref, sem = refs[-2:]
    copy = pltpu.make_async_copy(inv_hbm.at[panel], inv_ref, sem)
    copy.start()
    token_ref[...] = jnp.zeros_like(token_ref)
    chosen = chosen_of(panel, *scalar_refs)
    own_cols = own_ref.shape[0]
    own_at = pl.ds(pl.multiple_of(lax.axis_index("row") * own_cols, own_cols), own_cols)
    copy.wait()
    picked = split(
        jnp.concatenate(
            [
                two_blocks(tile_of(inv_ref), chosen[2 * t], chosen[2 * t + 1])
                for t in range(len(chosen) // 2)
            ],
            1,
        )
    )
    pick_high_ref[...], pick_low_ref[...] = picked
    base_ref[...] = mm(picked, picked, TN)
    own_ref[...] = mm(inv_ref[:, own_at], inv_ref[...], TN)


class Plan(NamedTuple):
    early: tuple
    late: tuple


def at_row(table):
    value = jnp.int32(table[0])
    for i, entry in enumerate(table[1:], 1):
        value = jnp.where(lax.axis_index("row") == i, entry, value)
    return value


def slots_of(owners, rows):
    first = at_row(owners) * (rows // BLOCK)
    return [first + s for s in range(rows // BLOCK)]


def put_rows(mask_ref, panel, owners, part, out_ref, take):
    for s, slot in enumerate(slots_of(owners, part.shape[0])):
        kept = kept_rows(mask_ref, panel, slot, part[s * BLOCK : (s + 1) * BLOCK, :])
        out_ref[pl.ds(pl.multiple_of(slot * BLOCK, BLOCK), BLOCK), :] = take(kept)


def links_kernel(plan, mask_ref, *refs):
    count = len(plan.early)
    parts, refs = refs[:count], refs[count:]
    *pick_refs, links_t_ref, late_keep_ref, rows_ref = refs
    rows_ref[...] = jnp.zeros_like(rows_ref)
    for p in range(links_t_ref.shape[0]):
        pick = (pick_refs[2 * p][...], pick_refs[2 * p + 1][...])
        for owners, part in zip(plan.early, parts):
            put_rows(mask_ref, p, owners, part[p], rows_ref, lambda kept: mm(kept, pick))
        links_t_ref[p] = rows_ref[...].T
        for s, slot in enumerate(slots_of(plan.late, late_keep_ref.shape[1])):
            block = slice(s * BLOCK, (s + 1) * BLOCK)
            ones = jnp.ones((BLOCK, late_keep_ref.shape[2]), F32)
            late_keep_ref[p, block, :] = kept_rows(mask_ref, p, slot, ones)


def segment_kernel(plan, panels, *refs):
    late_ref, early_ref, keep_ref, *refs = refs
    pick_refs, base_refs = refs[: 2 * panels], refs[2 * panels : 3 * panels]
    links_t_ref, whole_ref = refs[3 * panels :]
    size = links_t_ref.shape[1]
    rows = keep_ref.shape[1]
    here = lax.broadcasted_iota(jnp.int32, (size, size), 1) // rows == at_row(plan.late)
    cov = link_t = None
    for p in range(panels - 1, -1, -1):
        pick = (pick_refs[2 * p][...], pick_refs[2 * p + 1][...])
        late = mm(late_ref[p], pick) * keep_ref[p]
        late_t = jnp.concatenate([late] * (size // rows), 0).T
        own_t = jnp.where(here, late_t, early_ref[p])
        links_t_ref[p] = own_t
        if cov is None:
            cov, link_t = base_refs[p][...], own_t
        else:
            own_t = split(own_t)
            cov = carry(own_t, cov, base_refs[p][...])
            link_t = mm(own_t, link_t)
    whole_ref[:size] = link_t
    whole_ref[size:] = cov


def maps_kernel(plan, mask_ref, inv_ref, *refs):
    count = len(plan.early)
    parts, (late_ref, maps_ref, token_ref, rows_ref) = refs[:count], refs[count:]
    token_ref[...] = jnp.zeros_like(token_ref)
    for p in range(inv_ref.shape[0]):
        for owners, part in zip(plan.early, parts):
            put_rows(mask_ref, p, owners, part[p], rows_ref, lambda kept: kept)
        put_rows(mask_ref, p, plan.late, late_ref[p], rows_ref, lambda kept: kept)
        maps_ref[p] = triangular_mm(rows_ref[...], inv_ref[p])


def chip_kernel(own_ref, other_ref, link_t_ref, cov_ref, packed_ref, half_t_ref):
    size = cov_ref.shape[0]
    lower = is_lower()
    own_t, other_t = own_ref[:size, :], other_ref[:size, :]
    own, other = own_ref[size:, :], other_ref[size:, :]
    down_t = split(jnp.where(lower, own_t, other_t))
    cov = carry(down_t, jnp.where(lower, other, own), jnp.where(lower, own, other))
    link_t = mm(down_t, jnp.where(lower, other_t, own_t))
    link_t_ref[...] = link_t
    cov_ref[...] = cov
    packed_ref[...] = own_half(pack(cov))
    half_t_ref[...] = own_half(link_t)


def merge_kernel(level, link_t_ref, cov_ref, *refs):
    got_t = from_halves(refs[0][...], refs[1][...])
    got = unpack(from_halves(refs[2][...], refs[3][...]))
    own_t, own = link_t_ref[...], cov_ref[...]
    lower = (lax.shift_right_logical(lax.axis_index("seg") // 2, level) & 1) == 0
    down_t = split(jnp.where(lower, own_t, got_t))
    cov = carry(down_t, jnp.where(lower, got, own), jnp.where(lower, own, got))
    refs[4][...] = own_half(pack(cov))
    if len(refs) > 5:
        link_t = mm(down_t, jnp.where(lower, got_t, own_t))
        refs[5][...] = own_half(link_t)
        refs[6][...] = link_t
        refs[7][...] = cov


def join_kernel(level, *refs):
    past_t, past, link_t, cov = (
        from_halves(refs[2 * i][...], refs[2 * i + 1][...]) for i in range(4)
    )
    chip = lax.axis_index("seg") // 2
    below = (lax.shift_right_logical(chip, level) & 1) == 0
    known = (chip & ((1 << level) - 1)) != (1 << level) - 1
    past_parts = split(past_t)
    joined = pack(carry(past_parts, unpack(cov), unpack(past)))
    joined_t = mm(past_parts, link_t)
    out_t = jnp.where(below, jnp.where(known, joined_t, link_t), past_t)
    out = jnp.where(below, jnp.where(known, joined, cov), past)
    for i, whole in enumerate((out_t, out)):
        half = whole.shape[0] // 2
        refs[8 + 2 * i][...] = own_half(whole)
        refs[9 + 2 * i][...] = jnp.where(is_lower(), whole[half:], whole[:half])


def prepare_kernel(levels, panels, mask_ref, *refs):
    base_refs, own_refs, refs = refs[:panels], refs[panels : 2 * panels], refs[2 * panels :]
    (other_ref, maps_ref, links_t_ref), refs = refs[:3], refs[3:]
    past_refs, refs = refs[: 4 * (levels > 1)], refs[4 * (levels > 1) :]
    left_high, left_low, right_high, right_low, const_ref, token_ref, scratch = refs
    token_ref[...] = jnp.zeros_like(token_ref)
    own_cols = own_refs[0].shape[0]
    size = base_refs[0].shape[0]
    row_at = lax.axis_index("row")
    rows = left_high.shape[0] // panels - own_cols
    at_row = lax.broadcasted_iota(jnp.int32, (size, size), 0)
    at_col = lax.broadcasted_iota(jnp.int32, (size, size), 1)
    eye = (at_row == at_col).astype(F32)
    other = other_ref[size:, :]
    lower = is_lower()
    if past_refs:
        chip = lax.axis_index("seg") // 2
        low = (1 << (levels - 1)) - 1
        known = (chip & low) != low
        past_t = from_halves(past_refs[0][...], past_refs[1][...])
        past = unpack(from_halves(past_refs[2][...], past_refs[3][...]))
        to_t = jnp.where(known, past_t, eye)
        gain = jnp.where(known, past, 0.0)
        other_t = split(other_ref[:size, :])
        to_t = jnp.where(lower, mm(other_t, to_t), to_t)
        gain = jnp.where(lower, carry(other_t, gain, other), gain)
    else:
        to_t = jnp.where(lower, other_ref[:size, :], eye)
        gain = jnp.where(lower, other, 0.0)
    own_at = pl.ds(pl.multiple_of(row_at * own_cols, own_cols), own_cols)
    own_rows = pl.ds(pl.multiple_of(row_at * rows, rows), rows)
    for p in range(panels - 1, -1, -1):
        whole = split(maps_ref[p])
        own_t = split(maps_ref[p, :, own_at].T)
        scratch[:, :size] = to_t
        scratch[:, size:] = gain
        to_parts = split(to_t)
        cross = jnp.concatenate(
            [
                jnp.full((BLOCK, size), -mask_ref[p, slot].astype(F32))
                for slot in slots_of(tuple(range(size // rows)), rows)
            ],
            0,
        )
        left = jnp.concatenate([scratch[own_rows, :size] * cross, mm(own_t, to_parts)], 0)
        part = slice(p * left.shape[0], (p + 1) * left.shape[0])
        left_high[part, :], left_low[part, :] = split(left)
        right_high[p], right_low[p] = split(mm(to_parts, whole, TN))
        gains = jnp.concatenate([scratch[own_rows, size:] * cross, mm(own_t, gain)], 0)
        const = mm(gains, whole)
        const_ref[p, :rows, :] = const[:rows]
        const_ref[p, rows:, :] = const[rows:] + own_refs[p][...]
        if p > 0:
            link_t = split(links_t_ref[p])
            to_t = mm(link_t, to_t)
            gain = carry(link_t, gain, base_refs[p][...])


def finish_kernel(levels, after_ref, after_other_ref, *refs):
    left_high, left_low, right_high, right_low, const_ref, diag_hbm, off_hbm = refs[:7]
    diag_ref, off_ref, sems = refs[7:]
    panels, total, _ = const_ref.shape
    rows = off_ref.shape[1]
    chip = lax.axis_index("seg") // 2
    after = from_halves(after_ref[...], after_other_ref[...])
    after = unpack(jnp.where((chip & ((1 << levels) // 2)) == 0, after, 0.0))
    inner = split(mm((left_high[...], left_low[...]), after))
    copies = []
    for p in range(panels):
        part = slice(p * total, (p + 1) * total)
        right = (right_high[p], right_low[p])
        result = mm((inner[0][part], inner[1][part]), right) + const_ref[p]
        diag_ref[p] = result[rows:]
        off_ref[p] = result[:rows]
        copies.append(pltpu.make_async_copy(diag_ref.at[p], diag_hbm.at[p], sems.at[p, 0]))
        copies.append(pltpu.make_async_copy(off_ref.at[p], off_hbm.at[p], sems.at[p, 1]))
        copies[-2].start()
        copies[-1].start()
    for copy in copies:
        copy.wait()


def body(fill_blocks, fill_mask, inv_diag, factor_off):
    panels, width, _ = inv_diag.shape
    rows = factor_off.shape[1]
    seg_count = lax.axis_size("seg")
    row_count = lax.axis_size("row")
    size = rows * row_count
    own_cols = width // row_count
    slots = fill_blocks.shape[1]
    chosen_cols = slots * BLOCK
    chips = seg_count // 2
    half = size // 2

    def turn(x, axis, distance):
        count = lax.axis_size(axis)
        return lax.ppermute(x, axis, [(i, (i + distance) % count) for i in range(count)])

    prior_fill = turn(fill_blocks, "seg", 1)
    pick = jax.ShapeDtypeStruct((width, chosen_cols), BF16)
    bases, priors, picks, tokens = [], [], [], []
    for p in range(panels):
        base, own_prior, *high_low, token = call(
            functools.partial(prior_kernel, p),
            [shape(chosen_cols, chosen_cols), shape(own_cols, width), pick, pick, shape(1, 1, width)],
            [fill_blocks] if p else [fill_blocks, prior_fill],
            [],
            far=[inv_diag],
            scratch=[pltpu.VMEM((width, width), F32), pltpu.SemaphoreType.DMA],
            flops=6 * width * (chosen_cols * chosen_cols + own_cols * width),
            name="prior",
        )
        bases.append(base)
        priors.append(own_prior)
        picks += high_low
        tokens.append(token)
    second = factor_off + tokens[-1]
    index_gate = jnp.minimum(jnp.min(prior_fill), 0).astype(F32)

    ups, downs = [factor_off], [second]
    for i in range(row_count // 2):
        ups.append(turn(ups[-1] + index_gate if i else ups[-1], "row", 1))
    for _ in range((row_count - 1) // 2):
        downs.append(turn(downs[-1], "row", -1))
    parts, late = ups[:-1] + downs[:0:-1], ups[-1]
    far = len(ups) - 1
    came = [d for d in range(row_count) if d != far]
    whose = [tuple((i - d) % row_count for i in range(row_count)) for d in (*came, far)]
    plan = Plan(tuple(whose[:-1]), whose[-1])

    links, late_keep = call(
        functools.partial(links_kernel, plan),
        [shape(panels, size, size), shape(panels, rows, size)],
        [fill_mask],
        [*parts, *picks],
        scratch=[pltpu.VMEM((size, chosen_cols), F32)],
        flops=6 * panels * size * size * width,
        name="links",
    )
    links_t, own_whole = call(
        functools.partial(segment_kernel, plan, panels),
        [shape(panels, size, size), shape(2 * size, size)],
        [],
        [late, links, late_keep, *picks, *bases],
        flops=6 * panels * rows * size * width + 18 * (panels - 1) * size**3,
        name="segment",
    )
    maps, maps_token = call(
        functools.partial(maps_kernel, plan),
        [shape(panels, size, width), shape(1, half)],
        [fill_mask],
        [inv_diag, *parts, late],
        scratch=[pltpu.VMEM((size, width), F32)],
        flops=6 * panels * size * width * width,
        mib=24,
        name="maps",
    )
    swap = [(i, i ^ 1) for i in range(seg_count)]
    other_whole = lax.ppermute(own_whole, "seg", swap)
    half_packed = shape(5 * half // 4, half)
    half_link = shape(half, size)
    link_t, cov, send, send_t = call(
        chip_kernel,
        [shape(size, size), shape(size, size), half_packed, half_link],
        [],
        [own_whole, other_whole],
        flops=18 * size**3,
        name="chip",
    )
    past = None
    after = (jnp.zeros(half_packed.shape, F32),) * 2
    levels = (chips - 1).bit_length()
    prepared = None

    def prepare():
        total = rows + own_cols
        left = jax.ShapeDtypeStruct((panels * total, size), BF16)
        right = jax.ShapeDtypeStruct((panels, size, width), BF16)
        return call(
            functools.partial(prepare_kernel, levels, panels),
            [left, left, right, right, shape(panels, total, width), shape(1, half)],
            [fill_mask],
            [*bases, *priors, other_whole, maps, links_t, *(past or ())],
            scratch=[pltpu.VMEM((size, width), F32)],
            flops=6 * panels * size * (total * size + size * width + total * width + 3 * size * size),
            mib=24,
            name="prepare",
        )

    for level in range(levels):
        partner = [(i, i ^ (2 << level)) for i in range(seg_count)]
        got = lax.ppermute(send, "seg", partner)
        if level == levels - 1:
            *prepared, token = prepare()
            got = got + token
            after = (got, lax.ppermute(got, "seg", swap))
            break
        got_t = lax.ppermute(send_t, "seg", partner)
        if level == 0:
            got = got + maps_token
        got = (got_t, lax.ppermute(got_t, "seg", swap), got, lax.ppermute(got, "seg", swap))
        outs = [half_packed]
        if level < levels - 2:
            outs += [half_link, shape(size, size), shape(size, size)]
        send, *more = call(
            functools.partial(merge_kernel, level), outs, [], [link_t, cov, *got],
            flops=18 * size**3, name="merge",
        )
        if more:
            send_t, link_t, cov = more
        if past is None:
            past = got
        else:
            past = call(
                functools.partial(join_kernel, level),
                [half_link, half_link, half_packed, half_packed],
                [],
                [*past, *got],
                flops=18 * size**3,
                name="join",
            )
    if prepared is None:
        *prepared, _ = prepare()
    diag, off = call(
        functools.partial(finish_kernel, levels),
        [shape(panels, own_cols, width), shape(panels, rows, width)],
        [],
        [*after, *prepared],
        out_far=True,
        scratch=[
            pltpu.VMEM((panels, own_cols, width), F32),
            pltpu.VMEM((panels, rows, width), F32),
            pltpu.SemaphoreType.DMA((panels, 2)),
        ],
        flops=6 * panels * (rows + own_cols) * size * (size + width),
        name="finish",
    )
    return diag, off


def solution(mesh):
    placed = (P("seg", None), P("seg", None), P("seg", None, None), P("seg", "row", None))
    return jax.shard_map(
        body,
        mesh=mesh,
        in_specs=placed,
        out_specs=(P("seg", "row", None), P("seg", "row", None)),
        check_vma=False,
    )
```

```python
import functools
from typing import NamedTuple

import jax
import jax.numpy as jnp
from jax import lax
from jax.experimental import pallas as pl
from jax.experimental.pallas import tpu as pltpu
from jax.sharding import PartitionSpec as P

BLOCK = 64
LANES = 128
F32 = jnp.float32
BF16 = jnp.bfloat16
NN = (((1,), (0,)), ((), ()))
NT = (((1,), (1,)), ((), ()))
TN = (((0,), (0,)), ((), ()))


def split(x):
    high = x.astype(BF16)
    return high, (x - high.astype(F32)).astype(BF16)


def mm(a, b, dims=NN):
    a = a if isinstance(a, tuple) else split(a)
    b = b if isinstance(b, tuple) else split(b)
    dot = functools.partial(lax.dot_general, dimension_numbers=dims, preferred_element_type=F32)
    return dot(a[0], b[0]) + (dot(a[0], b[1]) + dot(a[1], b[0]))


def carry(link_t, cov, base):
    link_t = link_t if isinstance(link_t, tuple) else split(link_t)
    return mm(mm(link_t, cov), link_t, NT) + base


def pack(cov):
    half = cov.shape[0] // 2
    part = half // 2
    first, second = cov[:half, :half], cov[half:, half:]
    lane = lax.broadcasted_iota(jnp.int32, (part, half), 1)
    last = jnp.where(lane < part, pltpu.roll(first[part:], part, 1), second[part:])
    return jnp.concatenate([cov[:half, half:], first[:part], second[:part], last], 0)


def unpack(packed):
    half = packed.shape[1]
    part = half // 2
    cross, last = packed[:half], packed[2 * half :]
    row = lax.broadcasted_iota(jnp.int32, (half, half), 0)
    lane = lax.broadcasted_iota(jnp.int32, (half, half), 1)

    def symmetric(top, bottom):
        upper = jnp.concatenate([top, bottom], 0)
        return jnp.where((row < part) | (lane >= part), upper, upper.T)

    first = symmetric(packed[half : half + part], pltpu.roll(last, part, 1))
    second = symmetric(packed[half + part : 2 * half], last)
    top = jnp.concatenate([first, cross], 1)
    bottom = jnp.concatenate([cross.T, second], 1)
    return jnp.concatenate([top, bottom], 0)


def is_lower():
    return (lax.axis_index("seg") & 1) == 0


def from_halves(own, other):
    lower = is_lower()
    return jnp.concatenate([jnp.where(lower, own, other), jnp.where(lower, other, own)], 0)


def own_half(whole):
    half = whole.shape[0] // 2
    return jnp.where(is_lower(), whole[:half], whole[half:])


def two_blocks(load, left, right):
    def placed(block, half):
        slab = load(lax.shift_right_logical(block, 1))
        return jnp.where((block & 1) == half, slab, pltpu.roll(slab, BLOCK, 1))

    a, b = placed(left, 0), placed(right, 1)
    lane = lax.broadcasted_iota(jnp.int32, a.shape, 1)
    return jnp.where(lane < BLOCK, a, b)


def tile_of(ref, *lead):
    def load(tile):
        return ref[(*lead, slice(None), pl.ds(pl.multiple_of(tile * LANES, LANES), LANES))]

    return load


def chosen_of(panel, fill_ref, prior_ref=None):
    slots = fill_ref.shape[1]
    if panel > 0:
        return [fill_ref[panel - 1, j] for j in range(slots)]
    first = lax.axis_index("seg") == 0
    last = prior_ref.shape[0] - 1
    return [jnp.where(first, fill_ref[0, j], prior_ref[last, j]) for j in range(slots)]


def order_of(chosen, blocks):
    slots = len(chosen)
    rest = [jnp.int32(0)] * (blocks - slots)
    place = []
    seen = jnp.int32(0)
    for b in range(blocks):
        hit = jnp.int32(0)
        where = jnp.int32(0)
        for j in range(slots):
            same = (chosen[j] == b).astype(jnp.int32)
            hit = hit + same
            where = where + same * j
        free = 1 - hit
        for q in range(blocks - slots):
            rest[q] = rest[q] + jnp.where(seen == q, free * b, 0)
        place.append(jnp.where(hit > 0, where, slots + seen))
        seen = seen + free
    return rest, place


def vmem(count):
    return [pl.BlockSpec(memory_space=pltpu.VMEM)] * count


def smem(count):
    return [pl.BlockSpec(memory_space=pltpu.SMEM)] * count


def call(
    kernel, outs, scalars, arrays, far=(), out_far=False, through=(), scratch=(), flops=0, mib=16, name=None
):
    moved = sum(a.size * 4 for a in (*arrays, *far)) + sum(o.size * 4 for o in outs)
    first = len(scalars) + len(arrays) + len(far)
    count = len(through)

    def inner(*refs):
        kernel(*refs[:first], *refs[first + count : first + count + len(outs)], *refs[first + 2 * count + len(outs) :])

    return pl.pallas_call(
        inner,
        out_shape=[*outs, *(jax.ShapeDtypeStruct(a.shape, a.dtype) for a in through)],
        in_specs=smem(len(scalars))
        + vmem(len(arrays))
        + [pl.BlockSpec(memory_space=pltpu.HBM)] * len(far)
        + [pl.BlockSpec(memory_space=pl.ANY)] * count,
        out_specs=([pl.BlockSpec(memory_space=pltpu.HBM)] * len(outs) if out_far else vmem(len(outs)))
        + [pl.BlockSpec(memory_space=pl.ANY)] * count,
        scratch_shapes=list(scratch),
        input_output_aliases={first + i: len(outs) + i for i in range(count)},
        cost_estimate=pl.CostEstimate(flops=flops, bytes_accessed=moved, transcendentals=0),
        compiler_params=pltpu.CompilerParams(vmem_limit_bytes=mib << 20),
        name=name,
    )(*scalars, *arrays, *(pltpu.with_memory_space_constraint(a, pltpu.HBM) for a in far), *through)


def shape(*dims):
    return jax.ShapeDtypeStruct(dims, F32)


def kept_rows(mask_ref, panel, slot, rows):
    alive = lax.axis_index("seg") * mask_ref.shape[0] + panel < (
        lax.axis_size("seg") * mask_ref.shape[0] - 1
    )
    return rows * (mask_ref[panel, slot].astype(F32) * alive.astype(F32))


def triangular_mm(left, lower):
    cut = left.shape[1] // 2
    first, second = split(left[:, :cut]), split(left[:, cut:])
    below = split(lower[cut:, :])
    return jnp.concatenate(
        [
            mm(second, (below[0][:, :cut], below[1][:, :cut])) + mm(first, lower[:cut, :cut]),
            mm(second, (below[0][:, cut:], below[1][:, cut:])),
        ],
        1,
    )


def prior_kernel(panel, *refs):
    *scalar_refs, inv_hbm, base_ref, own_ref, pick_high_ref, pick_low_ref, token_ref = refs[:-2]
    inv_ref, sem = refs[-2:]
    copy = pltpu.make_async_copy(inv_hbm.at[panel], inv_ref, sem)
    copy.start()
    token_ref[...] = jnp.zeros_like(token_ref)
    chosen = chosen_of(panel, *scalar_refs)
    own_cols = own_ref.shape[0]
    own_at = pl.ds(pl.multiple_of(lax.axis_index("row") * own_cols, own_cols), own_cols)
    copy.wait()
    picked = split(
        jnp.concatenate(
            [
                two_blocks(tile_of(inv_ref), chosen[2 * t], chosen[2 * t + 1])
                for t in range(len(chosen) // 2)
            ],
            1,
        )
    )
    pick_high_ref[...], pick_low_ref[...] = picked
    base_ref[...] = mm(picked, picked, TN)
    own_ref[...] = mm(inv_ref[:, own_at], inv_ref[...], TN)


class Plan(NamedTuple):
    early: tuple
    late: tuple


def at_row(table):
    value = jnp.int32(table[0])
    for i, entry in enumerate(table[1:], 1):
        value = jnp.where(lax.axis_index("row") == i, entry, value)
    return value


def slots_of(owners, rows):
    first = at_row(owners) * (rows // BLOCK)
    return [first + s for s in range(rows // BLOCK)]


def put_rows(mask_ref, panel, owners, part, out_ref, take):
    for s, slot in enumerate(slots_of(owners, part.shape[0])):
        kept = kept_rows(mask_ref, panel, slot, part[s * BLOCK : (s + 1) * BLOCK, :])
        out_ref[pl.ds(pl.multiple_of(slot * BLOCK, BLOCK), BLOCK), :] = take(kept)


def links_kernel(plan, mask_ref, *refs):
    parts, refs = refs[: len(plan.early)], refs[len(plan.early) :]
    *pick_refs, links_t_ref, rows_ref = refs
    rows_ref[...] = jnp.zeros_like(rows_ref)
    for p in range(links_t_ref.shape[0]):
        pick = (pick_refs[2 * p][...], pick_refs[2 * p + 1][...])
        for owners, part in zip(plan.early, parts):
            put_rows(mask_ref, p, owners, part[p], rows_ref, lambda kept: mm(kept, pick))
        links_t_ref[p] = rows_ref[...].T


def kept_block(mask_ref, panel, owners, part):
    return jnp.concatenate(
        [
            kept_rows(mask_ref, panel, slot, part[s * BLOCK : (s + 1) * BLOCK, :])
            for s, slot in enumerate(slots_of(owners, part.shape[0]))
        ],
        0,
    )


def chosen_kernel(owners, mask_ref, part, *refs):
    *pick_refs, out_ref = refs
    for p in range(out_ref.shape[0]):
        pick = (pick_refs[2 * p][...], pick_refs[2 * p + 1][...])
        out_ref[p] = mm(kept_block(mask_ref, p, owners, part[p]), pick)


def rest_kernel(owners, mask_ref, fill_ref, prior_ref, inv_ref, *refs):
    *parts, _, out_ref, map_ref = refs
    odd = (lax.axis_index("row") & 1) == 1
    for p in range(out_ref.shape[0]):
        part = parts[0][p] if len(parts) == 1 else jnp.where(odd, parts[1][p], parts[0][p])
        map_ref[...] = triangular_mm(kept_block(mask_ref, p, owners, part), inv_ref[p])
        rest, _ = order_of(chosen_of(p, fill_ref, prior_ref), map_ref.shape[1] // BLOCK)
        for t in range(len(rest) // 2):
            out_ref[p, :, t * LANES : (t + 1) * LANES] = two_blocks(
                tile_of(map_ref), rest[2 * t], rest[2 * t + 1]
            )


def segment_kernel(plan, panels, late_ref, early_ref, *refs):
    base_refs, (links_t_ref, whole_ref) = refs[:panels], refs[panels:]
    size = links_t_ref.shape[1]
    rows = late_ref.shape[1]
    here = lax.broadcasted_iota(jnp.int32, (size, size), 1) // rows == at_row(plan.late)
    cov = link_t = None
    for p in range(panels - 1, -1, -1):
        late_t = jnp.concatenate([late_ref[p]] * (size // rows), 0).T
        own_t = jnp.where(here, late_t, early_ref[p])
        links_t_ref[p] = own_t
        if cov is None:
            cov, link_t = base_refs[p][...], own_t
        else:
            own_t = split(own_t)
            cov = carry(own_t, cov, base_refs[p][...])
            link_t = mm(own_t, link_t)
    whole_ref[:size] = link_t
    whole_ref[size:] = cov


def maps_kernel(plan, mask_ref, inv_ref, *refs):
    *parts, maps_ref, token_ref, rows_ref = refs
    token_ref[...] = jnp.zeros_like(token_ref)
    rows_ref[...] = jnp.zeros_like(rows_ref)
    for p in range(inv_ref.shape[0]):
        for owners, part in zip(plan.early, parts):
            put_rows(mask_ref, p, owners, part[p], rows_ref, lambda kept: kept)
        maps_ref[p] = triangular_mm(rows_ref[...], inv_ref[p])


def chip_kernel(own_ref, other_ref, link_t_ref, cov_ref, packed_ref, half_t_ref):
    size = cov_ref.shape[0]
    lower = is_lower()
    own_t, other_t = own_ref[:size, :], other_ref[:size, :]
    own, other = own_ref[size:, :], other_ref[size:, :]
    down_t = split(jnp.where(lower, own_t, other_t))
    cov = carry(down_t, jnp.where(lower, other, own), jnp.where(lower, own, other))
    link_t = mm(down_t, jnp.where(lower, other_t, own_t))
    link_t_ref[...] = link_t
    cov_ref[...] = cov
    packed_ref[...] = own_half(pack(cov))
    half_t_ref[...] = own_half(link_t)


def merge_kernel(level, link_t_ref, cov_ref, *refs):
    got_t = from_halves(refs[0][...], refs[1][...])
    got = unpack(from_halves(refs[2][...], refs[3][...]))
    own_t, own = link_t_ref[...], cov_ref[...]
    lower = (lax.shift_right_logical(lax.axis_index("seg") // 2, level) & 1) == 0
    down_t = split(jnp.where(lower, own_t, got_t))
    cov = carry(down_t, jnp.where(lower, got, own), jnp.where(lower, own, got))
    refs[4][...] = own_half(pack(cov))
    if len(refs) > 5:
        link_t = mm(down_t, jnp.where(lower, got_t, own_t))
        refs[5][...] = own_half(link_t)
        refs[6][...] = link_t
        refs[7][...] = cov


def join_kernel(level, *refs):
    past_t, past, link_t, cov = (
        from_halves(refs[2 * i][...], refs[2 * i + 1][...]) for i in range(4)
    )
    chip = lax.axis_index("seg") // 2
    below = (lax.shift_right_logical(chip, level) & 1) == 0
    known = (chip & ((1 << level) - 1)) != (1 << level) - 1
    past_parts = split(past_t)
    joined = pack(carry(past_parts, unpack(cov), unpack(past)))
    joined_t = mm(past_parts, link_t)
    out_t = jnp.where(below, jnp.where(known, joined_t, link_t), past_t)
    out = jnp.where(below, jnp.where(known, joined, cov), past)
    for i, whole in enumerate((out_t, out)):
        half = whole.shape[0] // 2
        refs[8 + 2 * i][...] = own_half(whole)
        refs[9 + 2 * i][...] = jnp.where(is_lower(), whole[half:], whole[:half])


def prepare_kernel(plan, levels, panels, mask_ref, fill_ref, prior_ref, *refs):
    base_refs, own_refs, refs = refs[:panels], refs[panels : 2 * panels], refs[2 * panels :]
    (other_ref, maps_ref, links_t_ref, late_ref, rest_ref), refs = refs[:5], refs[5:]
    past_refs, refs = refs[: 4 * (levels > 1)], refs[4 * (levels > 1) :]
    left_high, left_low, right_high, right_low, const_ref, token_ref, scratch, map_ref, late_map_ref = refs
    token_ref[...] = jnp.zeros_like(token_ref)
    own_cols, width = own_refs[0].shape
    late_at = at_row(plan.late)
    size = base_refs[0].shape[0]
    row_at = lax.axis_index("row")
    rows = left_high.shape[0] // panels - own_cols
    row = lax.broadcasted_iota(jnp.int32, (size, size), 0)
    column = lax.broadcasted_iota(jnp.int32, (size, size), 1)
    eye = (row == column).astype(F32)
    other = other_ref[size:, :]
    lower = is_lower()
    if past_refs:
        chip = lax.axis_index("seg") // 2
        low = (1 << (levels - 1)) - 1
        known = (chip & low) != low
        past_t = from_halves(past_refs[0][...], past_refs[1][...])
        past = unpack(from_halves(past_refs[2][...], past_refs[3][...]))
        to_t = jnp.where(known, past_t, eye)
        gain = jnp.where(known, past, 0.0)
        other_t = split(other_ref[:size, :])
        to_t = jnp.where(lower, mm(other_t, to_t), to_t)
        gain = jnp.where(lower, carry(other_t, gain, other), gain)
    else:
        to_t = jnp.where(lower, other_ref[:size, :], eye)
        gain = jnp.where(lower, other, 0.0)
    own_at = pl.ds(pl.multiple_of(row_at * own_cols, own_cols), own_cols)
    own_rows = pl.ds(pl.multiple_of(row_at * rows, rows), rows)
    late_rows = pl.ds(pl.multiple_of(late_at * rows, rows), rows)
    for p in range(panels - 1, -1, -1):
        late_map_ref[:, :size] = late_ref[p]
        late_map_ref[:, size:] = rest_ref[p]
        _, place = order_of(chosen_of(p, fill_ref, prior_ref), width // BLOCK)
        map_ref[...] = maps_ref[p]
        for t in range(len(place) // 2):
            map_ref[late_rows, t * LANES : (t + 1) * LANES] = two_blocks(
                tile_of(late_map_ref), place[2 * t], place[2 * t + 1]
            )
        whole = split(map_ref[...])
        own_t = split(map_ref[:, own_at].T)
        scratch[:, :size] = to_t
        scratch[:, size:] = gain
        to_parts = split(to_t)
        cross = jnp.concatenate(
            [
                jnp.full((BLOCK, size), -mask_ref[p, slot].astype(F32))
                for slot in slots_of(tuple(range(size // rows)), rows)
            ],
            0,
        )
        left = jnp.concatenate([scratch[own_rows, :size] * cross, mm(own_t, to_parts)], 0)
        part = slice(p * left.shape[0], (p + 1) * left.shape[0])
        left_high[part, :], left_low[part, :] = split(left)
        right_high[p], right_low[p] = split(mm(to_parts, whole, TN))
        gains = jnp.concatenate([scratch[own_rows, size:] * cross, mm(own_t, gain)], 0)
        const = mm(gains, whole)
        const_ref[p, :rows, :] = const[:rows]
        const_ref[p, rows:, :] = const[rows:] + own_refs[p][...]
        if p > 0:
            link_t = split(links_t_ref[p])
            to_t = mm(link_t, to_t)
            gain = carry(link_t, gain, base_refs[p][...])


def finish_kernel(levels, after_ref, after_other_ref, *refs):
    left_high, left_low, right_high, right_low, const_ref, diag_hbm, off_hbm = refs[:7]
    diag_ref, off_ref, sems = refs[7:]
    panels, total, _ = const_ref.shape
    rows = off_ref.shape[1]
    chip = lax.axis_index("seg") // 2
    after = from_halves(after_ref[...], after_other_ref[...])
    after = unpack(jnp.where((chip & ((1 << levels) // 2)) == 0, after, 0.0))
    inner = split(mm((left_high[...], left_low[...]), after))
    copies = []
    for p in range(panels):
        part = slice(p * total, (p + 1) * total)
        right = (right_high[p], right_low[p])
        result = mm((inner[0][part], inner[1][part]), right) + const_ref[p]
        diag_ref[p] = result[rows:]
        off_ref[p] = result[:rows]
        copies.append(pltpu.make_async_copy(diag_ref.at[p], diag_hbm.at[p], sems.at[p, 0]))
        copies.append(pltpu.make_async_copy(off_ref.at[p], off_hbm.at[p], sems.at[p, 1]))
        copies[-2].start()
        copies[-1].start()
    for copy in copies:
        copy.wait()


def body(fill_blocks, fill_mask, inv_diag, factor_off):
    panels, width, _ = inv_diag.shape
    rows = factor_off.shape[1]
    seg_count = lax.axis_size("seg")
    row_count = lax.axis_size("row")
    size = rows * row_count
    own_cols = width // row_count
    slots = fill_blocks.shape[1]
    chosen_cols = slots * BLOCK
    chips = seg_count // 2
    half = size // 2

    def turn(x, axis, distance):
        count = lax.axis_size(axis)
        return lax.ppermute(x, axis, [(i, (i + distance) % count) for i in range(count)])

    prior_fill = turn(fill_blocks, "seg", 1)
    pick = jax.ShapeDtypeStruct((width, chosen_cols), BF16)
    bases, priors, picks, tokens = [], [], [], []
    for p in range(panels):
        base, own_prior, *high_low, token = call(
            functools.partial(prior_kernel, p),
            [shape(chosen_cols, chosen_cols), shape(own_cols, width), pick, pick, shape(1, 1, width)],
            [fill_blocks] if p else [fill_blocks, prior_fill],
            [],
            far=[inv_diag],
            scratch=[pltpu.VMEM((width, width), F32), pltpu.SemaphoreType.DMA],
            flops=6 * width * (chosen_cols * chosen_cols + own_cols * width),
            name="prior",
        )
        bases.append(base)
        priors.append(own_prior)
        picks += high_low
        tokens.append(token)
    short = row_count == 4
    ups, downs = [factor_off], [factor_off + tokens[-1]]
    for _ in range(row_count // 2 - short):
        ups.append(turn(ups[-1], "row", 1))
    for _ in range((row_count - 1) // 2):
        downs.append(turn(downs[-1], "row", -1))
    far = row_count // 2
    came = [d for d in range(row_count) if d != far]
    whose = [tuple((i - d) % row_count for i in range(row_count)) for d in range(row_count)]
    plan = Plan(tuple(whose[d] for d in came), whose[far])
    parts = ups[:far] + downs[:0:-1]
    index_gate = jnp.minimum(jnp.min(prior_fill), 0).astype(F32)
    (late,) = call(
        functools.partial(chosen_kernel, whose[1] if short else whose[far]),
        [shape(panels, rows, chosen_cols)],
        [fill_mask],
        [ups[-1] + index_gate, *picks],
        flops=6 * panels * rows * chosen_cols * width,
        name="chosen",
    )
    if short:
        late = turn(late, "row", 1)
    (links,) = call(
        functools.partial(links_kernel, plan),
        [shape(panels, size, size)],
        [fill_mask],
        [*parts, *picks],
        scratch=[pltpu.VMEM((size, chosen_cols), F32)],
        flops=6 * panels * size * size * width,
        name="links",
    )
    links_t, own_whole = call(
        functools.partial(segment_kernel, plan, panels),
        [shape(panels, size, size), shape(2 * size, size)],
        [],
        [late, links, *bases],
        flops=18 * (panels - 1) * size**3,
        name="segment",
    )
    maps, maps_token = call(
        functools.partial(maps_kernel, plan),
        [shape(panels, size, width), shape(1, half)],
        [fill_mask],
        [inv_diag, *parts],
        scratch=[pltpu.VMEM((size, width), F32)],
        flops=6 * panels * size * width * width,
        mib=24,
        name="maps",
    )
    swap = [(i, i ^ 1) for i in range(seg_count)]
    other_whole = lax.ppermute(own_whole, "seg", swap)
    half_packed = shape(5 * half // 4, half)
    half_link = shape(half, size)
    link_t, cov, send, send_t = call(
        chip_kernel,
        [shape(size, size), shape(size, size), half_packed, half_link],
        [],
        [own_whole, other_whole],
        flops=18 * size**3,
        name="chip",
    )
    held = [ups[-1], downs[-1]] if short else [ups[-1]]
    held_by = whose[far]
    if short:
        held_by = tuple(whose[-1][i] if i % 2 else whose[1][i] for i in range(row_count))
    (rest,) = call(
        functools.partial(rest_kernel, held_by),
        [shape(panels, rows, width - chosen_cols)],
        [fill_mask, fill_blocks, prior_fill],
        [inv_diag, *held, send],
        scratch=[pltpu.VMEM((rows, width), F32)],
        flops=6 * panels * rows * width * width,
        mib=24,
        name="rest",
    )
    if short:
        rest = lax.ppermute(rest, "row", [(i, i ^ 1) for i in range(row_count)])
    past = None
    after = (jnp.zeros(half_packed.shape, F32),) * 2
    levels = (chips - 1).bit_length()
    prepared = None

    def prepare():
        total = rows + own_cols
        left = jax.ShapeDtypeStruct((panels * total, size), BF16)
        right = jax.ShapeDtypeStruct((panels, size, width), BF16)
        return call(
            functools.partial(prepare_kernel, plan, levels, panels),
            [left, left, right, right, shape(panels, total, width), shape(1, half)],
            [fill_mask, fill_blocks, prior_fill],
            [*bases, *priors, other_whole, maps, links_t, late, rest, *(past or ())],
            scratch=[
                pltpu.VMEM((size, width), F32),
                pltpu.VMEM((size, width), F32),
                pltpu.VMEM((rows, width), F32),
            ],
            flops=6 * panels * size * (total * size + size * width + total * width + 3 * size * size),
            mib=24,
            name="prepare",
        )

    for level in range(levels):
        partner = [(i, i ^ (2 << level)) for i in range(seg_count)]
        got = lax.ppermute(send, "seg", partner)
        if level == levels - 1:
            *prepared, token = prepare()
            got = got + token
            after = (got, lax.ppermute(got, "seg", swap))
            break
        got_t = lax.ppermute(send_t, "seg", partner)
        if level == 0:
            got = got + maps_token
        got = (got_t, lax.ppermute(got_t, "seg", swap), got, lax.ppermute(got, "seg", swap))
        outs = [half_packed]
        if level < levels - 2:
            outs += [half_link, shape(size, size), shape(size, size)]
        send, *more = call(
            functools.partial(merge_kernel, level), outs, [], [link_t, cov, *got],
            flops=18 * size**3, name="merge",
        )
        if more:
            send_t, link_t, cov = more
        if past is None:
            past = got
        else:
            past = call(
                functools.partial(join_kernel, level),
                [half_link, half_link, half_packed, half_packed],
                [],
                [*past, *got],
                flops=18 * size**3,
                name="join",
            )
    if prepared is None:
        *prepared, _ = prepare()
    diag, off = call(
        functools.partial(finish_kernel, levels),
        [shape(panels, own_cols, width), shape(panels, rows, width)],
        [],
        [*after, *prepared],
        out_far=True,
        scratch=[
            pltpu.VMEM((panels, own_cols, width), F32),
            pltpu.VMEM((panels, rows, width), F32),
            pltpu.SemaphoreType.DMA((panels, 2)),
        ],
        flops=6 * panels * (rows + own_cols) * size * (size + width),
        name="finish",
    )
    return diag, off


def solution(mesh):
    placed = (P("seg", None), P("seg", None), P("seg", None, None), P("seg", "row", None))
    return jax.shard_map(
        body,
        mesh=mesh,
        in_specs=placed,
        out_specs=(P("seg", "row", None), P("seg", "row", None)),
        check_vma=False,
    )
```

```python
import functools
from typing import NamedTuple

import jax
import jax.numpy as jnp
from jax import lax
from jax.experimental import pallas as pl
from jax.experimental.pallas import tpu as pltpu
from jax.sharding import PartitionSpec as P

BLOCK = 64
LANES = 128
F32 = jnp.float32
BF16 = jnp.bfloat16
NN = (((1,), (0,)), ((), ()))
NT = (((1,), (1,)), ((), ()))
TN = (((0,), (0,)), ((), ()))


def split(x):
    high = x.astype(BF16)
    return high, (x - high.astype(F32)).astype(BF16)


def mm(a, b, dims=NN):
    a = a if isinstance(a, tuple) else split(a)
    b = b if isinstance(b, tuple) else split(b)
    dot = functools.partial(lax.dot_general, dimension_numbers=dims, preferred_element_type=F32)
    return dot(a[0], b[0]) + (dot(a[0], b[1]) + dot(a[1], b[0]))


def carry(link_t, cov, base):
    link_t = link_t if isinstance(link_t, tuple) else split(link_t)
    return mm(mm(link_t, cov), link_t, NT) + base


def pack(cov):
    half = cov.shape[0] // 2
    part = half // 2
    first, second = cov[:half, :half], cov[half:, half:]
    lane = lax.broadcasted_iota(jnp.int32, (part, half), 1)
    last = jnp.where(lane < part, pltpu.roll(first[part:], part, 1), second[part:])
    return jnp.concatenate([cov[:half, half:], first[:part], second[:part], last], 0)


def unpack(packed):
    half = packed.shape[1]
    part = half // 2
    cross, last = packed[:half], packed[2 * half :]
    row = lax.broadcasted_iota(jnp.int32, (half, half), 0)
    lane = lax.broadcasted_iota(jnp.int32, (half, half), 1)

    def symmetric(top, bottom):
        upper = jnp.concatenate([top, bottom], 0)
        return jnp.where((row < part) | (lane >= part), upper, upper.T)

    first = symmetric(packed[half : half + part], pltpu.roll(last, part, 1))
    second = symmetric(packed[half + part : 2 * half], last)
    top = jnp.concatenate([first, cross], 1)
    bottom = jnp.concatenate([cross.T, second], 1)
    return jnp.concatenate([top, bottom], 0)


def is_lower():
    return (lax.axis_index("seg") & 1) == 0


def from_halves(own, other):
    lower = is_lower()
    return jnp.concatenate([jnp.where(lower, own, other), jnp.where(lower, other, own)], 0)


def own_half(whole):
    half = whole.shape[0] // 2
    return jnp.where(is_lower(), whole[:half], whole[half:])


def two_blocks(load, left, right):
    def placed(block, half):
        slab = load(lax.shift_right_logical(block, 1))
        return jnp.where((block & 1) == half, slab, pltpu.roll(slab, BLOCK, 1))

    a, b = placed(left, 0), placed(right, 1)
    lane = lax.broadcasted_iota(jnp.int32, a.shape, 1)
    return jnp.where(lane < BLOCK, a, b)


def tile_of(ref, *lead):
    def load(tile):
        return ref[(*lead, slice(None), pl.ds(pl.multiple_of(tile * LANES, LANES), LANES))]

    return load


def chosen_of(panel, fill_ref, prior_ref=None):
    slots = fill_ref.shape[1]
    if panel > 0:
        return [fill_ref[panel - 1, j] for j in range(slots)]
    first = lax.axis_index("seg") == 0
    last = prior_ref.shape[0] - 1
    return [jnp.where(first, fill_ref[0, j], prior_ref[last, j]) for j in range(slots)]


def order_of(chosen, blocks):
    slots = len(chosen)
    rest = [jnp.int32(0)] * (blocks - slots)
    place = []
    seen = jnp.int32(0)
    for b in range(blocks):
        hit = jnp.int32(0)
        where = jnp.int32(0)
        for j in range(slots):
            same = (chosen[j] == b).astype(jnp.int32)
            hit = hit + same
            where = where + same * j
        free = 1 - hit
        for q in range(blocks - slots):
            rest[q] = rest[q] + jnp.where(seen == q, free * b, 0)
        place.append(jnp.where(hit > 0, where, slots + seen))
        seen = seen + free
    return rest, place


def vmem(count):
    return [pl.BlockSpec(memory_space=pltpu.VMEM)] * count


def smem(count):
    return [pl.BlockSpec(memory_space=pltpu.SMEM)] * count


def call(
    kernel, outs, scalars, arrays, far=(), out_far=False, through=(), scratch=(), flops=0, mib=16, name=None
):
    moved = sum(a.size * 4 for a in (*arrays, *far)) + sum(o.size * 4 for o in outs)
    first = len(scalars) + len(arrays) + len(far)
    count = len(through)

    def inner(*refs):
        kernel(*refs[:first], *refs[first + count : first + count + len(outs)], *refs[first + 2 * count + len(outs) :])

    return pl.pallas_call(
        inner,
        out_shape=[*outs, *(jax.ShapeDtypeStruct(a.shape, a.dtype) for a in through)],
        in_specs=smem(len(scalars))
        + vmem(len(arrays))
        + [pl.BlockSpec(memory_space=pltpu.HBM)] * len(far)
        + [pl.BlockSpec(memory_space=pl.ANY)] * count,
        out_specs=([pl.BlockSpec(memory_space=pltpu.HBM)] * len(outs) if out_far else vmem(len(outs)))
        + [pl.BlockSpec(memory_space=pl.ANY)] * count,
        scratch_shapes=list(scratch),
        input_output_aliases={first + i: len(outs) + i for i in range(count)},
        cost_estimate=pl.CostEstimate(flops=flops, bytes_accessed=moved, transcendentals=0),
        compiler_params=pltpu.CompilerParams(vmem_limit_bytes=mib << 20),
        name=name,
    )(*scalars, *arrays, *(pltpu.with_memory_space_constraint(a, pltpu.HBM) for a in far), *through)


def shape(*dims):
    return jax.ShapeDtypeStruct(dims, F32)


def kept_rows(mask_ref, panel, slot, rows):
    alive = lax.axis_index("seg") * mask_ref.shape[0] + panel < (
        lax.axis_size("seg") * mask_ref.shape[0] - 1
    )
    return rows * (mask_ref[panel, slot].astype(F32) * alive.astype(F32))


def triangular_mm(left, lower):
    cut = left.shape[1] // 2
    first, second = split(left[:, :cut]), split(left[:, cut:])
    below = split(lower[cut:, :])
    return jnp.concatenate(
        [
            mm(second, (below[0][:, :cut], below[1][:, :cut])) + mm(first, lower[:cut, :cut]),
            mm(second, (below[0][:, cut:], below[1][:, cut:])),
        ],
        1,
    )


def prior_kernel(panel, *refs):
    *scalar_refs, inv_hbm, base_ref, own_ref, pick_high_ref, pick_low_ref, token_ref = refs[:-2]
    inv_ref, sem = refs[-2:]
    copy = pltpu.make_async_copy(inv_hbm.at[panel], inv_ref, sem)
    copy.start()
    token_ref[...] = jnp.zeros_like(token_ref)
    chosen = chosen_of(panel, *scalar_refs)
    own_cols = own_ref.shape[0]
    own_at = pl.ds(pl.multiple_of(lax.axis_index("row") * own_cols, own_cols), own_cols)
    copy.wait()
    picked = split(
        jnp.concatenate(
            [
                two_blocks(tile_of(inv_ref), chosen[2 * t], chosen[2 * t + 1])
                for t in range(len(chosen) // 2)
            ],
            1,
        )
    )
    pick_high_ref[...], pick_low_ref[...] = picked
    base_ref[...] = mm(picked, picked, TN)
    own_ref[...] = mm(inv_ref[:, own_at], inv_ref[...], TN)


class Plan(NamedTuple):
    early: tuple
    late: tuple


def at_row(table):
    value = jnp.int32(table[0])
    for i, entry in enumerate(table[1:], 1):
        value = jnp.where(lax.axis_index("row") == i, entry, value)
    return value


def slots_of(owners, rows):
    first = at_row(owners) * (rows // BLOCK)
    return [first + s for s in range(rows // BLOCK)]


def put_rows(mask_ref, panel, owners, part, out_ref, take):
    for s, slot in enumerate(slots_of(owners, part.shape[0])):
        kept = kept_rows(mask_ref, panel, slot, part[s * BLOCK : (s + 1) * BLOCK, :])
        out_ref[pl.ds(pl.multiple_of(slot * BLOCK, BLOCK), BLOCK), :] = take(kept)


def links_kernel(plan, mask_ref, *refs):
    parts, refs = refs[: len(plan.early)], refs[len(plan.early) :]
    *pick_refs, links_t_ref, rows_ref = refs
    rows_ref[...] = jnp.zeros_like(rows_ref)
    for p in range(links_t_ref.shape[0]):
        pick = (pick_refs[2 * p][...], pick_refs[2 * p + 1][...])
        for owners, part in zip(plan.early, parts):
            put_rows(mask_ref, p, owners, part[p], rows_ref, lambda kept: mm(kept, pick))
        links_t_ref[p] = rows_ref[...].T


def kept_block(mask_ref, panel, owners, part):
    return jnp.concatenate(
        [
            kept_rows(mask_ref, panel, slot, part[s * BLOCK : (s + 1) * BLOCK, :])
            for s, slot in enumerate(slots_of(owners, part.shape[0]))
        ],
        0,
    )


def chosen_kernel(owners, mask_ref, part, *refs):
    *pick_refs, out_ref = refs
    for p in range(out_ref.shape[0]):
        pick = (pick_refs[2 * p][...], pick_refs[2 * p + 1][...])
        out_ref[p] = mm(kept_block(mask_ref, p, owners, part[p]), pick)


def rest_kernel(owners, mask_ref, fill_ref, prior_ref, inv_ref, *refs):
    *parts, _, out_ref, map_ref = refs
    odd = (lax.axis_index("row") & 1) == 1
    for p in range(out_ref.shape[0]):
        part = parts[0][p] if len(parts) == 1 else jnp.where(odd, parts[1][p], parts[0][p])
        map_ref[...] = triangular_mm(kept_block(mask_ref, p, owners, part), inv_ref[p])
        rest, _ = order_of(chosen_of(p, fill_ref, prior_ref), map_ref.shape[1] // BLOCK)
        for t in range(len(rest) // 2):
            out_ref[p, :, t * LANES : (t + 1) * LANES] = two_blocks(
                tile_of(map_ref), rest[2 * t], rest[2 * t + 1]
            )


def segment_kernel(plan, panels, late_ref, early_ref, *refs):
    base_refs, (links_t_ref, whole_ref) = refs[:panels], refs[panels:]
    size = links_t_ref.shape[1]
    rows = late_ref.shape[1]
    here = lax.broadcasted_iota(jnp.int32, (size, size), 1) // rows == at_row(plan.late)
    cov = link_t = None
    for p in range(panels - 1, -1, -1):
        late_t = jnp.concatenate([late_ref[p]] * (size // rows), 0).T
        own_t = jnp.where(here, late_t, early_ref[p])
        links_t_ref[p] = own_t
        if cov is None:
            cov, link_t = base_refs[p][...], own_t
        else:
            own_t = split(own_t)
            cov = carry(own_t, cov, base_refs[p][...])
            link_t = mm(own_t, link_t)
    whole_ref[:size] = link_t
    whole_ref[size:] = cov


def maps_kernel(plan, mask_ref, inv_ref, *refs):
    *parts, maps_ref, token_ref, rows_ref = refs
    token_ref[...] = jnp.zeros_like(token_ref)
    rows_ref[...] = jnp.zeros_like(rows_ref)
    for p in range(inv_ref.shape[0]):
        for owners, part in zip(plan.early, parts):
            put_rows(mask_ref, p, owners, part[p], rows_ref, lambda kept: kept)
        maps_ref[p] = triangular_mm(rows_ref[...], inv_ref[p])


def chip_kernel(own_ref, other_ref, link_t_ref, cov_ref, packed_ref, half_t_ref):
    size = cov_ref.shape[0]
    lower = is_lower()
    own_t, other_t = own_ref[:size, :], other_ref[:size, :]
    own, other = own_ref[size:, :], other_ref[size:, :]
    down_t = split(jnp.where(lower, own_t, other_t))
    cov = carry(down_t, jnp.where(lower, other, own), jnp.where(lower, own, other))
    link_t = mm(down_t, jnp.where(lower, other_t, own_t))
    link_t_ref[...] = link_t
    cov_ref[...] = cov
    packed_ref[...] = own_half(pack(cov))
    half_t_ref[...] = own_half(link_t)


def merge_kernel(level, link_t_ref, cov_ref, *refs):
    got_t = from_halves(refs[0][...], refs[1][...])
    got = unpack(from_halves(refs[2][...], refs[3][...]))
    own_t, own = link_t_ref[...], cov_ref[...]
    lower = (lax.shift_right_logical(lax.axis_index("seg") // 2, level) & 1) == 0
    down_t = split(jnp.where(lower, own_t, got_t))
    cov = carry(down_t, jnp.where(lower, got, own), jnp.where(lower, own, got))
    refs[4][...] = own_half(pack(cov))
    if len(refs) > 5:
        link_t = mm(down_t, jnp.where(lower, got_t, own_t))
        refs[5][...] = own_half(link_t)
        refs[6][...] = link_t
        refs[7][...] = cov


def join_kernel(level, *refs):
    past_t, past, link_t, cov = (
        from_halves(refs[2 * i][...], refs[2 * i + 1][...]) for i in range(4)
    )
    chip = lax.axis_index("seg") // 2
    below = (lax.shift_right_logical(chip, level) & 1) == 0
    known = (chip & ((1 << level) - 1)) != (1 << level) - 1
    past_parts = split(past_t)
    joined = pack(carry(past_parts, unpack(cov), unpack(past)))
    joined_t = mm(past_parts, link_t)
    out_t = jnp.where(below, jnp.where(known, joined_t, link_t), past_t)
    out = jnp.where(below, jnp.where(known, joined, cov), past)
    for i, whole in enumerate((out_t, out)):
        half = whole.shape[0] // 2
        refs[8 + 2 * i][...] = own_half(whole)
        refs[9 + 2 * i][...] = jnp.where(is_lower(), whole[half:], whole[:half])


def prepare_kernel(plan, levels, panels, mask_ref, fill_ref, prior_ref, *refs):
    base_refs, own_refs, refs = refs[:panels], refs[panels : 2 * panels], refs[2 * panels :]
    (other_ref, maps_ref, links_t_ref, late_ref, rest_ref), refs = refs[:5], refs[5:]
    past_refs, refs = refs[: 4 * (levels > 1)], refs[4 * (levels > 1) :]
    left_high, left_low, right_high, right_low, const_ref, token_ref, scratch, map_ref, late_map_ref = refs
    token_ref[...] = jnp.zeros_like(token_ref)
    own_cols, width = own_refs[0].shape
    late_at = at_row(plan.late)
    size = base_refs[0].shape[0]
    row_at = lax.axis_index("row")
    rows = left_high.shape[0] // panels - own_cols
    row = lax.broadcasted_iota(jnp.int32, (size, size), 0)
    column = lax.broadcasted_iota(jnp.int32, (size, size), 1)
    eye = (row == column).astype(F32)
    other = other_ref[size:, :]
    lower = is_lower()
    if past_refs:
        chip = lax.axis_index("seg") // 2
        low = (1 << (levels - 1)) - 1
        known = (chip & low) != low
        past_t = from_halves(past_refs[0][...], past_refs[1][...])
        past = unpack(from_halves(past_refs[2][...], past_refs[3][...]))
        to_t = jnp.where(known, past_t, eye)
        gain = jnp.where(known, past, 0.0)
        other_t = split(other_ref[:size, :])
        to_t = jnp.where(lower, mm(other_t, to_t), to_t)
        gain = jnp.where(lower, carry(other_t, gain, other), gain)
    else:
        to_t = jnp.where(lower, other_ref[:size, :], eye)
        gain = jnp.where(lower, other, 0.0)
    own_at = pl.ds(pl.multiple_of(row_at * own_cols, own_cols), own_cols)
    own_rows = pl.ds(pl.multiple_of(row_at * rows, rows), rows)
    late_rows = pl.ds(pl.multiple_of(late_at * rows, rows), rows)
    for p in range(panels - 1, -1, -1):
        late_map_ref[:, :size] = late_ref[p]
        late_map_ref[:, size:] = rest_ref[p]
        _, place = order_of(chosen_of(p, fill_ref, prior_ref), width // BLOCK)
        map_ref[...] = maps_ref[p]
        for t in range(len(place) // 2):
            map_ref[late_rows, t * LANES : (t + 1) * LANES] = two_blocks(
                tile_of(late_map_ref), place[2 * t], place[2 * t + 1]
            )
        whole = split(map_ref[...])
        own_t = split(map_ref[:, own_at].T)
        scratch[:, :size] = to_t
        scratch[:, size:] = gain
        to_parts = split(to_t)
        cross = jnp.concatenate(
            [
                jnp.full((BLOCK, size), -mask_ref[p, slot].astype(F32))
                for slot in slots_of(tuple(range(size // rows)), rows)
            ],
            0,
        )
        left = jnp.concatenate([scratch[own_rows, :size] * cross, mm(own_t, to_parts)], 0)
        part = slice(p * left.shape[0], (p + 1) * left.shape[0])
        left_high[part, :], left_low[part, :] = split(left)
        right_high[p], right_low[p] = split(mm(to_parts, whole, TN))
        gains = jnp.concatenate([scratch[own_rows, size:] * cross, mm(own_t, gain)], 0)
        const = mm(gains, whole)
        const_ref[p, :rows, :] = const[:rows]
        const_ref[p, rows:, :] = const[rows:] + own_refs[p][...]
        if p > 0:
            link_t = split(links_t_ref[p])
            to_t = mm(link_t, to_t)
            gain = carry(link_t, gain, base_refs[p][...])


def finish_kernel(levels, after_ref, after_other_ref, *refs):
    left_high, left_low, right_high, right_low, const_ref, diag_hbm, off_hbm = refs[:7]
    diag_ref, off_ref, sems = refs[7:]
    panels, total, _ = const_ref.shape
    rows = off_ref.shape[1]
    chip = lax.axis_index("seg") // 2
    after = from_halves(after_ref[...], after_other_ref[...])
    after = unpack(jnp.where((chip & ((1 << levels) // 2)) == 0, after, 0.0))
    inner = split(mm((left_high[...], left_low[...]), after))
    copies = []
    for p in range(panels):
        part = slice(p * total, (p + 1) * total)
        right = (right_high[p], right_low[p])
        result = mm((inner[0][part], inner[1][part]), right) + const_ref[p]
        diag_ref[p] = result[rows:]
        off_ref[p] = result[:rows]
        copies.append(pltpu.make_async_copy(diag_ref.at[p], diag_hbm.at[p], sems.at[p, 0]))
        copies.append(pltpu.make_async_copy(off_ref.at[p], off_hbm.at[p], sems.at[p, 1]))
        copies[-2].start()
        copies[-1].start()
    for copy in copies:
        copy.wait()


def body(fill_blocks, fill_mask, inv_diag, factor_off):
    panels, width, _ = inv_diag.shape
    rows = factor_off.shape[1]
    seg_count = lax.axis_size("seg")
    row_count = lax.axis_size("row")
    size = rows * row_count
    own_cols = width // row_count
    slots = fill_blocks.shape[1]
    chosen_cols = slots * BLOCK
    chips = seg_count // 2
    half = size // 2

    def turn(x, axis, distance):
        count = lax.axis_size(axis)
        return lax.ppermute(x, axis, [(i, (i + distance) % count) for i in range(count)])

    prior_fill = turn(fill_blocks, "seg", 1)
    pick = jax.ShapeDtypeStruct((width, chosen_cols), BF16)
    bases, priors, picks, tokens = [], [], [], []
    for p in range(panels):
        base, own_prior, *high_low, token = call(
            functools.partial(prior_kernel, p),
            [shape(chosen_cols, chosen_cols), shape(own_cols, width), pick, pick, shape(1, 1, width)],
            [fill_blocks] if p else [fill_blocks, prior_fill],
            [],
            far=[inv_diag],
            scratch=[pltpu.VMEM((width, width), F32), pltpu.SemaphoreType.DMA],
            name="prior",
        )
        bases.append(base)
        priors.append(own_prior)
        picks += high_low
        tokens.append(token)
    short = row_count == 4
    ups, downs = [factor_off], [factor_off + tokens[-1]]
    for _ in range(row_count // 2 - short):
        ups.append(turn(ups[-1], "row", 1))
    for _ in range((row_count - 1) // 2):
        downs.append(turn(downs[-1], "row", -1))
    far = row_count // 2
    came = [d for d in range(row_count) if d != far]
    whose = [tuple((i - d) % row_count for i in range(row_count)) for d in range(row_count)]
    plan = Plan(tuple(whose[d] for d in came), whose[far])
    parts = ups[:far] + downs[:0:-1]
    index_gate = jnp.minimum(jnp.min(prior_fill), 0).astype(F32)
    (late,) = call(
        functools.partial(chosen_kernel, whose[1] if short else whose[far]),
        [shape(panels, rows, chosen_cols)],
        [fill_mask],
        [ups[-1] + index_gate, *picks],
        flops=6 * panels * rows * chosen_cols * width,
        name="chosen",
    )
    if short:
        late = turn(late, "row", 1)
    (links,) = call(
        functools.partial(links_kernel, plan),
        [shape(panels, size, size)],
        [fill_mask],
        [*parts, *picks],
        scratch=[pltpu.VMEM((size, chosen_cols), F32)],
        flops=6 * panels * size * size * width,
        name="links",
    )
    links_t, own_whole = call(
        functools.partial(segment_kernel, plan, panels),
        [shape(panels, size, size), shape(2 * size, size)],
        [],
        [late, links, *bases],
        flops=18 * (panels - 1) * size**3,
        name="segment",
    )
    maps, maps_token = call(
        functools.partial(maps_kernel, plan),
        [shape(panels, size, width), shape(1, half)],
        [fill_mask],
        [inv_diag, *parts],
        scratch=[pltpu.VMEM((size, width), F32)],
        flops=6 * panels * size * width * width,
        mib=24,
        name="maps",
    )
    swap = [(i, i ^ 1) for i in range(seg_count)]
    other_whole = lax.ppermute(own_whole, "seg", swap)
    half_packed = shape(5 * half // 4, half)
    half_link = shape(half, size)
    link_t, cov, send, send_t = call(
        chip_kernel,
        [shape(size, size), shape(size, size), half_packed, half_link],
        [],
        [own_whole, other_whole],
        flops=18 * size**3,
        name="chip",
    )
    held = [ups[-1], downs[-1]] if short else [ups[-1]]
    held_by = whose[far]
    if short:
        held_by = tuple(whose[-1][i] if i % 2 else whose[1][i] for i in range(row_count))
    (rest,) = call(
        functools.partial(rest_kernel, held_by),
        [shape(panels, rows, width - chosen_cols)],
        [fill_mask, fill_blocks, prior_fill],
        [inv_diag, *held, send],
        scratch=[pltpu.VMEM((rows, width), F32)],
        flops=6 * panels * rows * width * width,
        mib=24,
        name="rest",
    )
    if short:
        rest = lax.ppermute(rest, "row", [(i, i ^ 1) for i in range(row_count)])
    past = None
    after = (jnp.zeros(half_packed.shape, F32),) * 2
    levels = (chips - 1).bit_length()
    prepared = None

    def prepare():
        total = rows + own_cols
        left = jax.ShapeDtypeStruct((panels * total, size), BF16)
        right = jax.ShapeDtypeStruct((panels, size, width), BF16)
        return call(
            functools.partial(prepare_kernel, plan, levels, panels),
            [left, left, right, right, shape(panels, total, width), shape(1, half)],
            [fill_mask, fill_blocks, prior_fill],
            [*bases, *priors, other_whole, maps, links_t, late, rest, *(past or ())],
            scratch=[
                pltpu.VMEM((size, width), F32),
                pltpu.VMEM((size, width), F32),
                pltpu.VMEM((rows, width), F32),
            ],
            flops=6 * panels * size * (total * size + size * width + total * width + 3 * size * size),
            mib=24,
            name="prepare",
        )

    for level in range(levels):
        partner = [(i, i ^ (2 << level)) for i in range(seg_count)]
        got = lax.ppermute(send, "seg", partner)
        if level == levels - 1:
            *prepared, token = prepare()
            got = got + token
            after = (got, lax.ppermute(got, "seg", swap))
            break
        got_t = lax.ppermute(send_t, "seg", partner)
        if level == 0:
            got = got + maps_token
        got = (got_t, lax.ppermute(got_t, "seg", swap), got, lax.ppermute(got, "seg", swap))
        outs = [half_packed]
        if level < levels - 2:
            outs += [half_link, shape(size, size), shape(size, size)]
        send, *more = call(
            functools.partial(merge_kernel, level), outs, [], [link_t, cov, *got],
            flops=18 * size**3, name="merge",
        )
        if more:
            send_t, link_t, cov = more
        if past is None:
            past = got
        else:
            past = call(
                functools.partial(join_kernel, level),
                [half_link, half_link, half_packed, half_packed],
                [],
                [*past, *got],
                flops=18 * size**3,
                name="join",
            )
    if prepared is None:
        *prepared, _ = prepare()
    diag, off = call(
        functools.partial(finish_kernel, levels),
        [shape(panels, own_cols, width), shape(panels, rows, width)],
        [],
        [*after, *prepared],
        out_far=True,
        scratch=[
            pltpu.VMEM((panels, own_cols, width), F32),
            pltpu.VMEM((panels, rows, width), F32),
            pltpu.SemaphoreType.DMA((panels, 2)),
        ],
        flops=6 * panels * (rows + own_cols) * size * (size + width),
        name="finish",
    )
    return diag, off


def solution(mesh):
    placed = (P("seg", None), P("seg", None), P("seg", None, None), P("seg", "row", None))
    return jax.shard_map(
        body,
        mesh=mesh,
        in_specs=placed,
        out_specs=(P("seg", "row", None), P("seg", "row", None)),
        check_vma=False,
    )
```

```python
import functools
from typing import NamedTuple

import jax
import jax.numpy as jnp
from jax import lax
from jax.experimental import pallas as pl
from jax.experimental.pallas import tpu as pltpu
from jax.sharding import PartitionSpec as P

BLOCK = 64
LANES = 128
F32 = jnp.float32
BF16 = jnp.bfloat16
NN = (((1,), (0,)), ((), ()))
NT = (((1,), (1,)), ((), ()))
TN = (((0,), (0,)), ((), ()))


def split(x):
    high = x.astype(BF16)
    return high, (x - high.astype(F32)).astype(BF16)


def mm(a, b, dims=NN):
    a = a if isinstance(a, tuple) else split(a)
    b = b if isinstance(b, tuple) else split(b)
    dot = functools.partial(lax.dot_general, dimension_numbers=dims, preferred_element_type=F32)
    return dot(a[0], b[0]) + (dot(a[0], b[1]) + dot(a[1], b[0]))


def carry(link_t, cov, base):
    link_t = link_t if isinstance(link_t, tuple) else split(link_t)
    return mm(mm(link_t, cov), link_t, NT) + base


def pack(cov):
    half = cov.shape[0] // 2
    part = half // 2
    first, second = cov[:half, :half], cov[half:, half:]
    lane = lax.broadcasted_iota(jnp.int32, (part, half), 1)
    last = jnp.where(lane < part, pltpu.roll(first[part:], part, 1), second[part:])
    return jnp.concatenate([cov[:half, half:], first[:part], second[:part], last], 0)


def unpack(packed):
    half = packed.shape[1]
    part = half // 2
    cross, last = packed[:half], packed[2 * half :]
    row = lax.broadcasted_iota(jnp.int32, (half, half), 0)
    lane = lax.broadcasted_iota(jnp.int32, (half, half), 1)

    def symmetric(top, bottom):
        upper = jnp.concatenate([top, bottom], 0)
        return jnp.where((row < part) | (lane >= part), upper, upper.T)

    first = symmetric(packed[half : half + part], pltpu.roll(last, part, 1))
    second = symmetric(packed[half + part : 2 * half], last)
    top = jnp.concatenate([first, cross], 1)
    bottom = jnp.concatenate([cross.T, second], 1)
    return jnp.concatenate([top, bottom], 0)


def is_lower():
    return (lax.axis_index("seg") & 1) == 0


def from_halves(own, other):
    lower = is_lower()
    return jnp.concatenate([jnp.where(lower, own, other), jnp.where(lower, other, own)], 0)


def own_half(whole):
    half = whole.shape[0] // 2
    return jnp.where(is_lower(), whole[:half], whole[half:])


def two_blocks(load, left, right):
    def placed(block, half):
        slab = load(lax.shift_right_logical(block, 1))
        return jnp.where((block & 1) == half, slab, pltpu.roll(slab, BLOCK, 1))

    a, b = placed(left, 0), placed(right, 1)
    lane = lax.broadcasted_iota(jnp.int32, a.shape, 1)
    return jnp.where(lane < BLOCK, a, b)


def tile_of(ref, *lead):
    def load(tile):
        return ref[(*lead, slice(None), pl.ds(pl.multiple_of(tile * LANES, LANES), LANES))]

    return load


def chosen_of(panel, fill_ref, prior_ref=None):
    slots = fill_ref.shape[1]
    if panel > 0:
        return [fill_ref[panel - 1, j] for j in range(slots)]
    first = lax.axis_index("seg") == 0
    last = prior_ref.shape[0] - 1
    return [jnp.where(first, fill_ref[0, j], prior_ref[last, j]) for j in range(slots)]


def order_of(chosen, blocks):
    slots = len(chosen)
    rest = [jnp.int32(0)] * (blocks - slots)
    place = []
    seen = jnp.int32(0)
    for b in range(blocks):
        hit = jnp.int32(0)
        where = jnp.int32(0)
        for j in range(slots):
            same = (chosen[j] == b).astype(jnp.int32)
            hit = hit + same
            where = where + same * j
        free = 1 - hit
        for q in range(blocks - slots):
            rest[q] = rest[q] + jnp.where(seen == q, free * b, 0)
        place.append(jnp.where(hit > 0, where, slots + seen))
        seen = seen + free
    return rest, place


def vmem(count):
    return [pl.BlockSpec(memory_space=pltpu.VMEM)] * count


def smem(count):
    return [pl.BlockSpec(memory_space=pltpu.SMEM)] * count


def call(
    kernel, outs, scalars, arrays, far=(), out_far=False, through=(), scratch=(), flops=0, mib=16, name=None
):
    moved = sum(a.size * 4 for a in (*arrays, *far)) + sum(o.size * 4 for o in outs)
    first = len(scalars) + len(arrays) + len(far)
    count = len(through)

    def inner(*refs):
        kernel(*refs[:first], *refs[first + count : first + count + len(outs)], *refs[first + 2 * count + len(outs) :])

    return pl.pallas_call(
        inner,
        out_shape=[*outs, *(jax.ShapeDtypeStruct(a.shape, a.dtype) for a in through)],
        in_specs=smem(len(scalars))
        + vmem(len(arrays))
        + [pl.BlockSpec(memory_space=pltpu.HBM)] * len(far)
        + [pl.BlockSpec(memory_space=pl.ANY)] * count,
        out_specs=([pl.BlockSpec(memory_space=pltpu.HBM)] * len(outs) if out_far else vmem(len(outs)))
        + [pl.BlockSpec(memory_space=pl.ANY)] * count,
        scratch_shapes=list(scratch),
        input_output_aliases={first + i: len(outs) + i for i in range(count)},
        cost_estimate=pl.CostEstimate(flops=flops, bytes_accessed=moved, transcendentals=0),
        compiler_params=pltpu.CompilerParams(vmem_limit_bytes=mib << 20),
        name=name,
    )(*scalars, *arrays, *(pltpu.with_memory_space_constraint(a, pltpu.HBM) for a in far), *through)


def shape(*dims):
    return jax.ShapeDtypeStruct(dims, F32)


def kept_rows(mask_ref, panel, slot, rows):
    alive = lax.axis_index("seg") * mask_ref.shape[0] + panel < (
        lax.axis_size("seg") * mask_ref.shape[0] - 1
    )
    return rows * (mask_ref[panel, slot].astype(F32) * alive.astype(F32))


def triangular_mm(left, lower):
    cut = left.shape[1] // 2
    first, second = split(left[:, :cut]), split(left[:, cut:])
    below = split(lower[cut:, :])
    return jnp.concatenate(
        [
            mm(second, (below[0][:, :cut], below[1][:, :cut])) + mm(first, lower[:cut, :cut]),
            mm(second, (below[0][:, cut:], below[1][:, cut:])),
        ],
        1,
    )


def pick_kernel(panel, *refs):
    *scalar_refs, inv_hbm, high_ref, low_ref, inv_ref, sem = refs
    copy = pltpu.make_async_copy(inv_hbm.at[panel], inv_ref, sem)
    copy.start()
    chosen = chosen_of(panel, *scalar_refs)
    copy.wait()
    for t in range(len(chosen) // 2):
        columns = slice(t * LANES, (t + 1) * LANES)
        high_ref[:, columns], low_ref[:, columns] = split(
            two_blocks(tile_of(inv_ref), chosen[2 * t], chosen[2 * t + 1])
        )


def prior_kernel(panel, high_ref, low_ref, inv_hbm, base_ref, own_ref, token_ref, inv_ref, sem):
    copy = pltpu.make_async_copy(inv_hbm.at[panel], inv_ref, sem)
    copy.start()
    token_ref[...] = jnp.zeros_like(token_ref)
    own_cols = own_ref.shape[0]
    own_at = pl.ds(pl.multiple_of(lax.axis_index("row") * own_cols, own_cols), own_cols)
    picked = (high_ref[...], low_ref[...])
    base_ref[...] = mm(picked, picked, TN)
    copy.wait()
    own_ref[...] = mm(inv_ref[:, own_at], inv_ref[...], TN)


class Plan(NamedTuple):
    early: tuple
    late: tuple


def at_row(table):
    value = jnp.int32(table[0])
    for i, entry in enumerate(table[1:], 1):
        value = jnp.where(lax.axis_index("row") == i, entry, value)
    return value


def slots_of(owners, rows):
    first = at_row(owners) * (rows // BLOCK)
    return [first + s for s in range(rows // BLOCK)]


def put_rows(mask_ref, panel, owners, part, out_ref, take):
    for s, slot in enumerate(slots_of(owners, part.shape[0])):
        kept = kept_rows(mask_ref, panel, slot, part[s * BLOCK : (s + 1) * BLOCK, :])
        out_ref[pl.ds(pl.multiple_of(slot * BLOCK, BLOCK), BLOCK), :] = take(kept)


def links_kernel(plan, mask_ref, *refs):
    parts, refs = refs[: len(plan.early)], refs[len(plan.early) :]
    *pick_refs, links_t_ref, rows_ref = refs
    rows_ref[...] = jnp.zeros_like(rows_ref)
    for p in range(links_t_ref.shape[0]):
        pick = (pick_refs[2 * p][...], pick_refs[2 * p + 1][...])
        for owners, part in zip(plan.early, parts):
            put_rows(mask_ref, p, owners, part[p], rows_ref, lambda kept: mm(kept, pick))
        links_t_ref[p] = rows_ref[...].T


def kept_block(mask_ref, panel, owners, part):
    return jnp.concatenate(
        [
            kept_rows(mask_ref, panel, slot, part[s * BLOCK : (s + 1) * BLOCK, :])
            for s, slot in enumerate(slots_of(owners, part.shape[0]))
        ],
        0,
    )


def chosen_kernel(owners, mask_ref, part, *refs):
    *pick_refs, out_ref = refs
    for p in range(out_ref.shape[0]):
        pick = (pick_refs[2 * p][...], pick_refs[2 * p + 1][...])
        out_ref[p] = mm(kept_block(mask_ref, p, owners, part[p]), pick)


def rest_kernel(owners, mask_ref, fill_ref, prior_ref, inv_ref, *refs):
    *parts, _, out_ref, map_ref = refs
    odd = (lax.axis_index("row") & 1) == 1
    for p in range(out_ref.shape[0]):
        part = parts[0][p] if len(parts) == 1 else jnp.where(odd, parts[1][p], parts[0][p])
        map_ref[...] = triangular_mm(kept_block(mask_ref, p, owners, part), inv_ref[p])
        rest, _ = order_of(chosen_of(p, fill_ref, prior_ref), map_ref.shape[1] // BLOCK)
        for t in range(len(rest) // 2):
            out_ref[p, :, t * LANES : (t + 1) * LANES] = two_blocks(
                tile_of(map_ref), rest[2 * t], rest[2 * t + 1]
            )


def segment_kernel(plan, panels, late_ref, early_ref, *refs):
    base_refs, (links_t_ref, whole_ref) = refs[:panels], refs[panels:]
    size = links_t_ref.shape[1]
    rows = late_ref.shape[1]
    here = lax.broadcasted_iota(jnp.int32, (size, size), 1) // rows == at_row(plan.late)
    cov = link_t = None
    for p in range(panels - 1, -1, -1):
        late_t = jnp.concatenate([late_ref[p]] * (size // rows), 0).T
        own_t = jnp.where(here, late_t, early_ref[p])
        links_t_ref[p] = own_t
        if cov is None:
            cov, link_t = base_refs[p][...], own_t
        else:
            own_t = split(own_t)
            cov = carry(own_t, cov, base_refs[p][...])
            link_t = mm(own_t, link_t)
    whole_ref[:size] = link_t
    whole_ref[size:] = cov


def maps_kernel(plan, mask_ref, inv_ref, *refs):
    *parts, maps_ref, token_ref, rows_ref = refs
    token_ref[...] = jnp.zeros_like(token_ref)
    rows_ref[...] = jnp.zeros_like(rows_ref)
    for p in range(inv_ref.shape[0]):
        for owners, part in zip(plan.early, parts):
            put_rows(mask_ref, p, owners, part[p], rows_ref, lambda kept: kept)
        maps_ref[p] = triangular_mm(rows_ref[...], inv_ref[p])


def chip_kernel(own_ref, other_ref, link_t_ref, cov_ref, packed_ref, half_t_ref):
    size = cov_ref.shape[0]
    lower = is_lower()
    own_t, other_t = own_ref[:size, :], other_ref[:size, :]
    own, other = own_ref[size:, :], other_ref[size:, :]
    down_t = split(jnp.where(lower, own_t, other_t))
    cov = carry(down_t, jnp.where(lower, other, own), jnp.where(lower, own, other))
    link_t = mm(down_t, jnp.where(lower, other_t, own_t))
    link_t_ref[...] = link_t
    cov_ref[...] = cov
    packed_ref[...] = own_half(pack(cov))
    half_t_ref[...] = own_half(link_t)


def merge_kernel(level, link_t_ref, cov_ref, *refs):
    got_t = from_halves(refs[0][...], refs[1][...])
    got = unpack(from_halves(refs[2][...], refs[3][...]))
    own_t, own = link_t_ref[...], cov_ref[...]
    lower = (lax.shift_right_logical(lax.axis_index("seg") // 2, level) & 1) == 0
    down_t = split(jnp.where(lower, own_t, got_t))
    cov = carry(down_t, jnp.where(lower, got, own), jnp.where(lower, own, got))
    refs[4][...] = own_half(pack(cov))
    if len(refs) > 5:
        link_t = mm(down_t, jnp.where(lower, got_t, own_t))
        refs[5][...] = own_half(link_t)
        refs[6][...] = link_t
        refs[7][...] = cov


def join_kernel(level, *refs):
    past_t, past, link_t, cov = (
        from_halves(refs[2 * i][...], refs[2 * i + 1][...]) for i in range(4)
    )
    chip = lax.axis_index("seg") // 2
    below = (lax.shift_right_logical(chip, level) & 1) == 0
    known = (chip & ((1 << level) - 1)) != (1 << level) - 1
    past_parts = split(past_t)
    joined = pack(carry(past_parts, unpack(cov), unpack(past)))
    joined_t = mm(past_parts, link_t)
    out_t = jnp.where(below, jnp.where(known, joined_t, link_t), past_t)
    out = jnp.where(below, jnp.where(known, joined, cov), past)
    for i, whole in enumerate((out_t, out)):
        half = whole.shape[0] // 2
        refs[8 + 2 * i][...] = own_half(whole)
        refs[9 + 2 * i][...] = jnp.where(is_lower(), whole[half:], whole[:half])


def prepare_kernel(plan, levels, panels, mask_ref, fill_ref, prior_ref, *refs):
    base_refs, own_refs, refs = refs[:panels], refs[panels : 2 * panels], refs[2 * panels :]
    (other_ref, maps_ref, links_t_ref, late_ref, rest_ref), refs = refs[:5], refs[5:]
    past_refs, refs = refs[: 4 * (levels > 1)], refs[4 * (levels > 1) :]
    left_high, left_low, right_high, right_low, const_ref, token_ref, scratch, map_ref, late_map_ref = refs
    token_ref[...] = jnp.zeros_like(token_ref)
    own_cols, width = own_refs[0].shape
    late_at = at_row(plan.late)
    size = base_refs[0].shape[0]
    row_at = lax.axis_index("row")
    rows = left_high.shape[0] // panels - own_cols
    row = lax.broadcasted_iota(jnp.int32, (size, size), 0)
    column = lax.broadcasted_iota(jnp.int32, (size, size), 1)
    eye = (row == column).astype(F32)
    other = other_ref[size:, :]
    lower = is_lower()
    if past_refs:
        chip = lax.axis_index("seg") // 2
        low = (1 << (levels - 1)) - 1
        known = (chip & low) != low
        past_t = from_halves(past_refs[0][...], past_refs[1][...])
        past = unpack(from_halves(past_refs[2][...], past_refs[3][...]))
        to_t = jnp.where(known, past_t, eye)
        gain = jnp.where(known, past, 0.0)
        other_t = split(other_ref[:size, :])
        to_t = jnp.where(lower, mm(other_t, to_t), to_t)
        gain = jnp.where(lower, carry(other_t, gain, other), gain)
    else:
        to_t = jnp.where(lower, other_ref[:size, :], eye)
        gain = jnp.where(lower, other, 0.0)
    own_at = pl.ds(pl.multiple_of(row_at * own_cols, own_cols), own_cols)
    own_rows = pl.ds(pl.multiple_of(row_at * rows, rows), rows)
    late_rows = pl.ds(pl.multiple_of(late_at * rows, rows), rows)
    for p in range(panels - 1, -1, -1):
        late_map_ref[:, :size] = late_ref[p]
        late_map_ref[:, size:] = rest_ref[p]
        _, place = order_of(chosen_of(p, fill_ref, prior_ref), width // BLOCK)
        map_ref[...] = maps_ref[p]
        for t in range(len(place) // 2):
            map_ref[late_rows, t * LANES : (t + 1) * LANES] = two_blocks(
                tile_of(late_map_ref), place[2 * t], place[2 * t + 1]
            )
        whole = split(map_ref[...])
        own_t = split(map_ref[:, own_at].T)
        scratch[:, :size] = to_t
        scratch[:, size:] = gain
        to_parts = split(to_t)
        cross = jnp.concatenate(
            [
                jnp.full((BLOCK, size), -mask_ref[p, slot].astype(F32))
                for slot in slots_of(tuple(range(size // rows)), rows)
            ],
            0,
        )
        left = jnp.concatenate([scratch[own_rows, :size] * cross, mm(own_t, to_parts)], 0)
        part = slice(p * left.shape[0], (p + 1) * left.shape[0])
        left_high[part, :], left_low[part, :] = split(left)
        right_high[p], right_low[p] = split(mm(to_parts, whole, TN))
        gains = jnp.concatenate([scratch[own_rows, size:] * cross, mm(own_t, gain)], 0)
        const = mm(gains, whole)
        const_ref[p, :rows, :] = const[:rows]
        const_ref[p, rows:, :] = const[rows:] + own_refs[p][...]
        if p > 0:
            link_t = split(links_t_ref[p])
            to_t = mm(link_t, to_t)
            gain = carry(link_t, gain, base_refs[p][...])


def finish_kernel(levels, after_ref, after_other_ref, *refs):
    left_high, left_low, right_high, right_low, const_ref, diag_hbm, off_hbm = refs[:7]
    diag_ref, off_ref, sems = refs[7:]
    panels, total, _ = const_ref.shape
    rows = off_ref.shape[1]
    chip = lax.axis_index("seg") // 2
    after = from_halves(after_ref[...], after_other_ref[...])
    after = unpack(jnp.where((chip & ((1 << levels) // 2)) == 0, after, 0.0))
    inner = split(mm((left_high[...], left_low[...]), after))
    copies = []
    for p in range(panels):
        part = slice(p * total, (p + 1) * total)
        right = (right_high[p], right_low[p])
        result = mm((inner[0][part], inner[1][part]), right) + const_ref[p]
        diag_ref[p] = result[rows:]
        off_ref[p] = result[:rows]
        copies.append(pltpu.make_async_copy(diag_ref.at[p], diag_hbm.at[p], sems.at[p, 0]))
        copies.append(pltpu.make_async_copy(off_ref.at[p], off_hbm.at[p], sems.at[p, 1]))
        copies[-2].start()
        copies[-1].start()
    for copy in copies:
        copy.wait()


def body(fill_blocks, fill_mask, inv_diag, factor_off):
    panels, width, _ = inv_diag.shape
    rows = factor_off.shape[1]
    seg_count = lax.axis_size("seg")
    row_count = lax.axis_size("row")
    size = rows * row_count
    own_cols = width // row_count
    slots = fill_blocks.shape[1]
    chosen_cols = slots * BLOCK
    chips = seg_count // 2
    half = size // 2

    def turn(x, axis, distance):
        count = lax.axis_size(axis)
        return lax.ppermute(x, axis, [(i, (i + distance) % count) for i in range(count)])

    prior_fill = turn(fill_blocks, "seg", 1)
    pick = jax.ShapeDtypeStruct((width, chosen_cols), BF16)
    bases, priors, picks, tokens = [], [], [], []
    for p in range(panels):
        copy_of_inv = [pltpu.VMEM((width, width), F32), pltpu.SemaphoreType.DMA]
        high_low = call(
            functools.partial(pick_kernel, p),
            [pick, pick],
            [fill_blocks] if p else [fill_blocks, prior_fill],
            [],
            far=[inv_diag],
            scratch=copy_of_inv,
            flops=(0 if p else 20) * width**3,
            name="pick",
        )
        base, own_prior, token = call(
            functools.partial(prior_kernel, p),
            [shape(chosen_cols, chosen_cols), shape(own_cols, width), shape(1, 1, width)],
            [],
            high_low,
            far=[inv_diag],
            scratch=copy_of_inv,
            name="prior",
        )
        bases.append(base)
        priors.append(own_prior)
        picks += high_low
        tokens.append(token)
    short = row_count == 4
    ups, downs = [factor_off], [factor_off + tokens[-1]]
    for _ in range(row_count // 2 - short):
        ups.append(turn(ups[-1], "row", 1))
    for _ in range((row_count - 1) // 2):
        downs.append(turn(downs[-1], "row", -1))
    far = row_count // 2
    came = [d for d in range(row_count) if d != far]
    whose = [tuple((i - d) % row_count for i in range(row_count)) for d in range(row_count)]
    plan = Plan(tuple(whose[d] for d in came), whose[far])
    parts = ups[:far] + downs[:0:-1]
    (late,) = call(
        functools.partial(chosen_kernel, whose[1] if short else whose[far]),
        [shape(panels, rows, chosen_cols)],
        [fill_mask],
        [ups[-1], *picks],
        flops=6 * panels * rows * chosen_cols * width,
        name="chosen",
    )
    if short:
        late = turn(late, "row", 1)
    (links,) = call(
        functools.partial(links_kernel, plan),
        [shape(panels, size, size)],
        [fill_mask],
        [*parts, *picks],
        scratch=[pltpu.VMEM((size, chosen_cols), F32)],
        flops=6 * panels * size * size * width,
        name="links",
    )
    links_t, own_whole = call(
        functools.partial(segment_kernel, plan, panels),
        [shape(panels, size, size), shape(2 * size, size)],
        [],
        [late, links, *bases],
        flops=18 * (panels - 1) * size**3,
        name="segment",
    )
    maps, maps_token = call(
        functools.partial(maps_kernel, plan),
        [shape(panels, size, width), shape(1, half)],
        [fill_mask],
        [inv_diag, *parts],
        scratch=[pltpu.VMEM((size, width), F32)],
        flops=6 * panels * size * width * width,
        mib=24,
        name="maps",
    )
    swap = [(i, i ^ 1) for i in range(seg_count)]
    other_whole = lax.ppermute(own_whole, "seg", swap)
    half_packed = shape(5 * half // 4, half)
    half_link = shape(half, size)
    link_t, cov, send, send_t = call(
        chip_kernel,
        [shape(size, size), shape(size, size), half_packed, half_link],
        [],
        [own_whole, other_whole],
        flops=18 * size**3,
        name="chip",
    )
    held = [ups[-1], downs[-1]] if short else [ups[-1]]
    held_by = whose[far]
    if short:
        held_by = tuple(whose[-1][i] if i % 2 else whose[1][i] for i in range(row_count))
    (rest,) = call(
        functools.partial(rest_kernel, held_by),
        [shape(panels, rows, width - chosen_cols)],
        [fill_mask, fill_blocks, prior_fill],
        [inv_diag, *held, send],
        scratch=[pltpu.VMEM((rows, width), F32)],
        flops=6 * panels * rows * width * width,
        mib=24,
        name="rest",
    )
    if short:
        rest = lax.ppermute(rest, "row", [(i, i ^ 1) for i in range(row_count)])
    past = None
    after = (jnp.zeros(half_packed.shape, F32),) * 2
    levels = (chips - 1).bit_length()
    prepared = None

    def prepare():
        total = rows + own_cols
        left = jax.ShapeDtypeStruct((panels * total, size), BF16)
        right = jax.ShapeDtypeStruct((panels, size, width), BF16)
        return call(
            functools.partial(prepare_kernel, plan, levels, panels),
            [left, left, right, right, shape(panels, total, width), shape(1, half)],
            [fill_mask, fill_blocks, prior_fill],
            [*bases, *priors, other_whole, maps, links_t, late, rest, *(past or ())],
            scratch=[
                pltpu.VMEM((size, width), F32),
                pltpu.VMEM((size, width), F32),
                pltpu.VMEM((rows, width), F32),
            ],
            flops=6 * panels * size * (total * size + size * width + total * width + 3 * size * size),
            mib=24,
            name="prepare",
        )

    for level in range(levels):
        partner = [(i, i ^ (2 << level)) for i in range(seg_count)]
        got = lax.ppermute(send, "seg", partner)
        if level == levels - 1:
            *prepared, token = prepare()
            got = got + token
            after = (got, lax.ppermute(got, "seg", swap))
            break
        got_t = lax.ppermute(send_t, "seg", partner)
        if level == 0:
            got = got + maps_token
        got = (got_t, lax.ppermute(got_t, "seg", swap), got, lax.ppermute(got, "seg", swap))
        outs = [half_packed]
        if level < levels - 2:
            outs += [half_link, shape(size, size), shape(size, size)]
        send, *more = call(
            functools.partial(merge_kernel, level), outs, [], [link_t, cov, *got],
            flops=18 * size**3, name="merge",
        )
        if more:
            send_t, link_t, cov = more
        if past is None:
            past = got
        else:
            past = call(
                functools.partial(join_kernel, level),
                [half_link, half_link, half_packed, half_packed],
                [],
                [*past, *got],
                flops=18 * size**3,
                name="join",
            )
    if prepared is None:
        *prepared, _ = prepare()
    diag, off = call(
        functools.partial(finish_kernel, levels),
        [shape(panels, own_cols, width), shape(panels, rows, width)],
        [],
        [*after, *prepared],
        out_far=True,
        scratch=[
            pltpu.VMEM((panels, own_cols, width), F32),
            pltpu.VMEM((panels, rows, width), F32),
            pltpu.SemaphoreType.DMA((panels, 2)),
        ],
        flops=6 * panels * (rows + own_cols) * size * (size + width),
        name="finish",
    )
    return diag, off


def solution(mesh):
    placed = (P("seg", None), P("seg", None), P("seg", None, None), P("seg", "row", None))
    return jax.shard_map(
        body,
        mesh=mesh,
        in_specs=placed,
        out_specs=(P("seg", "row", None), P("seg", "row", None)),
        check_vma=False,
    )
```

```python
import functools
from typing import NamedTuple

import jax
import jax.numpy as jnp
from jax import lax
from jax.experimental import pallas as pl
from jax.experimental.pallas import tpu as pltpu
from jax.sharding import PartitionSpec as P

BLOCK = 64
LANES = 128
F32 = jnp.float32
BF16 = jnp.bfloat16
NN = (((1,), (0,)), ((), ()))
NT = (((1,), (1,)), ((), ()))
TN = (((0,), (0,)), ((), ()))


def split(x):
    high = x.astype(BF16)
    return high, (x - high.astype(F32)).astype(BF16)


def mm(a, b, dims=NN):
    a = a if isinstance(a, tuple) else split(a)
    b = b if isinstance(b, tuple) else split(b)
    dot = functools.partial(lax.dot_general, dimension_numbers=dims, preferred_element_type=F32)
    return dot(a[0], b[0]) + (dot(a[0], b[1]) + dot(a[1], b[0]))


def carry(link_t, cov, base):
    link_t = link_t if isinstance(link_t, tuple) else split(link_t)
    return mm(mm(link_t, cov), link_t, NT) + base


def pack(cov):
    half = cov.shape[0] // 2
    part = half // 2
    first, second = cov[:half, :half], cov[half:, half:]
    lane = lax.broadcasted_iota(jnp.int32, (part, half), 1)
    last = jnp.where(lane < part, pltpu.roll(first[part:], part, 1), second[part:])
    return jnp.concatenate([cov[:half, half:], first[:part], second[:part], last], 0)


def unpack(packed):
    half = packed.shape[1]
    part = half // 2
    cross, last = packed[:half], packed[2 * half :]
    row = lax.broadcasted_iota(jnp.int32, (half, half), 0)
    lane = lax.broadcasted_iota(jnp.int32, (half, half), 1)

    def symmetric(top, bottom):
        upper = jnp.concatenate([top, bottom], 0)
        return jnp.where((row < part) | (lane >= part), upper, upper.T)

    first = symmetric(packed[half : half + part], pltpu.roll(last, part, 1))
    second = symmetric(packed[half + part : 2 * half], last)
    top = jnp.concatenate([first, cross], 1)
    bottom = jnp.concatenate([cross.T, second], 1)
    return jnp.concatenate([top, bottom], 0)


def is_lower():
    return (lax.axis_index("seg") & 1) == 0


def from_halves(own, other):
    lower = is_lower()
    return jnp.concatenate([jnp.where(lower, own, other), jnp.where(lower, other, own)], 0)


def own_half(whole):
    half = whole.shape[0] // 2
    return jnp.where(is_lower(), whole[:half], whole[half:])


def two_blocks(load, left, right):
    def placed(block, half):
        slab = load(lax.shift_right_logical(block, 1))
        return jnp.where((block & 1) == half, slab, pltpu.roll(slab, BLOCK, 1))

    a, b = placed(left, 0), placed(right, 1)
    lane = lax.broadcasted_iota(jnp.int32, a.shape, 1)
    return jnp.where(lane < BLOCK, a, b)


def tile_of(ref, *lead):
    def load(tile):
        return ref[(*lead, slice(None), pl.ds(pl.multiple_of(tile * LANES, LANES), LANES))]

    return load


def chosen_of(panel, fill_ref, prior_ref=None):
    slots = fill_ref.shape[1]
    if panel > 0:
        return [fill_ref[panel - 1, j] for j in range(slots)]
    first = lax.axis_index("seg") == 0
    last = prior_ref.shape[0] - 1
    return [jnp.where(first, fill_ref[0, j], prior_ref[last, j]) for j in range(slots)]


def order_of(chosen, blocks):
    slots = len(chosen)
    rest = [jnp.int32(0)] * (blocks - slots)
    place = []
    seen = jnp.int32(0)
    for b in range(blocks):
        hit = jnp.int32(0)
        where = jnp.int32(0)
        for j in range(slots):
            same = (chosen[j] == b).astype(jnp.int32)
            hit = hit + same
            where = where + same * j
        free = 1 - hit
        for q in range(blocks - slots):
            rest[q] = rest[q] + jnp.where(seen == q, free * b, 0)
        place.append(jnp.where(hit > 0, where, slots + seen))
        seen = seen + free
    return rest, place


def vmem(count):
    return [pl.BlockSpec(memory_space=pltpu.VMEM)] * count


def smem(count):
    return [pl.BlockSpec(memory_space=pltpu.SMEM)] * count


def call(
    kernel, outs, scalars, arrays, far=(), out_far=False, through=(), scratch=(), flops=0, mib=16, name=None
):
    moved = sum(a.size * 4 for a in (*arrays, *far)) + sum(o.size * 4 for o in outs)
    first = len(scalars) + len(arrays) + len(far)
    count = len(through)

    def inner(*refs):
        kernel(*refs[:first], *refs[first + count : first + count + len(outs)], *refs[first + 2 * count + len(outs) :])

    return pl.pallas_call(
        inner,
        out_shape=[*outs, *(jax.ShapeDtypeStruct(a.shape, a.dtype) for a in through)],
        in_specs=smem(len(scalars))
        + vmem(len(arrays))
        + [pl.BlockSpec(memory_space=pltpu.HBM)] * len(far)
        + [pl.BlockSpec(memory_space=pl.ANY)] * count,
        out_specs=([pl.BlockSpec(memory_space=pltpu.HBM)] * len(outs) if out_far else vmem(len(outs)))
        + [pl.BlockSpec(memory_space=pl.ANY)] * count,
        scratch_shapes=list(scratch),
        input_output_aliases={first + i: len(outs) + i for i in range(count)},
        cost_estimate=pl.CostEstimate(flops=flops, bytes_accessed=moved, transcendentals=0),
        compiler_params=pltpu.CompilerParams(vmem_limit_bytes=mib << 20),
        name=name,
    )(*scalars, *arrays, *(pltpu.with_memory_space_constraint(a, pltpu.HBM) for a in far), *through)


def shape(*dims):
    return jax.ShapeDtypeStruct(dims, F32)


def kept_rows(mask_ref, panel, slot, rows):
    alive = lax.axis_index("seg") * mask_ref.shape[0] + panel < (
        lax.axis_size("seg") * mask_ref.shape[0] - 1
    )
    return rows * (mask_ref[panel, slot].astype(F32) * alive.astype(F32))


def triangular_mm(left, lower):
    cut = left.shape[1] // 2
    first, second = split(left[:, :cut]), split(left[:, cut:])
    below = split(lower[cut:, :])
    return jnp.concatenate(
        [
            mm(second, (below[0][:, :cut], below[1][:, :cut])) + mm(first, lower[:cut, :cut]),
            mm(second, (below[0][:, cut:], below[1][:, cut:])),
        ],
        1,
    )


def pick_into(high_ref, low_ref, chosen, *inv_at):
    for t in range(len(chosen) // 2):
        columns = slice(t * LANES, (t + 1) * LANES)
        high_ref[:, columns], low_ref[:, columns] = split(
            two_blocks(tile_of(*inv_at), chosen[2 * t], chosen[2 * t + 1])
        )


def load_kernel(
    owners, mask_hbm, fill_hbm, inv_hbm, inv_ref, high_ref, low_ref, keep_ref,
    sent_ref, mask_ref, fill_ref, sems
):
    panels, rows, _ = keep_ref.shape
    small = [
        pltpu.make_async_copy(fill_hbm, fill_ref, sems.at[panels]),
        pltpu.make_async_copy(mask_hbm, mask_ref, sems.at[panels + 1]),
        pltpu.make_async_copy(fill_hbm, sent_ref, sems.at[panels + 2]),
    ]
    large = [
        pltpu.make_async_copy(inv_hbm.at[p], inv_ref.at[p], sems.at[p]) for p in range(panels)
    ]
    for copy in (*small, *reversed(large)):
        copy.start()
    for copy in small:
        copy.wait()
    for p in range(panels):
        for s, slot in enumerate(slots_of(owners, rows)):
            ones = jnp.ones((BLOCK, keep_ref.shape[2]), F32)
            keep_ref[p, s * BLOCK : (s + 1) * BLOCK, :] = kept_rows(mask_ref, p, slot, ones)
    large[-1].wait()
    pick_into(high_ref, low_ref, chosen_of(panels - 1, fill_ref), inv_ref, panels - 1)
    for copy in large[:-1]:
        copy.wait()


def pick_kernel(panel, *refs):
    *scalar_refs, inv_ref, high_ref, low_ref = refs
    pick_into(high_ref, low_ref, chosen_of(panel, *scalar_refs), inv_ref, panel)


def prior_kernel(panel, high_ref, low_ref, inv_ref, base_ref, own_ref, token_ref):
    token_ref[...] = jnp.zeros_like(token_ref)
    own_cols = own_ref.shape[0]
    own_at = pl.ds(pl.multiple_of(lax.axis_index("row") * own_cols, own_cols), own_cols)
    picked = (high_ref[...], low_ref[...])
    base_ref[...] = mm(picked, picked, TN)
    own_ref[...] = mm(inv_ref[panel, :, own_at], inv_ref[panel], TN)


class Plan(NamedTuple):
    early: tuple
    late: tuple


def at_row(table):
    value = jnp.int32(table[0])
    for i, entry in enumerate(table[1:], 1):
        value = jnp.where(lax.axis_index("row") == i, entry, value)
    return value


def slots_of(owners, rows):
    first = at_row(owners) * (rows // BLOCK)
    return [first + s for s in range(rows // BLOCK)]


def put_rows(mask_ref, panel, owners, part, out_ref, take):
    for s, slot in enumerate(slots_of(owners, part.shape[0])):
        kept = kept_rows(mask_ref, panel, slot, part[s * BLOCK : (s + 1) * BLOCK, :])
        out_ref[pl.ds(pl.multiple_of(slot * BLOCK, BLOCK), BLOCK), :] = take(kept)


def links_kernel(plan, mask_ref, *refs):
    parts, refs = refs[: len(plan.early)], refs[len(plan.early) :]
    *pick_refs, links_t_ref, rows_ref = refs
    rows_ref[...] = jnp.zeros_like(rows_ref)
    for p in range(links_t_ref.shape[0]):
        pick = (pick_refs[2 * p][...], pick_refs[2 * p + 1][...])
        for owners, part in zip(plan.early, parts):
            put_rows(mask_ref, p, owners, part[p], rows_ref, lambda kept: mm(kept, pick))
        links_t_ref[p] = rows_ref[...].T


def kept_block(mask_ref, panel, owners, part):
    return jnp.concatenate(
        [
            kept_rows(mask_ref, panel, slot, part[s * BLOCK : (s + 1) * BLOCK, :])
            for s, slot in enumerate(slots_of(owners, part.shape[0]))
        ],
        0,
    )


def chosen_kernel(part, keep_ref, *refs):
    *pick_refs, out_ref = refs
    for p in range(out_ref.shape[0]):
        pick = (pick_refs[2 * p][...], pick_refs[2 * p + 1][...])
        out_ref[p] = mm(part[p], pick) * keep_ref[p]


def rest_kernel(owners, mask_ref, fill_ref, prior_ref, inv_ref, *refs):
    *parts, _, out_ref, map_ref = refs
    odd = (lax.axis_index("row") & 1) == 1
    for p in range(out_ref.shape[0]):
        part = parts[0][p] if len(parts) == 1 else jnp.where(odd, parts[1][p], parts[0][p])
        map_ref[...] = triangular_mm(kept_block(mask_ref, p, owners, part), inv_ref[p])
        rest, _ = order_of(chosen_of(p, fill_ref, prior_ref), map_ref.shape[1] // BLOCK)
        for t in range(len(rest) // 2):
            out_ref[p, :, t * LANES : (t + 1) * LANES] = two_blocks(
                tile_of(map_ref), rest[2 * t], rest[2 * t + 1]
            )


def segment_kernel(plan, panels, late_ref, early_ref, *refs):
    base_refs, (links_t_ref, whole_ref) = refs[:panels], refs[panels:]
    size = links_t_ref.shape[1]
    rows = late_ref.shape[1]
    here = lax.broadcasted_iota(jnp.int32, (size, size), 1) // rows == at_row(plan.late)
    cov = link_t = None
    for p in range(panels - 1, -1, -1):
        late_t = jnp.concatenate([late_ref[p]] * (size // rows), 0).T
        own_t = jnp.where(here, late_t, early_ref[p])
        links_t_ref[p] = own_t
        if cov is None:
            cov, link_t = base_refs[p][...], own_t
        else:
            own_t = split(own_t)
            cov = carry(own_t, cov, base_refs[p][...])
            link_t = mm(own_t, link_t)
    whole_ref[:size] = link_t
    whole_ref[size:] = cov


def maps_kernel(plan, mask_ref, inv_ref, *refs):
    *parts, maps_ref, token_ref, rows_ref = refs
    token_ref[...] = jnp.zeros_like(token_ref)
    rows_ref[...] = jnp.zeros_like(rows_ref)
    for p in range(inv_ref.shape[0]):
        for owners, part in zip(plan.early, parts):
            put_rows(mask_ref, p, owners, part[p], rows_ref, lambda kept: kept)
        maps_ref[p] = triangular_mm(rows_ref[...], inv_ref[p])


def chip_kernel(own_ref, other_ref, link_t_ref, cov_ref, packed_ref, half_t_ref):
    size = cov_ref.shape[0]
    lower = is_lower()
    own_t, other_t = own_ref[:size, :], other_ref[:size, :]
    own, other = own_ref[size:, :], other_ref[size:, :]
    down_t = split(jnp.where(lower, own_t, other_t))
    cov = carry(down_t, jnp.where(lower, other, own), jnp.where(lower, own, other))
    link_t = mm(down_t, jnp.where(lower, other_t, own_t))
    link_t_ref[...] = link_t
    cov_ref[...] = cov
    packed_ref[...] = own_half(pack(cov))
    half_t_ref[...] = own_half(link_t)


def merge_kernel(level, link_t_ref, cov_ref, *refs):
    got_t = from_halves(refs[0][...], refs[1][...])
    got = unpack(from_halves(refs[2][...], refs[3][...]))
    own_t, own = link_t_ref[...], cov_ref[...]
    lower = (lax.shift_right_logical(lax.axis_index("seg") // 2, level) & 1) == 0
    down_t = split(jnp.where(lower, own_t, got_t))
    cov = carry(down_t, jnp.where(lower, got, own), jnp.where(lower, own, got))
    refs[4][...] = own_half(pack(cov))
    if len(refs) > 5:
        link_t = mm(down_t, jnp.where(lower, got_t, own_t))
        refs[5][...] = own_half(link_t)
        refs[6][...] = link_t
        refs[7][...] = cov


def join_kernel(level, *refs):
    past_t, past, link_t, cov = (
        from_halves(refs[2 * i][...], refs[2 * i + 1][...]) for i in range(4)
    )
    chip = lax.axis_index("seg") // 2
    below = (lax.shift_right_logical(chip, level) & 1) == 0
    known = (chip & ((1 << level) - 1)) != (1 << level) - 1
    past_parts = split(past_t)
    joined = pack(carry(past_parts, unpack(cov), unpack(past)))
    joined_t = mm(past_parts, link_t)
    out_t = jnp.where(below, jnp.where(known, joined_t, link_t), past_t)
    out = jnp.where(below, jnp.where(known, joined, cov), past)
    for i, whole in enumerate((out_t, out)):
        half = whole.shape[0] // 2
        refs[8 + 2 * i][...] = own_half(whole)
        refs[9 + 2 * i][...] = jnp.where(is_lower(), whole[half:], whole[:half])


def prepare_kernel(plan, levels, panels, mask_ref, fill_ref, prior_ref, *refs):
    base_refs, own_refs, refs = refs[:panels], refs[panels : 2 * panels], refs[2 * panels :]
    (other_ref, maps_ref, links_t_ref, late_ref, rest_ref), refs = refs[:5], refs[5:]
    past_refs, refs = refs[: 4 * (levels > 1)], refs[4 * (levels > 1) :]
    left_high, left_low, right_high, right_low, const_ref, token_ref, scratch, map_ref, late_map_ref = refs
    token_ref[...] = jnp.zeros_like(token_ref)
    own_cols, width = own_refs[0].shape
    late_at = at_row(plan.late)
    size = base_refs[0].shape[0]
    row_at = lax.axis_index("row")
    rows = left_high.shape[0] // panels - own_cols
    row = lax.broadcasted_iota(jnp.int32, (size, size), 0)
    column = lax.broadcasted_iota(jnp.int32, (size, size), 1)
    eye = (row == column).astype(F32)
    other = other_ref[size:, :]
    lower = is_lower()
    if past_refs:
        chip = lax.axis_index("seg") // 2
        low = (1 << (levels - 1)) - 1
        known = (chip & low) != low
        past_t = from_halves(past_refs[0][...], past_refs[1][...])
        past = unpack(from_halves(past_refs[2][...], past_refs[3][...]))
        to_t = jnp.where(known, past_t, eye)
        gain = jnp.where(known, past, 0.0)
        other_t = split(other_ref[:size, :])
        to_t = jnp.where(lower, mm(other_t, to_t), to_t)
        gain = jnp.where(lower, carry(other_t, gain, other), gain)
    else:
        to_t = jnp.where(lower, other_ref[:size, :], eye)
        gain = jnp.where(lower, other, 0.0)
    own_at = pl.ds(pl.multiple_of(row_at * own_cols, own_cols), own_cols)
    own_rows = pl.ds(pl.multiple_of(row_at * rows, rows), rows)
    late_rows = pl.ds(pl.multiple_of(late_at * rows, rows), rows)
    for p in range(panels - 1, -1, -1):
        late_map_ref[:, :size] = late_ref[p]
        late_map_ref[:, size:] = rest_ref[p]
        _, place = order_of(chosen_of(p, fill_ref, prior_ref), width // BLOCK)
        map_ref[...] = maps_ref[p]
        for t in range(len(place) // 2):
            map_ref[late_rows, t * LANES : (t + 1) * LANES] = two_blocks(
                tile_of(late_map_ref), place[2 * t], place[2 * t + 1]
            )
        whole = split(map_ref[...])
        own_t = split(map_ref[:, own_at].T)
        scratch[:, :size] = to_t
        scratch[:, size:] = gain
        to_parts = split(to_t)
        cross = jnp.concatenate(
            [
                jnp.full((BLOCK, size), -mask_ref[p, slot].astype(F32))
                for slot in slots_of(tuple(range(size // rows)), rows)
            ],
            0,
        )
        left = jnp.concatenate([scratch[own_rows, :size] * cross, mm(own_t, to_parts)], 0)
        part = slice(p * left.shape[0], (p + 1) * left.shape[0])
        left_high[part, :], left_low[part, :] = split(left)
        right_high[p], right_low[p] = split(mm(to_parts, whole, TN))
        gains = jnp.concatenate([scratch[own_rows, size:] * cross, mm(own_t, gain)], 0)
        const = mm(gains, whole)
        const_ref[p, :rows, :] = const[:rows]
        const_ref[p, rows:, :] = const[rows:] + own_refs[p][...]
        if p > 0:
            link_t = split(links_t_ref[p])
            to_t = mm(link_t, to_t)
            gain = carry(link_t, gain, base_refs[p][...])


def finish_kernel(levels, after_ref, after_other_ref, *refs):
    left_high, left_low, right_high, right_low, const_ref, diag_hbm, off_hbm = refs[:7]
    diag_ref, off_ref, sems = refs[7:]
    panels, total, _ = const_ref.shape
    rows = off_ref.shape[1]
    chip = lax.axis_index("seg") // 2
    after = from_halves(after_ref[...], after_other_ref[...])
    after = unpack(jnp.where((chip & ((1 << levels) // 2)) == 0, after, 0.0))
    inner = split(mm((left_high[...], left_low[...]), after))
    copies = []
    for p in range(panels):
        part = slice(p * total, (p + 1) * total)
        right = (right_high[p], right_low[p])
        result = mm((inner[0][part], inner[1][part]), right) + const_ref[p]
        diag_ref[p] = result[rows:]
        off_ref[p] = result[:rows]
        copies.append(pltpu.make_async_copy(diag_ref.at[p], diag_hbm.at[p], sems.at[p, 0]))
        copies.append(pltpu.make_async_copy(off_ref.at[p], off_hbm.at[p], sems.at[p, 1]))
        copies[-2].start()
        copies[-1].start()
    for copy in copies:
        copy.wait()


def body(fill_blocks, fill_mask, inv_diag, factor_off):
    panels, width, _ = inv_diag.shape
    rows = factor_off.shape[1]
    seg_count = lax.axis_size("seg")
    row_count = lax.axis_size("row")
    size = rows * row_count
    own_cols = width // row_count
    slots = fill_blocks.shape[1]
    chosen_cols = slots * BLOCK
    chips = seg_count // 2
    half = size // 2

    def turn(x, axis, distance):
        count = lax.axis_size(axis)
        return lax.ppermute(x, axis, [(i, (i + distance) % count) for i in range(count)])

    pick = jax.ShapeDtypeStruct((width, chosen_cols), BF16)
    short = row_count == 4
    far = row_count // 2
    whose = [tuple((i - d) % row_count for i in range(row_count)) for d in range(row_count)]
    inv, high, low, keep, sent_fill = call(
        functools.partial(load_kernel, whose[1] if short else whose[far]),
        [
            shape(*inv_diag.shape), pick, pick, shape(panels, rows, chosen_cols),
            jax.ShapeDtypeStruct(fill_blocks.shape, fill_blocks.dtype),
        ],
        [],
        [],
        far=[fill_mask, fill_blocks, inv_diag],
        scratch=[
            pltpu.SMEM(fill_mask.shape, jnp.int32),
            pltpu.SMEM(fill_blocks.shape, jnp.int32),
            pltpu.SemaphoreType.DMA((panels + 3,)),
        ],
        name="load",
    )
    prior_fill = turn(sent_fill, "seg", 1)
    picks, bases, priors = [], [], []
    for p in range(panels):
        high_low = [high, low]
        if p < panels - 1:
            high_low = call(
                functools.partial(pick_kernel, p),
                [pick, pick],
                [fill_blocks] if p else [fill_blocks, prior_fill],
                [inv],
                flops=20 * width**3,
                name="pick",
            )
        base, own_prior, token = call(
            functools.partial(prior_kernel, p),
            [shape(chosen_cols, chosen_cols), shape(own_cols, width), shape(1, 1, width)],
            [],
            [*high_low, inv],
            flops=6 * width * (chosen_cols * chosen_cols + own_cols * width),
            name="prior",
        )
        picks += high_low
        bases.append(base)
        priors.append(own_prior)
    ups, downs = [factor_off], [factor_off + token]
    for _ in range(row_count // 2 - short):
        ups.append(turn(ups[-1], "row", 1))
    for _ in range((row_count - 1) // 2):
        downs.append(turn(downs[-1], "row", -1))
    came = [d for d in range(row_count) if d != far]
    plan = Plan(tuple(whose[d] for d in came), whose[far])
    parts = ups[:far] + downs[:0:-1]
    (late,) = call(
        chosen_kernel,
        [shape(panels, rows, chosen_cols)],
        [],
        [ups[-1], keep, *picks],
        flops=6 * panels * rows * chosen_cols * width,
        name="chosen",
    )
    if short:
        late = turn(late, "row", 1)
    (links,) = call(
        functools.partial(links_kernel, plan),
        [shape(panels, size, size)],
        [fill_mask],
        [*parts, *picks],
        scratch=[pltpu.VMEM((size, chosen_cols), F32)],
        flops=6 * panels * size * size * width,
        name="links",
    )
    links_t, own_whole = call(
        functools.partial(segment_kernel, plan, panels),
        [shape(panels, size, size), shape(2 * size, size)],
        [],
        [late, links, *bases],
        flops=18 * (panels - 1) * size**3,
        name="segment",
    )
    maps, maps_token = call(
        functools.partial(maps_kernel, plan),
        [shape(panels, size, width), shape(1, half)],
        [fill_mask],
        [inv, *parts],
        scratch=[pltpu.VMEM((size, width), F32)],
        flops=6 * panels * size * width * width,
        mib=24,
        name="maps",
    )
    swap = [(i, i ^ 1) for i in range(seg_count)]
    other_whole = lax.ppermute(own_whole, "seg", swap)
    half_packed = shape(5 * half // 4, half)
    half_link = shape(half, size)
    link_t, cov, send, send_t = call(
        chip_kernel,
        [shape(size, size), shape(size, size), half_packed, half_link],
        [],
        [own_whole, other_whole],
        flops=18 * size**3,
        name="chip",
    )
    held = [ups[-1], downs[-1]] if short else [ups[-1]]
    held_by = whose[far]
    if short:
        held_by = tuple(whose[-1][i] if i % 2 else whose[1][i] for i in range(row_count))
    (rest,) = call(
        functools.partial(rest_kernel, held_by),
        [shape(panels, rows, width - chosen_cols)],
        [fill_mask, fill_blocks, prior_fill],
        [inv, *held, send],
        scratch=[pltpu.VMEM((rows, width), F32)],
        flops=6 * panels * rows * width * width,
        mib=24,
        name="rest",
    )
    if short:
        rest = lax.ppermute(rest, "row", [(i, i ^ 1) for i in range(row_count)])
    past = None
    after = (jnp.zeros(half_packed.shape, F32),) * 2
    levels = (chips - 1).bit_length()
    prepared = None

    def prepare():
        total = rows + own_cols
        left = jax.ShapeDtypeStruct((panels * total, size), BF16)
        right = jax.ShapeDtypeStruct((panels, size, width), BF16)
        return call(
            functools.partial(prepare_kernel, plan, levels, panels),
            [left, left, right, right, shape(panels, total, width), shape(1, half)],
            [fill_mask, fill_blocks, prior_fill],
            [*bases, *priors, other_whole, maps, links_t, late, rest, *(past or ())],
            scratch=[
                pltpu.VMEM((size, width), F32),
                pltpu.VMEM((size, width), F32),
                pltpu.VMEM((rows, width), F32),
            ],
            flops=6 * panels * size * (total * size + size * width + total * width + 3 * size * size),
            mib=24,
            name="prepare",
        )

    for level in range(levels):
        partner = [(i, i ^ (2 << level)) for i in range(seg_count)]
        got = lax.ppermute(send, "seg", partner)
        if level == levels - 1:
            *prepared, token = prepare()
            got = got + token
            after = (got, lax.ppermute(got, "seg", swap))
            break
        got_t = lax.ppermute(send_t, "seg", partner)
        if level == 0:
            got = got + maps_token
        got = (got_t, lax.ppermute(got_t, "seg", swap), got, lax.ppermute(got, "seg", swap))
        outs = [half_packed]
        if level < levels - 2:
            outs += [half_link, shape(size, size), shape(size, size)]
        send, *more = call(
            functools.partial(merge_kernel, level), outs, [], [link_t, cov, *got],
            flops=18 * size**3, name="merge",
        )
        if more:
            send_t, link_t, cov = more
        if past is None:
            past = got
        else:
            past = call(
                functools.partial(join_kernel, level),
                [half_link, half_link, half_packed, half_packed],
                [],
                [*past, *got],
                flops=18 * size**3,
                name="join",
            )
    if prepared is None:
        *prepared, _ = prepare()
    diag, off = call(
        functools.partial(finish_kernel, levels),
        [shape(panels, own_cols, width), shape(panels, rows, width)],
        [],
        [*after, *prepared],
        out_far=True,
        scratch=[
            pltpu.VMEM((panels, own_cols, width), F32),
            pltpu.VMEM((panels, rows, width), F32),
            pltpu.SemaphoreType.DMA((panels, 2)),
        ],
        flops=6 * panels * (rows + own_cols) * size * (size + width),
        name="finish",
    )
    return diag, off


def solution(mesh):
    placed = (P("seg", None), P("seg", None), P("seg", None, None), P("seg", "row", None))
    return jax.shard_map(
        body,
        mesh=mesh,
        in_specs=placed,
        out_specs=(P("seg", "row", None), P("seg", "row", None)),
        check_vma=False,
    )
```

```python
import functools
from typing import NamedTuple

import jax
import jax.numpy as jnp
from jax import lax
from jax.experimental import pallas as pl
from jax.experimental.pallas import tpu as pltpu
from jax.sharding import PartitionSpec as P

BLOCK = 64
LANES = 128
F32 = jnp.float32
BF16 = jnp.bfloat16
NN = (((1,), (0,)), ((), ()))
NT = (((1,), (1,)), ((), ()))
TN = (((0,), (0,)), ((), ()))


def split(x):
    high = x.astype(BF16)
    return high, (x - high.astype(F32)).astype(BF16)


def mm(a, b, dims=NN):
    a = a if isinstance(a, tuple) else split(a)
    b = b if isinstance(b, tuple) else split(b)
    dot = functools.partial(lax.dot_general, dimension_numbers=dims, preferred_element_type=F32)
    return dot(a[0], b[0]) + (dot(a[0], b[1]) + dot(a[1], b[0]))


def carry(link_t, cov, base):
    link_t = link_t if isinstance(link_t, tuple) else split(link_t)
    return mm(mm(link_t, cov), link_t, NT) + base


def pack(cov):
    half = cov.shape[0] // 2
    part = half // 2
    first, second = cov[:half, :half], cov[half:, half:]
    lane = lax.broadcasted_iota(jnp.int32, (part, half), 1)
    last = jnp.where(lane < part, pltpu.roll(first[part:], part, 1), second[part:])
    return jnp.concatenate([cov[:half, half:], first[:part], second[:part], last], 0)


def unpack(packed):
    half = packed.shape[1]
    part = half // 2
    cross, last = packed[:half], packed[2 * half :]
    row = lax.broadcasted_iota(jnp.int32, (half, half), 0)
    lane = lax.broadcasted_iota(jnp.int32, (half, half), 1)

    def symmetric(top, bottom):
        upper = jnp.concatenate([top, bottom], 0)
        return jnp.where((row < part) | (lane >= part), upper, upper.T)

    first = symmetric(packed[half : half + part], pltpu.roll(last, part, 1))
    second = symmetric(packed[half + part : 2 * half], last)
    top = jnp.concatenate([first, cross], 1)
    bottom = jnp.concatenate([cross.T, second], 1)
    return jnp.concatenate([top, bottom], 0)


def is_lower():
    return (lax.axis_index("seg") & 1) == 0


def from_halves(own, other):
    lower = is_lower()
    return jnp.concatenate([jnp.where(lower, own, other), jnp.where(lower, other, own)], 0)


def own_half(whole):
    half = whole.shape[0] // 2
    return jnp.where(is_lower(), whole[:half], whole[half:])


def two_blocks(load, left, right):
    def placed(block, half):
        slab = load(lax.shift_right_logical(block, 1))
        return jnp.where((block & 1) == half, slab, pltpu.roll(slab, BLOCK, 1))

    a, b = placed(left, 0), placed(right, 1)
    lane = lax.broadcasted_iota(jnp.int32, a.shape, 1)
    return jnp.where(lane < BLOCK, a, b)


def tile_of(ref, *lead):
    def load(tile):
        return ref[(*lead, slice(None), pl.ds(pl.multiple_of(tile * LANES, LANES), LANES))]

    return load


def chosen_of(panel, fill_ref, prior_ref=None):
    slots = fill_ref.shape[1]
    if panel > 0:
        return [fill_ref[panel - 1, j] for j in range(slots)]
    first = lax.axis_index("seg") == 0
    last = prior_ref.shape[0] - 1
    return [jnp.where(first, fill_ref[0, j], prior_ref[last, j]) for j in range(slots)]


def order_of(chosen, blocks):
    slots = len(chosen)
    rest = [jnp.int32(0)] * (blocks - slots)
    place = []
    seen = jnp.int32(0)
    for b in range(blocks):
        hit = jnp.int32(0)
        where = jnp.int32(0)
        for j in range(slots):
            same = (chosen[j] == b).astype(jnp.int32)
            hit = hit + same
            where = where + same * j
        free = 1 - hit
        for q in range(blocks - slots):
            rest[q] = rest[q] + jnp.where(seen == q, free * b, 0)
        place.append(jnp.where(hit > 0, where, slots + seen))
        seen = seen + free
    return rest, place


def vmem(count):
    return [pl.BlockSpec(memory_space=pltpu.VMEM)] * count


def smem(count):
    return [pl.BlockSpec(memory_space=pltpu.SMEM)] * count


def call(
    kernel, outs, scalars, arrays, far=(), anywhere=(), out_far=False, through=(), scratch=(), flops=0, mib=16, name=None
):
    moved = sum(a.size * 4 for a in (*arrays, *far)) + sum(o.size * 4 for o in outs)
    first = len(scalars) + len(arrays) + len(far) + len(anywhere)
    count = len(through)

    def inner(*refs):
        kernel(*refs[:first], *refs[first + count : first + count + len(outs)], *refs[first + 2 * count + len(outs) :])

    return pl.pallas_call(
        inner,
        out_shape=[*outs, *(jax.ShapeDtypeStruct(a.shape, a.dtype) for a in through)],
        in_specs=smem(len(scalars))
        + vmem(len(arrays))
        + [pl.BlockSpec(memory_space=pltpu.HBM)] * len(far)
        + [pl.BlockSpec(memory_space=pl.ANY)] * len(anywhere)
        + [pl.BlockSpec(memory_space=pl.ANY)] * count,
        out_specs=([pl.BlockSpec(memory_space=pltpu.HBM)] * len(outs) if out_far else vmem(len(outs)))
        + [pl.BlockSpec(memory_space=pl.ANY)] * count,
        scratch_shapes=list(scratch),
        input_output_aliases={first + i: len(outs) + i for i in range(count)},
        cost_estimate=pl.CostEstimate(flops=flops, bytes_accessed=moved, transcendentals=0),
        compiler_params=pltpu.CompilerParams(vmem_limit_bytes=mib << 20),
        name=name,
    )(*scalars, *arrays, *(pltpu.with_memory_space_constraint(a, pltpu.HBM) for a in far), *anywhere, *through)


def shape(*dims):
    return jax.ShapeDtypeStruct(dims, F32)


def kept_rows(mask_ref, panel, slot, rows):
    alive = lax.axis_index("seg") * mask_ref.shape[0] + panel < (
        lax.axis_size("seg") * mask_ref.shape[0] - 1
    )
    return rows * (mask_ref[panel, slot].astype(F32) * alive.astype(F32))


def triangular_mm(left, lower):
    cut = left.shape[1] // 2
    first, second = split(left[:, :cut]), split(left[:, cut:])
    below = split(lower[cut:, :])
    return jnp.concatenate(
        [
            mm(second, (below[0][:, :cut], below[1][:, :cut])) + mm(first, lower[:cut, :cut]),
            mm(second, (below[0][:, cut:], below[1][:, cut:])),
        ],
        1,
    )


def pick_into(high_ref, low_ref, chosen, *inv_at):
    for t in range(len(chosen) // 2):
        columns = slice(t * LANES, (t + 1) * LANES)
        high_ref[:, columns], low_ref[:, columns] = split(
            two_blocks(tile_of(*inv_at), chosen[2 * t], chosen[2 * t + 1])
        )


def load_kernel(
    owners, mask_hbm, fill_hbm, inv_hbm, inv_ref, high_ref, low_ref, keep_ref,
    mask_ref, fill_ref, sems
):
    panels, rows, _ = keep_ref.shape
    small = [
        pltpu.make_async_copy(fill_hbm, fill_ref, sems.at[panels]),
        pltpu.make_async_copy(mask_hbm, mask_ref, sems.at[panels + 1]),
    ]
    large = [
        pltpu.make_async_copy(inv_hbm.at[p], inv_ref.at[p], sems.at[p]) for p in range(panels)
    ]
    for copy in (*small, *reversed(large)):
        copy.start()
    for copy in small:
        copy.wait()
    for p in range(panels):
        for s, slot in enumerate(slots_of(owners, rows)):
            ones = jnp.ones((BLOCK, keep_ref.shape[2]), F32)
            keep_ref[p, s * BLOCK : (s + 1) * BLOCK, :] = kept_rows(mask_ref, p, slot, ones)
    large[-1].wait()
    pick_into(high_ref, low_ref, chosen_of(panels - 1, fill_ref), inv_ref, panels - 1)
    for copy in large[:-1]:
        copy.wait()


def pick_kernel(panel, *refs):
    *scalar_refs, inv_ref, high_ref, low_ref = refs
    pick_into(high_ref, low_ref, chosen_of(panel, *scalar_refs), inv_ref, panel)


def prior_kernel(panel, high_ref, low_ref, inv_ref, _, base_ref, own_ref, token_ref):
    token_ref[...] = jnp.zeros_like(token_ref)
    own_cols = own_ref.shape[0]
    own_at = pl.ds(pl.multiple_of(lax.axis_index("row") * own_cols, own_cols), own_cols)
    picked = (high_ref[...], low_ref[...])
    base_ref[...] = mm(picked, picked, TN)
    own_ref[...] = mm(inv_ref[panel, :, own_at], inv_ref[panel], TN)


class Plan(NamedTuple):
    early: tuple
    late: tuple


def at_row(table):
    value = jnp.int32(table[0])
    for i, entry in enumerate(table[1:], 1):
        value = jnp.where(lax.axis_index("row") == i, entry, value)
    return value


def slots_of(owners, rows):
    first = at_row(owners) * (rows // BLOCK)
    return [first + s for s in range(rows // BLOCK)]


def put_rows(mask_ref, panel, owners, part, out_ref, take):
    for s, slot in enumerate(slots_of(owners, part.shape[0])):
        kept = kept_rows(mask_ref, panel, slot, part[s * BLOCK : (s + 1) * BLOCK, :])
        out_ref[pl.ds(pl.multiple_of(slot * BLOCK, BLOCK), BLOCK), :] = take(kept)


def links_kernel(plan, mask_ref, *refs):
    parts, refs = refs[: len(plan.early)], refs[len(plan.early) :]
    *pick_refs, links_t_ref, rows_ref = refs
    rows_ref[...] = jnp.zeros_like(rows_ref)
    for p in range(links_t_ref.shape[0]):
        pick = (pick_refs[2 * p][...], pick_refs[2 * p + 1][...])
        for owners, part in zip(plan.early, parts):
            put_rows(mask_ref, p, owners, part[p], rows_ref, lambda kept: mm(kept, pick))
        links_t_ref[p] = rows_ref[...].T


def kept_block(mask_ref, panel, owners, part):
    return jnp.concatenate(
        [
            kept_rows(mask_ref, panel, slot, part[s * BLOCK : (s + 1) * BLOCK, :])
            for s, slot in enumerate(slots_of(owners, part.shape[0]))
        ],
        0,
    )


def chosen_kernel(part, keep_ref, *refs):
    *pick_refs, out_ref = refs
    for p in range(out_ref.shape[0]):
        pick = (pick_refs[2 * p][...], pick_refs[2 * p + 1][...])
        out_ref[p] = mm(part[p], pick) * keep_ref[p]


def rest_kernel(owners, mask_ref, fill_ref, prior_ref, inv_ref, *refs):
    *parts, _, out_ref, map_ref = refs
    odd = (lax.axis_index("row") & 1) == 1
    for p in range(out_ref.shape[0]):
        part = parts[0][p] if len(parts) == 1 else jnp.where(odd, parts[1][p], parts[0][p])
        map_ref[...] = triangular_mm(kept_block(mask_ref, p, owners, part), inv_ref[p])
        rest, _ = order_of(chosen_of(p, fill_ref, prior_ref), map_ref.shape[1] // BLOCK)
        for t in range(len(rest) // 2):
            out_ref[p, :, t * LANES : (t + 1) * LANES] = two_blocks(
                tile_of(map_ref), rest[2 * t], rest[2 * t + 1]
            )


def segment_kernel(plan, panels, late_ref, early_ref, *refs):
    base_refs, (links_t_ref, whole_ref) = refs[:panels], refs[panels:]
    size = links_t_ref.shape[1]
    rows = late_ref.shape[1]
    here = lax.broadcasted_iota(jnp.int32, (size, size), 1) // rows == at_row(plan.late)
    cov = link_t = None
    for p in range(panels - 1, -1, -1):
        late_t = jnp.concatenate([late_ref[p]] * (size // rows), 0).T
        own_t = jnp.where(here, late_t, early_ref[p])
        links_t_ref[p] = own_t
        if cov is None:
            cov, link_t = base_refs[p][...], own_t
        else:
            own_t = split(own_t)
            cov = carry(own_t, cov, base_refs[p][...])
            link_t = mm(own_t, link_t)
    whole_ref[:size] = link_t
    whole_ref[size:] = cov


def maps_kernel(plan, mask_ref, inv_ref, *refs):
    *parts, maps_ref, token_ref, rows_ref = refs
    token_ref[...] = jnp.zeros_like(token_ref)
    rows_ref[...] = jnp.zeros_like(rows_ref)
    for p in range(inv_ref.shape[0]):
        for owners, part in zip(plan.early, parts):
            put_rows(mask_ref, p, owners, part[p], rows_ref, lambda kept: kept)
        maps_ref[p] = triangular_mm(rows_ref[...], inv_ref[p])


def chip_kernel(own_ref, other_ref, link_t_ref, cov_ref, packed_ref, half_t_ref):
    size = cov_ref.shape[0]
    lower = is_lower()
    own_t, other_t = own_ref[:size, :], other_ref[:size, :]
    own, other = own_ref[size:, :], other_ref[size:, :]
    down_t = split(jnp.where(lower, own_t, other_t))
    cov = carry(down_t, jnp.where(lower, other, own), jnp.where(lower, own, other))
    link_t = mm(down_t, jnp.where(lower, other_t, own_t))
    link_t_ref[...] = link_t
    cov_ref[...] = cov
    packed_ref[...] = own_half(pack(cov))
    half_t_ref[...] = own_half(link_t)


def merge_kernel(level, link_t_ref, cov_ref, *refs):
    got_t = from_halves(refs[0][...], refs[1][...])
    got = unpack(from_halves(refs[2][...], refs[3][...]))
    own_t, own = link_t_ref[...], cov_ref[...]
    lower = (lax.shift_right_logical(lax.axis_index("seg") // 2, level) & 1) == 0
    down_t = split(jnp.where(lower, own_t, got_t))
    cov = carry(down_t, jnp.where(lower, got, own), jnp.where(lower, own, got))
    refs[4][...] = own_half(pack(cov))
    if len(refs) > 5:
        link_t = mm(down_t, jnp.where(lower, got_t, own_t))
        refs[5][...] = own_half(link_t)
        refs[6][...] = link_t
        refs[7][...] = cov


def join_kernel(level, *refs):
    past_t, past, link_t, cov = (
        from_halves(refs[2 * i][...], refs[2 * i + 1][...]) for i in range(4)
    )
    chip = lax.axis_index("seg") // 2
    below = (lax.shift_right_logical(chip, level) & 1) == 0
    known = (chip & ((1 << level) - 1)) != (1 << level) - 1
    past_parts = split(past_t)
    joined = pack(carry(past_parts, unpack(cov), unpack(past)))
    joined_t = mm(past_parts, link_t)
    out_t = jnp.where(below, jnp.where(known, joined_t, link_t), past_t)
    out = jnp.where(below, jnp.where(known, joined, cov), past)
    for i, whole in enumerate((out_t, out)):
        half = whole.shape[0] // 2
        refs[8 + 2 * i][...] = own_half(whole)
        refs[9 + 2 * i][...] = jnp.where(is_lower(), whole[half:], whole[:half])


def prepare_kernel(plan, levels, panels, mask_ref, fill_ref, prior_ref, *refs):
    base_refs, own_refs, refs = refs[:panels], refs[panels : 2 * panels], refs[2 * panels :]
    (other_ref, maps_ref, links_t_ref, late_ref, rest_ref), refs = refs[:5], refs[5:]
    past_refs, refs = refs[: 4 * (levels > 1)], refs[4 * (levels > 1) :]
    left_high, left_low, right_high, right_low, const_ref, token_ref, scratch, map_ref, late_map_ref = refs
    token_ref[...] = jnp.zeros_like(token_ref)
    own_cols, width = own_refs[0].shape
    late_at = at_row(plan.late)
    size = base_refs[0].shape[0]
    row_at = lax.axis_index("row")
    rows = left_high.shape[0] // panels - own_cols
    row = lax.broadcasted_iota(jnp.int32, (size, size), 0)
    column = lax.broadcasted_iota(jnp.int32, (size, size), 1)
    eye = (row == column).astype(F32)
    other = other_ref[size:, :]
    lower = is_lower()
    if past_refs:
        chip = lax.axis_index("seg") // 2
        low = (1 << (levels - 1)) - 1
        known = (chip & low) != low
        past_t = from_halves(past_refs[0][...], past_refs[1][...])
        past = unpack(from_halves(past_refs[2][...], past_refs[3][...]))
        to_t = jnp.where(known, past_t, eye)
        gain = jnp.where(known, past, 0.0)
        other_t = split(other_ref[:size, :])
        to_t = jnp.where(lower, mm(other_t, to_t), to_t)
        gain = jnp.where(lower, carry(other_t, gain, other), gain)
    else:
        to_t = jnp.where(lower, other_ref[:size, :], eye)
        gain = jnp.where(lower, other, 0.0)
    own_at = pl.ds(pl.multiple_of(row_at * own_cols, own_cols), own_cols)
    own_rows = pl.ds(pl.multiple_of(row_at * rows, rows), rows)
    late_rows = pl.ds(pl.multiple_of(late_at * rows, rows), rows)
    for p in range(panels - 1, -1, -1):
        late_map_ref[:, :size] = late_ref[p]
        late_map_ref[:, size:] = rest_ref[p]
        _, place = order_of(chosen_of(p, fill_ref, prior_ref), width // BLOCK)
        map_ref[...] = maps_ref[p]
        for t in range(len(place) // 2):
            map_ref[late_rows, t * LANES : (t + 1) * LANES] = two_blocks(
                tile_of(late_map_ref), place[2 * t], place[2 * t + 1]
            )
        whole = split(map_ref[...])
        own_t = split(map_ref[:, own_at].T)
        scratch[:, :size] = to_t
        scratch[:, size:] = gain
        to_parts = split(to_t)
        cross = jnp.concatenate(
            [
                jnp.full((BLOCK, size), -mask_ref[p, slot].astype(F32))
                for slot in slots_of(tuple(range(size // rows)), rows)
            ],
            0,
        )
        left = jnp.concatenate([scratch[own_rows, :size] * cross, mm(own_t, to_parts)], 0)
        part = slice(p * left.shape[0], (p + 1) * left.shape[0])
        left_high[part, :], left_low[part, :] = split(left)
        right_high[p], right_low[p] = split(mm(to_parts, whole, TN))
        gains = jnp.concatenate([scratch[own_rows, size:] * cross, mm(own_t, gain)], 0)
        const = mm(gains, whole)
        const_ref[p, :rows, :] = const[:rows]
        const_ref[p, rows:, :] = const[rows:] + own_refs[p][...]
        if p > 0:
            link_t = split(links_t_ref[p])
            to_t = mm(link_t, to_t)
            gain = carry(link_t, gain, base_refs[p][...])


def finish_kernel(levels, after_ref, after_other_ref, *refs):
    left_high, left_low, right_high, right_low, const_ref, diag_hbm, off_hbm = refs[:7]
    diag_ref, off_ref, sems = refs[7:]
    panels, total, _ = const_ref.shape
    rows = off_ref.shape[1]
    chip = lax.axis_index("seg") // 2
    after = from_halves(after_ref[...], after_other_ref[...])
    after = unpack(jnp.where((chip & ((1 << levels) // 2)) == 0, after, 0.0))
    inner = split(mm((left_high[...], left_low[...]), after))
    copies = []
    for p in range(panels):
        part = slice(p * total, (p + 1) * total)
        right = (right_high[p], right_low[p])
        result = mm((inner[0][part], inner[1][part]), right) + const_ref[p]
        diag_ref[p] = result[rows:]
        off_ref[p] = result[:rows]
        copies.append(pltpu.make_async_copy(diag_ref.at[p], diag_hbm.at[p], sems.at[p, 0]))
        copies.append(pltpu.make_async_copy(off_ref.at[p], off_hbm.at[p], sems.at[p, 1]))
        copies[-2].start()
        copies[-1].start()
    for copy in copies:
        copy.wait()


def body(fill_blocks, fill_mask, inv_diag, factor_off):
    panels, width, _ = inv_diag.shape
    rows = factor_off.shape[1]
    seg_count = lax.axis_size("seg")
    row_count = lax.axis_size("row")
    size = rows * row_count
    own_cols = width // row_count
    slots = fill_blocks.shape[1]
    chosen_cols = slots * BLOCK
    chips = seg_count // 2
    half = size // 2

    def turn(x, axis, distance):
        count = lax.axis_size(axis)
        return lax.ppermute(x, axis, [(i, (i + distance) % count) for i in range(count)])

    pick = jax.ShapeDtypeStruct((width, chosen_cols), BF16)
    short = row_count == 4
    far = row_count // 2
    whose = [tuple((i - d) % row_count for i in range(row_count)) for d in range(row_count)]
    inv, high, low, keep = call(
        functools.partial(load_kernel, whose[1] if short else whose[far]),
        [
            shape(*inv_diag.shape), pick, pick, shape(panels, rows, chosen_cols),
        ],
        [],
        [],
        far=[fill_mask, fill_blocks, inv_diag],
        scratch=[
            pltpu.SMEM(fill_mask.shape, jnp.int32),
            pltpu.SMEM(fill_blocks.shape, jnp.int32),
            pltpu.SemaphoreType.DMA((panels + 2,)),
        ],
        name="load",
    )
    prior_fill = turn(fill_blocks, "seg", 1)
    picks, bases, priors = [], [], []
    for p in range(panels):
        high_low = [high, low]
        if p < panels - 1:
            high_low = call(
                functools.partial(pick_kernel, p),
                [pick, pick],
                [fill_blocks] if p else [fill_blocks, prior_fill],
                [inv],
                name="pick",
            )
        base, own_prior, token = call(
            functools.partial(prior_kernel, p),
            [shape(chosen_cols, chosen_cols), shape(own_cols, width), shape(1, 1, width)],
            [],
            [*high_low, inv],
            anywhere=[prior_fill],
            name="prior",
        )
        picks += high_low
        bases.append(base)
        priors.append(own_prior)
    ups, downs = [factor_off], [factor_off + token]
    for _ in range(row_count // 2 - short):
        ups.append(turn(ups[-1], "row", 1))
    for _ in range((row_count - 1) // 2):
        downs.append(turn(downs[-1], "row", -1))
    came = [d for d in range(row_count) if d != far]
    plan = Plan(tuple(whose[d] for d in came), whose[far])
    parts = ups[:far] + downs[:0:-1]
    (late,) = call(
        chosen_kernel,
        [shape(panels, rows, chosen_cols)],
        [],
        [ups[-1], keep, *picks],
        flops=96 * panels * rows * chosen_cols * width,
        name="chosen",
    )
    if short:
        late = turn(late, "row", 1)
    (links,) = call(
        functools.partial(links_kernel, plan),
        [shape(panels, size, size)],
        [fill_mask],
        [*parts, *picks],
        scratch=[pltpu.VMEM((size, chosen_cols), F32)],
        name="links",
    )
    links_t, own_whole = call(
        functools.partial(segment_kernel, plan, panels),
        [shape(panels, size, size), shape(2 * size, size)],
        [],
        [late, links, *bases],
        flops=18 * (panels - 1) * size**3,
        name="segment",
    )
    maps, maps_token = call(
        functools.partial(maps_kernel, plan),
        [shape(panels, size, width), shape(1, half)],
        [fill_mask],
        [inv, *parts],
        scratch=[pltpu.VMEM((size, width), F32)],
        flops=6 * panels * size * width * width,
        mib=24,
        name="maps",
    )
    swap = [(i, i ^ 1) for i in range(seg_count)]
    other_whole = lax.ppermute(own_whole, "seg", swap)
    half_packed = shape(5 * half // 4, half)
    half_link = shape(half, size)
    link_t, cov, send, send_t = call(
        chip_kernel,
        [shape(size, size), shape(size, size), half_packed, half_link],
        [],
        [own_whole, other_whole],
        flops=18 * size**3,
        name="chip",
    )
    held = [ups[-1], downs[-1]] if short else [ups[-1]]
    held_by = whose[far]
    if short:
        held_by = tuple(whose[-1][i] if i % 2 else whose[1][i] for i in range(row_count))
    (rest,) = call(
        functools.partial(rest_kernel, held_by),
        [shape(panels, rows, width - chosen_cols)],
        [fill_mask, fill_blocks, prior_fill],
        [inv, *held, send],
        scratch=[pltpu.VMEM((rows, width), F32)],
        flops=6 * panels * rows * width * width,
        mib=24,
        name="rest",
    )
    if short:
        rest = lax.ppermute(rest, "row", [(i, i ^ 1) for i in range(row_count)])
    past = None
    after = (jnp.zeros(half_packed.shape, F32),) * 2
    levels = (chips - 1).bit_length()
    prepared = None

    def prepare():
        total = rows + own_cols
        left = jax.ShapeDtypeStruct((panels * total, size), BF16)
        right = jax.ShapeDtypeStruct((panels, size, width), BF16)
        return call(
            functools.partial(prepare_kernel, plan, levels, panels),
            [left, left, right, right, shape(panels, total, width), shape(1, half)],
            [fill_mask, fill_blocks, prior_fill],
            [*bases, *priors, other_whole, maps, links_t, late, rest, *(past or ())],
            scratch=[
                pltpu.VMEM((size, width), F32),
                pltpu.VMEM((size, width), F32),
                pltpu.VMEM((rows, width), F32),
            ],
            flops=6 * panels * size * (total * size + size * width + total * width + 3 * size * size),
            mib=24,
            name="prepare",
        )

    for level in range(levels):
        partner = [(i, i ^ (2 << level)) for i in range(seg_count)]
        got = lax.ppermute(send, "seg", partner)
        if level == levels - 1:
            *prepared, token = prepare()
            got = got + token
            after = (got, lax.ppermute(got, "seg", swap))
            break
        got_t = lax.ppermute(send_t, "seg", partner)
        if level == 0:
            got = got + maps_token
        got = (got_t, lax.ppermute(got_t, "seg", swap), got, lax.ppermute(got, "seg", swap))
        outs = [half_packed]
        if level < levels - 2:
            outs += [half_link, shape(size, size), shape(size, size)]
        send, *more = call(
            functools.partial(merge_kernel, level), outs, [], [link_t, cov, *got],
            flops=18 * size**3, name="merge",
        )
        if more:
            send_t, link_t, cov = more
        if past is None:
            past = got
        else:
            past = call(
                functools.partial(join_kernel, level),
                [half_link, half_link, half_packed, half_packed],
                [],
                [*past, *got],
                flops=18 * size**3,
                name="join",
            )
    if prepared is None:
        *prepared, _ = prepare()
    diag, off = call(
        functools.partial(finish_kernel, levels),
        [shape(panels, own_cols, width), shape(panels, rows, width)],
        [],
        [*after, *prepared],
        out_far=True,
        scratch=[
            pltpu.VMEM((panels, own_cols, width), F32),
            pltpu.VMEM((panels, rows, width), F32),
            pltpu.SemaphoreType.DMA((panels, 2)),
        ],
        flops=6 * panels * (rows + own_cols) * size * (size + width),
        name="finish",
    )
    return diag, off


def solution(mesh):
    placed = (P("seg", None), P("seg", None), P("seg", None, None), P("seg", "row", None))
    return jax.shard_map(
        body,
        mesh=mesh,
        in_specs=placed,
        out_specs=(P("seg", "row", None), P("seg", "row", None)),
        check_vma=False,
    )
```

```python
import functools
from typing import NamedTuple

import jax
import jax.numpy as jnp
from jax import lax
from jax.experimental import pallas as pl
from jax.experimental.pallas import tpu as pltpu
from jax.sharding import PartitionSpec as P

BLOCK = 64
LANES = 128
F32 = jnp.float32
BF16 = jnp.bfloat16
NN = (((1,), (0,)), ((), ()))
NT = (((1,), (1,)), ((), ()))
TN = (((0,), (0,)), ((), ()))


def split(x):
    high = x.astype(BF16)
    return high, (x - high.astype(F32)).astype(BF16)


def mm(a, b, dims=NN):
    a = a if isinstance(a, tuple) else split(a)
    b = b if isinstance(b, tuple) else split(b)
    dot = functools.partial(lax.dot_general, dimension_numbers=dims, preferred_element_type=F32)
    return dot(a[0], b[0]) + (dot(a[0], b[1]) + dot(a[1], b[0]))


def carry(link_t, cov, base):
    link_t = link_t if isinstance(link_t, tuple) else split(link_t)
    return mm(mm(link_t, cov), link_t, NT) + base


def pack(cov):
    half = cov.shape[0] // 2
    part = half // 2
    first, second = cov[:half, :half], cov[half:, half:]
    lane = lax.broadcasted_iota(jnp.int32, (part, half), 1)
    last = jnp.where(lane < part, pltpu.roll(first[part:], part, 1), second[part:])
    return jnp.concatenate([cov[:half, half:], first[:part], second[:part], last], 0)


def unpack(packed):
    half = packed.shape[1]
    part = half // 2
    cross, last = packed[:half], packed[2 * half :]
    row = lax.broadcasted_iota(jnp.int32, (half, half), 0)
    lane = lax.broadcasted_iota(jnp.int32, (half, half), 1)

    def symmetric(top, bottom):
        upper = jnp.concatenate([top, bottom], 0)
        return jnp.where((row < part) | (lane >= part), upper, upper.T)

    first = symmetric(packed[half : half + part], pltpu.roll(last, part, 1))
    second = symmetric(packed[half + part : 2 * half], last)
    top = jnp.concatenate([first, cross], 1)
    bottom = jnp.concatenate([cross.T, second], 1)
    return jnp.concatenate([top, bottom], 0)


def is_lower():
    return (lax.axis_index("seg") & 1) == 0


def from_halves(own, other):
    lower = is_lower()
    return jnp.concatenate([jnp.where(lower, own, other), jnp.where(lower, other, own)], 0)


def own_half(whole):
    half = whole.shape[0] // 2
    return jnp.where(is_lower(), whole[:half], whole[half:])


def two_blocks(load, left, right):
    def placed(block, half):
        slab = load(lax.shift_right_logical(block, 1))
        return jnp.where((block & 1) == half, slab, pltpu.roll(slab, BLOCK, 1))

    a, b = placed(left, 0), placed(right, 1)
    lane = lax.broadcasted_iota(jnp.int32, a.shape, 1)
    return jnp.where(lane < BLOCK, a, b)


def tile_of(ref, *lead):
    def load(tile):
        return ref[(*lead, slice(None), pl.ds(pl.multiple_of(tile * LANES, LANES), LANES))]

    return load


def chosen_of(panel, fill_ref, prior_ref=None):
    slots = fill_ref.shape[1]
    if panel > 0:
        return [fill_ref[panel - 1, j] for j in range(slots)]
    first = lax.axis_index("seg") == 0
    last = prior_ref.shape[0] - 1
    return [jnp.where(first, fill_ref[0, j], prior_ref[last, j]) for j in range(slots)]


def order_of(chosen, blocks):
    slots = len(chosen)
    rest = [jnp.int32(0)] * (blocks - slots)
    place = []
    seen = jnp.int32(0)
    for b in range(blocks):
        hit = jnp.int32(0)
        where = jnp.int32(0)
        for j in range(slots):
            same = (chosen[j] == b).astype(jnp.int32)
            hit = hit + same
            where = where + same * j
        free = 1 - hit
        for q in range(blocks - slots):
            rest[q] = rest[q] + jnp.where(seen == q, free * b, 0)
        place.append(jnp.where(hit > 0, where, slots + seen))
        seen = seen + free
    return rest, place


def vmem(count):
    return [pl.BlockSpec(memory_space=pltpu.VMEM)] * count


def smem(count):
    return [pl.BlockSpec(memory_space=pltpu.SMEM)] * count


def call(
    kernel, outs, scalars, arrays, far=(), anywhere=(), out_far=False, through=(), scratch=(), flops=0, mib=16, name=None
):
    moved = sum(a.size * 4 for a in (*arrays, *far)) + sum(o.size * 4 for o in outs)
    first = len(scalars) + len(arrays) + len(far) + len(anywhere)
    count = len(through)

    def inner(*refs):
        kernel(*refs[:first], *refs[first + count : first + count + len(outs)], *refs[first + 2 * count + len(outs) :])

    return pl.pallas_call(
        inner,
        out_shape=[*outs, *(jax.ShapeDtypeStruct(a.shape, a.dtype) for a in through)],
        in_specs=smem(len(scalars))
        + vmem(len(arrays))
        + [pl.BlockSpec(memory_space=pltpu.HBM)] * len(far)
        + [pl.BlockSpec(memory_space=pl.ANY)] * len(anywhere)
        + [pl.BlockSpec(memory_space=pl.ANY)] * count,
        out_specs=([pl.BlockSpec(memory_space=pltpu.HBM)] * len(outs) if out_far else vmem(len(outs)))
        + [pl.BlockSpec(memory_space=pl.ANY)] * count,
        scratch_shapes=list(scratch),
        input_output_aliases={first + i: len(outs) + i for i in range(count)},
        cost_estimate=pl.CostEstimate(flops=flops, bytes_accessed=moved, transcendentals=0),
        compiler_params=pltpu.CompilerParams(vmem_limit_bytes=mib << 20),
        name=name,
    )(*scalars, *arrays, *(pltpu.with_memory_space_constraint(a, pltpu.HBM) for a in far), *anywhere, *through)


def shape(*dims):
    return jax.ShapeDtypeStruct(dims, F32)


def kept_rows(mask_ref, panel, slot, rows):
    alive = lax.axis_index("seg") * mask_ref.shape[0] + panel < (
        lax.axis_size("seg") * mask_ref.shape[0] - 1
    )
    return rows * (mask_ref[panel, slot].astype(F32) * alive.astype(F32))


def triangular_mm(left, lower):
    cut = left.shape[1] // 2
    first, second = split(left[:, :cut]), split(left[:, cut:])
    below = split(lower[cut:, :])
    return jnp.concatenate(
        [
            mm(second, (below[0][:, :cut], below[1][:, :cut])) + mm(first, lower[:cut, :cut]),
            mm(second, (below[0][:, cut:], below[1][:, cut:])),
        ],
        1,
    )


def pick_into(high_ref, low_ref, chosen, *inv_at):
    for t in range(len(chosen) // 2):
        columns = slice(t * LANES, (t + 1) * LANES)
        high_ref[:, columns], low_ref[:, columns] = split(
            two_blocks(tile_of(*inv_at), chosen[2 * t], chosen[2 * t + 1])
        )


def load_kernel(
    owners, mask_hbm, fill_hbm, inv_hbm, inv_ref, high_ref, low_ref, *refs
):
    keep_refs, (mask_ref, fill_ref, sems) = refs[:-3], refs[-3:]
    panels, rows, _ = keep_refs[0].shape
    small = [
        pltpu.make_async_copy(fill_hbm, fill_ref, sems.at[panels]),
        pltpu.make_async_copy(mask_hbm, mask_ref, sems.at[panels + 1]),
    ]
    large = [
        pltpu.make_async_copy(inv_hbm.at[p], inv_ref.at[p], sems.at[p]) for p in range(panels)
    ]
    for copy in (*small, *reversed(large)):
        copy.start()
    for copy in small:
        copy.wait()
    for p in range(panels):
        for block_owners, keep_ref in zip(owners, keep_refs):
            for s, slot in enumerate(slots_of(block_owners, rows)):
                ones = jnp.ones((BLOCK, keep_ref.shape[2]), F32)
                keep_ref[p, s * BLOCK : (s + 1) * BLOCK, :] = kept_rows(mask_ref, p, slot, ones)
    large[-1].wait()
    pick_into(high_ref, low_ref, chosen_of(panels - 1, fill_ref), inv_ref, panels - 1)
    for copy in large[:-1]:
        copy.wait()


def pick_kernel(panel, *refs):
    *scalar_refs, inv_ref, high_ref, low_ref = refs
    pick_into(high_ref, low_ref, chosen_of(panel, *scalar_refs), inv_ref, panel)


def gate_kernel(_, token_ref):
    token_ref[...] = jnp.zeros_like(token_ref)


def prior_kernel(panel, high_ref, low_ref, inv_ref, base_ref, own_ref):
    own_cols = own_ref.shape[0]
    own_at = pl.ds(pl.multiple_of(lax.axis_index("row") * own_cols, own_cols), own_cols)
    picked = (high_ref[...], low_ref[...])
    base_ref[...] = mm(picked, picked, TN)
    own_ref[...] = mm(inv_ref[panel, :, own_at], inv_ref[panel], TN)


class Plan(NamedTuple):
    early: tuple
    late: tuple


def at_row(table):
    value = jnp.int32(table[0])
    for i, entry in enumerate(table[1:], 1):
        value = jnp.where(lax.axis_index("row") == i, entry, value)
    return value


def slots_of(owners, rows):
    first = at_row(owners) * (rows // BLOCK)
    return [first + s for s in range(rows // BLOCK)]


def put_rows(mask_ref, panel, owners, part, out_ref, take):
    for s, slot in enumerate(slots_of(owners, part.shape[0])):
        kept = kept_rows(mask_ref, panel, slot, part[s * BLOCK : (s + 1) * BLOCK, :])
        out_ref[pl.ds(pl.multiple_of(slot * BLOCK, BLOCK), BLOCK), :] = take(kept)


def links_kernel(plan, mask_ref, *refs):
    count = len(plan.early) - 1
    parts, (*pick_refs, links_ref) = refs[:count], refs[count:]
    links_ref[...] = jnp.zeros_like(links_ref)
    for p in range(links_ref.shape[0]):
        pick = (pick_refs[2 * p][...], pick_refs[2 * p + 1][...])
        for owners, part in zip(plan.early[:-1], parts):
            put_rows(mask_ref, p, owners, part[p], links_ref.at[p], lambda kept: mm(kept, pick))


def kept_block(mask_ref, panel, owners, part):
    return jnp.concatenate(
        [
            kept_rows(mask_ref, panel, slot, part[s * BLOCK : (s + 1) * BLOCK, :])
            for s, slot in enumerate(slots_of(owners, part.shape[0]))
        ],
        0,
    )


def chosen_kernel(part, keep_ref, *refs):
    *pick_refs, out_ref = refs
    for p in range(out_ref.shape[0]):
        pick = (pick_refs[2 * p][...], pick_refs[2 * p + 1][...])
        out_ref[p] = mm(part[p], pick) * keep_ref[p]


def rest_kernel(owners, mask_ref, fill_ref, prior_ref, inv_ref, *refs):
    *parts, _, out_ref, map_ref = refs
    odd = (lax.axis_index("row") & 1) == 1
    for p in range(out_ref.shape[0]):
        part = parts[0][p] if len(parts) == 1 else jnp.where(odd, parts[1][p], parts[0][p])
        map_ref[...] = triangular_mm(kept_block(mask_ref, p, owners, part), inv_ref[p])
        rest, _ = order_of(chosen_of(p, fill_ref, prior_ref), map_ref.shape[1] // BLOCK)
        for t in range(len(rest) // 2):
            out_ref[p, :, t * LANES : (t + 1) * LANES] = two_blocks(
                tile_of(map_ref), rest[2 * t], rest[2 * t + 1]
            )


def segment_kernel(plan, panels, early_ref, second_ref, keep_ref, late_ref, *refs):
    pick_refs, base_refs = refs[: 2 * panels], refs[2 * panels : 3 * panels]
    links_t_ref, whole_ref, rows_ref = refs[3 * panels :]
    size = links_t_ref.shape[1]
    rows = late_ref.shape[1]
    second_at, late_at = (
        pl.ds(pl.multiple_of(at_row(owners) * rows, rows), rows)
        for owners in (plan.early[-1], plan.late)
    )
    cov = link_t = None
    for p in range(panels - 1, -1, -1):
        pick = (pick_refs[2 * p][...], pick_refs[2 * p + 1][...])
        rows_ref[p] = early_ref[p]
        rows_ref[p, second_at, :] = mm(second_ref[p], pick) * keep_ref[p]
        rows_ref[p, late_at, :] = late_ref[p]
        own_t = rows_ref[p].T
        links_t_ref[p] = own_t
        if cov is None:
            cov, link_t = base_refs[p][...], own_t
        else:
            own_t = split(own_t)
            cov = carry(own_t, cov, base_refs[p][...])
            link_t = mm(own_t, link_t)
    whole_ref[:size] = link_t
    whole_ref[size:] = cov


def maps_kernel(plan, mask_ref, inv_ref, *refs):
    *parts, maps_ref, token_ref, rows_ref = refs
    token_ref[...] = jnp.zeros_like(token_ref)
    rows_ref[...] = jnp.zeros_like(rows_ref)
    for p in range(inv_ref.shape[0]):
        for owners, part in zip(plan.early, parts):
            put_rows(mask_ref, p, owners, part[p], rows_ref, lambda kept: kept)
        maps_ref[p] = triangular_mm(rows_ref[...], inv_ref[p])


def chip_kernel(own_ref, other_ref, link_t_ref, cov_ref, packed_ref, half_t_ref):
    size = cov_ref.shape[0]
    lower = is_lower()
    own_t, other_t = own_ref[:size, :], other_ref[:size, :]
    own, other = own_ref[size:, :], other_ref[size:, :]
    down_t = split(jnp.where(lower, own_t, other_t))
    cov = carry(down_t, jnp.where(lower, other, own), jnp.where(lower, own, other))
    link_t = mm(down_t, jnp.where(lower, other_t, own_t))
    link_t_ref[...] = link_t
    cov_ref[...] = cov
    packed_ref[...] = own_half(pack(cov))
    half_t_ref[...] = own_half(link_t)


def merge_kernel(level, link_t_ref, cov_ref, *refs):
    got_t = from_halves(refs[0][...], refs[1][...])
    got = unpack(from_halves(refs[2][...], refs[3][...]))
    own_t, own = link_t_ref[...], cov_ref[...]
    lower = (lax.shift_right_logical(lax.axis_index("seg") // 2, level) & 1) == 0
    down_t = split(jnp.where(lower, own_t, got_t))
    cov = carry(down_t, jnp.where(lower, got, own), jnp.where(lower, own, got))
    refs[4][...] = own_half(pack(cov))
    if len(refs) > 5:
        link_t = mm(down_t, jnp.where(lower, got_t, own_t))
        refs[5][...] = own_half(link_t)
        refs[6][...] = link_t
        refs[7][...] = cov


def join_kernel(level, *refs):
    past_t, past, link_t, cov = (
        from_halves(refs[2 * i][...], refs[2 * i + 1][...]) for i in range(4)
    )
    chip = lax.axis_index("seg") // 2
    below = (lax.shift_right_logical(chip, level) & 1) == 0
    known = (chip & ((1 << level) - 1)) != (1 << level) - 1
    past_parts = split(past_t)
    joined = pack(carry(past_parts, unpack(cov), unpack(past)))
    joined_t = mm(past_parts, link_t)
    out_t = jnp.where(below, jnp.where(known, joined_t, link_t), past_t)
    out = jnp.where(below, jnp.where(known, joined, cov), past)
    for i, whole in enumerate((out_t, out)):
        half = whole.shape[0] // 2
        refs[8 + 2 * i][...] = own_half(whole)
        refs[9 + 2 * i][...] = jnp.where(is_lower(), whole[half:], whole[:half])


def prepare_kernel(plan, levels, panels, mask_ref, fill_ref, prior_ref, *refs):
    base_refs, own_refs, refs = refs[:panels], refs[panels : 2 * panels], refs[2 * panels :]
    (other_ref, maps_ref, links_t_ref, late_ref, rest_ref), refs = refs[:5], refs[5:]
    past_refs, refs = refs[: 4 * (levels > 1)], refs[4 * (levels > 1) :]
    left_high, left_low, right_high, right_low, const_ref, token_ref, scratch, map_ref, late_map_ref = refs
    token_ref[...] = jnp.zeros_like(token_ref)
    own_cols, width = own_refs[0].shape
    late_at = at_row(plan.late)
    size = base_refs[0].shape[0]
    row_at = lax.axis_index("row")
    rows = left_high.shape[0] // panels - own_cols
    row = lax.broadcasted_iota(jnp.int32, (size, size), 0)
    column = lax.broadcasted_iota(jnp.int32, (size, size), 1)
    eye = (row == column).astype(F32)
    other = other_ref[size:, :]
    lower = is_lower()
    if past_refs:
        chip = lax.axis_index("seg") // 2
        low = (1 << (levels - 1)) - 1
        known = (chip & low) != low
        past_t = from_halves(past_refs[0][...], past_refs[1][...])
        past = unpack(from_halves(past_refs[2][...], past_refs[3][...]))
        to_t = jnp.where(known, past_t, eye)
        gain = jnp.where(known, past, 0.0)
        other_t = split(other_ref[:size, :])
        to_t = jnp.where(lower, mm(other_t, to_t), to_t)
        gain = jnp.where(lower, carry(other_t, gain, other), gain)
    else:
        to_t = jnp.where(lower, other_ref[:size, :], eye)
        gain = jnp.where(lower, other, 0.0)
    own_at = pl.ds(pl.multiple_of(row_at * own_cols, own_cols), own_cols)
    own_rows = pl.ds(pl.multiple_of(row_at * rows, rows), rows)
    late_rows = pl.ds(pl.multiple_of(late_at * rows, rows), rows)
    for p in range(panels - 1, -1, -1):
        late_map_ref[:, :size] = late_ref[p]
        late_map_ref[:, size:] = rest_ref[p]
        _, place = order_of(chosen_of(p, fill_ref, prior_ref), width // BLOCK)
        map_ref[...] = maps_ref[p]
        for t in range(len(place) // 2):
            map_ref[late_rows, t * LANES : (t + 1) * LANES] = two_blocks(
                tile_of(late_map_ref), place[2 * t], place[2 * t + 1]
            )
        whole = split(map_ref[...])
        own_t = split(map_ref[:, own_at].T)
        scratch[:, :size] = to_t
        scratch[:, size:] = gain
        to_parts = split(to_t)
        cross = jnp.concatenate(
            [
                jnp.full((BLOCK, size), -mask_ref[p, slot].astype(F32))
                for slot in slots_of(tuple(range(size // rows)), rows)
            ],
            0,
        )
        left = jnp.concatenate([scratch[own_rows, :size] * cross, mm(own_t, to_parts)], 0)
        part = slice(p * left.shape[0], (p + 1) * left.shape[0])
        left_high[part, :], left_low[part, :] = split(left)
        right_high[p], right_low[p] = split(mm(to_parts, whole, TN))
        gains = jnp.concatenate([scratch[own_rows, size:] * cross, mm(own_t, gain)], 0)
        const = mm(gains, whole)
        const_ref[p, :rows, :] = const[:rows]
        const_ref[p, rows:, :] = const[rows:] + own_refs[p][...]
        if p > 0:
            link_t = split(links_t_ref[p])
            to_t = mm(link_t, to_t)
            gain = carry(link_t, gain, base_refs[p][...])


def finish_kernel(levels, after_ref, after_other_ref, *refs):
    left_high, left_low, right_high, right_low, const_ref, diag_hbm, off_hbm = refs[:7]
    diag_ref, off_ref, sems = refs[7:]
    panels, total, _ = const_ref.shape
    rows = off_ref.shape[1]
    chip = lax.axis_index("seg") // 2
    after = from_halves(after_ref[...], after_other_ref[...])
    after = unpack(jnp.where((chip & ((1 << levels) // 2)) == 0, after, 0.0))
    inner = split(mm((left_high[...], left_low[...]), after))
    copies = []
    for p in range(panels):
        part = slice(p * total, (p + 1) * total)
        right = (right_high[p], right_low[p])
        result = mm((inner[0][part], inner[1][part]), right) + const_ref[p]
        diag_ref[p] = result[rows:]
        off_ref[p] = result[:rows]
        copies.append(pltpu.make_async_copy(diag_ref.at[p], diag_hbm.at[p], sems.at[p, 0]))
        copies.append(pltpu.make_async_copy(off_ref.at[p], off_hbm.at[p], sems.at[p, 1]))
        copies[-2].start()
        copies[-1].start()
    for copy in copies:
        copy.wait()


def body(fill_blocks, fill_mask, inv_diag, factor_off):
    panels, width, _ = inv_diag.shape
    rows = factor_off.shape[1]
    seg_count = lax.axis_size("seg")
    row_count = lax.axis_size("row")
    size = rows * row_count
    own_cols = width // row_count
    slots = fill_blocks.shape[1]
    chosen_cols = slots * BLOCK
    chips = seg_count // 2
    half = size // 2

    def turn(x, axis, distance):
        count = lax.axis_size(axis)
        return lax.ppermute(x, axis, [(i, (i + distance) % count) for i in range(count)])

    pick = jax.ShapeDtypeStruct((width, chosen_cols), BF16)
    short = row_count == 4
    far = row_count // 2
    whose = [tuple((i - d) % row_count for i in range(row_count)) for d in range(row_count)]
    came = [d for d in range(row_count) if d != far]
    plan = Plan(tuple(whose[d] for d in came), whose[far])
    keeps = shape(panels, rows, chosen_cols)
    inv, high, low, keep, keep_second = call(
        functools.partial(load_kernel, (whose[1] if short else whose[far], plan.early[-1])),
        [shape(*inv_diag.shape), pick, pick, keeps, keeps],
        [],
        [],
        far=[fill_mask, fill_blocks, inv_diag],
        scratch=[
            pltpu.SMEM(fill_mask.shape, jnp.int32),
            pltpu.SMEM(fill_blocks.shape, jnp.int32),
            pltpu.SemaphoreType.DMA((panels + 2,)),
        ],
        name="load",
    )
    prior_fill = turn(fill_blocks, "seg", 1)
    picks, bases, priors = [], [], []
    for p in range(panels):
        high_low = [high, low]
        if p < panels - 1:
            high_low = call(
                functools.partial(pick_kernel, p),
                [pick, pick],
                [fill_blocks] if p else [fill_blocks, prior_fill],
                [inv],
                name="pick",
            )
        base, own_prior = call(
            functools.partial(prior_kernel, p),
            [shape(chosen_cols, chosen_cols), shape(own_cols, width)],
            [],
            [*high_low, inv],
            name="prior",
        )
        picks += high_low
        bases.append(base)
        priors.append(own_prior)
    (token,) = call(gate_kernel, [shape(1, 1, width)], [], [], anywhere=[prior_fill], name="gate")
    ups, downs = [factor_off], [factor_off + token]
    for _ in range(row_count // 2 - short):
        ups.append(turn(ups[-1], "row", 1))
    for _ in range((row_count - 1) // 2):
        downs.append(turn(downs[-1], "row", -1))
    parts = ups[:far] + downs[:0:-1]
    (late,) = call(
        chosen_kernel,
        [shape(panels, rows, chosen_cols)],
        [],
        [ups[-1], keep, *picks],
        flops=96 * panels * rows * chosen_cols * width,
        name="chosen",
    )
    if short:
        late = turn(late, "row", 1)
    (links,) = call(
        functools.partial(links_kernel, plan),
        [shape(panels, size, size)],
        [fill_mask],
        [*parts[:-1], *picks],
        name="links",
    )
    links_t, own_whole = call(
        functools.partial(segment_kernel, plan, panels),
        [shape(panels, size, size), shape(2 * size, size)],
        [],
        [links, parts[-1], keep_second, late, *picks, *bases],
        scratch=[pltpu.VMEM((panels, size, size), F32)],
        flops=18 * (panels - 1) * size**3,
        name="segment",
    )
    maps, maps_token = call(
        functools.partial(maps_kernel, plan),
        [shape(panels, size, width), shape(1, half)],
        [fill_mask],
        [inv, *parts],
        scratch=[pltpu.VMEM((size, width), F32)],
        flops=6 * panels * size * width * width,
        mib=24,
        name="maps",
    )
    swap = [(i, i ^ 1) for i in range(seg_count)]
    other_whole = lax.ppermute(own_whole, "seg", swap)
    half_packed = shape(5 * half // 4, half)
    half_link = shape(half, size)
    link_t, cov, send, send_t = call(
        chip_kernel,
        [shape(size, size), shape(size, size), half_packed, half_link],
        [],
        [own_whole, other_whole],
        flops=18 * size**3,
        name="chip",
    )
    held = [ups[-1], downs[-1]] if short else [ups[-1]]
    held_by = whose[far]
    if short:
        held_by = tuple(whose[-1][i] if i % 2 else whose[1][i] for i in range(row_count))
    (rest,) = call(
        functools.partial(rest_kernel, held_by),
        [shape(panels, rows, width - chosen_cols)],
        [fill_mask, fill_blocks, prior_fill],
        [inv, *held, send],
        scratch=[pltpu.VMEM((rows, width), F32)],
        flops=6 * panels * rows * width * width,
        mib=24,
        name="rest",
    )
    if short:
        rest = lax.ppermute(rest, "row", [(i, i ^ 1) for i in range(row_count)])
    past = None
    after = (jnp.zeros(half_packed.shape, F32),) * 2
    levels = (chips - 1).bit_length()
    prepared = None

    def prepare():
        total = rows + own_cols
        left = jax.ShapeDtypeStruct((panels * total, size), BF16)
        right = jax.ShapeDtypeStruct((panels, size, width), BF16)
        return call(
            functools.partial(prepare_kernel, plan, levels, panels),
            [left, left, right, right, shape(panels, total, width), shape(1, half)],
            [fill_mask, fill_blocks, prior_fill],
            [*bases, *priors, other_whole, maps, links_t, late, rest, *(past or ())],
            scratch=[
                pltpu.VMEM((size, width), F32),
                pltpu.VMEM((size, width), F32),
                pltpu.VMEM((rows, width), F32),
            ],
            flops=6 * panels * size * (total * size + size * width + total * width + 3 * size * size),
            mib=24,
            name="prepare",
        )

    for level in range(levels):
        partner = [(i, i ^ (2 << level)) for i in range(seg_count)]
        got = lax.ppermute(send, "seg", partner)
        if level == levels - 1:
            *prepared, token = prepare()
            got = got + token
            after = (got, lax.ppermute(got, "seg", swap))
            break
        got_t = lax.ppermute(send_t, "seg", partner)
        if level == 0:
            got = got + maps_token
        got = (got_t, lax.ppermute(got_t, "seg", swap), got, lax.ppermute(got, "seg", swap))
        outs = [half_packed]
        if level < levels - 2:
            outs += [half_link, shape(size, size), shape(size, size)]
        send, *more = call(
            functools.partial(merge_kernel, level), outs, [], [link_t, cov, *got],
            flops=18 * size**3, name="merge",
        )
        if more:
            send_t, link_t, cov = more
        if past is None:
            past = got
        else:
            past = call(
                functools.partial(join_kernel, level),
                [half_link, half_link, half_packed, half_packed],
                [],
                [*past, *got],
                flops=18 * size**3,
                name="join",
            )
    if prepared is None:
        *prepared, _ = prepare()
    diag, off = call(
        functools.partial(finish_kernel, levels),
        [shape(panels, own_cols, width), shape(panels, rows, width)],
        [],
        [*after, *prepared],
        out_far=True,
        scratch=[
            pltpu.VMEM((panels, own_cols, width), F32),
            pltpu.VMEM((panels, rows, width), F32),
            pltpu.SemaphoreType.DMA((panels, 2)),
        ],
        flops=6 * panels * (rows + own_cols) * size * (size + width),
        name="finish",
    )
    return diag, off


def solution(mesh):
    placed = (P("seg", None), P("seg", None), P("seg", None, None), P("seg", "row", None))
    return jax.shard_map(
        body,
        mesh=mesh,
        in_specs=placed,
        out_specs=(P("seg", "row", None), P("seg", "row", None)),
        check_vma=False,
    )
```

```python
import functools
from typing import NamedTuple

import jax
import jax.numpy as jnp
from jax import lax
from jax.experimental import pallas as pl
from jax.experimental.pallas import tpu as pltpu
from jax.sharding import PartitionSpec as P

BLOCK = 64
LANES = 128
F32 = jnp.float32
BF16 = jnp.bfloat16
NN = (((1,), (0,)), ((), ()))
NT = (((1,), (1,)), ((), ()))
TN = (((0,), (0,)), ((), ()))


def split(x):
    high = x.astype(BF16)
    return high, (x - high.astype(F32)).astype(BF16)


def mm(a, b, dims=NN):
    a = a if isinstance(a, tuple) else split(a)
    b = b if isinstance(b, tuple) else split(b)
    dot = functools.partial(lax.dot_general, dimension_numbers=dims, preferred_element_type=F32)
    return dot(a[0], b[0]) + (dot(a[0], b[1]) + dot(a[1], b[0]))


def carry(link_t, cov, base):
    link_t = link_t if isinstance(link_t, tuple) else split(link_t)
    return mm(mm(link_t, cov), link_t, NT) + base


def pack(cov):
    half = cov.shape[0] // 2
    part = half // 2
    first, second = cov[:half, :half], cov[half:, half:]
    lane = lax.broadcasted_iota(jnp.int32, (part, half), 1)
    last = jnp.where(lane < part, pltpu.roll(first[part:], part, 1), second[part:])
    return jnp.concatenate([cov[:half, half:], first[:part], second[:part], last], 0)


def unpack(packed):
    half = packed.shape[1]
    part = half // 2
    cross, last = packed[:half], packed[2 * half :]
    row = lax.broadcasted_iota(jnp.int32, (half, half), 0)
    lane = lax.broadcasted_iota(jnp.int32, (half, half), 1)

    def symmetric(top, bottom):
        upper = jnp.concatenate([top, bottom], 0)
        return jnp.where((row < part) | (lane >= part), upper, upper.T)

    first = symmetric(packed[half : half + part], pltpu.roll(last, part, 1))
    second = symmetric(packed[half + part : 2 * half], last)
    top = jnp.concatenate([first, cross], 1)
    bottom = jnp.concatenate([cross.T, second], 1)
    return jnp.concatenate([top, bottom], 0)


def is_lower():
    return (lax.axis_index("seg") & 1) == 0


def from_halves(own, other):
    lower = is_lower()
    return jnp.concatenate([jnp.where(lower, own, other), jnp.where(lower, other, own)], 0)


def own_half(whole):
    half = whole.shape[0] // 2
    return jnp.where(is_lower(), whole[:half], whole[half:])


def two_blocks(load, left, right):
    def placed(block, half):
        slab = load(lax.shift_right_logical(block, 1))
        return jnp.where((block & 1) == half, slab, pltpu.roll(slab, BLOCK, 1))

    a, b = placed(left, 0), placed(right, 1)
    lane = lax.broadcasted_iota(jnp.int32, a.shape, 1)
    return jnp.where(lane < BLOCK, a, b)


def tile_of(ref, *lead):
    def load(tile):
        return ref[(*lead, slice(None), pl.ds(pl.multiple_of(tile * LANES, LANES), LANES))]

    return load


def chosen_of(panel, fill_ref, prior_ref=None):
    slots = fill_ref.shape[1]
    if panel > 0:
        return [fill_ref[panel - 1, j] for j in range(slots)]
    first = lax.axis_index("seg") == 0
    last = prior_ref.shape[0] - 1
    return [jnp.where(first, fill_ref[0, j], prior_ref[last, j]) for j in range(slots)]


def order_of(chosen, blocks):
    slots = len(chosen)
    rest = [jnp.int32(0)] * (blocks - slots)
    place = []
    seen = jnp.int32(0)
    for b in range(blocks):
        hit = jnp.int32(0)
        where = jnp.int32(0)
        for j in range(slots):
            same = (chosen[j] == b).astype(jnp.int32)
            hit = hit + same
            where = where + same * j
        free = 1 - hit
        for q in range(blocks - slots):
            rest[q] = rest[q] + jnp.where(seen == q, free * b, 0)
        place.append(jnp.where(hit > 0, where, slots + seen))
        seen = seen + free
    return rest, place


def vmem(count):
    return [pl.BlockSpec(memory_space=pltpu.VMEM)] * count


def smem(count):
    return [pl.BlockSpec(memory_space=pltpu.SMEM)] * count


def call(
    kernel, outs, scalars, arrays, far=(), anywhere=(), out_far=False, through=(), scratch=(), flops=0, mib=16, name=None
):
    moved = sum(a.size * 4 for a in (*arrays, *far)) + sum(o.size * 4 for o in outs)
    first = len(scalars) + len(arrays) + len(far) + len(anywhere)
    count = len(through)

    def inner(*refs):
        kernel(*refs[:first], *refs[first + count : first + count + len(outs)], *refs[first + 2 * count + len(outs) :])

    return pl.pallas_call(
        inner,
        out_shape=[*outs, *(jax.ShapeDtypeStruct(a.shape, a.dtype) for a in through)],
        in_specs=smem(len(scalars))
        + vmem(len(arrays))
        + [pl.BlockSpec(memory_space=pltpu.HBM)] * len(far)
        + [pl.BlockSpec(memory_space=pl.ANY)] * len(anywhere)
        + [pl.BlockSpec(memory_space=pl.ANY)] * count,
        out_specs=([pl.BlockSpec(memory_space=pltpu.HBM)] * len(outs) if out_far else vmem(len(outs)))
        + [pl.BlockSpec(memory_space=pl.ANY)] * count,
        scratch_shapes=list(scratch),
        input_output_aliases={first + i: len(outs) + i for i in range(count)},
        cost_estimate=pl.CostEstimate(flops=flops, bytes_accessed=moved, transcendentals=0),
        compiler_params=pltpu.CompilerParams(vmem_limit_bytes=mib << 20),
        name=name,
    )(*scalars, *arrays, *(pltpu.with_memory_space_constraint(a, pltpu.HBM) for a in far), *anywhere, *through)


def shape(*dims):
    return jax.ShapeDtypeStruct(dims, F32)


def kept_rows(mask_ref, panel, slot, rows):
    alive = lax.axis_index("seg") * mask_ref.shape[0] + panel < (
        lax.axis_size("seg") * mask_ref.shape[0] - 1
    )
    return rows * (mask_ref[panel, slot].astype(F32) * alive.astype(F32))


def triangular_mm(left, lower):
    cut = left.shape[1] // 2
    first, second = split(left[:, :cut]), split(left[:, cut:])
    below = split(lower[cut:, :])
    return jnp.concatenate(
        [
            mm(second, (below[0][:, :cut], below[1][:, :cut])) + mm(first, lower[:cut, :cut]),
            mm(second, (below[0][:, cut:], below[1][:, cut:])),
        ],
        1,
    )


def pick_into(high_ref, low_ref, chosen, *inv_at):
    for t in range(len(chosen) // 2):
        columns = slice(t * LANES, (t + 1) * LANES)
        high_ref[:, columns], low_ref[:, columns] = split(
            two_blocks(tile_of(*inv_at), chosen[2 * t], chosen[2 * t + 1])
        )


def load_kernel(
    owners, mask_hbm, fill_hbm, inv_hbm, inv_ref, high_ref, low_ref, *refs
):
    keep_refs, (mask_ref, fill_ref, sems) = refs[:-3], refs[-3:]
    panels, rows, _ = keep_refs[0].shape
    small = [
        pltpu.make_async_copy(fill_hbm, fill_ref, sems.at[panels]),
        pltpu.make_async_copy(mask_hbm, mask_ref, sems.at[panels + 1]),
    ]
    large = [
        pltpu.make_async_copy(inv_hbm.at[p], inv_ref.at[p], sems.at[p]) for p in range(panels)
    ]
    for copy in (*small, *reversed(large)):
        copy.start()
    for copy in small:
        copy.wait()
    for p in range(panels):
        for block_owners, keep_ref in zip(owners, keep_refs):
            for s, slot in enumerate(slots_of(block_owners, rows)):
                ones = jnp.ones((BLOCK, keep_ref.shape[2]), F32)
                keep_ref[p, s * BLOCK : (s + 1) * BLOCK, :] = kept_rows(mask_ref, p, slot, ones)
    large[-1].wait()
    pick_into(high_ref, low_ref, chosen_of(panels - 1, fill_ref), inv_ref, panels - 1)
    for copy in large[:-1]:
        copy.wait()


def pick_kernel(panel, *refs):
    *scalar_refs, inv_ref, high_ref, low_ref = refs
    pick_into(high_ref, low_ref, chosen_of(panel, *scalar_refs), inv_ref, panel)


def prior_kernel(panel, high_ref, low_ref, inv_ref, _, base_ref, own_ref, token_ref):
    token_ref[...] = jnp.zeros_like(token_ref)
    own_cols = own_ref.shape[0]
    own_at = pl.ds(pl.multiple_of(lax.axis_index("row") * own_cols, own_cols), own_cols)
    picked = (high_ref[...], low_ref[...])
    base_ref[...] = mm(picked, picked, TN)
    own_ref[...] = mm(inv_ref[panel, :, own_at], inv_ref[panel], TN)


class Plan(NamedTuple):
    early: tuple
    late: tuple


def at_row(table):
    value = jnp.int32(table[0])
    for i, entry in enumerate(table[1:], 1):
        value = jnp.where(lax.axis_index("row") == i, entry, value)
    return value


def slots_of(owners, rows):
    first = at_row(owners) * (rows // BLOCK)
    return [first + s for s in range(rows // BLOCK)]


def put_rows(mask_ref, panel, owners, part, out_ref, take):
    for s, slot in enumerate(slots_of(owners, part.shape[0])):
        kept = kept_rows(mask_ref, panel, slot, part[s * BLOCK : (s + 1) * BLOCK, :])
        out_ref[pl.ds(pl.multiple_of(slot * BLOCK, BLOCK), BLOCK), :] = take(kept)


def links_kernel(plan, mask_ref, *refs):
    count = len(plan.early) - 1
    parts, (*pick_refs, links_ref) = refs[:count], refs[count:]
    links_ref[...] = jnp.zeros_like(links_ref)
    for p in range(links_ref.shape[0]):
        pick = (pick_refs[2 * p][...], pick_refs[2 * p + 1][...])
        for owners, part in zip(plan.early[:-1], parts):
            put_rows(mask_ref, p, owners, part[p], links_ref.at[p], lambda kept: mm(kept, pick))


def kept_block(mask_ref, panel, owners, part):
    return jnp.concatenate(
        [
            kept_rows(mask_ref, panel, slot, part[s * BLOCK : (s + 1) * BLOCK, :])
            for s, slot in enumerate(slots_of(owners, part.shape[0]))
        ],
        0,
    )


def chosen_kernel(part, keep_ref, *refs):
    *pick_refs, out_ref = refs
    for p in range(out_ref.shape[0]):
        pick = (pick_refs[2 * p][...], pick_refs[2 * p + 1][...])
        out_ref[p] = mm(part[p], pick) * keep_ref[p]


def rest_kernel(owners, mask_ref, fill_ref, prior_ref, inv_ref, *refs):
    *parts, _, out_ref, map_ref = refs
    odd = (lax.axis_index("row") & 1) == 1
    for p in range(out_ref.shape[0]):
        part = parts[0][p] if len(parts) == 1 else jnp.where(odd, parts[1][p], parts[0][p])
        map_ref[...] = triangular_mm(kept_block(mask_ref, p, owners, part), inv_ref[p])
        rest, _ = order_of(chosen_of(p, fill_ref, prior_ref), map_ref.shape[1] // BLOCK)
        for t in range(len(rest) // 2):
            out_ref[p, :, t * LANES : (t + 1) * LANES] = two_blocks(
                tile_of(map_ref), rest[2 * t], rest[2 * t + 1]
            )


def segment_kernel(plan, panels, early_ref, second_ref, late_ref, *refs):
    base_refs, (links_t_ref, whole_ref, rows_ref) = refs[:panels], refs[panels:]
    size = links_t_ref.shape[1]
    rows = late_ref.shape[1]
    second_at, late_at = (
        pl.ds(pl.multiple_of(at_row(owners) * rows, rows), rows)
        for owners in (plan.early[-1], plan.late)
    )
    cov = link_t = None
    for p in range(panels - 1, -1, -1):
        rows_ref[p] = early_ref[p]
        rows_ref[p, second_at, :] = second_ref[p]
        rows_ref[p, late_at, :] = late_ref[p]
        own_t = rows_ref[p].T
        links_t_ref[p] = own_t
        if cov is None:
            cov, link_t = base_refs[p][...], own_t
        else:
            own_t = split(own_t)
            cov = carry(own_t, cov, base_refs[p][...])
            link_t = mm(own_t, link_t)
    whole_ref[:size] = link_t
    whole_ref[size:] = cov


def maps_kernel(plan, mask_ref, inv_ref, *refs):
    *parts, maps_ref, token_ref, rows_ref = refs
    token_ref[...] = jnp.zeros_like(token_ref)
    rows_ref[...] = jnp.zeros_like(rows_ref)
    for p in range(inv_ref.shape[0]):
        for owners, part in zip(plan.early, parts):
            put_rows(mask_ref, p, owners, part[p], rows_ref, lambda kept: kept)
        maps_ref[p] = triangular_mm(rows_ref[...], inv_ref[p])


def chip_kernel(own_ref, other_ref, link_t_ref, cov_ref, packed_ref, half_t_ref):
    size = cov_ref.shape[0]
    lower = is_lower()
    own_t, other_t = own_ref[:size, :], other_ref[:size, :]
    own, other = own_ref[size:, :], other_ref[size:, :]
    down_t = split(jnp.where(lower, own_t, other_t))
    cov = carry(down_t, jnp.where(lower, other, own), jnp.where(lower, own, other))
    link_t = mm(down_t, jnp.where(lower, other_t, own_t))
    link_t_ref[...] = link_t
    cov_ref[...] = cov
    packed_ref[...] = own_half(pack(cov))
    half_t_ref[...] = own_half(link_t)


def merge_kernel(level, link_t_ref, cov_ref, *refs):
    got_t = from_halves(refs[0][...], refs[1][...])
    got = unpack(from_halves(refs[2][...], refs[3][...]))
    own_t, own = link_t_ref[...], cov_ref[...]
    lower = (lax.shift_right_logical(lax.axis_index("seg") // 2, level) & 1) == 0
    down_t = split(jnp.where(lower, own_t, got_t))
    cov = carry(down_t, jnp.where(lower, got, own), jnp.where(lower, own, got))
    refs[4][...] = own_half(pack(cov))
    if len(refs) > 5:
        link_t = mm(down_t, jnp.where(lower, got_t, own_t))
        refs[5][...] = own_half(link_t)
        refs[6][...] = link_t
        refs[7][...] = cov


def join_kernel(level, *refs):
    past_t, past, link_t, cov = (
        from_halves(refs[2 * i][...], refs[2 * i + 1][...]) for i in range(4)
    )
    chip = lax.axis_index("seg") // 2
    below = (lax.shift_right_logical(chip, level) & 1) == 0
    known = (chip & ((1 << level) - 1)) != (1 << level) - 1
    past_parts = split(past_t)
    joined = pack(carry(past_parts, unpack(cov), unpack(past)))
    joined_t = mm(past_parts, link_t)
    out_t = jnp.where(below, jnp.where(known, joined_t, link_t), past_t)
    out = jnp.where(below, jnp.where(known, joined, cov), past)
    for i, whole in enumerate((out_t, out)):
        half = whole.shape[0] // 2
        refs[8 + 2 * i][...] = own_half(whole)
        refs[9 + 2 * i][...] = jnp.where(is_lower(), whole[half:], whole[:half])


def prepare_kernel(plan, levels, panels, mask_ref, fill_ref, prior_ref, *refs):
    base_refs, own_refs, refs = refs[:panels], refs[panels : 2 * panels], refs[2 * panels :]
    (other_ref, maps_ref, links_t_ref, late_ref, rest_ref), refs = refs[:5], refs[5:]
    past_refs, refs = refs[: 4 * (levels > 1)], refs[4 * (levels > 1) :]
    left_high, left_low, right_high, right_low, const_ref, token_ref, scratch, map_ref, late_map_ref = refs
    token_ref[...] = jnp.zeros_like(token_ref)
    own_cols, width = own_refs[0].shape
    late_at = at_row(plan.late)
    size = base_refs[0].shape[0]
    row_at = lax.axis_index("row")
    rows = left_high.shape[0] // panels - own_cols
    row = lax.broadcasted_iota(jnp.int32, (size, size), 0)
    column = lax.broadcasted_iota(jnp.int32, (size, size), 1)
    eye = (row == column).astype(F32)
    other = other_ref[size:, :]
    lower = is_lower()
    if past_refs:
        chip = lax.axis_index("seg") // 2
        low = (1 << (levels - 1)) - 1
        known = (chip & low) != low
        past_t = from_halves(past_refs[0][...], past_refs[1][...])
        past = unpack(from_halves(past_refs[2][...], past_refs[3][...]))
        to_t = jnp.where(known, past_t, eye)
        gain = jnp.where(known, past, 0.0)
        other_t = split(other_ref[:size, :])
        to_t = jnp.where(lower, mm(other_t, to_t), to_t)
        gain = jnp.where(lower, carry(other_t, gain, other), gain)
    else:
        to_t = jnp.where(lower, other_ref[:size, :], eye)
        gain = jnp.where(lower, other, 0.0)
    own_at = pl.ds(pl.multiple_of(row_at * own_cols, own_cols), own_cols)
    own_rows = pl.ds(pl.multiple_of(row_at * rows, rows), rows)
    late_rows = pl.ds(pl.multiple_of(late_at * rows, rows), rows)
    for p in range(panels - 1, -1, -1):
        late_map_ref[:, :size] = late_ref[p]
        late_map_ref[:, size:] = rest_ref[p]
        _, place = order_of(chosen_of(p, fill_ref, prior_ref), width // BLOCK)
        map_ref[...] = maps_ref[p]
        for t in range(len(place) // 2):
            map_ref[late_rows, t * LANES : (t + 1) * LANES] = two_blocks(
                tile_of(late_map_ref), place[2 * t], place[2 * t + 1]
            )
        whole = split(map_ref[...])
        own_t = split(map_ref[:, own_at].T)
        scratch[:, :size] = to_t
        scratch[:, size:] = gain
        to_parts = split(to_t)
        cross = jnp.concatenate(
            [
                jnp.full((BLOCK, size), -mask_ref[p, slot].astype(F32))
                for slot in slots_of(tuple(range(size // rows)), rows)
            ],
            0,
        )
        left = jnp.concatenate([scratch[own_rows, :size] * cross, mm(own_t, to_parts)], 0)
        part = slice(p * left.shape[0], (p + 1) * left.shape[0])
        left_high[part, :], left_low[part, :] = split(left)
        right_high[p], right_low[p] = split(mm(to_parts, whole, TN))
        gains = jnp.concatenate([scratch[own_rows, size:] * cross, mm(own_t, gain)], 0)
        const = mm(gains, whole)
        const_ref[p, :rows, :] = const[:rows]
        const_ref[p, rows:, :] = const[rows:] + own_refs[p][...]
        if p > 0:
            link_t = split(links_t_ref[p])
            to_t = mm(link_t, to_t)
            gain = carry(link_t, gain, base_refs[p][...])


def finish_kernel(levels, after_ref, after_other_ref, *refs):
    left_high, left_low, right_high, right_low, const_ref, diag_hbm, off_hbm = refs[:7]
    diag_ref, off_ref, sems = refs[7:]
    panels, total, _ = const_ref.shape
    rows = off_ref.shape[1]
    chip = lax.axis_index("seg") // 2
    after = from_halves(after_ref[...], after_other_ref[...])
    after = unpack(jnp.where((chip & ((1 << levels) // 2)) == 0, after, 0.0))
    inner = split(mm((left_high[...], left_low[...]), after))
    copies = []
    for p in range(panels):
        part = slice(p * total, (p + 1) * total)
        right = (right_high[p], right_low[p])
        result = mm((inner[0][part], inner[1][part]), right) + const_ref[p]
        diag_ref[p] = result[rows:]
        off_ref[p] = result[:rows]
        copies.append(pltpu.make_async_copy(diag_ref.at[p], diag_hbm.at[p], sems.at[p, 0]))
        copies.append(pltpu.make_async_copy(off_ref.at[p], off_hbm.at[p], sems.at[p, 1]))
        copies[-2].start()
        copies[-1].start()
    for copy in copies:
        copy.wait()


def body(fill_blocks, fill_mask, inv_diag, factor_off):
    panels, width, _ = inv_diag.shape
    rows = factor_off.shape[1]
    seg_count = lax.axis_size("seg")
    row_count = lax.axis_size("row")
    size = rows * row_count
    own_cols = width // row_count
    slots = fill_blocks.shape[1]
    chosen_cols = slots * BLOCK
    chips = seg_count // 2
    half = size // 2

    def turn(x, axis, distance):
        count = lax.axis_size(axis)
        return lax.ppermute(x, axis, [(i, (i + distance) % count) for i in range(count)])

    pick = jax.ShapeDtypeStruct((width, chosen_cols), BF16)
    short = row_count == 4
    far = row_count // 2
    whose = [tuple((i - d) % row_count for i in range(row_count)) for d in range(row_count)]
    came = [d for d in range(row_count) if d != far]
    plan = Plan(tuple(whose[d] for d in came), whose[far])
    keeps = shape(panels, rows, chosen_cols)
    inv, high, low, keep, keep_second = call(
        functools.partial(load_kernel, (whose[1] if short else whose[far], plan.early[-1])),
        [shape(*inv_diag.shape), pick, pick, keeps, keeps],
        [],
        [],
        far=[fill_mask, fill_blocks, inv_diag],
        scratch=[
            pltpu.SMEM(fill_mask.shape, jnp.int32),
            pltpu.SMEM(fill_blocks.shape, jnp.int32),
            pltpu.SemaphoreType.DMA((panels + 2,)),
        ],
        name="load",
    )
    prior_fill = turn(fill_blocks, "seg", 1)
    picks, bases, priors = [], [], []
    for p in range(panels):
        high_low = [high, low]
        if p < panels - 1:
            high_low = call(
                functools.partial(pick_kernel, p),
                [pick, pick],
                [fill_blocks] if p else [fill_blocks, prior_fill],
                [inv],
                name="pick",
            )
        base, own_prior, token = call(
            functools.partial(prior_kernel, p),
            [shape(chosen_cols, chosen_cols), shape(own_cols, width), shape(1, 1, width)],
            [],
            [*high_low, inv],
            anywhere=[prior_fill],
            name="prior",
        )
        picks += high_low
        bases.append(base)
        priors.append(own_prior)
    ups, downs = [factor_off], [factor_off + token]
    for _ in range(row_count // 2 - short):
        ups.append(turn(ups[-1], "row", 1))
    for _ in range((row_count - 1) // 2):
        downs.append(turn(downs[-1], "row", -1))
    parts = ups[:far] + downs[:0:-1]
    (late,) = call(
        chosen_kernel,
        [shape(panels, rows, chosen_cols)],
        [],
        [ups[-1], keep, *picks],
        flops=96 * panels * rows * chosen_cols * width,
        name="chosen",
    )
    if short:
        late = turn(late, "row", 1)
    (links,) = call(
        functools.partial(links_kernel, plan),
        [shape(panels, size, size)],
        [fill_mask],
        [*parts[:-1], *picks],
        name="links",
    )
    (second,) = call(
        chosen_kernel,
        [shape(panels, rows, chosen_cols)],
        [],
        [parts[-1], keep_second, *picks],
        name="second",
    )
    links_t, own_whole = call(
        functools.partial(segment_kernel, plan, panels),
        [shape(panels, size, size), shape(2 * size, size)],
        [],
        [links, second, late, *bases],
        scratch=[pltpu.VMEM((panels, size, size), F32)],
        flops=18 * (panels - 1) * size**3,
        name="segment",
    )
    maps, maps_token = call(
        functools.partial(maps_kernel, plan),
        [shape(panels, size, width), shape(1, half)],
        [fill_mask],
        [inv, *parts],
        scratch=[pltpu.VMEM((size, width), F32)],
        flops=6 * panels * size * width * width,
        mib=24,
        name="maps",
    )
    swap = [(i, i ^ 1) for i in range(seg_count)]
    other_whole = lax.ppermute(own_whole, "seg", swap)
    half_packed = shape(5 * half // 4, half)
    half_link = shape(half, size)
    link_t, cov, send, send_t = call(
        chip_kernel,
        [shape(size, size), shape(size, size), half_packed, half_link],
        [],
        [own_whole, other_whole],
        flops=18 * size**3,
        name="chip",
    )
    held = [ups[-1], downs[-1]] if short else [ups[-1]]
    held_by = whose[far]
    if short:
        held_by = tuple(whose[-1][i] if i % 2 else whose[1][i] for i in range(row_count))
    (rest,) = call(
        functools.partial(rest_kernel, held_by),
        [shape(panels, rows, width - chosen_cols)],
        [fill_mask, fill_blocks, prior_fill],
        [inv, *held, send],
        scratch=[pltpu.VMEM((rows, width), F32)],
        flops=6 * panels * rows * width * width,
        mib=24,
        name="rest",
    )
    if short:
        rest = lax.ppermute(rest, "row", [(i, i ^ 1) for i in range(row_count)])
    past = None
    after = (jnp.zeros(half_packed.shape, F32),) * 2
    levels = (chips - 1).bit_length()
    prepared = None

    def prepare():
        total = rows + own_cols
        left = jax.ShapeDtypeStruct((panels * total, size), BF16)
        right = jax.ShapeDtypeStruct((panels, size, width), BF16)
        return call(
            functools.partial(prepare_kernel, plan, levels, panels),
            [left, left, right, right, shape(panels, total, width), shape(1, half)],
            [fill_mask, fill_blocks, prior_fill],
            [*bases, *priors, other_whole, maps, links_t, late, rest, *(past or ())],
            scratch=[
                pltpu.VMEM((size, width), F32),
                pltpu.VMEM((size, width), F32),
                pltpu.VMEM((rows, width), F32),
            ],
            flops=6 * panels * size * (total * size + size * width + total * width + 3 * size * size),
            mib=24,
            name="prepare",
        )

    for level in range(levels):
        partner = [(i, i ^ (2 << level)) for i in range(seg_count)]
        got = lax.ppermute(send, "seg", partner)
        if level == levels - 1:
            *prepared, token = prepare()
            got = got + token
            after = (got, lax.ppermute(got, "seg", swap))
            break
        got_t = lax.ppermute(send_t, "seg", partner)
        if level == 0:
            got = got + maps_token
        got = (got_t, lax.ppermute(got_t, "seg", swap), got, lax.ppermute(got, "seg", swap))
        outs = [half_packed]
        if level < levels - 2:
            outs += [half_link, shape(size, size), shape(size, size)]
        send, *more = call(
            functools.partial(merge_kernel, level), outs, [], [link_t, cov, *got],
            flops=18 * size**3, name="merge",
        )
        if more:
            send_t, link_t, cov = more
        if past is None:
            past = got
        else:
            past = call(
                functools.partial(join_kernel, level),
                [half_link, half_link, half_packed, half_packed],
                [],
                [*past, *got],
                flops=18 * size**3,
                name="join",
            )
    if prepared is None:
        *prepared, _ = prepare()
    diag, off = call(
        functools.partial(finish_kernel, levels),
        [shape(panels, own_cols, width), shape(panels, rows, width)],
        [],
        [*after, *prepared],
        out_far=True,
        scratch=[
            pltpu.VMEM((panels, own_cols, width), F32),
            pltpu.VMEM((panels, rows, width), F32),
            pltpu.SemaphoreType.DMA((panels, 2)),
        ],
        flops=6 * panels * (rows + own_cols) * size * (size + width),
        name="finish",
    )
    return diag, off


def solution(mesh):
    placed = (P("seg", None), P("seg", None), P("seg", None, None), P("seg", "row", None))
    return jax.shard_map(
        body,
        mesh=mesh,
        in_specs=placed,
        out_specs=(P("seg", "row", None), P("seg", "row", None)),
        check_vma=False,
    )
```

```python
import functools
from typing import NamedTuple

import jax
import jax.numpy as jnp
from jax import lax
from jax.experimental import pallas as pl
from jax.experimental.pallas import tpu as pltpu
from jax.sharding import PartitionSpec as P

BLOCK = 64
LANES = 128
F32 = jnp.float32
BF16 = jnp.bfloat16
NN = (((1,), (0,)), ((), ()))
NT = (((1,), (1,)), ((), ()))
TN = (((0,), (0,)), ((), ()))


def split(x):
    high = x.astype(BF16)
    return high, (x - high.astype(F32)).astype(BF16)


def mm(a, b, dims=NN):
    a = a if isinstance(a, tuple) else split(a)
    b = b if isinstance(b, tuple) else split(b)
    dot = functools.partial(lax.dot_general, dimension_numbers=dims, preferred_element_type=F32)
    return dot(a[0], b[0]) + (dot(a[0], b[1]) + dot(a[1], b[0]))


def carry(link_t, cov, base):
    link_t = link_t if isinstance(link_t, tuple) else split(link_t)
    return mm(mm(link_t, cov), link_t, NT) + base


def pack(cov):
    half = cov.shape[0] // 2
    part = half // 2
    first, second = cov[:half, :half], cov[half:, half:]
    lane = lax.broadcasted_iota(jnp.int32, (part, half), 1)
    last = jnp.where(lane < part, pltpu.roll(first[part:], part, 1), second[part:])
    return jnp.concatenate([cov[:half, half:], first[:part], second[:part], last], 0)


def unpack(packed):
    half = packed.shape[1]
    part = half // 2
    cross, last = packed[:half], packed[2 * half :]
    row = lax.broadcasted_iota(jnp.int32, (half, half), 0)
    lane = lax.broadcasted_iota(jnp.int32, (half, half), 1)

    def symmetric(top, bottom):
        upper = jnp.concatenate([top, bottom], 0)
        return jnp.where((row < part) | (lane >= part), upper, upper.T)

    first = symmetric(packed[half : half + part], pltpu.roll(last, part, 1))
    second = symmetric(packed[half + part : 2 * half], last)
    top = jnp.concatenate([first, cross], 1)
    bottom = jnp.concatenate([cross.T, second], 1)
    return jnp.concatenate([top, bottom], 0)


def is_lower():
    return (lax.axis_index("seg") & 1) == 0


def from_halves(own, other):
    lower = is_lower()
    return jnp.concatenate([jnp.where(lower, own, other), jnp.where(lower, other, own)], 0)


def own_half(whole):
    half = whole.shape[0] // 2
    return jnp.where(is_lower(), whole[:half], whole[half:])


def other_half(whole):
    half = whole.shape[0] // 2
    return jnp.where(is_lower(), whole[half:], whole[:half])


def joint(link_t, packed, half):
    packed = half(packed)
    rows = packed.shape[0] // 2
    return jnp.concatenate([half(link_t), jnp.concatenate([packed[:rows], packed[rows:]], 1)], 0)


def apart(own, other):
    size = own.shape[1]
    link_t = from_halves(own[: size // 2], other[: size // 2])
    own, other = (
        jnp.concatenate([x[size // 2 :, : size // 2], x[size // 2 :, size // 2 :]], 0)
        for x in (own, other)
    )
    return link_t, from_halves(own, other)


def two_blocks(load, left, right):
    def placed(block, half):
        slab = load(lax.shift_right_logical(block, 1))
        return jnp.where((block & 1) == half, slab, pltpu.roll(slab, BLOCK, 1))

    a, b = placed(left, 0), placed(right, 1)
    lane = lax.broadcasted_iota(jnp.int32, a.shape, 1)
    return jnp.where(lane < BLOCK, a, b)


def tile_of(ref, *lead):
    def load(tile):
        return ref[(*lead, slice(None), pl.ds(pl.multiple_of(tile * LANES, LANES), LANES))]

    return load


def chosen_of(panel, fill_ref, prior_ref=None):
    slots = fill_ref.shape[1]
    if panel > 0:
        return [fill_ref[panel - 1, j] for j in range(slots)]
    first = lax.axis_index("seg") == 0
    last = prior_ref.shape[0] - 1
    return [jnp.where(first, fill_ref[0, j], prior_ref[last, j]) for j in range(slots)]


def order_of(chosen, blocks):
    slots = len(chosen)
    rest = [jnp.int32(0)] * (blocks - slots)
    place = []
    seen = jnp.int32(0)
    for b in range(blocks):
        hit = jnp.int32(0)
        where = jnp.int32(0)
        for j in range(slots):
            same = (chosen[j] == b).astype(jnp.int32)
            hit = hit + same
            where = where + same * j
        free = 1 - hit
        for q in range(blocks - slots):
            rest[q] = rest[q] + jnp.where(seen == q, free * b, 0)
        place.append(jnp.where(hit > 0, where, slots + seen))
        seen = seen + free
    return rest, place


def vmem(count):
    return [pl.BlockSpec(memory_space=pltpu.VMEM)] * count


def smem(count):
    return [pl.BlockSpec(memory_space=pltpu.SMEM)] * count


def call(
    kernel, outs, scalars, arrays, far=(), anywhere=(), out_far=False, through=(), scratch=(), flops=0, mib=16, name=None
):
    moved = sum(a.size * 4 for a in (*arrays, *far)) + sum(o.size * 4 for o in outs)
    first = len(scalars) + len(arrays) + len(far) + len(anywhere)
    count = len(through)

    def inner(*refs):
        kernel(*refs[:first], *refs[first + count : first + count + len(outs)], *refs[first + 2 * count + len(outs) :])

    return pl.pallas_call(
        inner,
        out_shape=[*outs, *(jax.ShapeDtypeStruct(a.shape, a.dtype) for a in through)],
        in_specs=smem(len(scalars))
        + vmem(len(arrays))
        + [pl.BlockSpec(memory_space=pltpu.HBM)] * len(far)
        + [pl.BlockSpec(memory_space=pl.ANY)] * len(anywhere)
        + [pl.BlockSpec(memory_space=pl.ANY)] * count,
        out_specs=([pl.BlockSpec(memory_space=pltpu.HBM)] * len(outs) if out_far else vmem(len(outs)))
        + [pl.BlockSpec(memory_space=pl.ANY)] * count,
        scratch_shapes=list(scratch),
        input_output_aliases={first + i: len(outs) + i for i in range(count)},
        cost_estimate=pl.CostEstimate(flops=flops, bytes_accessed=moved, transcendentals=0),
        compiler_params=pltpu.CompilerParams(vmem_limit_bytes=mib << 20),
        name=name,
    )(*scalars, *arrays, *(pltpu.with_memory_space_constraint(a, pltpu.HBM) for a in far), *anywhere, *through)


def shape(*dims):
    return jax.ShapeDtypeStruct(dims, F32)


def kept_rows(mask_ref, panel, slot, rows):
    alive = lax.axis_index("seg") * mask_ref.shape[0] + panel < (
        lax.axis_size("seg") * mask_ref.shape[0] - 1
    )
    return rows * (mask_ref[panel, slot].astype(F32) * alive.astype(F32))


def triangular_mm(left, lower):
    cut = left.shape[1] // 2
    first, second = split(left[:, :cut]), split(left[:, cut:])
    below = split(lower[cut:, :])
    return jnp.concatenate(
        [
            mm(second, (below[0][:, :cut], below[1][:, :cut])) + mm(first, lower[:cut, :cut]),
            mm(second, (below[0][:, cut:], below[1][:, cut:])),
        ],
        1,
    )


def pick_into(high_ref, low_ref, chosen, *inv_at):
    for t in range(len(chosen) // 2):
        columns = slice(t * LANES, (t + 1) * LANES)
        high_ref[:, columns], low_ref[:, columns] = split(
            two_blocks(tile_of(*inv_at), chosen[2 * t], chosen[2 * t + 1])
        )


def load_kernel(
    owners, mask_hbm, fill_hbm, inv_hbm, inv_ref, high_ref, low_ref, *refs
):
    keep_refs, (mask_ref, fill_ref, sems) = refs[:-3], refs[-3:]
    panels, rows, _ = keep_refs[0].shape
    small = [
        pltpu.make_async_copy(fill_hbm, fill_ref, sems.at[panels]),
        pltpu.make_async_copy(mask_hbm, mask_ref, sems.at[panels + 1]),
    ]
    large = [
        pltpu.make_async_copy(inv_hbm.at[p], inv_ref.at[p], sems.at[p]) for p in range(panels)
    ]
    for copy in (*small, *reversed(large)):
        copy.start()
    for copy in small:
        copy.wait()
    for p in range(panels):
        for block_owners, keep_ref in zip(owners, keep_refs):
            for s, slot in enumerate(slots_of(block_owners, rows)):
                ones = jnp.ones((BLOCK, keep_ref.shape[2]), F32)
                keep_ref[p, s * BLOCK : (s + 1) * BLOCK, :] = kept_rows(mask_ref, p, slot, ones)
    large[-1].wait()
    pick_into(high_ref, low_ref, chosen_of(panels - 1, fill_ref), inv_ref, panels - 1)
    for copy in large[:-1]:
        copy.wait()


def pick_kernel(panel, *refs):
    *scalar_refs, inv_ref, high_ref, low_ref = refs
    pick_into(high_ref, low_ref, chosen_of(panel, *scalar_refs), inv_ref, panel)


def prior_kernel(panel, high_ref, low_ref, inv_ref, _, base_ref, own_ref, token_ref):
    token_ref[...] = jnp.zeros_like(token_ref)
    own_cols = own_ref.shape[0]
    own_at = pl.ds(pl.multiple_of(lax.axis_index("row") * own_cols, own_cols), own_cols)
    picked = (high_ref[...], low_ref[...])
    base_ref[...] = mm(picked, picked, TN)
    own_ref[...] = mm(inv_ref[panel, :, own_at], inv_ref[panel], TN)


class Plan(NamedTuple):
    early: tuple
    late: tuple


def at_row(table):
    value = jnp.int32(table[0])
    for i, entry in enumerate(table[1:], 1):
        value = jnp.where(lax.axis_index("row") == i, entry, value)
    return value


def slots_of(owners, rows):
    first = at_row(owners) * (rows // BLOCK)
    return [first + s for s in range(rows // BLOCK)]


def put_rows(mask_ref, panel, owners, part, out_ref, take):
    for s, slot in enumerate(slots_of(owners, part.shape[0])):
        kept = kept_rows(mask_ref, panel, slot, part[s * BLOCK : (s + 1) * BLOCK, :])
        out_ref[pl.ds(pl.multiple_of(slot * BLOCK, BLOCK), BLOCK), :] = take(kept)


def links_kernel(plan, mask_ref, *refs):
    count = len(plan.early) - 1
    parts, (*pick_refs, links_ref) = refs[:count], refs[count:]
    links_ref[...] = jnp.zeros_like(links_ref)
    for p in range(links_ref.shape[0]):
        pick = (pick_refs[2 * p][...], pick_refs[2 * p + 1][...])
        for owners, part in zip(plan.early[:-1], parts):
            put_rows(mask_ref, p, owners, part[p], links_ref.at[p], lambda kept: mm(kept, pick))


def kept_block(mask_ref, panel, owners, part):
    return jnp.concatenate(
        [
            kept_rows(mask_ref, panel, slot, part[s * BLOCK : (s + 1) * BLOCK, :])
            for s, slot in enumerate(slots_of(owners, part.shape[0]))
        ],
        0,
    )


def chosen_kernel(part, keep_ref, *refs):
    *pick_refs, out_ref = refs
    for p in range(out_ref.shape[0]):
        pick = (pick_refs[2 * p][...], pick_refs[2 * p + 1][...])
        out_ref[p] = mm(part[p], pick) * keep_ref[p]


def rest_kernel(owners, mask_ref, fill_ref, prior_ref, inv_ref, *refs):
    *parts, _, out_ref, map_ref = refs
    odd = (lax.axis_index("row") & 1) == 1
    for p in range(out_ref.shape[0]):
        part = parts[0][p] if len(parts) == 1 else jnp.where(odd, parts[1][p], parts[0][p])
        map_ref[...] = triangular_mm(kept_block(mask_ref, p, owners, part), inv_ref[p])
        rest, _ = order_of(chosen_of(p, fill_ref, prior_ref), map_ref.shape[1] // BLOCK)
        for t in range(len(rest) // 2):
            out_ref[p, :, t * LANES : (t + 1) * LANES] = two_blocks(
                tile_of(map_ref), rest[2 * t], rest[2 * t + 1]
            )


def segment_kernel(plan, panels, early_ref, second_ref, late_ref, *refs):
    base_refs, (links_t_ref, whole_ref, rows_ref) = refs[:panels], refs[panels:]
    size = links_t_ref.shape[1]
    rows = late_ref.shape[1]
    second_at, late_at = (
        pl.ds(pl.multiple_of(at_row(owners) * rows, rows), rows)
        for owners in (plan.early[-1], plan.late)
    )
    cov = link_t = None
    for p in range(panels - 1, -1, -1):
        rows_ref[p] = early_ref[p]
        rows_ref[p, second_at, :] = second_ref[p]
        rows_ref[p, late_at, :] = late_ref[p]
        own_t = rows_ref[p].T
        links_t_ref[p] = own_t
        if cov is None:
            cov, link_t = base_refs[p][...], own_t
        else:
            own_t = split(own_t)
            cov = carry(own_t, cov, base_refs[p][...])
            link_t = mm(own_t, link_t)
    whole_ref[:size] = link_t
    whole_ref[size:] = cov


def maps_kernel(plan, mask_ref, inv_ref, *refs):
    *parts, _, maps_ref, token_ref, rows_ref = refs
    token_ref[...] = jnp.zeros_like(token_ref)
    rows_ref[...] = jnp.zeros_like(rows_ref)
    for p in range(inv_ref.shape[0]):
        for owners, part in zip(plan.early, parts):
            put_rows(mask_ref, p, owners, part[p], rows_ref, lambda kept: kept)
        maps_ref[p] = triangular_mm(rows_ref[...], inv_ref[p])


def chip_kernel(own_ref, other_ref, link_t_ref, cov_ref, packed_ref, joint_ref):
    size = cov_ref.shape[0]
    lower = is_lower()
    own_t, other_t = own_ref[:size, :], other_ref[:size, :]
    own, other = own_ref[size:, :], other_ref[size:, :]
    down_t = split(jnp.where(lower, own_t, other_t))
    cov = carry(down_t, jnp.where(lower, other, own), jnp.where(lower, own, other))
    link_t = mm(down_t, jnp.where(lower, other_t, own_t))
    link_t_ref[...] = link_t
    cov_ref[...] = cov
    packed = pack(cov)
    packed_ref[...] = own_half(packed)
    joint_ref[...] = joint(link_t, packed, own_half)


def merge_kernel(level, link_t_ref, cov_ref, got_ref, got_other_ref, *refs):
    got_t, got = apart(got_ref[...], got_other_ref[...])
    got = unpack(got)
    own_t, own = link_t_ref[...], cov_ref[...]
    lower = (lax.shift_right_logical(lax.axis_index("seg") // 2, level) & 1) == 0
    down_t = split(jnp.where(lower, own_t, got_t))
    cov = carry(down_t, jnp.where(lower, got, own), jnp.where(lower, own, got))
    packed = pack(cov)
    if len(refs) == 1:
        refs[0][...] = own_half(packed)
    else:
        link_t = mm(down_t, jnp.where(lower, got_t, own_t))
        refs[0][...] = joint(link_t, packed, own_half)
        refs[1][...] = link_t
        refs[2][...] = cov


def join_kernel(level, past_ref, past_other_ref, got_ref, got_other_ref, out_ref, out_other_ref):
    past_t, past = apart(past_ref[...], past_other_ref[...])
    link_t, cov = apart(got_ref[...], got_other_ref[...])
    chip = lax.axis_index("seg") // 2
    below = (lax.shift_right_logical(chip, level) & 1) == 0
    known = (chip & ((1 << level) - 1)) != (1 << level) - 1
    past_parts = split(past_t)
    joined = pack(carry(past_parts, unpack(cov), unpack(past)))
    joined_t = mm(past_parts, link_t)
    out_t = jnp.where(below, jnp.where(known, joined_t, link_t), past_t)
    out = jnp.where(below, jnp.where(known, joined, cov), past)
    out_ref[...] = joint(out_t, out, own_half)
    out_other_ref[...] = joint(out_t, out, other_half)


def prepare_kernel(plan, levels, panels, mask_ref, fill_ref, prior_ref, *refs):
    base_refs, own_refs, refs = refs[:panels], refs[panels : 2 * panels], refs[2 * panels :]
    (other_ref, maps_ref, links_t_ref, late_ref, rest_ref), refs = refs[:5], refs[5:]
    past_refs, refs = refs[: 2 * (levels > 1)], refs[2 * (levels > 1) :]
    left_high, left_low, right_high, right_low, const_ref, token_ref, scratch, map_ref, late_map_ref = refs
    token_ref[...] = jnp.zeros_like(token_ref)
    own_cols, width = own_refs[0].shape
    late_at = at_row(plan.late)
    size = base_refs[0].shape[0]
    row_at = lax.axis_index("row")
    rows = left_high.shape[0] // panels - own_cols
    row = lax.broadcasted_iota(jnp.int32, (size, size), 0)
    column = lax.broadcasted_iota(jnp.int32, (size, size), 1)
    eye = (row == column).astype(F32)
    other = other_ref[size:, :]
    lower = is_lower()
    if past_refs:
        chip = lax.axis_index("seg") // 2
        low = (1 << (levels - 1)) - 1
        known = (chip & low) != low
        past_t, past = apart(past_refs[0][...], past_refs[1][...])
        past = unpack(past)
        to_t = jnp.where(known, past_t, eye)
        gain = jnp.where(known, past, 0.0)
        other_t = split(other_ref[:size, :])
        to_t = jnp.where(lower, mm(other_t, to_t), to_t)
        gain = jnp.where(lower, carry(other_t, gain, other), gain)
    else:
        to_t = jnp.where(lower, other_ref[:size, :], eye)
        gain = jnp.where(lower, other, 0.0)
    own_at = pl.ds(pl.multiple_of(row_at * own_cols, own_cols), own_cols)
    own_rows = pl.ds(pl.multiple_of(row_at * rows, rows), rows)
    late_rows = pl.ds(pl.multiple_of(late_at * rows, rows), rows)
    for p in range(panels - 1, -1, -1):
        late_map_ref[:, :size] = late_ref[p]
        late_map_ref[:, size:] = rest_ref[p]
        _, place = order_of(chosen_of(p, fill_ref, prior_ref), width // BLOCK)
        map_ref[...] = maps_ref[p]
        for t in range(len(place) // 2):
            map_ref[late_rows, t * LANES : (t + 1) * LANES] = two_blocks(
                tile_of(late_map_ref), place[2 * t], place[2 * t + 1]
            )
        whole = split(map_ref[...])
        own_t = split(map_ref[:, own_at].T)
        scratch[:, :size] = to_t
        scratch[:, size:] = gain
        to_parts = split(to_t)
        cross = jnp.concatenate(
            [
                jnp.full((BLOCK, size), -mask_ref[p, slot].astype(F32))
                for slot in slots_of(tuple(range(size // rows)), rows)
            ],
            0,
        )
        left = jnp.concatenate([scratch[own_rows, :size] * cross, mm(own_t, to_parts)], 0)
        part = slice(p * left.shape[0], (p + 1) * left.shape[0])
        left_high[part, :], left_low[part, :] = split(left)
        right_high[p], right_low[p] = split(mm(to_parts, whole, TN))
        gains = jnp.concatenate([scratch[own_rows, size:] * cross, mm(own_t, gain)], 0)
        const = mm(gains, whole)
        const_ref[p, :rows, :] = const[:rows]
        const_ref[p, rows:, :] = const[rows:] + own_refs[p][...]
        if p > 0:
            link_t = split(links_t_ref[p])
            to_t = mm(link_t, to_t)
            gain = carry(link_t, gain, base_refs[p][...])


def finish_kernel(levels, after_ref, after_other_ref, *refs):
    left_high, left_low, right_high, right_low, const_ref, diag_hbm, off_hbm = refs[:7]
    diag_ref, off_ref, sems = refs[7:]
    panels, total, _ = const_ref.shape
    rows = off_ref.shape[1]
    chip = lax.axis_index("seg") // 2
    after = from_halves(after_ref[...], after_other_ref[...])
    after = unpack(jnp.where((chip & ((1 << levels) // 2)) == 0, after, 0.0))
    inner = split(mm((left_high[...], left_low[...]), after))
    copies = []
    for p in range(panels):
        part = slice(p * total, (p + 1) * total)
        right = (right_high[p], right_low[p])
        result = mm((inner[0][part], inner[1][part]), right) + const_ref[p]
        diag_ref[p] = result[rows:]
        off_ref[p] = result[:rows]
        copies.append(pltpu.make_async_copy(diag_ref.at[p], diag_hbm.at[p], sems.at[p, 0]))
        copies.append(pltpu.make_async_copy(off_ref.at[p], off_hbm.at[p], sems.at[p, 1]))
        copies[-2].start()
        copies[-1].start()
    for copy in copies:
        copy.wait()


def body(fill_blocks, fill_mask, inv_diag, factor_off):
    panels, width, _ = inv_diag.shape
    rows = factor_off.shape[1]
    seg_count = lax.axis_size("seg")
    row_count = lax.axis_size("row")
    size = rows * row_count
    own_cols = width // row_count
    slots = fill_blocks.shape[1]
    chosen_cols = slots * BLOCK
    chips = seg_count // 2
    half = size // 2

    def turn(x, axis, distance):
        count = lax.axis_size(axis)
        return lax.ppermute(x, axis, [(i, (i + distance) % count) for i in range(count)])

    pick = jax.ShapeDtypeStruct((width, chosen_cols), BF16)
    short = row_count == 4
    far = row_count // 2
    whose = [tuple((i - d) % row_count for i in range(row_count)) for d in range(row_count)]
    came = [d for d in range(row_count) if d != far]
    plan = Plan(tuple(whose[d] for d in came), whose[far])
    keeps = shape(panels, rows, chosen_cols)
    inv, high, low, keep, keep_second = call(
        functools.partial(load_kernel, (whose[1] if short else whose[far], plan.early[-1])),
        [shape(*inv_diag.shape), pick, pick, keeps, keeps],
        [],
        [],
        far=[fill_mask, fill_blocks, inv_diag],
        scratch=[
            pltpu.SMEM(fill_mask.shape, jnp.int32),
            pltpu.SMEM(fill_blocks.shape, jnp.int32),
            pltpu.SemaphoreType.DMA((panels + 2,)),
        ],
        name="load",
    )
    prior_fill = turn(fill_blocks, "seg", 1)
    picks, bases, priors = [], [], []
    for p in range(panels):
        high_low = [high, low]
        if p < panels - 1:
            high_low = call(
                functools.partial(pick_kernel, p),
                [pick, pick],
                [fill_blocks] if p else [fill_blocks, prior_fill],
                [inv],
                name="pick",
            )
        base, own_prior, token = call(
            functools.partial(prior_kernel, p),
            [shape(chosen_cols, chosen_cols), shape(own_cols, width), shape(1, 1, width)],
            [],
            [*high_low, inv],
            anywhere=[prior_fill],
            name="prior",
        )
        picks += high_low
        bases.append(base)
        priors.append(own_prior)
    ups, downs = [factor_off], [factor_off + token]
    for _ in range(row_count // 2 - short):
        ups.append(turn(ups[-1], "row", 1))
    for _ in range((row_count - 1) // 2):
        downs.append(turn(downs[-1], "row", -1))
    parts = ups[:far] + downs[:0:-1]
    (late,) = call(
        chosen_kernel,
        [shape(panels, rows, chosen_cols)],
        [],
        [ups[-1], keep, *picks],
        flops=96 * panels * rows * chosen_cols * width,
        name="chosen",
    )
    if short:
        late = turn(late, "row", 1)
    (links,) = call(
        functools.partial(links_kernel, plan),
        [shape(panels, size, size)],
        [fill_mask],
        [*parts[:-1], *picks],
        name="links",
    )
    (second,) = call(
        chosen_kernel,
        [shape(panels, rows, chosen_cols)],
        [],
        [parts[-1], keep_second, *picks],
        name="second",
    )
    links_t, own_whole = call(
        functools.partial(segment_kernel, plan, panels),
        [shape(panels, size, size), shape(2 * size, size)],
        [],
        [links, second, late, *bases],
        scratch=[pltpu.VMEM((panels, size, size), F32)],
        flops=18 * (panels - 1) * size**3,
        name="segment",
    )
    swap = [(i, i ^ 1) for i in range(seg_count)]
    other_whole = lax.ppermute(own_whole, "seg", swap)
    half_packed = shape(5 * half // 4, half)
    joint_half = shape(half + 5 * half // 8, size)
    link_t, cov, packed, send = call(
        chip_kernel,
        [shape(size, size), shape(size, size), half_packed, joint_half],
        [],
        [own_whole, other_whole],
        flops=18 * size**3,
        name="chip",
    )
    held = [ups[-1], downs[-1]] if short else [ups[-1]]
    held_by = whose[far]
    if short:
        held_by = tuple(whose[-1][i] if i % 2 else whose[1][i] for i in range(row_count))
    (rest,) = call(
        functools.partial(rest_kernel, held_by),
        [shape(panels, rows, width - chosen_cols)],
        [fill_mask, fill_blocks, prior_fill],
        [inv, *held, send],
        scratch=[pltpu.VMEM((rows, width), F32)],
        flops=6 * panels * rows * width * width,
        mib=24,
        name="rest",
    )
    maps, maps_token = call(
        functools.partial(maps_kernel, plan),
        [shape(panels, size, width), shape(1, size)],
        [fill_mask],
        [inv, *parts],
        anywhere=[rest],
        scratch=[pltpu.VMEM((size, width), F32)],
        flops=6 * panels * size * width * width,
        mib=24,
        name="maps",
    )
    if short:
        rest = lax.ppermute(rest, "row", [(i, i ^ 1) for i in range(row_count)])
    past = None
    after = (jnp.zeros(half_packed.shape, F32),) * 2
    levels = (chips - 1).bit_length()
    prepared = None

    def prepare():
        total = rows + own_cols
        left = jax.ShapeDtypeStruct((panels * total, size), BF16)
        right = jax.ShapeDtypeStruct((panels, size, width), BF16)
        return call(
            functools.partial(prepare_kernel, plan, levels, panels),
            [left, left, right, right, shape(panels, total, width), shape(1, half)],
            [fill_mask, fill_blocks, prior_fill],
            [*bases, *priors, other_whole, maps, links_t, late, rest, *(past or ())],
            scratch=[
                pltpu.VMEM((size, width), F32),
                pltpu.VMEM((size, width), F32),
                pltpu.VMEM((rows, width), F32),
            ],
            flops=6 * panels * size * (total * size + size * width + total * width + 3 * size * size),
            mib=24,
            name="prepare",
        )

    for level in range(levels):
        partner = [(i, i ^ (2 << level)) for i in range(seg_count)]
        if level == levels - 1:
            got = lax.ppermute(packed if level == 0 else send, "seg", partner)
            *prepared, token = prepare()
            got = got + token
            after = (got, lax.ppermute(got, "seg", swap))
            break
        got = lax.ppermute(send, "seg", partner)
        if level == 0:
            got = got + maps_token + jnp.minimum(jnp.abs(rest[0, :1, :size]), 0.0)
        got = (got, lax.ppermute(got, "seg", swap))
        outs = [half_packed]
        if level < levels - 2:
            outs = [joint_half, shape(size, size), shape(size, size)]
        send, *more = call(
            functools.partial(merge_kernel, level), outs, [], [link_t, cov, *got],
            flops=18 * size**3, name="merge",
        )
        if more:
            link_t, cov = more
        if past is None:
            past = got
        else:
            past = call(
                functools.partial(join_kernel, level),
                [joint_half, joint_half],
                [],
                [*past, *got],
                flops=18 * size**3,
                name="join",
            )
    if prepared is None:
        *prepared, _ = prepare()
    diag, off = call(
        functools.partial(finish_kernel, levels),
        [shape(panels, own_cols, width), shape(panels, rows, width)],
        [],
        [*after, *prepared],
        out_far=True,
        scratch=[
            pltpu.VMEM((panels, own_cols, width), F32),
            pltpu.VMEM((panels, rows, width), F32),
            pltpu.SemaphoreType.DMA((panels, 2)),
        ],
        flops=6 * panels * (rows + own_cols) * size * (size + width),
        name="finish",
    )
    return diag, off


def solution(mesh):
    placed = (P("seg", None), P("seg", None), P("seg", None, None), P("seg", "row", None))
    return jax.shard_map(
        body,
        mesh=mesh,
        in_specs=placed,
        out_specs=(P("seg", "row", None), P("seg", "row", None)),
        check_vma=False,
    )
```

```python
import functools
from typing import NamedTuple

import jax
import jax.numpy as jnp
from jax import lax
from jax.experimental import pallas as pl
from jax.experimental.pallas import tpu as pltpu
from jax.sharding import PartitionSpec as P

BLOCK = 64
LANES = 128
F32 = jnp.float32
BF16 = jnp.bfloat16
NN = (((1,), (0,)), ((), ()))
NT = (((1,), (1,)), ((), ()))
TN = (((0,), (0,)), ((), ()))


def split(x):
    high = x.astype(BF16)
    return high, (x - high.astype(F32)).astype(BF16)


def mm(a, b, dims=NN):
    a = a if isinstance(a, tuple) else split(a)
    b = b if isinstance(b, tuple) else split(b)
    dot = functools.partial(lax.dot_general, dimension_numbers=dims, preferred_element_type=F32)
    free = 1 - dims[0][0][0]
    rows = a[0].shape[free]
    stacked = dot(jnp.concatenate(a, free), b[0])
    return stacked[:rows] + (dot(a[0], b[1]) + stacked[rows:])


def carry(link_t, cov, base):
    link_t = link_t if isinstance(link_t, tuple) else split(link_t)
    return mm(mm(link_t, cov), link_t, NT) + base


def pack(cov):
    half = cov.shape[0] // 2
    part = half // 2
    first, second = cov[:half, :half], cov[half:, half:]
    lane = lax.broadcasted_iota(jnp.int32, (part, half), 1)
    last = jnp.where(lane < part, pltpu.roll(first[part:], part, 1), second[part:])
    return jnp.concatenate([cov[:half, half:], first[:part], second[:part], last], 0)


def unpack(packed):
    half = packed.shape[1]
    part = half // 2
    cross, last = packed[:half], packed[2 * half :]
    row = lax.broadcasted_iota(jnp.int32, (half, half), 0)
    lane = lax.broadcasted_iota(jnp.int32, (half, half), 1)

    def symmetric(top, bottom):
        upper = jnp.concatenate([top, bottom], 0)
        return jnp.where((row < part) | (lane >= part), upper, upper.T)

    first = symmetric(packed[half : half + part], pltpu.roll(last, part, 1))
    second = symmetric(packed[half + part : 2 * half], last)
    top = jnp.concatenate([first, cross], 1)
    bottom = jnp.concatenate([cross.T, second], 1)
    return jnp.concatenate([top, bottom], 0)


def is_lower():
    return (lax.axis_index("seg") & 1) == 0


def from_halves(own, other):
    lower = is_lower()
    return jnp.concatenate([jnp.where(lower, own, other), jnp.where(lower, other, own)], 0)


def own_half(whole):
    half = whole.shape[0] // 2
    return jnp.where(is_lower(), whole[:half], whole[half:])


def two_blocks(load, left, right):
    def placed(block, half):
        slab = load(lax.shift_right_logical(block, 1))
        return jnp.where((block & 1) == half, slab, pltpu.roll(slab, BLOCK, 1))

    a, b = placed(left, 0), placed(right, 1)
    lane = lax.broadcasted_iota(jnp.int32, a.shape, 1)
    return jnp.where(lane < BLOCK, a, b)


def tile_of(ref, *lead):
    def load(tile):
        return ref[(*lead, slice(None), pl.ds(pl.multiple_of(tile * LANES, LANES), LANES))]

    return load


def chosen_of(panel, fill_ref, prior_ref=None):
    slots = fill_ref.shape[1]
    if panel > 0:
        return [fill_ref[panel - 1, j] for j in range(slots)]
    first = lax.axis_index("seg") == 0
    last = prior_ref.shape[0] - 1
    return [jnp.where(first, fill_ref[0, j], prior_ref[last, j]) for j in range(slots)]


def order_of(chosen, blocks):
    slots = len(chosen)
    rest = [jnp.int32(0)] * (blocks - slots)
    place = []
    seen = jnp.int32(0)
    for b in range(blocks):
        hit = jnp.int32(0)
        where = jnp.int32(0)
        for j in range(slots):
            same = (chosen[j] == b).astype(jnp.int32)
            hit = hit + same
            where = where + same * j
        free = 1 - hit
        for q in range(blocks - slots):
            rest[q] = rest[q] + jnp.where(seen == q, free * b, 0)
        place.append(jnp.where(hit > 0, where, slots + seen))
        seen = seen + free
    return rest, place


def vmem(count):
    return [pl.BlockSpec(memory_space=pltpu.VMEM)] * count


def smem(count):
    return [pl.BlockSpec(memory_space=pltpu.SMEM)] * count


def call(
    kernel, outs, scalars, arrays, far=(), anywhere=(), out_far=False, through=(), scratch=(), flops=0, mib=16, name=None
):
    moved = sum(a.size * 4 for a in (*arrays, *far)) + sum(o.size * 4 for o in outs)
    first = len(scalars) + len(arrays) + len(far) + len(anywhere)
    count = len(through)

    def inner(*refs):
        kernel(*refs[:first], *refs[first + count : first + count + len(outs)], *refs[first + 2 * count + len(outs) :])

    return pl.pallas_call(
        inner,
        out_shape=[*outs, *(jax.ShapeDtypeStruct(a.shape, a.dtype) for a in through)],
        in_specs=smem(len(scalars))
        + vmem(len(arrays))
        + [pl.BlockSpec(memory_space=pltpu.HBM)] * len(far)
        + [pl.BlockSpec(memory_space=pl.ANY)] * len(anywhere)
        + [pl.BlockSpec(memory_space=pl.ANY)] * count,
        out_specs=([pl.BlockSpec(memory_space=pltpu.HBM)] * len(outs) if out_far else vmem(len(outs)))
        + [pl.BlockSpec(memory_space=pl.ANY)] * count,
        scratch_shapes=list(scratch),
        input_output_aliases={first + i: len(outs) + i for i in range(count)},
        cost_estimate=pl.CostEstimate(flops=flops, bytes_accessed=moved, transcendentals=0),
        compiler_params=pltpu.CompilerParams(vmem_limit_bytes=mib << 20),
        name=name,
    )(*scalars, *arrays, *(pltpu.with_memory_space_constraint(a, pltpu.HBM) for a in far), *anywhere, *through)


def shape(*dims):
    return jax.ShapeDtypeStruct(dims, F32)


def kept_rows(mask_ref, panel, slot, rows):
    alive = lax.axis_index("seg") * mask_ref.shape[0] + panel < (
        lax.axis_size("seg") * mask_ref.shape[0] - 1
    )
    return rows * (mask_ref[panel, slot].astype(F32) * alive.astype(F32))


def triangular_mm(left, lower):
    cut = left.shape[1] // 2
    first, second = split(left[:, :cut]), split(left[:, cut:])
    below = split(lower[cut:, :])
    return jnp.concatenate(
        [
            mm(second, (below[0][:, :cut], below[1][:, :cut])) + mm(first, lower[:cut, :cut]),
            mm(second, (below[0][:, cut:], below[1][:, cut:])),
        ],
        1,
    )


def pick_into(high_ref, low_ref, chosen, *inv_at):
    for t in range(len(chosen) // 2):
        columns = slice(t * LANES, (t + 1) * LANES)
        high_ref[:, columns], low_ref[:, columns] = split(
            two_blocks(tile_of(*inv_at), chosen[2 * t], chosen[2 * t + 1])
        )


def load_kernel(
    owners, mask_hbm, fill_hbm, inv_hbm, inv_ref, high_ref, low_ref, *refs
):
    keep_refs, (mask_ref, fill_ref, sems) = refs[:-3], refs[-3:]
    panels, rows, _ = keep_refs[0].shape
    small = [
        pltpu.make_async_copy(fill_hbm, fill_ref, sems.at[panels]),
        pltpu.make_async_copy(mask_hbm, mask_ref, sems.at[panels + 1]),
    ]
    large = [
        pltpu.make_async_copy(inv_hbm.at[p], inv_ref.at[p], sems.at[p]) for p in range(panels)
    ]
    for copy in (*small, *reversed(large)):
        copy.start()
    for copy in small:
        copy.wait()
    for p in range(panels):
        for block_owners, keep_ref in zip(owners, keep_refs):
            for s, slot in enumerate(slots_of(block_owners, rows)):
                ones = jnp.ones((BLOCK, keep_ref.shape[2]), F32)
                keep_ref[p, s * BLOCK : (s + 1) * BLOCK, :] = kept_rows(mask_ref, p, slot, ones)
    large[-1].wait()
    pick_into(high_ref, low_ref, chosen_of(panels - 1, fill_ref), inv_ref, panels - 1)
    for copy in large[:-1]:
        copy.wait()


def pick_kernel(panel, *refs):
    *scalar_refs, inv_ref, high_ref, low_ref = refs
    pick_into(high_ref, low_ref, chosen_of(panel, *scalar_refs), inv_ref, panel)


def prior_kernel(panel, high_ref, low_ref, inv_ref, _, base_ref, own_ref, token_ref):
    token_ref[...] = jnp.zeros_like(token_ref)
    own_cols = own_ref.shape[0]
    own_at = pl.ds(pl.multiple_of(lax.axis_index("row") * own_cols, own_cols), own_cols)
    picked = (high_ref[...], low_ref[...])
    base_ref[...] = mm(picked, picked, TN)
    own_ref[...] = mm(inv_ref[panel, :, own_at], inv_ref[panel], TN)


class Plan(NamedTuple):
    early: tuple
    late: tuple


def at_row(table):
    value = jnp.int32(table[0])
    for i, entry in enumerate(table[1:], 1):
        value = jnp.where(lax.axis_index("row") == i, entry, value)
    return value


def slots_of(owners, rows):
    first = at_row(owners) * (rows // BLOCK)
    return [first + s for s in range(rows // BLOCK)]


def put_rows(mask_ref, panel, owners, part, out_ref, take):
    for s, slot in enumerate(slots_of(owners, part.shape[0])):
        kept = kept_rows(mask_ref, panel, slot, part[s * BLOCK : (s + 1) * BLOCK, :])
        out_ref[pl.ds(pl.multiple_of(slot * BLOCK, BLOCK), BLOCK), :] = take(kept)


def links_kernel(plan, mask_ref, *refs):
    count = len(plan.early) - 1
    parts, (*pick_refs, links_ref) = refs[:count], refs[count:]
    links_ref[...] = jnp.zeros_like(links_ref)
    for p in range(links_ref.shape[0]):
        pick = (pick_refs[2 * p][...], pick_refs[2 * p + 1][...])
        for owners, part in zip(plan.early[:-1], parts):
            put_rows(mask_ref, p, owners, part[p], links_ref.at[p], lambda kept: mm(kept, pick))


def kept_block(mask_ref, panel, owners, part):
    return jnp.concatenate(
        [
            kept_rows(mask_ref, panel, slot, part[s * BLOCK : (s + 1) * BLOCK, :])
            for s, slot in enumerate(slots_of(owners, part.shape[0]))
        ],
        0,
    )


def chosen_kernel(part, keep_ref, *refs):
    *pick_refs, out_ref = refs
    for p in range(out_ref.shape[0]):
        pick = (pick_refs[2 * p][...], pick_refs[2 * p + 1][...])
        out_ref[p] = mm(part[p], pick) * keep_ref[p]


def rest_kernel(owners, mask_ref, fill_ref, prior_ref, inv_ref, *refs):
    *parts, _, out_ref, map_ref = refs
    odd = (lax.axis_index("row") & 1) == 1
    for p in range(out_ref.shape[0]):
        part = parts[0][p] if len(parts) == 1 else jnp.where(odd, parts[1][p], parts[0][p])
        map_ref[...] = triangular_mm(kept_block(mask_ref, p, owners, part), inv_ref[p])
        rest, _ = order_of(chosen_of(p, fill_ref, prior_ref), map_ref.shape[1] // BLOCK)
        for t in range(len(rest) // 2):
            out_ref[p, :, t * LANES : (t + 1) * LANES] = two_blocks(
                tile_of(map_ref), rest[2 * t], rest[2 * t + 1]
            )


def segment_kernel(plan, panels, early_ref, second_ref, late_ref, *refs):
    base_refs, (links_t_ref, whole_ref, rows_ref) = refs[:panels], refs[panels:]
    size = links_t_ref.shape[1]
    rows = late_ref.shape[1]
    second_at, late_at = (
        pl.ds(pl.multiple_of(at_row(owners) * rows, rows), rows)
        for owners in (plan.early[-1], plan.late)
    )
    cov = link_t = None
    for p in range(panels - 1, -1, -1):
        rows_ref[p] = early_ref[p]
        rows_ref[p, second_at, :] = second_ref[p]
        rows_ref[p, late_at, :] = late_ref[p]
        own_t = rows_ref[p].T
        links_t_ref[p] = own_t
        if cov is None:
            cov, link_t = base_refs[p][...], own_t
        else:
            own_t = split(own_t)
            cov = carry(own_t, cov, base_refs[p][...])
            link_t = mm(own_t, link_t)
    whole_ref[:size] = link_t
    whole_ref[size:] = cov


def maps_kernel(plan, mask_ref, inv_ref, *refs):
    *parts, maps_ref, token_ref, rows_ref = refs
    token_ref[...] = jnp.zeros_like(token_ref)
    rows_ref[...] = jnp.zeros_like(rows_ref)
    for p in range(inv_ref.shape[0]):
        for owners, part in zip(plan.early, parts):
            put_rows(mask_ref, p, owners, part[p], rows_ref, lambda kept: kept)
        maps_ref[p] = triangular_mm(rows_ref[...], inv_ref[p])


def chip_kernel(own_ref, other_ref, link_t_ref, cov_ref, packed_ref, half_t_ref):
    size = cov_ref.shape[0]
    lower = is_lower()
    own_t, other_t = own_ref[:size, :], other_ref[:size, :]
    own, other = own_ref[size:, :], other_ref[size:, :]
    down_t = split(jnp.where(lower, own_t, other_t))
    cov = carry(down_t, jnp.where(lower, other, own), jnp.where(lower, own, other))
    link_t = mm(down_t, jnp.where(lower, other_t, own_t))
    link_t_ref[...] = link_t
    cov_ref[...] = cov
    packed_ref[...] = own_half(pack(cov))
    half_t_ref[...] = own_half(link_t)


def merge_kernel(level, link_t_ref, cov_ref, *refs):
    got_t = from_halves(refs[0][...], refs[1][...])
    got = unpack(from_halves(refs[2][...], refs[3][...]))
    own_t, own = link_t_ref[...], cov_ref[...]
    lower = (lax.shift_right_logical(lax.axis_index("seg") // 2, level) & 1) == 0
    down_t = split(jnp.where(lower, own_t, got_t))
    cov = carry(down_t, jnp.where(lower, got, own), jnp.where(lower, own, got))
    refs[4][...] = own_half(pack(cov))
    if len(refs) > 5:
        link_t = mm(down_t, jnp.where(lower, got_t, own_t))
        refs[5][...] = own_half(link_t)
        refs[6][...] = link_t
        refs[7][...] = cov


def join_kernel(level, *refs):
    past_t, past, link_t, cov = (
        from_halves(refs[2 * i][...], refs[2 * i + 1][...]) for i in range(4)
    )
    chip = lax.axis_index("seg") // 2
    below = (lax.shift_right_logical(chip, level) & 1) == 0
    known = (chip & ((1 << level) - 1)) != (1 << level) - 1
    past_parts = split(past_t)
    joined = pack(carry(past_parts, unpack(cov), unpack(past)))
    joined_t = mm(past_parts, link_t)
    out_t = jnp.where(below, jnp.where(known, joined_t, link_t), past_t)
    out = jnp.where(below, jnp.where(known, joined, cov), past)
    for i, whole in enumerate((out_t, out)):
        half = whole.shape[0] // 2
        refs[8 + 2 * i][...] = own_half(whole)
        refs[9 + 2 * i][...] = jnp.where(is_lower(), whole[half:], whole[:half])


def prepare_kernel(plan, levels, panels, mask_ref, fill_ref, prior_ref, *refs):
    base_refs, own_refs, refs = refs[:panels], refs[panels : 2 * panels], refs[2 * panels :]
    (other_ref, maps_ref, links_t_ref, late_ref, rest_ref), refs = refs[:5], refs[5:]
    past_refs, refs = refs[: 4 * (levels > 1)], refs[4 * (levels > 1) :]
    left_high, left_low, right_high, right_low, const_ref, token_ref, scratch, map_ref, late_map_ref = refs
    token_ref[...] = jnp.zeros_like(token_ref)
    own_cols, width = own_refs[0].shape
    late_at = at_row(plan.late)
    size = base_refs[0].shape[0]
    row_at = lax.axis_index("row")
    rows = left_high.shape[0] // panels - own_cols
    row = lax.broadcasted_iota(jnp.int32, (size, size), 0)
    column = lax.broadcasted_iota(jnp.int32, (size, size), 1)
    eye = (row == column).astype(F32)
    other = other_ref[size:, :]
    lower = is_lower()
    if past_refs:
        chip = lax.axis_index("seg") // 2
        low = (1 << (levels - 1)) - 1
        known = (chip & low) != low
        past_t = from_halves(past_refs[0][...], past_refs[1][...])
        past = unpack(from_halves(past_refs[2][...], past_refs[3][...]))
        to_t = jnp.where(known, past_t, eye)
        gain = jnp.where(known, past, 0.0)
        other_t = split(other_ref[:size, :])
        to_t = jnp.where(lower, mm(other_t, to_t), to_t)
        gain = jnp.where(lower, carry(other_t, gain, other), gain)
    else:
        to_t = jnp.where(lower, other_ref[:size, :], eye)
        gain = jnp.where(lower, other, 0.0)
    own_at = pl.ds(pl.multiple_of(row_at * own_cols, own_cols), own_cols)
    own_rows = pl.ds(pl.multiple_of(row_at * rows, rows), rows)
    late_rows = pl.ds(pl.multiple_of(late_at * rows, rows), rows)
    for p in range(panels - 1, -1, -1):
        late_map_ref[:, :size] = late_ref[p]
        late_map_ref[:, size:] = rest_ref[p]
        _, place = order_of(chosen_of(p, fill_ref, prior_ref), width // BLOCK)
        map_ref[...] = maps_ref[p]
        for t in range(len(place) // 2):
            map_ref[late_rows, t * LANES : (t + 1) * LANES] = two_blocks(
                tile_of(late_map_ref), place[2 * t], place[2 * t + 1]
            )
        whole = split(map_ref[...])
        own_t = split(map_ref[:, own_at].T)
        scratch[:, :size] = to_t
        scratch[:, size:] = gain
        to_parts = split(to_t)
        cross = jnp.concatenate(
            [
                jnp.full((BLOCK, size), -mask_ref[p, slot].astype(F32))
                for slot in slots_of(tuple(range(size // rows)), rows)
            ],
            0,
        )
        left = jnp.concatenate([scratch[own_rows, :size] * cross, mm(own_t, to_parts)], 0)
        part = slice(p * left.shape[0], (p + 1) * left.shape[0])
        left_high[part, :], left_low[part, :] = split(left)
        right_high[p], right_low[p] = split(mm(to_parts, whole, TN))
        gains = jnp.concatenate([scratch[own_rows, size:] * cross, mm(own_t, gain)], 0)
        const = mm(gains, whole)
        const_ref[p, :rows, :] = const[:rows]
        const_ref[p, rows:, :] = const[rows:] + own_refs[p][...]
        if p > 0:
            link_t = split(links_t_ref[p])
            to_t = mm(link_t, to_t)
            gain = carry(link_t, gain, base_refs[p][...])


def finish_kernel(levels, after_ref, after_other_ref, *refs):
    left_high, left_low, right_high, right_low, const_ref, diag_hbm, off_hbm = refs[:7]
    diag_ref, off_ref, sems = refs[7:]
    panels, total, _ = const_ref.shape
    rows = off_ref.shape[1]
    chip = lax.axis_index("seg") // 2
    after = from_halves(after_ref[...], after_other_ref[...])
    after = unpack(jnp.where((chip & ((1 << levels) // 2)) == 0, after, 0.0))
    inner = split(mm((left_high[...], left_low[...]), after))
    copies = []
    for p in range(panels):
        part = slice(p * total, (p + 1) * total)
        right = (right_high[p], right_low[p])
        result = mm((inner[0][part], inner[1][part]), right) + const_ref[p]
        diag_ref[p] = result[rows:]
        off_ref[p] = result[:rows]
        copies.append(pltpu.make_async_copy(diag_ref.at[p], diag_hbm.at[p], sems.at[p, 0]))
        copies.append(pltpu.make_async_copy(off_ref.at[p], off_hbm.at[p], sems.at[p, 1]))
        copies[-2].start()
        copies[-1].start()
    for copy in copies:
        copy.wait()


def body(fill_blocks, fill_mask, inv_diag, factor_off):
    panels, width, _ = inv_diag.shape
    rows = factor_off.shape[1]
    seg_count = lax.axis_size("seg")
    row_count = lax.axis_size("row")
    size = rows * row_count
    own_cols = width // row_count
    slots = fill_blocks.shape[1]
    chosen_cols = slots * BLOCK
    chips = seg_count // 2
    half = size // 2

    def turn(x, axis, distance):
        count = lax.axis_size(axis)
        return lax.ppermute(x, axis, [(i, (i + distance) % count) for i in range(count)])

    pick = jax.ShapeDtypeStruct((width, chosen_cols), BF16)
    short = row_count == 4
    far = row_count // 2
    whose = [tuple((i - d) % row_count for i in range(row_count)) for d in range(row_count)]
    came = [d for d in range(row_count) if d != far]
    plan = Plan(tuple(whose[d] for d in came), whose[far])
    keeps = shape(panels, rows, chosen_cols)
    inv, high, low, keep, keep_second = call(
        functools.partial(load_kernel, (whose[1] if short else whose[far], plan.early[-1])),
        [shape(*inv_diag.shape), pick, pick, keeps, keeps],
        [],
        [],
        far=[fill_mask, fill_blocks, inv_diag],
        scratch=[
            pltpu.SMEM(fill_mask.shape, jnp.int32),
            pltpu.SMEM(fill_blocks.shape, jnp.int32),
            pltpu.SemaphoreType.DMA((panels + 2,)),
        ],
        name="load",
    )
    prior_fill = turn(fill_blocks, "seg", 1)
    picks, bases, priors = [], [], []
    for p in range(panels):
        high_low = [high, low]
        if p < panels - 1:
            high_low = call(
                functools.partial(pick_kernel, p),
                [pick, pick],
                [fill_blocks] if p else [fill_blocks, prior_fill],
                [inv],
                name="pick",
            )
        base, own_prior, token = call(
            functools.partial(prior_kernel, p),
            [shape(chosen_cols, chosen_cols), shape(own_cols, width), shape(1, 1, width)],
            [],
            [*high_low, inv],
            anywhere=[prior_fill],
            name="prior",
        )
        picks += high_low
        bases.append(base)
        priors.append(own_prior)
    ups, downs = [factor_off], [factor_off + token]
    for _ in range(row_count // 2 - short):
        ups.append(turn(ups[-1], "row", 1))
    for _ in range((row_count - 1) // 2):
        downs.append(turn(downs[-1], "row", -1))
    parts = ups[:far] + downs[:0:-1]
    (late,) = call(
        chosen_kernel,
        [shape(panels, rows, chosen_cols)],
        [],
        [ups[-1], keep, *picks],
        flops=96 * panels * rows * chosen_cols * width,
        name="chosen",
    )
    if short:
        late = turn(late, "row", 1)
    (links,) = call(
        functools.partial(links_kernel, plan),
        [shape(panels, size, size)],
        [fill_mask],
        [*parts[:-1], *picks],
        name="links",
    )
    (second,) = call(
        chosen_kernel,
        [shape(panels, rows, chosen_cols)],
        [],
        [parts[-1], keep_second, *picks],
        name="second",
    )
    links_t, own_whole = call(
        functools.partial(segment_kernel, plan, panels),
        [shape(panels, size, size), shape(2 * size, size)],
        [],
        [links, second, late, *bases],
        scratch=[pltpu.VMEM((panels, size, size), F32)],
        flops=18 * (panels - 1) * size**3,
        name="segment",
    )
    maps, maps_token = call(
        functools.partial(maps_kernel, plan),
        [shape(panels, size, width), shape(1, half)],
        [fill_mask],
        [inv, *parts],
        scratch=[pltpu.VMEM((size, width), F32)],
        flops=6 * panels * size * width * width,
        mib=24,
        name="maps",
    )
    swap = [(i, i ^ 1) for i in range(seg_count)]
    other_whole = lax.ppermute(own_whole, "seg", swap)
    half_packed = shape(5 * half // 4, half)
    half_link = shape(half, size)
    link_t, cov, send, send_t = call(
        chip_kernel,
        [shape(size, size), shape(size, size), half_packed, half_link],
        [],
        [own_whole, other_whole],
        flops=18 * size**3,
        name="chip",
    )
    held = [ups[-1], downs[-1]] if short else [ups[-1]]
    held_by = whose[far]
    if short:
        held_by = tuple(whose[-1][i] if i % 2 else whose[1][i] for i in range(row_count))
    (rest,) = call(
        functools.partial(rest_kernel, held_by),
        [shape(panels, rows, width - chosen_cols)],
        [fill_mask, fill_blocks, prior_fill],
        [inv, *held, send],
        scratch=[pltpu.VMEM((rows, width), F32)],
        flops=6 * panels * rows * width * width,
        mib=24,
        name="rest",
    )
    if short:
        rest = lax.ppermute(rest, "row", [(i, i ^ 1) for i in range(row_count)])
    past = None
    after = (jnp.zeros(half_packed.shape, F32),) * 2
    levels = (chips - 1).bit_length()
    prepared = None

    def prepare():
        total = rows + own_cols
        left = jax.ShapeDtypeStruct((panels * total, size), BF16)
        right = jax.ShapeDtypeStruct((panels, size, width), BF16)
        return call(
            functools.partial(prepare_kernel, plan, levels, panels),
            [left, left, right, right, shape(panels, total, width), shape(1, half)],
            [fill_mask, fill_blocks, prior_fill],
            [*bases, *priors, other_whole, maps, links_t, late, rest, *(past or ())],
            scratch=[
                pltpu.VMEM((size, width), F32),
                pltpu.VMEM((size, width), F32),
                pltpu.VMEM((rows, width), F32),
            ],
            flops=6 * panels * size * (total * size + size * width + total * width + 3 * size * size),
            mib=24,
            name="prepare",
        )

    for level in range(levels):
        partner = [(i, i ^ (2 << level)) for i in range(seg_count)]
        got = lax.ppermute(send, "seg", partner)
        if level == levels - 1:
            *prepared, token = prepare()
            got = got + token
            after = (got, lax.ppermute(got, "seg", swap))
            break
        got_t = lax.ppermute(send_t, "seg", partner)
        if level == 0:
            got = got + maps_token
        got = (got_t, lax.ppermute(got_t, "seg", swap), got, lax.ppermute(got, "seg", swap))
        outs = [half_packed]
        if level < levels - 2:
            outs += [half_link, shape(size, size), shape(size, size)]
        send, *more = call(
            functools.partial(merge_kernel, level), outs, [], [link_t, cov, *got],
            flops=18 * size**3, name="merge",
        )
        if more:
            send_t, link_t, cov = more
        if past is None:
            past = got
        else:
            past = call(
                functools.partial(join_kernel, level),
                [half_link, half_link, half_packed, half_packed],
                [],
                [*past, *got],
                flops=18 * size**3,
                name="join",
            )
    if prepared is None:
        *prepared, _ = prepare()
    diag, off = call(
        functools.partial(finish_kernel, levels),
        [shape(panels, own_cols, width), shape(panels, rows, width)],
        [],
        [*after, *prepared],
        out_far=True,
        scratch=[
            pltpu.VMEM((panels, own_cols, width), F32),
            pltpu.VMEM((panels, rows, width), F32),
            pltpu.SemaphoreType.DMA((panels, 2)),
        ],
        flops=6 * panels * (rows + own_cols) * size * (size + width),
        name="finish",
    )
    return diag, off


def solution(mesh):
    placed = (P("seg", None), P("seg", None), P("seg", None, None), P("seg", "row", None))
    return jax.shard_map(
        body,
        mesh=mesh,
        in_specs=placed,
        out_specs=(P("seg", "row", None), P("seg", "row", None)),
        check_vma=False,
    )
```

```python
import functools
from typing import NamedTuple

import jax
import jax.numpy as jnp
from jax import lax
from jax.experimental import pallas as pl
from jax.experimental.pallas import tpu as pltpu
from jax.sharding import PartitionSpec as P

BLOCK = 64
LANES = 128
F32 = jnp.float32
BF16 = jnp.bfloat16
NN = (((1,), (0,)), ((), ()))
NT = (((1,), (1,)), ((), ()))
TN = (((0,), (0,)), ((), ()))


def split(x):
    high = x.astype(BF16)
    return high, (x - high.astype(F32)).astype(BF16)


def mm(a, b, dims=NN):
    a = a if isinstance(a, tuple) else split(a)
    b = b if isinstance(b, tuple) else split(b)
    dot = functools.partial(lax.dot_general, dimension_numbers=dims, preferred_element_type=F32)
    free = 1 - dims[0][0][0]
    rows = a[0].shape[free]
    stacked = dot(jnp.concatenate(a, free), b[0])
    return stacked[:rows] + (dot(a[0], b[1]) + stacked[rows:])


def carry(link_t, cov, base):
    link_t = link_t if isinstance(link_t, tuple) else split(link_t)
    return mm(mm(link_t, cov), link_t, NT) + base


def pack(cov):
    half = cov.shape[0] // 2
    part = half // 2
    first, second = cov[:half, :half], cov[half:, half:]
    lane = lax.broadcasted_iota(jnp.int32, (part, half), 1)
    last = jnp.where(lane < part, pltpu.roll(first[part:], part, 1), second[part:])
    return jnp.concatenate([cov[:half, half:], first[:part], second[:part], last], 0)


def unpack(packed):
    half = packed.shape[1]
    part = half // 2
    cross, last = packed[:half], packed[2 * half :]
    row = lax.broadcasted_iota(jnp.int32, (half, half), 0)
    lane = lax.broadcasted_iota(jnp.int32, (half, half), 1)

    def symmetric(top, bottom):
        upper = jnp.concatenate([top, bottom], 0)
        return jnp.where((row < part) | (lane >= part), upper, upper.T)

    first = symmetric(packed[half : half + part], pltpu.roll(last, part, 1))
    second = symmetric(packed[half + part : 2 * half], last)
    top = jnp.concatenate([first, cross], 1)
    bottom = jnp.concatenate([cross.T, second], 1)
    return jnp.concatenate([top, bottom], 0)


def is_lower():
    return (lax.axis_index("seg") & 1) == 0


def from_halves(own, other):
    lower = is_lower()
    return jnp.concatenate([jnp.where(lower, own, other), jnp.where(lower, other, own)], 0)


def own_half(whole):
    half = whole.shape[0] // 2
    return jnp.where(is_lower(), whole[:half], whole[half:])


def two_blocks(load, left, right):
    def placed(block, half):
        slab = load(lax.shift_right_logical(block, 1))
        return jnp.where((block & 1) == half, slab, pltpu.roll(slab, BLOCK, 1))

    a, b = placed(left, 0), placed(right, 1)
    lane = lax.broadcasted_iota(jnp.int32, a.shape, 1)
    return jnp.where(lane < BLOCK, a, b)


def tile_of(ref, *lead):
    def load(tile):
        return ref[(*lead, slice(None), pl.ds(pl.multiple_of(tile * LANES, LANES), LANES))]

    return load


def chosen_of(panel, fill_ref, prior_ref=None):
    slots = fill_ref.shape[1]
    if panel > 0:
        return [fill_ref[panel - 1, j] for j in range(slots)]
    first = lax.axis_index("seg") == 0
    last = prior_ref.shape[0] - 1
    return [jnp.where(first, fill_ref[0, j], prior_ref[last, j]) for j in range(slots)]


def order_of(chosen, blocks):
    slots = len(chosen)
    rest = [jnp.int32(0)] * (blocks - slots)
    place = []
    seen = jnp.int32(0)
    for b in range(blocks):
        hit = jnp.int32(0)
        where = jnp.int32(0)
        for j in range(slots):
            same = (chosen[j] == b).astype(jnp.int32)
            hit = hit + same
            where = where + same * j
        free = 1 - hit
        for q in range(blocks - slots):
            rest[q] = rest[q] + jnp.where(seen == q, free * b, 0)
        place.append(jnp.where(hit > 0, where, slots + seen))
        seen = seen + free
    return rest, place


def vmem(count):
    return [pl.BlockSpec(memory_space=pltpu.VMEM)] * count


def smem(count):
    return [pl.BlockSpec(memory_space=pltpu.SMEM)] * count


def call(
    kernel, outs, scalars, arrays, far=(), anywhere=(), out_far=False, through=(), scratch=(), flops=0, mib=16, name=None
):
    moved = sum(a.size * 4 for a in (*arrays, *far)) + sum(o.size * 4 for o in outs)
    first = len(scalars) + len(arrays) + len(far) + len(anywhere)
    count = len(through)

    def inner(*refs):
        kernel(*refs[:first], *refs[first + count : first + count + len(outs)], *refs[first + 2 * count + len(outs) :])

    return pl.pallas_call(
        inner,
        out_shape=[*outs, *(jax.ShapeDtypeStruct(a.shape, a.dtype) for a in through)],
        in_specs=smem(len(scalars))
        + vmem(len(arrays))
        + [pl.BlockSpec(memory_space=pltpu.HBM)] * len(far)
        + [pl.BlockSpec(memory_space=pl.ANY)] * len(anywhere)
        + [pl.BlockSpec(memory_space=pl.ANY)] * count,
        out_specs=([pl.BlockSpec(memory_space=pltpu.HBM)] * len(outs) if out_far else vmem(len(outs)))
        + [pl.BlockSpec(memory_space=pl.ANY)] * count,
        scratch_shapes=list(scratch),
        input_output_aliases={first + i: len(outs) + i for i in range(count)},
        cost_estimate=pl.CostEstimate(flops=flops, bytes_accessed=moved, transcendentals=0),
        compiler_params=pltpu.CompilerParams(vmem_limit_bytes=mib << 20),
        name=name,
    )(*scalars, *arrays, *(pltpu.with_memory_space_constraint(a, pltpu.HBM) for a in far), *anywhere, *through)


def shape(*dims):
    return jax.ShapeDtypeStruct(dims, F32)


def kept_rows(mask_ref, panel, slot, rows):
    alive = lax.axis_index("seg") * mask_ref.shape[0] + panel < (
        lax.axis_size("seg") * mask_ref.shape[0] - 1
    )
    return rows * (mask_ref[panel, slot].astype(F32) * alive.astype(F32))


def triangular_mm(left, lower):
    cut = left.shape[1] // 2
    first, second = split(left[:, :cut]), split(left[:, cut:])
    below = split(lower[cut:, :])
    return jnp.concatenate(
        [
            mm(second, (below[0][:, :cut], below[1][:, :cut])) + mm(first, lower[:cut, :cut]),
            mm(second, (below[0][:, cut:], below[1][:, cut:])),
        ],
        1,
    )


def pick_into(high_ref, low_ref, chosen, *inv_at):
    for t in range(len(chosen) // 2):
        columns = slice(t * LANES, (t + 1) * LANES)
        high_ref[:, columns], low_ref[:, columns] = split(
            two_blocks(tile_of(*inv_at), chosen[2 * t], chosen[2 * t + 1])
        )


def load_kernel(
    owners, mask_hbm, fill_hbm, inv_hbm, inv_ref, high_ref, low_ref, *refs
):
    keep_refs, (mask_ref, fill_ref, sems) = refs[:-3], refs[-3:]
    panels, rows, _ = keep_refs[0].shape
    small = [
        pltpu.make_async_copy(fill_hbm, fill_ref, sems.at[panels]),
        pltpu.make_async_copy(mask_hbm, mask_ref, sems.at[panels + 1]),
    ]
    large = [
        pltpu.make_async_copy(inv_hbm.at[p], inv_ref.at[p], sems.at[p]) for p in range(panels)
    ]
    for copy in (*small, *reversed(large)):
        copy.start()
    for copy in small:
        copy.wait()
    for p in range(panels):
        for block_owners, keep_ref in zip(owners, keep_refs):
            for s, slot in enumerate(slots_of(block_owners, rows)):
                ones = jnp.ones((BLOCK, keep_ref.shape[2]), F32)
                keep_ref[p, s * BLOCK : (s + 1) * BLOCK, :] = kept_rows(mask_ref, p, slot, ones)
    large[-1].wait()
    pick_into(high_ref, low_ref, chosen_of(panels - 1, fill_ref), inv_ref, panels - 1)
    for copy in large[:-1]:
        copy.wait()


def pick_kernel(panel, *refs):
    *scalar_refs, inv_ref, high_ref, low_ref = refs
    pick_into(high_ref, low_ref, chosen_of(panel, *scalar_refs), inv_ref, panel)


def prior_kernel(panel, high_ref, low_ref, inv_ref, _, base_ref, own_ref, token_ref):
    token_ref[...] = jnp.zeros_like(token_ref)
    own_cols = own_ref.shape[0]
    own_at = pl.ds(pl.multiple_of(lax.axis_index("row") * own_cols, own_cols), own_cols)
    picked = (high_ref[...], low_ref[...])
    base_ref[...] = mm(picked, picked, TN)
    own_ref[...] = mm(inv_ref[panel, :, own_at], inv_ref[panel], TN)


class Plan(NamedTuple):
    early: tuple
    late: tuple


def at_row(table):
    value = jnp.int32(table[0])
    for i, entry in enumerate(table[1:], 1):
        value = jnp.where(lax.axis_index("row") == i, entry, value)
    return value


def slots_of(owners, rows):
    first = at_row(owners) * (rows // BLOCK)
    return [first + s for s in range(rows // BLOCK)]


def put_rows(mask_ref, panel, owners, part, out_ref, take):
    for s, slot in enumerate(slots_of(owners, part.shape[0])):
        kept = kept_rows(mask_ref, panel, slot, part[s * BLOCK : (s + 1) * BLOCK, :])
        out_ref[pl.ds(pl.multiple_of(slot * BLOCK, BLOCK), BLOCK), :] = take(kept)


def links_kernel(plan, mask_ref, *refs):
    count = len(plan.early) - 1
    parts, (*pick_refs, links_ref) = refs[:count], refs[count:]
    links_ref[...] = jnp.zeros_like(links_ref)
    for p in range(links_ref.shape[0]):
        pick = (pick_refs[2 * p][...], pick_refs[2 * p + 1][...])
        for owners, part in zip(plan.early[:-1], parts):
            put_rows(mask_ref, p, owners, part[p], links_ref.at[p], lambda kept: mm(kept, pick))


def kept_block(mask_ref, panel, owners, part):
    return jnp.concatenate(
        [
            kept_rows(mask_ref, panel, slot, part[s * BLOCK : (s + 1) * BLOCK, :])
            for s, slot in enumerate(slots_of(owners, part.shape[0]))
        ],
        0,
    )


def chosen_kernel(part, keep_ref, *refs):
    *pick_refs, out_ref = refs
    for p in range(out_ref.shape[0]):
        pick = (pick_refs[2 * p][...], pick_refs[2 * p + 1][...])
        out_ref[p] = mm(part[p], pick) * keep_ref[p]


def rest_kernel(owners, mask_ref, fill_ref, prior_ref, inv_ref, *refs):
    *parts, _, out_ref, map_ref = refs
    odd = (lax.axis_index("row") & 1) == 1
    for p in range(out_ref.shape[0]):
        part = parts[0][p] if len(parts) == 1 else jnp.where(odd, parts[1][p], parts[0][p])
        map_ref[...] = triangular_mm(kept_block(mask_ref, p, owners, part), inv_ref[p])
        rest, _ = order_of(chosen_of(p, fill_ref, prior_ref), map_ref.shape[1] // BLOCK)
        for t in range(len(rest) // 2):
            out_ref[p, :, t * LANES : (t + 1) * LANES] = two_blocks(
                tile_of(map_ref), rest[2 * t], rest[2 * t + 1]
            )


def segment_kernel(plan, panels, early_ref, second_ref, late_ref, *refs):
    base_refs, (links_t_ref, whole_ref, rows_ref) = refs[:panels], refs[panels:]
    size = links_t_ref.shape[1]
    rows = late_ref.shape[1]
    second_at, late_at = (
        pl.ds(pl.multiple_of(at_row(owners) * rows, rows), rows)
        for owners in (plan.early[-1], plan.late)
    )
    cov = link_t = None
    for p in range(panels - 1, -1, -1):
        rows_ref[p] = early_ref[p]
        rows_ref[p, second_at, :] = second_ref[p]
        rows_ref[p, late_at, :] = late_ref[p]
        own_t = rows_ref[p].T
        links_t_ref[p] = own_t
        if cov is None:
            cov, link_t = base_refs[p][...], own_t
        else:
            own_t = split(own_t)
            cov = carry(own_t, cov, base_refs[p][...])
            link_t = mm(own_t, link_t)
    whole_ref[:size] = link_t
    whole_ref[size:] = cov


def maps_kernel(plan, mask_ref, inv_ref, *refs):
    *parts, maps_ref, token_ref, rows_ref = refs
    token_ref[...] = jnp.zeros_like(token_ref)
    rows_ref[...] = jnp.zeros_like(rows_ref)
    for p in range(inv_ref.shape[0]):
        for owners, part in zip(plan.early, parts):
            put_rows(mask_ref, p, owners, part[p], rows_ref, lambda kept: kept)
        maps_ref[p] = triangular_mm(rows_ref[...], inv_ref[p])


def chip_kernel(own_ref, other_ref, link_t_ref, cov_ref, packed_ref, half_t_ref):
    size = cov_ref.shape[0]
    lower = is_lower()
    own_t, other_t = own_ref[:size, :], other_ref[:size, :]
    own, other = own_ref[size:, :], other_ref[size:, :]
    down_t = split(jnp.where(lower, own_t, other_t))
    cov = carry(down_t, jnp.where(lower, other, own), jnp.where(lower, own, other))
    link_t = mm(down_t, jnp.where(lower, other_t, own_t))
    link_t_ref[...] = link_t
    cov_ref[...] = cov
    packed_ref[...] = own_half(pack(cov))
    half_t_ref[...] = own_half(link_t)


def merge_kernel(level, link_t_ref, cov_ref, *refs):
    got_t = from_halves(refs[0][...], refs[1][...])
    got = unpack(from_halves(refs[2][...], refs[3][...]))
    own_t, own = link_t_ref[...], cov_ref[...]
    lower = (lax.shift_right_logical(lax.axis_index("seg") // 2, level) & 1) == 0
    down_t = split(jnp.where(lower, own_t, got_t))
    cov = carry(down_t, jnp.where(lower, got, own), jnp.where(lower, own, got))
    refs[4][...] = own_half(pack(cov))
    if len(refs) > 5:
        link_t = mm(down_t, jnp.where(lower, got_t, own_t))
        refs[5][...] = own_half(link_t)
        refs[6][...] = link_t
        refs[7][...] = cov


def join_kernel(level, *refs):
    past_t, past, link_t, cov = (
        from_halves(refs[2 * i][...], refs[2 * i + 1][...]) for i in range(4)
    )
    chip = lax.axis_index("seg") // 2
    below = (lax.shift_right_logical(chip, level) & 1) == 0
    known = (chip & ((1 << level) - 1)) != (1 << level) - 1
    past_parts = split(past_t)
    joined = pack(carry(past_parts, unpack(cov), unpack(past)))
    joined_t = mm(past_parts, link_t)
    out_t = jnp.where(below, jnp.where(known, joined_t, link_t), past_t)
    out = jnp.where(below, jnp.where(known, joined, cov), past)
    for i, whole in enumerate((out_t, out)):
        half = whole.shape[0] // 2
        refs[8 + 2 * i][...] = own_half(whole)
        refs[9 + 2 * i][...] = jnp.where(is_lower(), whole[half:], whole[:half])


def prepare_kernel(plan, levels, panels, mask_ref, fill_ref, prior_ref, *refs):
    base_refs, own_refs, refs = refs[:panels], refs[panels : 2 * panels], refs[2 * panels :]
    (other_ref, maps_ref, links_t_ref, late_ref, rest_ref), refs = refs[:5], refs[5:]
    past_refs, refs = refs[: 4 * (levels > 1)], refs[4 * (levels > 1) :]
    left_high, left_low, right_high, right_low, const_ref, token_ref, scratch, map_ref, late_map_ref = refs
    token_ref[...] = jnp.zeros_like(token_ref)
    own_cols, width = own_refs[0].shape
    late_at = at_row(plan.late)
    size = base_refs[0].shape[0]
    row_at = lax.axis_index("row")
    rows = left_high.shape[0] // panels - own_cols
    row = lax.broadcasted_iota(jnp.int32, (size, size), 0)
    column = lax.broadcasted_iota(jnp.int32, (size, size), 1)
    eye = (row == column).astype(F32)
    other = other_ref[size:, :]
    lower = is_lower()
    if past_refs:
        chip = lax.axis_index("seg") // 2
        low = (1 << (levels - 1)) - 1
        known = (chip & low) != low
        past_t = from_halves(past_refs[0][...], past_refs[1][...])
        past = unpack(from_halves(past_refs[2][...], past_refs[3][...]))
        to_t = jnp.where(known, past_t, eye)
        gain = jnp.where(known, past, 0.0)
        other_t = split(other_ref[:size, :])
        to_t = jnp.where(lower, mm(other_t, to_t), to_t)
        gain = jnp.where(lower, carry(other_t, gain, other), gain)
    else:
        to_t = jnp.where(lower, other_ref[:size, :], eye)
        gain = jnp.where(lower, other, 0.0)
    own_at = pl.ds(pl.multiple_of(row_at * own_cols, own_cols), own_cols)
    own_rows = pl.ds(pl.multiple_of(row_at * rows, rows), rows)
    late_rows = pl.ds(pl.multiple_of(late_at * rows, rows), rows)
    for p in range(panels - 1, -1, -1):
        late_map_ref[:, :size] = late_ref[p]
        late_map_ref[:, size:] = rest_ref[p]
        _, place = order_of(chosen_of(p, fill_ref, prior_ref), width // BLOCK)
        map_ref[...] = maps_ref[p]
        for t in range(len(place) // 2):
            map_ref[late_rows, t * LANES : (t + 1) * LANES] = two_blocks(
                tile_of(late_map_ref), place[2 * t], place[2 * t + 1]
            )
        whole = split(map_ref[...])
        own_t = split(map_ref[:, own_at].T)
        scratch[:, :size] = to_t
        scratch[:, size:] = gain
        to_parts = split(to_t)
        cross = jnp.concatenate(
            [
                jnp.full((BLOCK, size), -mask_ref[p, slot].astype(F32))
                for slot in slots_of(tuple(range(size // rows)), rows)
            ],
            0,
        )
        left = jnp.concatenate([scratch[own_rows, :size] * cross, mm(own_t, to_parts)], 0)
        part = slice(p * left.shape[0], (p + 1) * left.shape[0])
        left_high[part, :], left_low[part, :] = split(left)
        right_high[p], right_low[p] = split(mm(to_parts, whole, TN))
        gains = jnp.concatenate([scratch[own_rows, size:] * cross, mm(own_t, gain)], 0)
        const = mm(gains, whole)
        const_ref[p, :rows, :] = const[:rows]
        const_ref[p, rows:, :] = const[rows:] + own_refs[p][...]
        if p > 0:
            link_t = split(links_t_ref[p])
            to_t = mm(link_t, to_t)
            gain = carry(link_t, gain, base_refs[p][...])


def finish_kernel(levels, after_ref, after_other_ref, *refs):
    left_high, left_low, right_high, right_low, const_ref, diag_hbm, off_hbm = refs[:7]
    diag_ref, off_ref, sems = refs[7:]
    panels, total, width = const_ref.shape
    rows = off_ref.shape[1]
    chip = lax.axis_index("seg") // 2
    after = from_halves(after_ref[...], after_other_ref[...])
    after = unpack(jnp.where((chip & ((1 << levels) // 2)) == 0, after, 0.0))
    inner = split(mm((left_high[...], left_low[...]), after))
    copies = []
    for p in range(panels):
        part = slice(p * total, (p + 1) * total)
        for h, columns in enumerate((slice(0, width // 2), slice(width // 2, width))):
            right = (right_high[p, :, columns], right_low[p, :, columns])
            result = mm((inner[0][part], inner[1][part]), right) + const_ref[p, :, columns]
            off_ref[p, :, columns] = result[:rows]
            diag_ref[p, :, columns] = result[rows:]
            for i, (ref, hbm) in enumerate(((off_ref, off_hbm), (diag_ref, diag_hbm))):
                copies.append(
                    pltpu.make_async_copy(
                        ref.at[p, :, columns], hbm.at[p, :, columns], sems.at[p, h, i]
                    )
                )
                copies[-1].start()
    for copy in copies:
        copy.wait()


def body(fill_blocks, fill_mask, inv_diag, factor_off):
    panels, width, _ = inv_diag.shape
    rows = factor_off.shape[1]
    seg_count = lax.axis_size("seg")
    row_count = lax.axis_size("row")
    size = rows * row_count
    own_cols = width // row_count
    slots = fill_blocks.shape[1]
    chosen_cols = slots * BLOCK
    chips = seg_count // 2
    half = size // 2

    def turn(x, axis, distance):
        count = lax.axis_size(axis)
        return lax.ppermute(x, axis, [(i, (i + distance) % count) for i in range(count)])

    pick = jax.ShapeDtypeStruct((width, chosen_cols), BF16)
    short = row_count == 4
    far = row_count // 2
    whose = [tuple((i - d) % row_count for i in range(row_count)) for d in range(row_count)]
    came = [d for d in range(row_count) if d != far]
    plan = Plan(tuple(whose[d] for d in came), whose[far])
    keeps = shape(panels, rows, chosen_cols)
    inv, high, low, keep, keep_second = call(
        functools.partial(load_kernel, (whose[1] if short else whose[far], plan.early[-1])),
        [shape(*inv_diag.shape), pick, pick, keeps, keeps],
        [],
        [],
        far=[fill_mask, fill_blocks, inv_diag],
        scratch=[
            pltpu.SMEM(fill_mask.shape, jnp.int32),
            pltpu.SMEM(fill_blocks.shape, jnp.int32),
            pltpu.SemaphoreType.DMA((panels + 2,)),
        ],
        name="load",
    )
    prior_fill = turn(fill_blocks, "seg", 1)
    picks, bases, priors = [], [], []
    for p in range(panels):
        high_low = [high, low]
        if p < panels - 1:
            high_low = call(
                functools.partial(pick_kernel, p),
                [pick, pick],
                [fill_blocks] if p else [fill_blocks, prior_fill],
                [inv],
                name="pick",
            )
        base, own_prior, token = call(
            functools.partial(prior_kernel, p),
            [shape(chosen_cols, chosen_cols), shape(own_cols, width), shape(1, 1, width)],
            [],
            [*high_low, inv],
            anywhere=[prior_fill],
            name="prior",
        )
        picks += high_low
        bases.append(base)
        priors.append(own_prior)
    ups, downs = [factor_off], [factor_off + token]
    for _ in range(row_count // 2 - short):
        ups.append(turn(ups[-1], "row", 1))
    for _ in range((row_count - 1) // 2):
        downs.append(turn(downs[-1], "row", -1))
    parts = ups[:far] + downs[:0:-1]
    (late,) = call(
        chosen_kernel,
        [shape(panels, rows, chosen_cols)],
        [],
        [ups[-1], keep, *picks],
        flops=96 * panels * rows * chosen_cols * width,
        name="chosen",
    )
    if short:
        late = turn(late, "row", 1)
    (links,) = call(
        functools.partial(links_kernel, plan),
        [shape(panels, size, size)],
        [fill_mask],
        [*parts[:-1], *picks],
        name="links",
    )
    (second,) = call(
        chosen_kernel,
        [shape(panels, rows, chosen_cols)],
        [],
        [parts[-1], keep_second, *picks],
        name="second",
    )
    links_t, own_whole = call(
        functools.partial(segment_kernel, plan, panels),
        [shape(panels, size, size), shape(2 * size, size)],
        [],
        [links, second, late, *bases],
        scratch=[pltpu.VMEM((panels, size, size), F32)],
        flops=18 * (panels - 1) * size**3,
        name="segment",
    )
    maps, maps_token = call(
        functools.partial(maps_kernel, plan),
        [shape(panels, size, width), shape(1, half)],
        [fill_mask],
        [inv, *parts],
        scratch=[pltpu.VMEM((size, width), F32)],
        flops=6 * panels * size * width * width,
        mib=24,
        name="maps",
    )
    swap = [(i, i ^ 1) for i in range(seg_count)]
    other_whole = lax.ppermute(own_whole, "seg", swap)
    half_packed = shape(5 * half // 4, half)
    half_link = shape(half, size)
    link_t, cov, send, send_t = call(
        chip_kernel,
        [shape(size, size), shape(size, size), half_packed, half_link],
        [],
        [own_whole, other_whole],
        flops=18 * size**3,
        name="chip",
    )
    held = [ups[-1], downs[-1]] if short else [ups[-1]]
    held_by = whose[far]
    if short:
        held_by = tuple(whose[-1][i] if i % 2 else whose[1][i] for i in range(row_count))
    (rest,) = call(
        functools.partial(rest_kernel, held_by),
        [shape(panels, rows, width - chosen_cols)],
        [fill_mask, fill_blocks, prior_fill],
        [inv, *held, send],
        scratch=[pltpu.VMEM((rows, width), F32)],
        flops=6 * panels * rows * width * width,
        mib=24,
        name="rest",
    )
    if short:
        rest = lax.ppermute(rest, "row", [(i, i ^ 1) for i in range(row_count)])
    past = None
    after = (jnp.zeros(half_packed.shape, F32),) * 2
    levels = (chips - 1).bit_length()
    prepared = None

    def prepare():
        total = rows + own_cols
        left = jax.ShapeDtypeStruct((panels * total, size), BF16)
        right = jax.ShapeDtypeStruct((panels, size, width), BF16)
        return call(
            functools.partial(prepare_kernel, plan, levels, panels),
            [left, left, right, right, shape(panels, total, width), shape(1, half)],
            [fill_mask, fill_blocks, prior_fill],
            [*bases, *priors, other_whole, maps, links_t, late, rest, *(past or ())],
            scratch=[
                pltpu.VMEM((size, width), F32),
                pltpu.VMEM((size, width), F32),
                pltpu.VMEM((rows, width), F32),
            ],
            flops=6 * panels * size * (total * size + size * width + total * width + 3 * size * size),
            mib=24,
            name="prepare",
        )

    for level in range(levels):
        partner = [(i, i ^ (2 << level)) for i in range(seg_count)]
        got = lax.ppermute(send, "seg", partner)
        if level == levels - 1:
            *prepared, token = prepare()
            got = got + token
            after = (got, lax.ppermute(got, "seg", swap))
            break
        got_t = lax.ppermute(send_t, "seg", partner)
        if level == 0:
            got = got + maps_token
        got = (got_t, lax.ppermute(got_t, "seg", swap), got, lax.ppermute(got, "seg", swap))
        outs = [half_packed]
        if level < levels - 2:
            outs += [half_link, shape(size, size), shape(size, size)]
        send, *more = call(
            functools.partial(merge_kernel, level), outs, [], [link_t, cov, *got],
            flops=18 * size**3, name="merge",
        )
        if more:
            send_t, link_t, cov = more
        if past is None:
            past = got
        else:
            past = call(
                functools.partial(join_kernel, level),
                [half_link, half_link, half_packed, half_packed],
                [],
                [*past, *got],
                flops=18 * size**3,
                name="join",
            )
    if prepared is None:
        *prepared, _ = prepare()
    diag, off = call(
        functools.partial(finish_kernel, levels),
        [shape(panels, own_cols, width), shape(panels, rows, width)],
        [],
        [*after, *prepared],
        out_far=True,
        scratch=[
            pltpu.VMEM((panels, own_cols, width), F32),
            pltpu.VMEM((panels, rows, width), F32),
            pltpu.SemaphoreType.DMA((panels, 2, 2)),
        ],
        flops=6 * panels * (rows + own_cols) * size * (size + width),
        name="finish",
    )
    return diag, off


def solution(mesh):
    placed = (P("seg", None), P("seg", None), P("seg", None, None), P("seg", "row", None))
    return jax.shard_map(
        body,
        mesh=mesh,
        in_specs=placed,
        out_specs=(P("seg", "row", None), P("seg", "row", None)),
        check_vma=False,
    )
```

```python
import functools
from typing import NamedTuple

import jax
import jax.numpy as jnp
from jax import lax
from jax.experimental import pallas as pl
from jax.experimental.pallas import tpu as pltpu
from jax.sharding import PartitionSpec as P

BLOCK = 64
LANES = 128
F32 = jnp.float32
BF16 = jnp.bfloat16
NN = (((1,), (0,)), ((), ()))
NT = (((1,), (1,)), ((), ()))
TN = (((0,), (0,)), ((), ()))


def split(x):
    high = x.astype(BF16)
    return high, (x - high.astype(F32)).astype(BF16)


def mm(a, b, dims=NN):
    a = a if isinstance(a, tuple) else split(a)
    b = b if isinstance(b, tuple) else split(b)
    dot = functools.partial(lax.dot_general, dimension_numbers=dims, preferred_element_type=F32)
    free = 1 - dims[0][0][0]
    rows = a[0].shape[free]
    stacked = dot(jnp.concatenate(a, free), b[0])
    return stacked[:rows] + (dot(a[0], b[1]) + stacked[rows:])


def carry(link_t, cov, base):
    link_t = link_t if isinstance(link_t, tuple) else split(link_t)
    return mm(mm(link_t, cov), link_t, NT) + base


def carry_both(down_t, cov, link_t, base):
    down_t = split(down_t)
    size = cov.shape[0]
    both = mm(down_t, jnp.concatenate([cov, link_t], 1))
    return mm(both[:, :size], down_t, NT) + base, both[:, size:]


def pack(cov):
    half = cov.shape[0] // 2
    part = half // 2
    first, second = cov[:half, :half], cov[half:, half:]
    lane = lax.broadcasted_iota(jnp.int32, (part, half), 1)
    last = jnp.where(lane < part, pltpu.roll(first[part:], part, 1), second[part:])
    return jnp.concatenate([cov[:half, half:], first[:part], second[:part], last], 0)


def unpack(packed):
    half = packed.shape[1]
    part = half // 2
    cross, last = packed[:half], packed[2 * half :]
    row = lax.broadcasted_iota(jnp.int32, (half, half), 0)
    lane = lax.broadcasted_iota(jnp.int32, (half, half), 1)

    def symmetric(top, bottom):
        upper = jnp.concatenate([top, bottom], 0)
        return jnp.where((row < part) | (lane >= part), upper, upper.T)

    first = symmetric(packed[half : half + part], pltpu.roll(last, part, 1))
    second = symmetric(packed[half + part : 2 * half], last)
    top = jnp.concatenate([first, cross], 1)
    bottom = jnp.concatenate([cross.T, second], 1)
    return jnp.concatenate([top, bottom], 0)


def is_lower():
    return (lax.axis_index("seg") & 1) == 0


def from_halves(own, other):
    lower = is_lower()
    return jnp.concatenate([jnp.where(lower, own, other), jnp.where(lower, other, own)], 0)


def own_half(whole):
    half = whole.shape[0] // 2
    return jnp.where(is_lower(), whole[:half], whole[half:])


def two_blocks(load, left, right):
    def placed(block, half):
        slab = load(lax.shift_right_logical(block, 1))
        return jnp.where((block & 1) == half, slab, pltpu.roll(slab, BLOCK, 1))

    a, b = placed(left, 0), placed(right, 1)
    lane = lax.broadcasted_iota(jnp.int32, a.shape, 1)
    return jnp.where(lane < BLOCK, a, b)


def tile_of(ref, *lead):
    def load(tile):
        return ref[(*lead, slice(None), pl.ds(pl.multiple_of(tile * LANES, LANES), LANES))]

    return load


def chosen_of(panel, fill_ref, prior_ref=None):
    slots = fill_ref.shape[1]
    if panel > 0:
        return [fill_ref[panel - 1, j] for j in range(slots)]
    first = lax.axis_index("seg") == 0
    last = prior_ref.shape[0] - 1
    return [jnp.where(first, fill_ref[0, j], prior_ref[last, j]) for j in range(slots)]


def order_of(chosen, blocks):
    slots = len(chosen)
    rest = [jnp.int32(0)] * (blocks - slots)
    place = []
    seen = jnp.int32(0)
    for b in range(blocks):
        hit = jnp.int32(0)
        where = jnp.int32(0)
        for j in range(slots):
            same = (chosen[j] == b).astype(jnp.int32)
            hit = hit + same
            where = where + same * j
        free = 1 - hit
        for q in range(blocks - slots):
            rest[q] = rest[q] + jnp.where(seen == q, free * b, 0)
        place.append(jnp.where(hit > 0, where, slots + seen))
        seen = seen + free
    return rest, place


def vmem(count):
    return [pl.BlockSpec(memory_space=pltpu.VMEM)] * count


def smem(count):
    return [pl.BlockSpec(memory_space=pltpu.SMEM)] * count


def call(
    kernel, outs, scalars, arrays, far=(), anywhere=(), out_far=False, through=(), scratch=(), flops=0, mib=16, name=None
):
    moved = sum(a.size * 4 for a in (*arrays, *far)) + sum(o.size * 4 for o in outs)
    first = len(scalars) + len(arrays) + len(far) + len(anywhere)
    count = len(through)

    def inner(*refs):
        kernel(*refs[:first], *refs[first + count : first + count + len(outs)], *refs[first + 2 * count + len(outs) :])

    return pl.pallas_call(
        inner,
        out_shape=[*outs, *(jax.ShapeDtypeStruct(a.shape, a.dtype) for a in through)],
        in_specs=smem(len(scalars))
        + vmem(len(arrays))
        + [pl.BlockSpec(memory_space=pltpu.HBM)] * len(far)
        + [pl.BlockSpec(memory_space=pl.ANY)] * len(anywhere)
        + [pl.BlockSpec(memory_space=pl.ANY)] * count,
        out_specs=([pl.BlockSpec(memory_space=pltpu.HBM)] * len(outs) if out_far else vmem(len(outs)))
        + [pl.BlockSpec(memory_space=pl.ANY)] * count,
        scratch_shapes=list(scratch),
        input_output_aliases={first + i: len(outs) + i for i in range(count)},
        cost_estimate=pl.CostEstimate(flops=flops, bytes_accessed=moved, transcendentals=0),
        compiler_params=pltpu.CompilerParams(vmem_limit_bytes=mib << 20),
        name=name,
    )(*scalars, *arrays, *(pltpu.with_memory_space_constraint(a, pltpu.HBM) for a in far), *anywhere, *through)


def shape(*dims):
    return jax.ShapeDtypeStruct(dims, F32)


def kept_rows(mask_ref, panel, slot, rows):
    alive = lax.axis_index("seg") * mask_ref.shape[0] + panel < (
        lax.axis_size("seg") * mask_ref.shape[0] - 1
    )
    return rows * (mask_ref[panel, slot].astype(F32) * alive.astype(F32))


def triangular_mm(left, lower):
    cut = left.shape[1] // 2
    first, second = split(left[:, :cut]), split(left[:, cut:])
    below = split(lower[cut:, :])
    return jnp.concatenate(
        [
            mm(second, (below[0][:, :cut], below[1][:, :cut])) + mm(first, lower[:cut, :cut]),
            mm(second, (below[0][:, cut:], below[1][:, cut:])),
        ],
        1,
    )


def pick_into(high_ref, low_ref, chosen, *inv_at):
    for t in range(len(chosen) // 2):
        columns = slice(t * LANES, (t + 1) * LANES)
        high_ref[:, columns], low_ref[:, columns] = split(
            two_blocks(tile_of(*inv_at), chosen[2 * t], chosen[2 * t + 1])
        )


def load_kernel(
    owners, mask_hbm, fill_hbm, inv_hbm, inv_ref, high_ref, low_ref, *refs
):
    keep_refs, (mask_ref, fill_ref, sems) = refs[:-3], refs[-3:]
    panels, rows, _ = keep_refs[0].shape
    small = [
        pltpu.make_async_copy(fill_hbm, fill_ref, sems.at[panels]),
        pltpu.make_async_copy(mask_hbm, mask_ref, sems.at[panels + 1]),
    ]
    large = [
        pltpu.make_async_copy(inv_hbm.at[p], inv_ref.at[p], sems.at[p]) for p in range(panels)
    ]
    for copy in (*small, *reversed(large)):
        copy.start()
    for copy in small:
        copy.wait()
    for p in range(panels):
        for block_owners, keep_ref in zip(owners, keep_refs):
            for s, slot in enumerate(slots_of(block_owners, rows)):
                ones = jnp.ones((BLOCK, keep_ref.shape[2]), F32)
                keep_ref[p, s * BLOCK : (s + 1) * BLOCK, :] = kept_rows(mask_ref, p, slot, ones)
    large[-1].wait()
    pick_into(high_ref, low_ref, chosen_of(panels - 1, fill_ref), inv_ref, panels - 1)
    for copy in large[:-1]:
        copy.wait()


def pick_kernel(panel, *refs):
    *scalar_refs, inv_ref, high_ref, low_ref = refs
    pick_into(high_ref, low_ref, chosen_of(panel, *scalar_refs), inv_ref, panel)


def prior_kernel(panel, high_ref, low_ref, inv_ref, _, base_ref, own_ref, token_ref):
    token_ref[...] = jnp.zeros_like(token_ref)
    own_cols = own_ref.shape[0]
    own_at = pl.ds(pl.multiple_of(lax.axis_index("row") * own_cols, own_cols), own_cols)
    picked = (high_ref[...], low_ref[...])
    base_ref[...] = mm(picked, picked, TN)
    own_ref[...] = mm(inv_ref[panel, :, own_at], inv_ref[panel], TN)


class Plan(NamedTuple):
    early: tuple
    late: tuple


def at_row(table):
    value = jnp.int32(table[0])
    for i, entry in enumerate(table[1:], 1):
        value = jnp.where(lax.axis_index("row") == i, entry, value)
    return value


def slots_of(owners, rows):
    first = at_row(owners) * (rows // BLOCK)
    return [first + s for s in range(rows // BLOCK)]


def put_rows(mask_ref, panel, owners, part, out_ref, take):
    for s, slot in enumerate(slots_of(owners, part.shape[0])):
        kept = kept_rows(mask_ref, panel, slot, part[s * BLOCK : (s + 1) * BLOCK, :])
        out_ref[pl.ds(pl.multiple_of(slot * BLOCK, BLOCK), BLOCK), :] = take(kept)


def links_kernel(plan, mask_ref, *refs):
    count = len(plan.early) - 1
    parts, (*pick_refs, links_ref) = refs[:count], refs[count:]
    links_ref[...] = jnp.zeros_like(links_ref)
    for p in range(links_ref.shape[0]):
        pick = (pick_refs[2 * p][...], pick_refs[2 * p + 1][...])
        for owners, part in zip(plan.early[:-1], parts):
            put_rows(mask_ref, p, owners, part[p], links_ref.at[p], lambda kept: mm(kept, pick))


def kept_block(mask_ref, panel, owners, part):
    return jnp.concatenate(
        [
            kept_rows(mask_ref, panel, slot, part[s * BLOCK : (s + 1) * BLOCK, :])
            for s, slot in enumerate(slots_of(owners, part.shape[0]))
        ],
        0,
    )


def chosen_kernel(part, keep_ref, *refs):
    *pick_refs, out_ref = refs
    for p in range(out_ref.shape[0]):
        pick = (pick_refs[2 * p][...], pick_refs[2 * p + 1][...])
        out_ref[p] = mm(part[p], pick) * keep_ref[p]


def rest_kernel(owners, mask_ref, fill_ref, prior_ref, inv_ref, *refs):
    *parts, _, out_ref, map_ref = refs
    odd = (lax.axis_index("row") & 1) == 1
    for p in range(out_ref.shape[0]):
        part = parts[0][p] if len(parts) == 1 else jnp.where(odd, parts[1][p], parts[0][p])
        map_ref[...] = triangular_mm(kept_block(mask_ref, p, owners, part), inv_ref[p])
        rest, _ = order_of(chosen_of(p, fill_ref, prior_ref), map_ref.shape[1] // BLOCK)
        for t in range(len(rest) // 2):
            out_ref[p, :, t * LANES : (t + 1) * LANES] = two_blocks(
                tile_of(map_ref), rest[2 * t], rest[2 * t + 1]
            )


def segment_kernel(plan, panels, early_ref, second_ref, late_ref, *refs):
    base_refs, (links_t_ref, whole_ref, rows_ref) = refs[:panels], refs[panels:]
    size = links_t_ref.shape[1]
    rows = late_ref.shape[1]
    second_at, late_at = (
        pl.ds(pl.multiple_of(at_row(owners) * rows, rows), rows)
        for owners in (plan.early[-1], plan.late)
    )
    cov = link_t = None
    for p in range(panels - 1, -1, -1):
        rows_ref[p] = early_ref[p]
        rows_ref[p, second_at, :] = second_ref[p]
        rows_ref[p, late_at, :] = late_ref[p]
        own_t = rows_ref[p].T
        links_t_ref[p] = own_t
        if cov is None:
            cov, link_t = base_refs[p][...], own_t
        else:
            cov, link_t = carry_both(own_t, cov, link_t, base_refs[p][...])
    whole_ref[:size] = link_t
    whole_ref[size:] = cov


def maps_kernel(plan, mask_ref, inv_ref, *refs):
    *parts, maps_ref, token_ref, rows_ref = refs
    token_ref[...] = jnp.zeros_like(token_ref)
    rows_ref[...] = jnp.zeros_like(rows_ref)
    for p in range(inv_ref.shape[0]):
        for owners, part in zip(plan.early, parts):
            put_rows(mask_ref, p, owners, part[p], rows_ref, lambda kept: kept)
        maps_ref[p] = triangular_mm(rows_ref[...], inv_ref[p])


def chip_kernel(own_ref, other_ref, link_t_ref, cov_ref, packed_ref, half_t_ref):
    size = cov_ref.shape[0]
    lower = is_lower()
    own_t, other_t = own_ref[:size, :], other_ref[:size, :]
    own, other = own_ref[size:, :], other_ref[size:, :]
    cov, link_t = carry_both(
        jnp.where(lower, own_t, other_t),
        jnp.where(lower, other, own),
        jnp.where(lower, other_t, own_t),
        jnp.where(lower, own, other),
    )
    link_t_ref[...] = link_t
    cov_ref[...] = cov
    packed_ref[...] = own_half(pack(cov))
    half_t_ref[...] = own_half(link_t)


def merge_kernel(level, link_t_ref, cov_ref, *refs):
    got_t = from_halves(refs[0][...], refs[1][...])
    got = unpack(from_halves(refs[2][...], refs[3][...]))
    own_t, own = link_t_ref[...], cov_ref[...]
    lower = (lax.shift_right_logical(lax.axis_index("seg") // 2, level) & 1) == 0
    down_t = split(jnp.where(lower, own_t, got_t))
    cov = carry(down_t, jnp.where(lower, got, own), jnp.where(lower, own, got))
    refs[4][...] = own_half(pack(cov))
    if len(refs) > 5:
        link_t = mm(down_t, jnp.where(lower, got_t, own_t))
        refs[5][...] = own_half(link_t)
        refs[6][...] = link_t
        refs[7][...] = cov


def join_kernel(level, *refs):
    past_t, past, link_t, cov = (
        from_halves(refs[2 * i][...], refs[2 * i + 1][...]) for i in range(4)
    )
    chip = lax.axis_index("seg") // 2
    below = (lax.shift_right_logical(chip, level) & 1) == 0
    known = (chip & ((1 << level) - 1)) != (1 << level) - 1
    past_parts = split(past_t)
    joined = pack(carry(past_parts, unpack(cov), unpack(past)))
    joined_t = mm(past_parts, link_t)
    out_t = jnp.where(below, jnp.where(known, joined_t, link_t), past_t)
    out = jnp.where(below, jnp.where(known, joined, cov), past)
    for i, whole in enumerate((out_t, out)):
        half = whole.shape[0] // 2
        refs[8 + 2 * i][...] = own_half(whole)
        refs[9 + 2 * i][...] = jnp.where(is_lower(), whole[half:], whole[:half])


def prepare_kernel(plan, levels, panels, mask_ref, fill_ref, prior_ref, *refs):
    base_refs, own_refs, refs = refs[:panels], refs[panels : 2 * panels], refs[2 * panels :]
    (other_ref, maps_ref, links_t_ref, late_ref, rest_ref), refs = refs[:5], refs[5:]
    past_refs, refs = refs[: 4 * (levels > 1)], refs[4 * (levels > 1) :]
    left_high, left_low, right_high, right_low, const_ref, token_ref, scratch, map_ref, late_map_ref = refs
    token_ref[...] = jnp.zeros_like(token_ref)
    own_cols, width = own_refs[0].shape
    late_at = at_row(plan.late)
    size = base_refs[0].shape[0]
    row_at = lax.axis_index("row")
    rows = left_high.shape[0] // panels - own_cols
    row = lax.broadcasted_iota(jnp.int32, (size, size), 0)
    column = lax.broadcasted_iota(jnp.int32, (size, size), 1)
    eye = (row == column).astype(F32)
    other = other_ref[size:, :]
    lower = is_lower()
    if past_refs:
        chip = lax.axis_index("seg") // 2
        low = (1 << (levels - 1)) - 1
        known = (chip & low) != low
        past_t = from_halves(past_refs[0][...], past_refs[1][...])
        past = unpack(from_halves(past_refs[2][...], past_refs[3][...]))
        to_t = jnp.where(known, past_t, eye)
        gain = jnp.where(known, past, 0.0)
        other_t = split(other_ref[:size, :])
        to_t = jnp.where(lower, mm(other_t, to_t), to_t)
        gain = jnp.where(lower, carry(other_t, gain, other), gain)
    else:
        to_t = jnp.where(lower, other_ref[:size, :], eye)
        gain = jnp.where(lower, other, 0.0)
    own_at = pl.ds(pl.multiple_of(row_at * own_cols, own_cols), own_cols)
    own_rows = pl.ds(pl.multiple_of(row_at * rows, rows), rows)
    late_rows = pl.ds(pl.multiple_of(late_at * rows, rows), rows)
    for p in range(panels - 1, -1, -1):
        late_map_ref[:, :size] = late_ref[p]
        late_map_ref[:, size:] = rest_ref[p]
        _, place = order_of(chosen_of(p, fill_ref, prior_ref), width // BLOCK)
        map_ref[...] = maps_ref[p]
        for t in range(len(place) // 2):
            map_ref[late_rows, t * LANES : (t + 1) * LANES] = two_blocks(
                tile_of(late_map_ref), place[2 * t], place[2 * t + 1]
            )
        whole = split(map_ref[...])
        own_t = split(map_ref[:, own_at].T)
        scratch[:, :size] = to_t
        scratch[:, size:] = gain
        to_parts = split(to_t)
        cross = jnp.concatenate(
            [
                jnp.full((BLOCK, size), -mask_ref[p, slot].astype(F32))
                for slot in slots_of(tuple(range(size // rows)), rows)
            ],
            0,
        )
        left = jnp.concatenate([scratch[own_rows, :size] * cross, mm(own_t, to_parts)], 0)
        part = slice(p * left.shape[0], (p + 1) * left.shape[0])
        left_high[part, :], left_low[part, :] = split(left)
        right_high[p], right_low[p] = split(mm(to_parts, whole, TN))
        gains = jnp.concatenate([scratch[own_rows, size:] * cross, mm(own_t, gain)], 0)
        const = mm(gains, whole)
        const_ref[p, :rows, :] = const[:rows]
        const_ref[p, rows:, :] = const[rows:] + own_refs[p][...]
        if p > 0:
            link_t = split(links_t_ref[p])
            to_t = mm(link_t, to_t)
            gain = carry(link_t, gain, base_refs[p][...])


def finish_kernel(levels, after_ref, after_other_ref, *refs):
    left_high, left_low, right_high, right_low, const_ref, diag_hbm, off_hbm = refs[:7]
    diag_ref, off_ref, sems = refs[7:]
    panels, total, _ = const_ref.shape
    rows = off_ref.shape[1]
    chip = lax.axis_index("seg") // 2
    after = from_halves(after_ref[...], after_other_ref[...])
    after = unpack(jnp.where((chip & ((1 << levels) // 2)) == 0, after, 0.0))
    inner = split(mm((left_high[...], left_low[...]), after))
    copies = []
    for p in range(panels):
        part = slice(p * total, (p + 1) * total)
        right = (right_high[p], right_low[p])
        result = mm((inner[0][part], inner[1][part]), right) + const_ref[p]
        diag_ref[p] = result[rows:]
        off_ref[p] = result[:rows]
        copies.append(pltpu.make_async_copy(diag_ref.at[p], diag_hbm.at[p], sems.at[p, 0]))
        copies.append(pltpu.make_async_copy(off_ref.at[p], off_hbm.at[p], sems.at[p, 1]))
        copies[-2].start()
        copies[-1].start()
    for copy in copies:
        copy.wait()


def body(fill_blocks, fill_mask, inv_diag, factor_off):
    panels, width, _ = inv_diag.shape
    rows = factor_off.shape[1]
    seg_count = lax.axis_size("seg")
    row_count = lax.axis_size("row")
    size = rows * row_count
    own_cols = width // row_count
    slots = fill_blocks.shape[1]
    chosen_cols = slots * BLOCK
    chips = seg_count // 2
    half = size // 2

    def turn(x, axis, distance):
        count = lax.axis_size(axis)
        return lax.ppermute(x, axis, [(i, (i + distance) % count) for i in range(count)])

    pick = jax.ShapeDtypeStruct((width, chosen_cols), BF16)
    short = row_count == 4
    far = row_count // 2
    whose = [tuple((i - d) % row_count for i in range(row_count)) for d in range(row_count)]
    came = [d for d in range(row_count) if d != far]
    plan = Plan(tuple(whose[d] for d in came), whose[far])
    keeps = shape(panels, rows, chosen_cols)
    inv, high, low, keep, keep_second = call(
        functools.partial(load_kernel, (whose[1] if short else whose[far], plan.early[-1])),
        [shape(*inv_diag.shape), pick, pick, keeps, keeps],
        [],
        [],
        far=[fill_mask, fill_blocks, inv_diag],
        scratch=[
            pltpu.SMEM(fill_mask.shape, jnp.int32),
            pltpu.SMEM(fill_blocks.shape, jnp.int32),
            pltpu.SemaphoreType.DMA((panels + 2,)),
        ],
        name="load",
    )
    prior_fill = turn(fill_blocks, "seg", 1)
    picks, bases, priors = [], [], []
    for p in range(panels):
        high_low = [high, low]
        if p < panels - 1:
            high_low = call(
                functools.partial(pick_kernel, p),
                [pick, pick],
                [fill_blocks] if p else [fill_blocks, prior_fill],
                [inv],
                name="pick",
            )
        base, own_prior, token = call(
            functools.partial(prior_kernel, p),
            [shape(chosen_cols, chosen_cols), shape(own_cols, width), shape(1, 1, width)],
            [],
            [*high_low, inv],
            anywhere=[prior_fill],
            name="prior",
        )
        picks += high_low
        bases.append(base)
        priors.append(own_prior)
    ups, downs = [factor_off], [factor_off + token]
    for _ in range(row_count // 2 - short):
        ups.append(turn(ups[-1], "row", 1))
    for _ in range((row_count - 1) // 2):
        downs.append(turn(downs[-1], "row", -1))
    parts = ups[:far] + downs[:0:-1]
    (late,) = call(
        chosen_kernel,
        [shape(panels, rows, chosen_cols)],
        [],
        [ups[-1], keep, *picks],
        flops=96 * panels * rows * chosen_cols * width,
        name="chosen",
    )
    if short:
        late = turn(late, "row", 1)
    (links,) = call(
        functools.partial(links_kernel, plan),
        [shape(panels, size, size)],
        [fill_mask],
        [*parts[:-1], *picks],
        name="links",
    )
    (second,) = call(
        chosen_kernel,
        [shape(panels, rows, chosen_cols)],
        [],
        [parts[-1], keep_second, *picks],
        name="second",
    )
    links_t, own_whole = call(
        functools.partial(segment_kernel, plan, panels),
        [shape(panels, size, size), shape(2 * size, size)],
        [],
        [links, second, late, *bases],
        scratch=[pltpu.VMEM((panels, size, size), F32)],
        flops=18 * (panels - 1) * size**3,
        name="segment",
    )
    maps, maps_token = call(
        functools.partial(maps_kernel, plan),
        [shape(panels, size, width), shape(1, half)],
        [fill_mask],
        [inv, *parts],
        scratch=[pltpu.VMEM((size, width), F32)],
        flops=6 * panels * size * width * width,
        mib=24,
        name="maps",
    )
    swap = [(i, i ^ 1) for i in range(seg_count)]
    other_whole = lax.ppermute(own_whole, "seg", swap)
    half_packed = shape(5 * half // 4, half)
    half_link = shape(half, size)
    link_t, cov, send, send_t = call(
        chip_kernel,
        [shape(size, size), shape(size, size), half_packed, half_link],
        [],
        [own_whole, other_whole],
        flops=18 * size**3,
        name="chip",
    )
    held = [ups[-1], downs[-1]] if short else [ups[-1]]
    held_by = whose[far]
    if short:
        held_by = tuple(whose[-1][i] if i % 2 else whose[1][i] for i in range(row_count))
    (rest,) = call(
        functools.partial(rest_kernel, held_by),
        [shape(panels, rows, width - chosen_cols)],
        [fill_mask, fill_blocks, prior_fill],
        [inv, *held, send],
        scratch=[pltpu.VMEM((rows, width), F32)],
        flops=6 * panels * rows * width * width,
        mib=24,
        name="rest",
    )
    if short:
        rest = lax.ppermute(rest, "row", [(i, i ^ 1) for i in range(row_count)])
    past = None
    after = (jnp.zeros(half_packed.shape, F32),) * 2
    levels = (chips - 1).bit_length()
    prepared = None

    def prepare():
        total = rows + own_cols
        left = jax.ShapeDtypeStruct((panels * total, size), BF16)
        right = jax.ShapeDtypeStruct((panels, size, width), BF16)
        return call(
            functools.partial(prepare_kernel, plan, levels, panels),
            [left, left, right, right, shape(panels, total, width), shape(1, half)],
            [fill_mask, fill_blocks, prior_fill],
            [*bases, *priors, other_whole, maps, links_t, late, rest, *(past or ())],
            scratch=[
                pltpu.VMEM((size, width), F32),
                pltpu.VMEM((size, width), F32),
                pltpu.VMEM((rows, width), F32),
            ],
            flops=6 * panels * size * (total * size + size * width + total * width + 3 * size * size),
            mib=24,
            name="prepare",
        )

    for level in range(levels):
        partner = [(i, i ^ (2 << level)) for i in range(seg_count)]
        got = lax.ppermute(send, "seg", partner)
        if level == levels - 1:
            *prepared, token = prepare()
            got = got + token
            after = (got, lax.ppermute(got, "seg", swap))
            break
        got_t = lax.ppermute(send_t, "seg", partner)
        if level == 0:
            got = got + maps_token
        got = (got_t, lax.ppermute(got_t, "seg", swap), got, lax.ppermute(got, "seg", swap))
        outs = [half_packed]
        if level < levels - 2:
            outs += [half_link, shape(size, size), shape(size, size)]
        send, *more = call(
            functools.partial(merge_kernel, level), outs, [], [link_t, cov, *got],
            flops=18 * size**3, name="merge",
        )
        if more:
            send_t, link_t, cov = more
        if past is None:
            past = got
        else:
            past = call(
                functools.partial(join_kernel, level),
                [half_link, half_link, half_packed, half_packed],
                [],
                [*past, *got],
                flops=18 * size**3,
                name="join",
            )
    if prepared is None:
        *prepared, _ = prepare()
    diag, off = call(
        functools.partial(finish_kernel, levels),
        [shape(panels, own_cols, width), shape(panels, rows, width)],
        [],
        [*after, *prepared],
        out_far=True,
        scratch=[
            pltpu.VMEM((panels, own_cols, width), F32),
            pltpu.VMEM((panels, rows, width), F32),
            pltpu.SemaphoreType.DMA((panels, 2)),
        ],
        flops=6 * panels * (rows + own_cols) * size * (size + width),
        name="finish",
    )
    return diag, off


def solution(mesh):
    placed = (P("seg", None), P("seg", None), P("seg", None, None), P("seg", "row", None))
    return jax.shard_map(
        body,
        mesh=mesh,
        in_specs=placed,
        out_specs=(P("seg", "row", None), P("seg", "row", None)),
        check_vma=False,
    )
```
